32 devices in a mesh: seq: 8 (over z, y), batch: 4 (over x, core).
Axes of the slice: x: 2, y: 2, z: 4, core: 2. Of those that a mesh axis runs over, the one named last changes fastest.
Arguments:
- inputs: bfloat16 [4, 8192, 2048], P('batch', 'seq'), may hold values from -6 to 6
- input_map: bfloat16 [4, 8192, 128], P('batch', 'seq'), may hold values from -0.5 to 0.5
- output_map: bfloat16 [4, 8192, 128], P('batch', 'seq'), may hold values from -0.5 to 0.5
- step_raw: float32 [4, 32, 8192], P('batch', None, 'seq'), may hold values from -4.5 to 4.5
- step_bias: float32 [32], replicated, may hold values from -2 to 0
- decay_rate: float32 [32], replicated, may hold values from 3.0517578e-05 to 0.05
- skip_gain: float32 [32], replicated, may hold values from 0.5 to 1.5
- cotangent: bfloat16 [4, 8192, 2048], P('batch', 'seq'), may hold values from -6 to 6
Outputs:
- grad_inputs: bfloat16 [4, 8192, 2048], P('batch', 'seq')
- grad_input_map: float32 [4, 8192, 128], P('batch', 'seq')
- grad_output_map: float32 [4, 8192, 128], P('batch', 'seq')
- grad_step_raw: float32 [4, 32, 8192], P('batch', None, 'seq')
- grad_params: float32 [2, 32], replicated
- grad_decay_rate: float32 [32], replicated
The draws below stay inside these ranges and needn't reach their ends.
All inputs are finite; a program needn't handle non-finite values.
Results may differ from the reference program's by a relative error of at most 0.034.
Values sent between devices are 32-bit elements; how exact they have to be, the bound alone decides.
No kernel may reach another device: no remote copies, remote signals or barrier semaphores. Data moves between devices by JAX's collectives and lax.ppermute only.
A program may use at most 192 MiB of HBM per device.

```python
import math
import jax
import jax.numpy as jnp
from jax import lax

H = 32
P_SIZE = 64
N = 128
GROUP = 256
TOK_DEV = 1024
E = 2048
SEQLEN = 8192
SEQS = 4


def draw_step_raw(key, part):
    blocks = SEQLEN // TOK_DEV
    key_order = jax.random.fold_in(key, 11)
    key_jitter = jax.random.fold_in(key, 12)
    key_noise = jax.random.fold_in(key, 13)
    order = jax.vmap(lambda k: jax.random.permutation(k, blocks))(jax.random.split(key_order, SEQS))
    level = -2.0 + 4.0 * order.astype(jnp.float32) / max(blocks - 1, 1)
    jitter = jax.random.uniform(key_jitter, (SEQS, H, blocks), jnp.float32, -0.5, 0.5)
    offset = jnp.repeat(level[:, None, :] + jitter, TOK_DEV, axis=2)
    noise = jnp.clip(0.5 * jax.random.normal(key_noise, (SEQS, H, SEQLEN), jnp.float32), -2.0, 2.0)
    return (offset + noise).astype(jnp.float32)


def steps_of(rng, extent, cuts, least, high):
    def one(position, blocks):
        draws = jax.random.uniform(jax.random.fold_in(jax.random.fold_in(rng, 6), position), (blocks,), jnp.float32, least / len(cuts), high / len(cuts))
        return jnp.repeat(jnp.exp(draws), extent[position] // blocks).reshape((-1,) + (1,) * (len(extent) - position - 1))

    loudness = one(*cuts[0])
    for cut in cuts[1:]:
        loudness = loudness * one(*cut)
    return loudness


def normal_values(own_key, shape, spread, limit, cuts=(), kind=jnp.bfloat16):
    entries = spread * jax.random.normal(own_key, shape, jnp.float32)
    if cuts:
        entries = entries * steps_of(own_key, shape, cuts, -0.22, 0.18)
    return jnp.clip(entries, -limit, limit).astype(kind)


def setup_inputs(seed: int = 0) -> dict:
    key_list = jax.random.split(jax.random.key(seed), 9)
    return {
        "inputs": normal_values(key_list[0], (SEQS, SEQLEN, E), 1.0, 6.0, ((0, 4), (1, 8))),
        "input_map": normal_values(key_list[1], (SEQS, SEQLEN, N), N ** -0.5, 0.5, ((0, 4), (1, 8))),
        "output_map": normal_values(key_list[2], (SEQS, SEQLEN, N), N ** -0.5, 0.5, ((0, 4), (1, 8))),
        "step_raw": draw_step_raw(jax.random.fold_in(key_list[8], 71), 0),
        "step_bias": jnp.clip(jax.random.uniform(key_list[4], (H,), jnp.float32, -2.0, 0.0), -2.0, 0.0),
        "decay_rate": jnp.clip(jnp.exp(jax.random.uniform(key_list[5], (H,), jnp.float32, math.log(3.0517578125e-05), math.log(0.05))), 3.0517578125e-05, 0.05),
        "skip_gain": jnp.clip(jax.random.uniform(key_list[6], (H,), jnp.float32, 0.5, 1.5), 0.5, 1.5),
        "cotangent": normal_values(key_list[7], (SEQS, SEQLEN, E), 1.0, 6.0, ((0, 4), (1, 8))),
    }


def block_step(state, items, skip_gain):
    xc, bc, cc, stepc, logc = items
    width = xc.shape[0]
    cum = jnp.cumsum(logc, axis=1)
    rows = lax.broadcasted_iota(jnp.int32, (width, width), 0)
    cols = lax.broadcasted_iota(jnp.int32, (width, width), 1)
    lower = cols <= rows
    gap = jnp.where(lower[None], cum[:, :, None] - cum[:, None, :], -1e+30)
    decay = jnp.exp(gap)
    scores = jnp.einsum('tn,sn->ts', cc, bc, preferred_element_type=jnp.float32)
    weights = (scores[None] * decay * stepc[:, None, :]).astype(jnp.bfloat16)
    inner = jnp.einsum('hts,shp->thp', weights, xc, preferred_element_type=jnp.float32)
    carried = jnp.einsum('tn,hpn->thp', cc, state.astype(jnp.bfloat16), preferred_element_type=jnp.float32) * jnp.exp(cum).T[:, :, None]
    output = inner + carried + skip_gain[None, :, None] * xc.astype(jnp.float32)
    tail = jnp.exp(cum[:, -1:] - cum) * stepc
    scaled = (xc.astype(jnp.float32) * tail.T[:, :, None]).astype(jnp.bfloat16)
    fresh = jnp.einsum('shp,sn->hpn', scaled, bc, preferred_element_type=jnp.float32)
    new_state = jnp.exp(cum[:, -1])[:, None, None] * state + fresh
    return (new_state, output.astype(jnp.bfloat16))

def scan_forward(xb, bb, cb, raw, step_bias, decay_rate, skip_gain, start_state):
    length, heads, head_size = xb.shape
    states = bb.shape[1]
    blocks = length // GROUP
    step = jax.nn.softplus(raw + step_bias[:, None])
    logd = -decay_rate[:, None] * step
    xs = xb.reshape(blocks, GROUP, heads, head_size)
    bs = bb.reshape(blocks, GROUP, states)
    cs = cb.reshape(blocks, GROUP, states)
    steps = step.reshape(heads, blocks, GROUP).transpose(1, 0, 2)
    logs = logd.reshape(heads, blocks, GROUP).transpose(1, 0, 2)
    body_fn = jax.checkpoint(lambda s, it: block_step(s, it, skip_gain))
    end_state, outs = lax.scan(body_fn, start_state, (xs, bs, cs, steps, logs))
    return (outs.reshape(length, heads, head_size), end_state)

def reference(inputs, input_map, output_map, step_raw, step_bias, decay_rate, skip_gain, cotangent):

    def one_sequence(items):
        xs, bs, cs, raw, dys = items
        length = xs.shape[0]
        xb = xs.reshape(length, H, P_SIZE)
        dyb = dys.reshape(length, H, P_SIZE)
        zero_state = jnp.zeros((H, P_SIZE, N), jnp.float32)

        def forward(xv, bv, cv, rv, biasv, ratev, skipv):
            return scan_forward(xv, bv, cv, rv, biasv, ratev, skipv, zero_state)[0]
        outs, pull = jax.vjp(forward, xb, bs, cs, raw, step_bias, decay_rate, skip_gain)
        grads = pull(dyb)
        params = jnp.stack([grads[4], grads[5], grads[6]])
        return (grads[0].reshape(length, H * P_SIZE).astype(jnp.bfloat16), grads[1].astype(jnp.float32), grads[2].astype(jnp.float32), grads[3], params)
    gx, gb, gc, gr, gp = lax.map(one_sequence, (inputs, input_map, output_map, step_raw, cotangent))
    scale = 1.0 / math.sqrt(SEQS * SEQLEN)
    summed = lax.optimization_barrier(jnp.sum(gp, axis=0)) * scale
    return (gx, gb, gc, gr, jnp.stack([summed[0], summed[2]]), summed[1])
```

```python
import functools
import math

import jax
import jax.numpy as jnp
from jax import lax
from jax.experimental import pallas as pl
from jax.experimental.pallas import tpu as pltpu
from jax.sharding import PartitionSpec as P

GROUP = 256
PARTS = 2
VMEM_LIMIT = 48 * 1024 * 1024
F32 = jnp.float32
BF16 = jnp.bfloat16


def dot(a, b, dims):
    return lax.dot_general(a, b, (dims, ((), ())), preferred_element_type=F32)


NN = ((1,), (0,))
NT = ((1,), (1,))
TN = ((0,), (0,))


def split2(a):
    hi = a.astype(BF16).astype(F32)
    return hi, a - hi


def head_matrix(heads, width):
    size = width // heads
    row = lax.broadcasted_iota(jnp.int32, (heads, width), 0)
    col = lax.broadcasted_iota(jnp.int32, (heads, width), 1)
    return ((col >= row * size) & (col < (row + 1) * size)).astype(F32)


def spread(rows, twice):
    hi, lo = split2(rows)
    return dot(jnp.concatenate([hi, lo], axis=0).astype(BF16), twice, TN)


def head_sums(values, member):
    hi, lo = split2(values)
    return dot(member, hi.astype(BF16), NT) + dot(member, lo.astype(BF16), NT)


def running(rows, upper):
    hi, rest = split2(rows)
    mid, lo = split2(rest)
    k = rows.shape[0]
    out = dot(jnp.concatenate([hi, mid, lo], axis=0).astype(BF16), upper, NN)
    return out[:k] + out[k : 2 * k] + out[2 * k :]


def triangle(width, lower):
    row = lax.broadcasted_iota(jnp.int32, (width, width), 0)
    col = lax.broadcasted_iota(jnp.int32, (width, width), 1)
    return (row >= col) if lower else (row <= col)


def softplus(v):
    return jnp.maximum(v, 0.0) + jnp.log1p(jnp.exp(-jnp.abs(v)))


def local_kernel(
    at_ref, x_ref, dy_ref, b_ref, c_ref, raw_ref, bias_ref, rate_ref, out_ref, state, grad, decay
):
    k = pl.program_id(0)
    heads = raw_ref.shape[1]
    width = x_ref.shape[1]
    states = b_ref.shape[1]
    member = head_matrix(heads, width)
    twice = jnp.concatenate([member, member], axis=0).astype(BF16)

    @pl.when(k == 0)
    def _():
        state[...] = jnp.zeros_like(state)
        grad[...] = jnp.zeros_like(grad)
        decay[...] = jnp.ones_like(decay)

    step = softplus(raw_ref[0] + bias_ref[0])
    cum = running(-rate_ref[0] * step, triangle(GROUP, False).astype(BF16))
    total = cum[:, GROUP - 1 :]
    scaled_x = x_ref[...].astype(F32) * spread(jnp.exp(total - cum) * step, twice)
    scaled_dy = dy_ref[...].astype(F32) * spread(jnp.exp(cum), twice)
    whole = spread(jnp.broadcast_to(jnp.exp(total), (heads, 8)), twice)
    before = decay[...]
    state[...] = whole[:1] * state[...] + dot(b_ref[...], scaled_x.astype(BF16), TN)
    grad[...] += before[:1] * dot(c_ref[...], scaled_dy.astype(BF16), TN)
    decay[...] = before * whole

    @pl.when(k == pl.num_programs(0) - 1)
    def _():
        out_ref[:states] = state[...]
        out_ref[states : 2 * states] = grad[...]
        out_ref[2 * states :] = decay[...]


def local_states(at, x, dy, b, c, raw, bias, rate):
    length, channels = x.shape
    pieces, heads, _ = raw.shape
    width = channels // pieces
    states = b.shape[1]
    grid_spec = pltpu.PrefetchScalarGridSpec(
        num_scalar_prefetch=1,
        grid=(length // GROUP,),
        in_specs=[
            pl.BlockSpec((GROUP, width), lambda k, at: (k, at[0])),
            pl.BlockSpec((GROUP, width), lambda k, at: (k, at[0])),
            pl.BlockSpec((GROUP, states), lambda k, at: (k, 0)),
            pl.BlockSpec((GROUP, states), lambda k, at: (k, 0)),
            pl.BlockSpec((1, heads, GROUP), lambda k, at: (at[0], 0, k)),
            pl.BlockSpec((1, heads, 1), lambda k, at: (at[0], 0, 0)),
            pl.BlockSpec((1, heads, 1), lambda k, at: (at[0], 0, 0)),
        ],
        out_specs=pl.BlockSpec((2 * states + 8, width), lambda k, at: (0, 0)),
        scratch_shapes=[
            pltpu.VMEM((states, width), F32),
            pltpu.VMEM((states, width), F32),
            pltpu.VMEM((8, width), F32),
        ],
    )
    return pl.pallas_call(
        local_kernel,
        grid_spec=grid_spec,
        out_shape=jax.ShapeDtypeStruct((2 * states + 8, width), F32),
        compiler_params=pltpu.CompilerParams(vmem_limit_bytes=VMEM_LIMIT),
        cost_estimate=pl.CostEstimate(
            flops=4 * length * width * states,
            bytes_accessed=4 * length * width + 8 * states * width,
            transcendentals=0,
        ),
        name="local_states",
    )(at, x, dy, b, c, raw, bias, rate)


def grads_kernel(first, *refs):
    y_ref, x_ref, dy_ref, b_ref, c_ref, raw_ref, bias_ref, rate_ref, skip_ref, mine_ref, other_ref = refs[:11]
    refs = refs[11:]
    if not first:
        dc_in, db_in = refs[:2]
        refs = refs[4:]
    dx_ref, dc_ref, db_ref, draw_ref, par_ref, left, right, carried, gains, sums, tail = refs
    g = pl.program_id(0)
    heads = raw_ref.shape[1]
    width = x_ref.shape[1]
    states = b_ref.shape[1]
    length = x_ref.shape[0]
    blocks = length // GROUP
    member = head_matrix(heads, width)
    twice = jnp.concatenate([member, member], axis=0).astype(BF16)
    member = member.astype(BF16)
    upper = triangle(GROUP, False)
    lower = triangle(GROUP, True)
    upper_ones = upper.astype(BF16)
    lower_ones = lower.astype(BF16)
    rows = [slice(n * GROUP, (n + 1) * GROUP) for n in range(blocks)]

    @pl.when(g == 0)
    def _():
        for n in range(blocks):
            b, c = b_ref[rows[n], :], c_ref[rows[n], :]
            left[n, :, :GROUP] = jnp.where(lower, dot(c, b, NT), 0.0).astype(BF16)
            left[n, :, GROUP:] = c
            right[n, :, :GROUP] = jnp.where(upper, dot(b, c, NT), 0.0).astype(BF16)
            right[n, :, GROUP:] = b
        sums[...] = jnp.zeros_like(sums)
        tail[...] = jnp.zeros_like(tail)

    raw = raw_ref[0] + bias_ref[0]
    rate = rate_ref[0]
    step = softplus(raw)
    gate = 1.0 / (1.0 + jnp.exp(-raw))
    logs = -rate * step
    cums = [running(logs[:, rows[n]], upper_ones) for n in range(blocks)]
    totals = [cum[:, GROUP - 1 :] for cum in cums]
    own = g == y_ref[0]
    state = jnp.where(own, mine_ref[:states], other_ref[:states])
    grad = jnp.where(own, mine_ref[states:], other_ref[states:])
    wholes = [
        spread(jnp.broadcast_to(jnp.exp(totals[n]), (heads, 8)), twice)[:1] for n in range(blocks)
    ]
    ends = []
    for n in range(blocks):
        weight = spread(jnp.exp(totals[n] - cums[n]) * step[:, rows[n]], twice)
        gains[n] = weight
        scaled = (x_ref[rows[n], :].astype(F32) * weight).astype(BF16)
        carried[n, :GROUP] = scaled
        state = wholes[n] * state
        carried[n, GROUP:] = state.astype(BF16)
        state = state + dot(b_ref[rows[n], :], scaled, TN)
        ends.append(state)
    skip = jnp.max(spread(jnp.broadcast_to(skip_ref[0], (heads, 8)), twice), axis=0, keepdims=True)
    direct = jnp.zeros((8, width), F32)
    bias_sum = jnp.zeros((heads, 1), F32)
    rate_sum = jnp.zeros((heads, 1), F32)
    for n in reversed(range(blocks)):
        dy = dy_ref[rows[n], :].astype(F32)
        x = x_ref[rows[n], :].astype(F32)
        direct = direct + jnp.sum((dy * x).reshape(GROUP // 8, 8, width), axis=0)
        scaled_dy = (dy * spread(jnp.exp(cums[n] - totals[n]), twice)).astype(BF16)
        scaled_x = carried[n, :GROUP]
        grad_low = grad.astype(BF16)
        forward = dot(left[n], carried[n], NN)
        backward = dot(right[n], jnp.concatenate([scaled_dy, grad_low], axis=0), NN)
        dx_ref[rows[n], :] = (gains[n] * backward + skip * dy).astype(dx_ref.dtype)
        u = head_sums(scaled_dy.astype(F32) * forward, member)
        v = head_sums(scaled_x.astype(F32) * backward, member)
        edge = head_sums(
            jnp.broadcast_to(jnp.sum(ends[n] * grad, axis=0, keepdims=True), (8, width)), member
        )
        slope = running(u - v, lower_ones) + edge[:, :1]
        here = step[:, rows[n]]
        draw = (v / here - rate * slope) * gate[:, rows[n]]
        draw_ref[0, :, rows[n]] = draw
        bias_sum = bias_sum + jnp.sum(draw, axis=1, keepdims=True)
        rate_sum = rate_sum - jnp.sum(here * slope, axis=1, keepdims=True)
        sums[n] += dot(scaled_dy, carried[n], NT)
        tail[n] += dot(scaled_x, grad_low, NT)
        grad = wholes[n] * (grad + dot(c_ref[rows[n], :], scaled_dy, TN))
    skip_sum = jnp.sum(head_sums(direct, member), axis=1, keepdims=True)
    lane = lax.broadcasted_iota(jnp.int32, (heads, 128), 1)
    par_ref[0] = jnp.where(
        lane == 0, bias_sum, jnp.where(lane == 1, skip_sum, jnp.where(lane == 2, rate_sum, 0.0))
    )

    @pl.when(g == pl.num_programs(0) - 1)
    def _():
        for n in range(blocks):
            pair = jnp.where(lower, sums[n, :, :GROUP], 0.0).astype(BF16)
            dc = dot(pair, b_ref[rows[n], :], NN) + sums[n, :, GROUP:]
            db = dot(pair, c_ref[rows[n], :], TN) + tail[n]
            if not first:
                dc = dc + dc_in[rows[n], :]
                db = db + db_in[rows[n], :]
            dc_ref[rows[n], :] = dc
            db_ref[rows[n], :] = db


def local_grads(part, y, x, dy, b, c, raw, bias, rate, skip, mine, other, before):
    length, channels = x.shape
    pieces, heads, _ = raw.shape
    width = channels // pieces
    states = b.shape[1]
    blocks = length // GROUP
    half = pieces // 2
    first = before is None
    place = lambda g, y: g * half + part
    columns = pl.BlockSpec((length, width), lambda g, y: (0, place(g, y)))
    maps = pl.BlockSpec((length, states), lambda g, y: (0, 0))
    line = pl.BlockSpec((1, heads, 1), lambda g, y: (place(g, y), 0, 0))
    lines = pl.BlockSpec((1, heads, length), lambda g, y: (place(g, y), 0, 0))
    held = pl.BlockSpec((2 * states, width), lambda g, y: (0, 0))
    anywhere = pl.BlockSpec(memory_space=pl.ANY)
    in_specs = [columns, columns, maps, maps, lines, line, line, line, held, held]
    args = [x, dy, b, c, raw, bias, rate, skip, mine, other]
    aliases = {}
    if not first:
        dx, dc, db, draw = before
        args += [dc, db, dx, draw]
        in_specs += [maps, maps, anywhere, anywhere]
        aliases = {13: 0, 14: 3}
    grid_spec = pltpu.PrefetchScalarGridSpec(
        num_scalar_prefetch=1,
        grid=(2,),
        in_specs=in_specs,
        out_specs=[
            columns,
            maps,
            maps,
            lines,
            pl.BlockSpec((1, heads, 128), lambda g, y: (g, 0, 0)),
        ],
        scratch_shapes=[
            pltpu.VMEM((blocks, GROUP, GROUP + states), BF16),
            pltpu.VMEM((blocks, GROUP, GROUP + states), BF16),
            pltpu.VMEM((blocks, GROUP + states, width), BF16),
            pltpu.VMEM((blocks, GROUP, width), F32),
            pltpu.VMEM((blocks, GROUP, GROUP + states), F32),
            pltpu.VMEM((blocks, GROUP, states), F32),
        ],
    )
    return pl.pallas_call(
        functools.partial(grads_kernel, first),
        grid_spec=grid_spec,
        out_shape=[
            jax.ShapeDtypeStruct((length, channels), BF16),
            jax.ShapeDtypeStruct((length, states), F32),
            jax.ShapeDtypeStruct((length, states), F32),
            jax.ShapeDtypeStruct((pieces, heads, length), F32),
            jax.ShapeDtypeStruct((2, heads, 128), F32),
        ],
        input_output_aliases=aliases,
        compiler_params=pltpu.CompilerParams(vmem_limit_bytes=VMEM_LIMIT),
        cost_estimate=pl.CostEstimate(
            flops=24 * length * width * (GROUP + states),
            bytes_accessed=12 * length * width,
            transcendentals=0,
        ),
        name="local_grads",
    )(y, *args)


def entering(sent, kept, states):
    size = lax.axis_size("seq")
    pairs = size // 2
    index = lax.axis_index("seq")
    place, second = index // 2, index % 2 == 1
    swap = [(i, i ^ 1) for i in range(size)]
    got = lax.ppermute(sent, "seq", swap)

    def parts(a):
        return a[:states], a[states : 2 * states], a[2 * states : 2 * states + 1]

    (own_l, own_k, own_d), (got_l, got_k, got_d) = parts(kept), parts(got)
    l1, k1, d1 = [jnp.where(second, b, a) for a, b in ((own_l, got_l), (own_k, got_k), (own_d, got_d))]
    l2, k2, d2 = [jnp.where(second, a, b) for a, b in ((own_l, got_l), (own_k, got_k), (own_d, got_d))]
    whole_l = d2 * l1 + l2
    whole_k = k1 + d1 * k2
    whole_d = d1 * d2
    start = jnp.zeros_like(whole_l)
    end = jnp.zeros_like(whole_k)
    for hop in range(1, pairs):
        message = jnp.where(place == hop - 1, whole_d * start + whole_l, whole_d * end + whole_k)
        route = []
        for y in range(2):
            route.append((2 * (hop - 1) + y, 2 * hop + y))
            route.append((2 * (pairs - hop) + y, 2 * (pairs - hop - 1) + y))
        arrived = lax.ppermute(message, "seq", route)
        start = jnp.where(place == hop, arrived, start)
        end = jnp.where(place == pairs - 1 - hop, arrived, end)
    for_first = jnp.concatenate([start, k2 + d2 * end], axis=0)
    for_second = jnp.concatenate([d1 * start + l1, end], axis=0)
    mine = jnp.where(second, for_second, for_first)
    other = lax.ppermute(jnp.where(second, for_first, for_second), "seq", swap)
    return mine, other


def shards(inputs, input_map, output_map, step_raw, step_bias, decay_rate, skip_gain, cotangent):
    length, channels = inputs.shape[1:]
    heads = step_raw.shape[1]
    states = input_map.shape[2]
    pieces = 2 * PARTS
    group = heads // pieces
    x, b, c, dy = inputs[0], input_map[0], output_map[0], cotangent[0]
    raw = step_raw[0].reshape(pieces, group, length)
    bias = step_bias.reshape(pieces, group, 1)
    rate = decay_rate.reshape(pieces, group, 1)
    skip = skip_gain.reshape(pieces, group, 1)
    y = lax.axis_index("seq") % 2

    def local(half, part):
        at = jnp.reshape(half * PARTS + part, (1,)).astype(jnp.int32)
        return local_states(at, x, dy, b, c, raw, bias, rate)

    sent = [local(1 - y, part) for part in range(PARTS)]
    kept = [local(y, part) for part in range(PARTS)]
    met = [entering(sent[part], kept[part], states) for part in range(PARTS)]
    here = jnp.reshape(y, (1,)).astype(jnp.int32)
    before = None
    params = []
    for part in range(PARTS):
        mine, other = met[part]
        *before, par = local_grads(
            part, here, x, dy, b, c, raw, bias, rate, skip, mine, other, before
        )
        params.append(par[:, :, :3])
    dx, dc, db, draw = before
    params = jnp.stack(params, axis=1).reshape(heads, 3).T
    total_tokens = length * lax.axis_size("seq") * lax.axis_size("batch")
    summed = lax.psum(params, ("seq", "batch")) * (1.0 / math.sqrt(total_tokens))
    return (
        dx[None],
        db[None],
        dc[None],
        draw.reshape(heads, length)[None],
        summed[:2],
        summed[2],
    )


def solution(mesh):
    in_specs = (
        P("batch", "seq", None),
        P("batch", "seq", None),
        P("batch", "seq", None),
        P("batch", None, "seq"),
        P(),
        P(),
        P(),
        P("batch", "seq", None),
    )
    out_specs = (
        P("batch", "seq", None),
        P("batch", "seq", None),
        P("batch", "seq", None),
        P("batch", None, "seq"),
        P(),
        P(),
    )
    return jax.shard_map(shards, mesh=mesh, in_specs=in_specs, out_specs=out_specs, check_vma=False)
```

```python
import functools
import math

import jax
import jax.numpy as jnp
from jax import lax
from jax.experimental import pallas as pl
from jax.experimental.pallas import tpu as pltpu
from jax.sharding import PartitionSpec as P

GROUP = 256
PARTS = 2
VMEM_LIMIT = 61 * 1024 * 1024
F32 = jnp.float32
BF16 = jnp.bfloat16


def dot(a, b, dims):
    return lax.dot_general(a, b, (dims, ((), ())), preferred_element_type=F32)


NN = ((1,), (0,))
NT = ((1,), (1,))
TN = ((0,), (0,))


def split2(a):
    hi = a.astype(BF16).astype(F32)
    return hi, a - hi


def head_matrix(heads, width):
    size = width // heads
    row = lax.broadcasted_iota(jnp.int32, (heads, width), 0)
    col = lax.broadcasted_iota(jnp.int32, (heads, width), 1)
    return ((col >= row * size) & (col < (row + 1) * size)).astype(F32)


def spread(rows, twice):
    hi, lo = split2(rows)
    return dot(jnp.concatenate([hi, lo], axis=0).astype(BF16), twice, TN)


def head_sums(values, member):
    hi, lo = split2(values)
    return dot(member, hi.astype(BF16), NT) + dot(member, lo.astype(BF16), NT)


def running(rows, upper):
    hi, rest = split2(rows)
    mid, lo = split2(rest)
    k = rows.shape[0]
    out = dot(jnp.concatenate([hi, mid, lo], axis=0).astype(BF16), upper, NN)
    return out[:k] + out[k : 2 * k] + out[2 * k :]


def triangle(width, lower):
    row = lax.broadcasted_iota(jnp.int32, (width, width), 0)
    col = lax.broadcasted_iota(jnp.int32, (width, width), 1)
    return (row >= col) if lower else (row <= col)


def softplus(v):
    return jnp.maximum(v, 0.0) + jnp.log1p(jnp.exp(-jnp.abs(v)))


def column(line, piece, heads):
    shape = (heads, line.shape[1])
    row = lax.broadcasted_iota(jnp.int32, shape, 0)
    col = lax.broadcasted_iota(jnp.int32, shape, 1)
    return jnp.sum(jnp.where(col == row + piece * heads, line, 0.0), axis=1, keepdims=True)


def block_sums(logs, blocks):
    heads = logs.shape[0]
    ones = triangle(GROUP, False).astype(BF16)
    stacked = jnp.concatenate([logs[:, n * GROUP : (n + 1) * GROUP] for n in range(blocks)], axis=0)
    cums = running(stacked, ones)
    return [cums[n * heads : (n + 1) * heads] for n in range(blocks)]


def local_kernel(
    at_ref, x_ref, dy_ref, b_ref, c_ref, raw_ref, bias_ref, rate_ref, *refs
):
    outs, (bt, ct) = refs[:-2], refs[-2:]
    g = pl.program_id(0)
    heads = raw_ref.shape[1]
    length, width = x_ref.shape
    states = b_ref.shape[1]
    blocks = length // GROUP
    piece = at_ref[0] + g
    member = head_matrix(heads, width)
    twice = jnp.concatenate([member, member], axis=0).astype(BF16)

    @pl.when(g == 0)
    def _():
        bt[...] = b_ref[...].T
        ct[...] = c_ref[...].T

    step = softplus(raw_ref[0] + column(bias_ref[...], piece, heads))
    cums = block_sums(-column(rate_ref[...], piece, heads) * step, blocks)
    total = jnp.zeros((heads, 1), F32)
    for n in range(blocks):
        cums[n] = cums[n] + total
        total = cums[n][:, GROUP - 1 :]
    state = jnp.zeros((states, width), F32)
    grad = jnp.zeros((states, width), F32)
    for n in range(blocks):
        rows = slice(n * GROUP, (n + 1) * GROUP)
        weight = spread(jnp.exp(total - cums[n]) * step[:, rows], twice)
        scaled_x = (x_ref[rows, :].astype(F32) * weight).astype(BF16)
        state = state + dot(bt[:, rows], scaled_x, NN)
        scaled_dy = (dy_ref[rows, :].astype(F32) * spread(jnp.exp(cums[n]), twice)).astype(BF16)
        grad = grad + dot(ct[:, rows], scaled_dy, NN)
    decay = spread(jnp.broadcast_to(jnp.exp(total), (heads, 8)), twice)
    for k, out_ref in enumerate(outs):

        @pl.when(g == k)
        def _():
            out_ref[:states] = state
            out_ref[states : 2 * states] = grad
            out_ref[2 * states :] = decay


def local_states(at, x, dy, b, c, raw, bias, rate):
    length, channels = x.shape
    pieces, heads, _ = raw.shape
    width = channels // pieces
    states = b.shape[1]
    columns = pl.BlockSpec((length, width), lambda g, at: (0, at[0] + g))
    maps = pl.BlockSpec((length, states), lambda g, at: (0, 0))
    line = pl.BlockSpec(bias.shape, lambda g, at: (0, 0))
    grid_spec = pltpu.PrefetchScalarGridSpec(
        num_scalar_prefetch=1,
        grid=(PARTS,),
        in_specs=[
            columns,
            columns,
            maps,
            maps,
            pl.BlockSpec((1, heads, length), lambda g, at: (at[0] + g, 0, 0)),
            line,
            line,
        ],
        out_specs=[pl.BlockSpec((2 * states + 8, width), lambda g, at: (0, 0))] * PARTS,
        scratch_shapes=[
            pltpu.VMEM((states, length), BF16),
            pltpu.VMEM((states, length), BF16),
        ],
    )
    return pl.pallas_call(
        local_kernel,
        grid_spec=grid_spec,
        out_shape=[jax.ShapeDtypeStruct((2 * states + 8, width), F32)] * PARTS,
        compiler_params=pltpu.CompilerParams(vmem_limit_bytes=VMEM_LIMIT),
        cost_estimate=pl.CostEstimate(
            flops=8 * PARTS * length * width * states,
            bytes_accessed=4 * PARTS * length * width,
            transcendentals=0,
        ),
        name="local_states",
    )(at, x, dy, b, c, raw, bias, rate)


def grads_kernel(first, scale, part, half, *refs):
    y_ref, x_ref, dy_ref, b_ref, c_ref, raw_ref, bias_ref, rate_ref, skip_ref, mine_ref, other_ref = refs[:11]
    refs = refs[11:]
    if not first:
        dc_in, db_in, par_in = refs[:3]
        refs = refs[5:]
    dx_ref, dc_ref, db_ref, draw_ref, par_ref, left, right, carried, gains, sums, tail, bt, ct = refs
    g = pl.program_id(0)
    heads = raw_ref.shape[1]
    width = x_ref.shape[1]
    states = b_ref.shape[1]
    length = x_ref.shape[0]
    blocks = length // GROUP
    piece = g * half + part
    member = head_matrix(heads, width)
    twice = jnp.concatenate([member, member], axis=0).astype(BF16)
    row = lax.broadcasted_iota(jnp.int32, (3 * width, 128), 0)
    col = lax.broadcasted_iota(jnp.int32, (3 * width, 128), 1)
    size = width // heads
    low = jnp.where(row < width, row, jnp.where(row < 2 * width, row - width, row - 2 * width))
    want = jnp.where(row < 2 * width, col, col - heads)
    adder = ((low >= want * size) & (low < (want + 1) * size)).astype(BF16)
    upper = triangle(GROUP, False)
    lower = triangle(GROUP, True)
    lower_ones = lower.astype(BF16)
    rows = [slice(n * GROUP, (n + 1) * GROUP) for n in range(blocks)]

    @pl.when(g == 0)
    def _():
        bt[...] = b_ref[...].T
        ct[...] = c_ref[...].T
        for n in range(blocks):
            b, c = b_ref[rows[n], :], c_ref[rows[n], :]
            left[n, :, :GROUP] = jnp.where(lower, dot(c, b, NT), 0.0).astype(BF16)
            left[n, :, GROUP:] = c
            right[n, :, :GROUP] = jnp.where(upper, dot(b, c, NT), 0.0).astype(BF16)
            right[n, :, GROUP:] = b
        sums[...] = jnp.zeros_like(sums)
        tail[...] = jnp.zeros_like(tail)
        par_ref[...] = jnp.zeros_like(par_ref) if first else par_in[...]

    raw = raw_ref[0] + column(bias_ref[...], piece, heads)
    rate = column(rate_ref[...], piece, heads)
    step = softplus(raw)
    gate = 1.0 / (1.0 + jnp.exp(-raw))
    cums = block_sums(-rate * step, blocks)
    totals = [cum[:, GROUP - 1 :] for cum in cums]
    own = g == y_ref[0]
    state = jnp.where(own, mine_ref[:states], other_ref[:states])
    grad = jnp.where(own, mine_ref[states:], other_ref[states:])
    gathered = jnp.concatenate(
        [jnp.exp(t) for t in totals] + [column(skip_ref[...], piece, heads)] * (8 - blocks), axis=1
    )
    gathered = spread(gathered, twice)
    wholes = [gathered[n : n + 1] for n in range(blocks)]
    skip = gathered[blocks : blocks + 1]
    ends = []
    for n in range(blocks):
        weight = spread(jnp.exp(totals[n] - cums[n]) * step[:, rows[n]], twice)
        gains[n] = weight
        scaled = (x_ref[rows[n], :].astype(F32) * weight).astype(BF16)
        carried[n, :GROUP] = scaled
        state = wholes[n] * state
        carried[n, GROUP:] = state.astype(BF16)
        state = state + dot(bt[:, rows[n]], scaled, NN)
        ends.append(state)
    direct = jnp.zeros((8, width), F32)
    bias_sum = jnp.zeros((heads, 1), F32)
    rate_sum = jnp.zeros((heads, 1), F32)
    for n in reversed(range(blocks)):
        dy = dy_ref[rows[n], :].astype(F32)
        x = x_ref[rows[n], :].astype(F32)
        direct = direct + jnp.sum((dy * x).reshape(GROUP // 8, 8, width), axis=0)
        scaled_dy = (dy * spread(jnp.exp(cums[n] - totals[n]), twice)).astype(BF16)
        scaled_x = carried[n, :GROUP]
        grad_low = grad.astype(BF16)
        forward = dot(left[n], carried[n], NN)
        backward = dot(right[n], jnp.concatenate([scaled_dy, grad_low], axis=0), NN)
        dx_ref[rows[n], :] = (gains[n] * backward + skip * dy).astype(dx_ref.dtype)
        v = scaled_x.astype(F32) * backward
        difference = scaled_dy.astype(F32) * forward - v
        hi = difference.astype(BF16)
        lo = (difference - hi.astype(F32)).astype(BF16)
        added = dot(jnp.concatenate([hi, lo, v.astype(BF16)], axis=1), adder, NN).T
        edge = head_sums(
            jnp.broadcast_to(jnp.sum(ends[n] * grad, axis=0, keepdims=True), (8, width)),
            member.astype(BF16),
        )
        slope = running(added[:heads], lower_ones) + edge[:, :1]
        here = step[:, rows[n]]
        draw = (added[heads : 2 * heads] / here - rate * slope) * gate[:, rows[n]]
        draw_ref[0, :, rows[n]] = draw
        bias_sum = bias_sum + jnp.sum(draw, axis=1, keepdims=True)
        rate_sum = rate_sum - jnp.sum(here * slope, axis=1, keepdims=True)
        sums[n] += dot(scaled_dy, carried[n], NT)
        tail[n] += dot(scaled_x, grad_low, NT)
        grad = wholes[n] * (grad + dot(ct[:, rows[n]], scaled_dy, NN))
    skip_sum = jnp.sum(head_sums(direct, member.astype(BF16)), axis=1, keepdims=True)
    shape = (heads, par_ref.shape[1])
    spot = lax.broadcasted_iota(jnp.int32, shape, 1) == (
        lax.broadcasted_iota(jnp.int32, shape, 0) + piece * heads
    )
    for k, value in enumerate((bias_sum, skip_sum, rate_sum)):
        par_ref[k : k + 1] += jnp.sum(jnp.where(spot, value * scale, 0.0), axis=0, keepdims=True)

    @pl.when(g == pl.num_programs(0) - 1)
    def _():
        for n in range(blocks):
            pair = jnp.where(lower, sums[n, :, :GROUP], 0.0).astype(BF16)
            dc = dot(pair, b_ref[rows[n], :], NN) + sums[n, :, GROUP:]
            db = dot(pair, c_ref[rows[n], :], TN) + tail[n]
            if not first:
                dc = dc + dc_in[rows[n], :]
                db = db + db_in[rows[n], :]
            dc_ref[rows[n], :] = dc
            db_ref[rows[n], :] = db


def local_grads(part, scale, y, x, dy, b, c, raw, bias, rate, skip, mine, other, before):
    length, channels = x.shape
    pieces, heads, _ = raw.shape
    width = channels // pieces
    states = b.shape[1]
    blocks = length // GROUP
    half = pieces // 2
    first = before is None
    place = lambda g, y: g * half + part
    columns = pl.BlockSpec((length, width), lambda g, y: (0, place(g, y)))
    maps = pl.BlockSpec((length, states), lambda g, y: (0, 0))
    line = pl.BlockSpec(bias.shape, lambda g, y: (0, 0))
    lines = pl.BlockSpec((1, heads, length), lambda g, y: (place(g, y), 0, 0))
    held = pl.BlockSpec((2 * states, width), lambda g, y: (0, 0))
    params = pl.BlockSpec((8, 128), lambda g, y: (0, 0))
    anywhere = pl.BlockSpec(memory_space=pl.ANY)
    in_specs = [columns, columns, maps, maps, lines, line, line, line, held, held]
    args = [x, dy, b, c, raw, bias, rate, skip, mine, other]
    aliases = {}
    if not first:
        dx, dc, db, draw, par = before
        args += [dc, db, par, dx, draw]
        in_specs += [maps, maps, params, anywhere, anywhere]
        aliases = {14: 0, 15: 3}
    grid_spec = pltpu.PrefetchScalarGridSpec(
        num_scalar_prefetch=1,
        grid=(2,),
        in_specs=in_specs,
        out_specs=[columns, maps, maps, lines, params],
        scratch_shapes=[
            pltpu.VMEM((blocks, GROUP, GROUP + states), BF16),
            pltpu.VMEM((blocks, GROUP, GROUP + states), BF16),
            pltpu.VMEM((blocks, GROUP + states, width), BF16),
            pltpu.VMEM((blocks, GROUP, width), F32),
            pltpu.VMEM((blocks, GROUP, GROUP + states), F32),
            pltpu.VMEM((blocks, GROUP, states), F32),
            pltpu.VMEM((states, length), BF16),
            pltpu.VMEM((states, length), BF16),
        ],
    )
    return pl.pallas_call(
        functools.partial(grads_kernel, first, scale, part, half),
        grid_spec=grid_spec,
        out_shape=[
            jax.ShapeDtypeStruct((length, channels), BF16),
            jax.ShapeDtypeStruct((length, states), F32),
            jax.ShapeDtypeStruct((length, states), F32),
            jax.ShapeDtypeStruct((pieces, heads, length), F32),
            jax.ShapeDtypeStruct((8, 128), F32),
        ],
        input_output_aliases=aliases,
        compiler_params=pltpu.CompilerParams(vmem_limit_bytes=VMEM_LIMIT),
        cost_estimate=pl.CostEstimate(
            flops=24 * length * width * (GROUP + states),
            bytes_accessed=12 * length * width,
            transcendentals=0,
        ),
        name="local_grads",
    )(y, *args)


def summed_over(value, axis):
    size = lax.axis_size(axis)
    if size & (size - 1):
        return lax.psum(value, axis)
    bit = 1
    while bit < size:
        steps = (bit, 2 * bit, 3 * bit) if 4 * bit <= size else (bit,)
        got = [lax.ppermute(value, axis, [(i, i ^ s) for i in range(size)]) for s in steps]
        value = value + got[0]
        if len(got) == 3:
            value = value + (got[1] + got[2])
        bit *= 4 if len(got) == 3 else 2
    return value


def entering(sent, kept, states):
    size = lax.axis_size("seq")
    pairs = size // 2
    index = lax.axis_index("seq")
    place, second = index // 2, index % 2 == 1
    swap = [(i, i ^ 1) for i in range(size)]
    got = lax.ppermute(sent, "seq", swap)

    def parts(a):
        return a[:states], a[states : 2 * states], a[2 * states : 2 * states + 1]

    (own_l, own_k, own_d), (got_l, got_k, got_d) = parts(kept), parts(got)
    l1, k1, d1 = [jnp.where(second, b, a) for a, b in ((own_l, got_l), (own_k, got_k), (own_d, got_d))]
    l2, k2, d2 = [jnp.where(second, a, b) for a, b in ((own_l, got_l), (own_k, got_k), (own_d, got_d))]
    whole_l = d2 * l1 + l2
    whole_k = k1 + d1 * k2
    whole_d = d1 * d2
    start = jnp.zeros_like(whole_l)
    end = jnp.zeros_like(whole_k)
    for hop in range(1, pairs):
        message = jnp.where(place == hop - 1, whole_d * start + whole_l, whole_d * end + whole_k)
        route = []
        for y in range(2):
            route.append((2 * (hop - 1) + y, 2 * hop + y))
            route.append((2 * (pairs - hop) + y, 2 * (pairs - hop - 1) + y))
        arrived = lax.ppermute(message, "seq", route)
        start = jnp.where(place == hop, arrived, start)
        end = jnp.where(place == pairs - 1 - hop, arrived, end)
    for_first = jnp.concatenate([start, k2 + d2 * end], axis=0)
    for_second = jnp.concatenate([d1 * start + l1, end], axis=0)
    mine = jnp.where(second, for_second, for_first)
    other = lax.ppermute(jnp.where(second, for_first, for_second), "seq", swap)
    return mine, other


def shards(inputs, input_map, output_map, step_raw, step_bias, decay_rate, skip_gain, cotangent):
    length, channels = inputs.shape[1:]
    heads = step_raw.shape[1]
    states = input_map.shape[2]
    pieces = 2 * PARTS
    group = heads // pieces
    x, b, c, dy = inputs[0], input_map[0], output_map[0], cotangent[0]
    raw = step_raw[0].reshape(pieces, group, length)
    bias = step_bias.reshape(1, heads)
    rate = decay_rate.reshape(1, heads)
    skip = skip_gain.reshape(1, heads)
    y = lax.axis_index("seq") % 2
    scale = 1.0 / math.sqrt(length * lax.axis_size("seq") * lax.axis_size("batch"))

    def local(half):
        at = jnp.reshape(half * PARTS, (1,)).astype(jnp.int32)
        return local_states(at, x, dy, b, c, raw, bias, rate)

    sent, kept = local(1 - y), local(y)
    met = [entering(sent[part], kept[part], states) for part in range(PARTS)]
    here = jnp.reshape(y, (1,)).astype(jnp.int32)
    before = None
    for part in range(PARTS):
        mine, other = met[part]
        before = local_grads(
            part, scale, here, x, dy, b, c, raw, bias, rate, skip, mine, other, before
        )
    dx, dc, db, draw, params = before
    summed = summed_over(summed_over(params, "batch"), "seq")
    return (
        dx[None],
        db[None],
        dc[None],
        draw.reshape(heads, length)[None],
        summed[:2, :heads],
        summed[2, :heads],
    )


def solution(mesh):
    in_specs = (
        P("batch", "seq", None),
        P("batch", "seq", None),
        P("batch", "seq", None),
        P("batch", None, "seq"),
        P(),
        P(),
        P(),
        P("batch", "seq", None),
    )
    out_specs = (
        P("batch", "seq", None),
        P("batch", "seq", None),
        P("batch", "seq", None),
        P("batch", None, "seq"),
        P(),
        P(),
    )
    return jax.shard_map(shards, mesh=mesh, in_specs=in_specs, out_specs=out_specs, check_vma=False)
```

```python
import functools
import math

import jax
import jax.numpy as jnp
from jax import lax
from jax.experimental import pallas as pl
from jax.experimental.pallas import tpu as pltpu
from jax.sharding import PartitionSpec as P

GROUP = 256
PARTS = 2
VMEM_LIMIT = 61 * 1024 * 1024
F32 = jnp.float32
BF16 = jnp.bfloat16


def dot(a, b, dims):
    return lax.dot_general(a, b, (dims, ((), ())), preferred_element_type=F32)


NN = ((1,), (0,))
NT = ((1,), (1,))
TN = ((0,), (0,))


def split2(a):
    hi = a.astype(BF16).astype(F32)
    return hi, a - hi


def head_matrix(heads, width):
    size = width // heads
    row = lax.broadcasted_iota(jnp.int32, (heads, width), 0)
    col = lax.broadcasted_iota(jnp.int32, (heads, width), 1)
    return ((col >= row * size) & (col < (row + 1) * size)).astype(F32)


def head_sums(values, member):
    hi, lo = split2(values)
    return dot(member, hi.astype(BF16), NT) + dot(member, lo.astype(BF16), NT)


def running(rows, upper):
    hi, rest = split2(rows)
    mid, lo = split2(rest)
    k = rows.shape[0]
    out = dot(jnp.concatenate([hi, mid, lo], axis=0).astype(BF16), upper, NN)
    return out[:k] + out[k : 2 * k] + out[2 * k :]


def triangle(width, lower):
    row = lax.broadcasted_iota(jnp.int32, (width, width), 0)
    col = lax.broadcasted_iota(jnp.int32, (width, width), 1)
    return (row >= col) if lower else (row <= col)


def softplus(v):
    return jnp.maximum(v, 0.0) + jnp.log1p(jnp.exp(-jnp.abs(v)))


def column(line, piece, heads):
    shape = (heads, line.shape[1])
    row = lax.broadcasted_iota(jnp.int32, shape, 0)
    col = lax.broadcasted_iota(jnp.int32, shape, 1)
    return jnp.sum(jnp.where(col == row + piece * heads, line, 0.0), axis=1, keepdims=True)


def block_sums(logs, blocks):
    heads = logs.shape[0]
    ones = triangle(GROUP, False).astype(BF16)
    stacked = jnp.concatenate([logs[:, n * GROUP : (n + 1) * GROUP] for n in range(blocks)], axis=0)
    cums = running(stacked, ones)
    return [cums[n * heads : (n + 1) * heads] for n in range(blocks)]


def factors(raw, bias, rate, skip, columns_ref, table_ref):
    heads, length = raw.shape
    width = table_ref.shape[1]
    blocks = length // GROUP
    step = softplus(raw + bias)
    cums = block_sums(-rate * step, blocks)
    totals = [cum[:, GROUP - 1 :] for cum in cums]
    before = [jnp.zeros((heads, 1), F32)]
    for total in totals:
        before.append(before[-1] + total)
    for n in range(blocks):
        rows = slice(n * GROUP, (n + 1) * GROUP)
        gain = split2(jnp.exp(totals[n] - cums[n]) * step[:, rows])
        lift = split2(jnp.exp(cums[n] - totals[n]))
        columns_ref[rows, :] = jnp.concatenate([*gain, *lift], axis=0).T.astype(BF16)
    whole = before[-1]
    lines = [jnp.exp(t) for t in totals]
    lines += [jnp.exp(whole - before[n + 1]) for n in range(blocks)]
    lines += [jnp.exp(before[n + 1]) for n in range(blocks)]
    lines += [jnp.exp(whole), skip]
    lines += [skip] * (-len(lines) % 8)
    hi, lo = split2(jnp.concatenate(lines, axis=1).T)
    member = head_matrix(heads, width).astype(BF16)
    table_ref[...] = dot(hi.astype(BF16), member, NN) + dot(lo.astype(BF16), member, NN)


def picker(piece, heads, all_heads, width, first):
    shape = (4 * all_heads, width)
    row = lax.broadcasted_iota(jnp.int32, shape, 0)
    col = lax.broadcasted_iota(jnp.int32, shape, 1)
    size = width // heads
    base = (0 if first else 2 * all_heads) + piece * heads
    hit = None
    for term in range(2):
        low = (row - (base + term * all_heads)) * size
        one = (col >= low) & (col < low + size)
        hit = one if hit is None else hit | one
    return hit.astype(BF16)


def local_kernel(first, *refs):
    at_ref, x_ref, dy_ref, b_ref, c_ref = refs[:5]
    if first:
        raw_ref, bias_ref, rate_ref, skip_ref = refs[5:9]
        outs = refs[9 : 9 + PARTS]
        xs_ref, ys_ref, direct_ref, columns_ref, table_ref, bt, ct = refs[9 + PARTS :]
    else:
        columns_ref, table_ref = refs[5:7]
        outs = refs[10 : 10 + PARTS]
        xs_ref, ys_ref, direct_ref, bt, ct = refs[10 + PARTS :]
    g = pl.program_id(0)
    length, width = x_ref.shape
    states = b_ref.shape[1]
    blocks = length // GROUP
    piece = at_ref[0] + g
    all_heads = columns_ref.shape[1] // 4
    heads = all_heads * width // table_ref.shape[1]

    @pl.when(g == 0)
    def _():
        bt[...] = b_ref[...].T
        ct[...] = c_ref[...].T
        if first:
            factors(
                raw_ref[0],
                column(bias_ref[...], 0, all_heads),
                column(rate_ref[...], 0, all_heads),
                column(skip_ref[...], 0, all_heads),
                columns_ref,
                table_ref,
            )

    gain = picker(piece, heads, all_heads, width, True)
    lift = picker(piece, heads, all_heads, width, False)
    table = table_ref[:, pl.ds(pl.multiple_of(piece * width, width), width)]
    state = jnp.zeros((states, width), F32)
    grad = jnp.zeros((states, width), F32)
    direct = jnp.zeros((8, width), F32)
    for n in range(blocks):
        rows = slice(n * GROUP, (n + 1) * GROUP)
        x = x_ref[rows, :].astype(F32)
        dy = dy_ref[rows, :].astype(F32)
        direct = direct + jnp.sum((dy * x).reshape(GROUP // 8, 8, width), axis=0)
        scaled_x = (x * dot(columns_ref[rows, :], gain, NN)).astype(BF16)
        scaled_dy = (dy * dot(columns_ref[rows, :], lift, NN)).astype(BF16)
        xs_ref[rows, :] = scaled_x
        ys_ref[rows, :] = scaled_dy
        later = table[blocks + n : blocks + n + 1]
        earlier = table[2 * blocks + n : 2 * blocks + n + 1]
        state = state + later * dot(bt[:, rows], scaled_x, NN)
        grad = grad + earlier * dot(ct[:, rows], scaled_dy, NN)
    direct_ref[...] = direct
    decay = jnp.broadcast_to(table[3 * blocks : 3 * blocks + 1], (8, width))
    for k, out_ref in enumerate(outs):

        @pl.when(g == k)
        def _():
            out_ref[:states] = state
            out_ref[states : 2 * states] = grad
            out_ref[2 * states :] = decay


def local_states(at, x, dy, b, c, vectors, before):
    length, channels = x.shape
    states = b.shape[1]
    pieces = 2 * PARTS
    width = channels // pieces
    lines = 3 * (length // GROUP) + 2
    lines += -lines % 8
    first = before is None
    whole = lambda g, at: (0, 0)
    columns = pl.BlockSpec((length, width), lambda g, at: (0, at[0] + g))
    strip = pl.BlockSpec((8, width), lambda g, at: (0, at[0] + g))
    maps = pl.BlockSpec((length, states), whole)
    anywhere = pl.BlockSpec(memory_space=pl.ANY)
    in_specs = [columns, columns, maps, maps]
    out_specs = [pl.BlockSpec((2 * states + 8, width), whole)] * PARTS + [columns, columns, strip]
    out_shape = [jax.ShapeDtypeStruct((2 * states + 8, width), F32)] * PARTS + [
        jax.ShapeDtypeStruct((length, channels), BF16),
        jax.ShapeDtypeStruct((length, channels), BF16),
        jax.ShapeDtypeStruct((8, channels), F32),
    ]
    aliases = {}
    if first:
        raw, bias, rate, skip = vectors
        heads = raw.shape[1]
        args = [raw, bias, rate, skip]
        in_specs += [pl.BlockSpec(raw.shape, lambda g, at: (0, 0, 0))]
        in_specs += [pl.BlockSpec(bias.shape, whole)] * 3
        tables = [
            jax.ShapeDtypeStruct((length, 4 * heads), BF16),
            jax.ShapeDtypeStruct((lines, channels), F32),
        ]
        out_shape += tables
        out_specs += [pl.BlockSpec(t.shape, whole) for t in tables]
    else:
        xs, ys, direct, factor_columns, table = before
        args = [factor_columns, table, xs, ys, direct]
        in_specs += [pl.BlockSpec(factor_columns.shape, whole), pl.BlockSpec(table.shape, whole)]
        in_specs += [anywhere] * 3
        aliases = {7: PARTS, 8: PARTS + 1, 9: PARTS + 2}
    grid_spec = pltpu.PrefetchScalarGridSpec(
        num_scalar_prefetch=1,
        grid=(PARTS,),
        in_specs=in_specs,
        out_specs=out_specs,
        scratch_shapes=[
            pltpu.VMEM((states, length), BF16),
            pltpu.VMEM((states, length), BF16),
        ],
    )
    out = pl.pallas_call(
        functools.partial(local_kernel, first),
        grid_spec=grid_spec,
        out_shape=out_shape,
        input_output_aliases=aliases,
        compiler_params=pltpu.CompilerParams(vmem_limit_bytes=VMEM_LIMIT),
        cost_estimate=pl.CostEstimate(
            flops=8 * PARTS * length * width * states,
            bytes_accessed=8 * PARTS * length * width,
            transcendentals=0,
        ),
        name="local_states",
    )(at, x, dy, b, c, *args)
    return out[:PARTS], list(out[PARTS:])


def grads_kernel(first, scale, part, half, *refs):
    y_ref, xs_ref, ys_ref, dy_ref, direct_ref, b_ref, c_ref, columns_ref, table_ref = refs[:9]
    raw_ref, bias_ref, rate_ref, mine_ref, other_ref = refs[9:14]
    refs = refs[14:]
    if not first:
        dc_in, db_in, par_in = refs[:3]
        refs = refs[5:]
    dx_ref, dc_ref, db_ref, draw_ref, par_ref = refs[:5]
    left, right, sums, dc_sum, db_sum, bt, ct, adder = refs[5:]
    g = pl.program_id(0)
    heads = raw_ref.shape[1]
    length, width = xs_ref.shape
    states = b_ref.shape[1]
    blocks = length // GROUP
    piece = g * half + part
    all_heads = columns_ref.shape[1] // 4
    member = head_matrix(heads, width).astype(BF16)
    lower = triangle(GROUP, True)
    rows = [slice(n * GROUP, (n + 1) * GROUP) for n in range(blocks)]

    @pl.when(g == 0)
    def _():
        bt[...] = b_ref[...].T
        ct[...] = c_ref[...].T
        upper = triangle(GROUP, False)
        for n in range(blocks):
            b, c = b_ref[rows[n], :], c_ref[rows[n], :]
            left[n] = jnp.where(lower, dot(c, b, NT), 0.0).astype(BF16)
            right[n] = jnp.where(upper, dot(b, c, NT), 0.0).astype(BF16)
        sums[...] = jnp.zeros_like(sums)
        dc_sum[...] = jnp.zeros_like(dc_sum)
        db_sum[...] = jnp.zeros_like(db_sum)
        par_ref[...] = jnp.zeros_like(par_ref) if first else par_in[...]
        row = lax.broadcasted_iota(jnp.int32, (width, 128), 0)
        col = lax.broadcasted_iota(jnp.int32, (width, 128), 1)
        size = width // heads
        one = ((row >= col * size) & (row < (col + 1) * size)).astype(BF16)
        col = col - heads
        two = ((row >= col * size) & (row < (col + 1) * size)).astype(BF16)
        adder[:width] = one
        adder[width : 2 * width] = one
        adder[2 * width :] = two

    own = g == y_ref[0]
    state = jnp.where(own, mine_ref[:states], other_ref[:states])
    grad = jnp.where(own, mine_ref[states:], other_ref[states:])
    table = table_ref[...]
    skip = table[3 * blocks + 1 : 3 * blocks + 2]
    entering_low, ends = [], []
    for n in range(blocks):
        state = table[n : n + 1] * state
        entering_low.append(state.astype(BF16))
        state = state + dot(bt[:, rows[n]], xs_ref[rows[n], :], NN)
        ends.append(state)
    leaving_low, edges = [None] * blocks, [None] * blocks
    for n in reversed(range(blocks)):
        leaving_low[n] = grad.astype(BF16)
        edges[n] = jnp.sum(ends[n] * grad, axis=0, keepdims=True)
        grad = table[n : n + 1] * (grad + dot(ct[:, rows[n]], ys_ref[rows[n], :], NN))
    gain = picker(piece, heads, all_heads, width, True)
    added = []
    for n in range(blocks):
        scaled_x, scaled_dy = xs_ref[rows[n], :], ys_ref[rows[n], :]
        forward = dot(left[n], scaled_x, NN) + dot(c_ref[rows[n], :], entering_low[n], NN)
        backward = dot(right[n], scaled_dy, NN) + dot(b_ref[rows[n], :], leaving_low[n], NN)
        weight = dot(columns_ref[rows[n], :], gain, NN)
        dx_ref[rows[n], :] = (weight * backward + skip * dy_ref[rows[n], :].astype(F32)).astype(
            dx_ref.dtype
        )
        v = scaled_x.astype(F32) * backward
        difference = scaled_dy.astype(F32) * forward - v
        hi = difference.astype(BF16)
        lo = (difference - hi.astype(F32)).astype(BF16)
        added.append(dot(jnp.concatenate([hi, lo, v.astype(BF16)], axis=1), adder[...], NN))
        sums[n] += dot(scaled_dy, scaled_x, NT)
        dc_sum[n] += dot(scaled_dy, entering_low[n], NT)
        db_sum[n] += dot(scaled_x, leaving_low[n], NT)
    added = [a.T for a in added]
    edge = head_sums(jnp.concatenate(edges + [edges[0]] * (8 - blocks), axis=0), member)
    slopes = running(
        jnp.concatenate([a[:heads] for a in added], axis=0), lower.astype(BF16)
    )
    slope = jnp.concatenate(
        [slopes[n * heads : (n + 1) * heads] + edge[:, n : n + 1] for n in range(blocks)], axis=1
    )
    v = jnp.concatenate([a[heads : 2 * heads] for a in added], axis=1)
    raw = raw_ref[0] + column(bias_ref[...], piece, heads)
    step = softplus(raw)
    draw = (v / step - column(rate_ref[...], piece, heads) * slope) / (1.0 + jnp.exp(-raw))
    draw_ref[0] = draw
    values = (
        jnp.sum(draw, axis=1, keepdims=True),
        jnp.sum(head_sums(direct_ref[...], member), axis=1, keepdims=True),
        -jnp.sum(step * slope, axis=1, keepdims=True),
    )
    shape = (heads, par_ref.shape[1])
    spot = lax.broadcasted_iota(jnp.int32, shape, 1) == (
        lax.broadcasted_iota(jnp.int32, shape, 0) + piece * heads
    )
    for k, value in enumerate(values):
        par_ref[k : k + 1] += jnp.sum(jnp.where(spot, value * scale, 0.0), axis=0, keepdims=True)

    @pl.when(g == pl.num_programs(0) - 1)
    def _():
        for n in range(blocks):
            pair = jnp.where(lower, sums[n], 0.0).astype(BF16)
            dc = dot(pair, b_ref[rows[n], :], NN) + dc_sum[n]
            db = dot(pair, c_ref[rows[n], :], TN) + db_sum[n]
            if not first:
                dc = dc + dc_in[rows[n], :]
                db = db + db_in[rows[n], :]
            dc_ref[rows[n], :] = dc
            db_ref[rows[n], :] = db


def local_grads(part, scale, y, saved, dy, b, c, vectors, mine, other, before):
    xs, ys, direct, factor_columns, table = saved
    raw, bias, rate, _ = vectors
    length, channels = xs.shape
    pieces = 2 * PARTS
    heads = raw.shape[1] // pieces
    raw = raw.reshape(pieces, heads, length)
    width = channels // pieces
    states = b.shape[1]
    blocks = length // GROUP
    half = pieces // 2
    first = before is None
    whole = lambda g, y: (0, 0)
    place = lambda g, y: (0, g * half + part)
    columns = pl.BlockSpec((length, width), place)
    maps = pl.BlockSpec((length, states), whole)
    line = pl.BlockSpec(bias.shape, whole)
    lines = pl.BlockSpec((1, heads, length), lambda g, y: (g * half + part, 0, 0))
    held = pl.BlockSpec((2 * states, width), whole)
    params = pl.BlockSpec((8, 128), whole)
    anywhere = pl.BlockSpec(memory_space=pl.ANY)
    in_specs = [columns, columns, columns, pl.BlockSpec((8, width), place), maps, maps]
    in_specs += [
        pl.BlockSpec(factor_columns.shape, whole),
        pl.BlockSpec((table.shape[0], width), place),
    ]
    in_specs += [lines, line, line, held, held]
    args = [xs, ys, dy, direct, b, c, factor_columns, table, raw, bias, rate, mine, other]
    aliases = {}
    if not first:
        dx, dc, db, draw, par = before
        args += [dc, db, par, dx, draw]
        in_specs += [maps, maps, params, anywhere, anywhere]
        aliases = {17: 0, 18: 3}
    grid_spec = pltpu.PrefetchScalarGridSpec(
        num_scalar_prefetch=1,
        grid=(2,),
        in_specs=in_specs,
        out_specs=[columns, maps, maps, lines, params],
        scratch_shapes=[
            pltpu.VMEM((blocks, GROUP, GROUP), BF16),
            pltpu.VMEM((blocks, GROUP, GROUP), BF16),
            pltpu.VMEM((blocks, GROUP, GROUP), F32),
            pltpu.VMEM((blocks, GROUP, states), F32),
            pltpu.VMEM((blocks, GROUP, states), F32),
            pltpu.VMEM((states, length), BF16),
            pltpu.VMEM((states, length), BF16),
            pltpu.VMEM((3 * width, 128), BF16),
        ],
    )
    return pl.pallas_call(
        functools.partial(grads_kernel, first, scale, part, half),
        grid_spec=grid_spec,
        out_shape=[
            jax.ShapeDtypeStruct((length, channels), BF16),
            jax.ShapeDtypeStruct((length, states), F32),
            jax.ShapeDtypeStruct((length, states), F32),
            jax.ShapeDtypeStruct((pieces, heads, length), F32),
            jax.ShapeDtypeStruct((8, 128), F32),
        ],
        input_output_aliases=aliases,
        compiler_params=pltpu.CompilerParams(vmem_limit_bytes=VMEM_LIMIT),
        cost_estimate=pl.CostEstimate(
            flops=24 * length * width * (GROUP + states),
            bytes_accessed=12 * length * width,
            transcendentals=0,
        ),
        name="local_grads",
    )(y, *args)


def summed_over(value, axis):
    size = lax.axis_size(axis)
    if size & (size - 1):
        return lax.psum(value, axis)
    bit = 1
    while bit < size:
        steps = (bit, 2 * bit, 3 * bit) if 4 * bit <= size else (bit,)
        got = [lax.ppermute(value, axis, [(i, i ^ s) for i in range(size)]) for s in steps]
        value = value + got[0]
        if len(got) == 3:
            value = value + (got[1] + got[2])
        bit *= 4 if len(got) == 3 else 2
    return value


def entering(got, kept, states):
    size = lax.axis_size("seq")
    pairs = size // 2
    index = lax.axis_index("seq")
    place, second = index // 2, index % 2 == 1
    swap = [(i, i ^ 1) for i in range(size)]

    def parts(a):
        return a[:states], a[states : 2 * states], a[2 * states : 2 * states + 1]

    (own_l, own_k, own_d), (got_l, got_k, got_d) = parts(kept), parts(got)
    l1, k1, d1 = [jnp.where(second, b, a) for a, b in ((own_l, got_l), (own_k, got_k), (own_d, got_d))]
    l2, k2, d2 = [jnp.where(second, a, b) for a, b in ((own_l, got_l), (own_k, got_k), (own_d, got_d))]
    whole_l = d2 * l1 + l2
    whole_k = k1 + d1 * k2
    whole_d = d1 * d2
    start = jnp.zeros_like(whole_l)
    end = jnp.zeros_like(whole_k)
    for hop in range(1, pairs):
        message = jnp.where(place == hop - 1, whole_d * start + whole_l, whole_d * end + whole_k)
        route = []
        for y in range(2):
            route.append((2 * (hop - 1) + y, 2 * hop + y))
            route.append((2 * (pairs - hop) + y, 2 * (pairs - hop - 1) + y))
        arrived = lax.ppermute(message, "seq", route)
        start = jnp.where(place == hop, arrived, start)
        end = jnp.where(place == pairs - 1 - hop, arrived, end)
    for_first = jnp.concatenate([start, k2 + d2 * end], axis=0)
    for_second = jnp.concatenate([d1 * start + l1, end], axis=0)
    mine = jnp.where(second, for_second, for_first)
    other = lax.ppermute(jnp.where(second, for_first, for_second), "seq", swap)
    return mine, other


def shards(inputs, input_map, output_map, step_raw, step_bias, decay_rate, skip_gain, cotangent):
    length, channels = inputs.shape[1:]
    heads = step_raw.shape[1]
    states = input_map.shape[2]
    x, b, c, dy = inputs[0], input_map[0], output_map[0], cotangent[0]
    vectors = (
        step_raw,
        step_bias.reshape(1, heads),
        decay_rate.reshape(1, heads),
        skip_gain.reshape(1, heads),
    )
    size = lax.axis_size("seq")
    y = lax.axis_index("seq") % 2
    scale = 1.0 / math.sqrt(length * size * lax.axis_size("batch"))
    at = lambda half: jnp.reshape(half * PARTS, (1,)).astype(jnp.int32)
    sent, saved = local_states(at(1 - y), x, dy, b, c, vectors, None)
    kept, saved[:3] = local_states(at(y), x, dy, b, c, vectors, saved)
    got = []
    for part in range(PARTS):
        message = sent[part]
        if got:
            message, got[-1] = lax.optimization_barrier((message, got[-1]))
        got.append(lax.ppermute(message, "seq", [(i, i ^ 1) for i in range(size)]))
    met = [entering(got[part], kept[part], states) for part in range(PARTS)]
    here = jnp.reshape(y, (1,)).astype(jnp.int32)
    before = None
    for part in range(PARTS):
        mine, other = met[part]
        before = local_grads(part, scale, here, saved, dy, b, c, vectors, mine, other, before)
    dx, dc, db, draw, params = before
    summed = summed_over(summed_over(params, "batch"), "seq")
    return (
        dx[None],
        db[None],
        dc[None],
        draw.reshape(heads, length)[None],
        summed[:2, :heads],
        summed[2, :heads],
    )


def solution(mesh):
    in_specs = (
        P("batch", "seq", None),
        P("batch", "seq", None),
        P("batch", "seq", None),
        P("batch", None, "seq"),
        P(),
        P(),
        P(),
        P("batch", "seq", None),
    )
    out_specs = (
        P("batch", "seq", None),
        P("batch", "seq", None),
        P("batch", "seq", None),
        P("batch", None, "seq"),
        P(),
        P(),
    )
    return jax.shard_map(shards, mesh=mesh, in_specs=in_specs, out_specs=out_specs, check_vma=False)
```

```python
import functools
import math

import jax
import jax.numpy as jnp
from jax import lax
from jax.experimental import pallas as pl
from jax.experimental.pallas import tpu as pltpu
from jax.sharding import PartitionSpec as P

GROUP = 256
PARTS = 2
VMEM_LIMIT = 60 * 1024 * 1024
F32 = jnp.float32
BF16 = jnp.bfloat16


def dot(a, b, dims):
    return lax.dot_general(a, b, (dims, ((), ())), preferred_element_type=F32)


NN = ((1,), (0,))
NT = ((1,), (1,))
TN = ((0,), (0,))


def split2(a):
    hi = a.astype(BF16).astype(F32)
    return hi, a - hi


def head_matrix(heads, width):
    size = width // heads
    row = lax.broadcasted_iota(jnp.int32, (heads, width), 0)
    col = lax.broadcasted_iota(jnp.int32, (heads, width), 1)
    return ((col >= row * size) & (col < (row + 1) * size)).astype(F32)


def head_sums(values, member):
    hi, lo = split2(values)
    return dot(member, hi.astype(BF16), NT) + dot(member, lo.astype(BF16), NT)


def running(rows, upper):
    hi, rest = split2(rows)
    mid, lo = split2(rest)
    k = rows.shape[0]
    out = dot(jnp.concatenate([hi, mid, lo], axis=0).astype(BF16), upper, NN)
    return out[:k] + out[k : 2 * k] + out[2 * k :]


def triangle(width, lower):
    row = lax.broadcasted_iota(jnp.int32, (width, width), 0)
    col = lax.broadcasted_iota(jnp.int32, (width, width), 1)
    return (row >= col) if lower else (row <= col)


def softplus(v):
    return jnp.maximum(v, 0.0) + jnp.log1p(jnp.exp(-jnp.abs(v)))


def column(line, piece, heads):
    shape = (heads, line.shape[1])
    row = lax.broadcasted_iota(jnp.int32, shape, 0)
    col = lax.broadcasted_iota(jnp.int32, shape, 1)
    return jnp.sum(jnp.where(col == row + piece * heads, line, 0.0), axis=1, keepdims=True)


def block_sums(logs, blocks):
    heads = logs.shape[0]
    ones = triangle(GROUP, False).astype(BF16)
    stacked = jnp.concatenate([logs[:, n * GROUP : (n + 1) * GROUP] for n in range(blocks)], axis=0)
    cums = running(stacked, ones)
    return [cums[n * heads : (n + 1) * heads] for n in range(blocks)]


def factors(raw, bias, rate, skip, columns_ref, table_ref):
    heads, length = raw.shape
    width = table_ref.shape[1]
    blocks = length // GROUP
    step = softplus(raw + bias)
    cums = block_sums(-rate * step, blocks)
    totals = [cum[:, GROUP - 1 :] for cum in cums]
    before = [jnp.zeros((heads, 1), F32)]
    for total in totals:
        before.append(before[-1] + total)
    for n in range(blocks):
        rows = slice(n * GROUP, (n + 1) * GROUP)
        gain = split2(jnp.exp(totals[n] - cums[n]) * step[:, rows])
        lift = split2(jnp.exp(cums[n] - totals[n]))
        columns_ref[rows, :] = jnp.concatenate([*gain, *lift], axis=0).T.astype(BF16)
    whole = before[-1]
    lines = [jnp.exp(t) for t in totals]
    lines += [jnp.exp(whole - before[n + 1]) for n in range(blocks)]
    lines += [jnp.exp(before[n + 1]) for n in range(blocks)]
    lines += [jnp.exp(whole), skip]
    lines += [skip] * (-len(lines) % 8)
    hi, lo = split2(jnp.concatenate(lines, axis=1).T)
    member = head_matrix(heads, width).astype(BF16)
    table_ref[...] = dot(hi.astype(BF16), member, NN) + dot(lo.astype(BF16), member, NN)


def picker(piece, heads, all_heads, width, first):
    shape = (4 * all_heads, width)
    row = lax.broadcasted_iota(jnp.int32, shape, 0)
    col = lax.broadcasted_iota(jnp.int32, shape, 1)
    size = width // heads
    base = (0 if first else 2 * all_heads) + piece * heads
    hit = None
    for term in range(2):
        low = (row - (base + term * all_heads)) * size
        one = (col >= low) & (col < low + size)
        hit = one if hit is None else hit | one
    return hit.astype(BF16)


def local_kernel(first, *refs):
    at_ref, x_ref, dy_ref, b_ref, c_ref = refs[:5]
    if first:
        raw_ref, bias_ref, rate_ref, skip_ref = refs[5:9]
        outs = refs[9:-7]
        xs_ref, ys_ref, direct_ref, columns_ref, table_ref, bt, ct = refs[-7:]
    else:
        columns_ref, table_ref = refs[5:7]
        outs = refs[10:-5]
        xs_ref, ys_ref, direct_ref, bt, ct = refs[-5:]
    g = pl.program_id(0)
    length, width = x_ref.shape
    states = b_ref.shape[1]
    blocks = length // GROUP
    piece = at_ref[0] + g
    all_heads = columns_ref.shape[1] // 4
    heads = all_heads * width // table_ref.shape[1]

    @pl.when(g == 0)
    def _():
        bt[...] = b_ref[...].T
        ct[...] = c_ref[...].T
        if first:
            factors(
                raw_ref[0],
                column(bias_ref[...], 0, all_heads),
                column(rate_ref[...], 0, all_heads),
                column(skip_ref[...], 0, all_heads),
                columns_ref,
                table_ref,
            )

    gain = picker(piece, heads, all_heads, width, True)
    lift = picker(piece, heads, all_heads, width, False)
    table = table_ref[:, pl.ds(pl.multiple_of(piece * width, width), width)]
    state = jnp.zeros((states, width), F32)
    grad = jnp.zeros((states, width), F32)
    direct = jnp.zeros((8, width), F32)
    for n in range(blocks):
        rows = slice(n * GROUP, (n + 1) * GROUP)
        x = x_ref[rows, :].astype(F32)
        dy = dy_ref[rows, :].astype(F32)
        direct = direct + jnp.sum((dy * x).reshape(GROUP // 8, 8, width), axis=0)
        scaled_x = (x * dot(columns_ref[rows, :], gain, NN)).astype(BF16)
        scaled_dy = (dy * dot(columns_ref[rows, :], lift, NN)).astype(BF16)
        xs_ref[rows, :] = scaled_x
        ys_ref[rows, :] = scaled_dy
        later = table[blocks + n : blocks + n + 1]
        earlier = table[2 * blocks + n : 2 * blocks + n + 1]
        state = state + later * dot(bt[:, rows], scaled_x, NN)
        grad = grad + earlier * dot(ct[:, rows], scaled_dy, NN)
    direct_ref[...] = direct
    decay = jnp.broadcast_to(table[3 * blocks : 3 * blocks + 1], (8, width))
    for k, out_ref in enumerate(outs):

        @pl.when(g == k)
        def _():
            out_ref[:states] = state
            out_ref[states : 2 * states] = grad
            out_ref[2 * states :] = decay


def local_states(at, count, x, dy, b, c, vectors, before):
    length, channels = x.shape
    states = b.shape[1]
    pieces = 2 * PARTS
    width = channels // pieces
    lines = 3 * (length // GROUP) + 2
    lines += -lines % 8
    first = before is None
    whole = lambda g, at: (0, 0)
    columns = pl.BlockSpec((length, width), lambda g, at: (0, at[0] + g))
    strip = pl.BlockSpec((8, width), lambda g, at: (0, at[0] + g))
    maps = pl.BlockSpec((length, states), whole)
    anywhere = pl.BlockSpec(memory_space=pl.ANY)
    in_specs = [columns, columns, maps, maps]
    out_specs = [pl.BlockSpec((2 * states + 8, width), whole)] * count + [columns, columns, strip]
    out_shape = [jax.ShapeDtypeStruct((2 * states + 8, width), F32)] * count + [
        jax.ShapeDtypeStruct((length, channels), BF16),
        jax.ShapeDtypeStruct((length, channels), BF16),
        jax.ShapeDtypeStruct((8, channels), F32),
    ]
    aliases = {}
    if first:
        raw, bias, rate, skip = vectors
        heads = raw.shape[1]
        args = [raw, bias, rate, skip]
        in_specs += [pl.BlockSpec(raw.shape, lambda g, at: (0, 0, 0))]
        in_specs += [pl.BlockSpec(bias.shape, whole)] * 3
        tables = [
            jax.ShapeDtypeStruct((length, 4 * heads), BF16),
            jax.ShapeDtypeStruct((lines, channels), F32),
        ]
        out_shape += tables
        out_specs += [pl.BlockSpec(t.shape, whole) for t in tables]
    else:
        xs, ys, direct, factor_columns, table = before
        args = [factor_columns, table, xs, ys, direct]
        in_specs += [pl.BlockSpec(factor_columns.shape, whole), pl.BlockSpec(table.shape, whole)]
        in_specs += [anywhere] * 3
        aliases = {7: count, 8: count + 1, 9: count + 2}
    grid_spec = pltpu.PrefetchScalarGridSpec(
        num_scalar_prefetch=1,
        grid=(count,),
        in_specs=in_specs,
        out_specs=out_specs,
        scratch_shapes=[
            pltpu.VMEM((states, length), BF16),
            pltpu.VMEM((states, length), BF16),
        ],
    )
    out = pl.pallas_call(
        functools.partial(local_kernel, first),
        grid_spec=grid_spec,
        out_shape=out_shape,
        input_output_aliases=aliases,
        compiler_params=pltpu.CompilerParams(vmem_limit_bytes=VMEM_LIMIT),
        cost_estimate=pl.CostEstimate(
            flops=8 * count * length * width * states,
            bytes_accessed=8 * count * length * width,
            transcendentals=0,
        ),
        name="local_states",
    )(at, x, dy, b, c, *args)
    return out[:count], list(out[count:])


def grads_kernel(first, scale, part, half, *refs):
    y_ref, xs_ref, ys_ref, dy_ref, direct_ref, b_ref, c_ref, columns_ref, table_ref = refs[:9]
    raw_ref, bias_ref, rate_ref, mine_ref, other_ref = refs[9:14]
    refs = refs[14:]
    if not first:
        dc_in, db_in, par_in = refs[:3]
        refs = refs[5:]
    dx_ref, dc_ref, db_ref, draw_ref, par_ref = refs[:5]
    left, right, sums, dc_sum, db_sum, bt, ct, adder = refs[5:]
    g = pl.program_id(0)
    heads = raw_ref.shape[1]
    length, width = xs_ref.shape
    states = b_ref.shape[1]
    blocks = length // GROUP
    piece = g * half + part
    all_heads = columns_ref.shape[1] // 4
    member = head_matrix(heads, width).astype(BF16)
    lower = triangle(GROUP, True)
    rows = [slice(n * GROUP, (n + 1) * GROUP) for n in range(blocks)]

    @pl.when(g == 0)
    def _():
        bt[...] = b_ref[...].T
        ct[...] = c_ref[...].T
        upper = triangle(GROUP, False)
        for n in range(blocks):
            b, c = b_ref[rows[n], :], c_ref[rows[n], :]
            left[n] = jnp.where(lower, dot(c, b, NT), 0.0).astype(BF16)
            right[n] = jnp.where(upper, dot(b, c, NT), 0.0).astype(BF16)
        sums[...] = jnp.zeros_like(sums)
        dc_sum[...] = jnp.zeros_like(dc_sum)
        db_sum[...] = jnp.zeros_like(db_sum)
        par_ref[...] = jnp.zeros_like(par_ref) if first else par_in[...]
        row = lax.broadcasted_iota(jnp.int32, (width, 128), 0)
        col = lax.broadcasted_iota(jnp.int32, (width, 128), 1)
        size = width // heads
        one = ((row >= col * size) & (row < (col + 1) * size)).astype(BF16)
        col = col - heads
        two = ((row >= col * size) & (row < (col + 1) * size)).astype(BF16)
        adder[:width] = one
        adder[width : 2 * width] = one
        adder[2 * width :] = two

    own = g == y_ref[0]
    state = jnp.where(own, mine_ref[:states], other_ref[:states])
    grad = jnp.where(own, mine_ref[states:], other_ref[states:])
    table = table_ref[...]
    skip = table[3 * blocks + 1 : 3 * blocks + 2]
    entering_low, ends = [], []
    for n in range(blocks):
        state = table[n : n + 1] * state
        entering_low.append(state.astype(BF16))
        state = state + dot(bt[:, rows[n]], xs_ref[rows[n], :], NN)
        ends.append(state)
    leaving_low, edges = [None] * blocks, [None] * blocks
    for n in reversed(range(blocks)):
        leaving_low[n] = grad.astype(BF16)
        edges[n] = jnp.sum(ends[n] * grad, axis=0, keepdims=True)
        grad = table[n : n + 1] * (grad + dot(ct[:, rows[n]], ys_ref[rows[n], :], NN))
    gain = picker(piece, heads, all_heads, width, True)
    added = []
    for n in range(blocks):
        scaled_x, scaled_dy = xs_ref[rows[n], :], ys_ref[rows[n], :]
        forward = dot(left[n], scaled_x, NN) + dot(c_ref[rows[n], :], entering_low[n], NN)
        backward = dot(right[n], scaled_dy, NN) + dot(b_ref[rows[n], :], leaving_low[n], NN)
        weight = dot(columns_ref[rows[n], :], gain, NN)
        dx_ref[rows[n], :] = (weight * backward + skip * dy_ref[rows[n], :].astype(F32)).astype(
            dx_ref.dtype
        )
        v = scaled_x.astype(F32) * backward
        difference = scaled_dy.astype(F32) * forward - v
        hi = difference.astype(BF16)
        lo = (difference - hi.astype(F32)).astype(BF16)
        added.append(dot(jnp.concatenate([hi, lo, v.astype(BF16)], axis=1), adder[...], NN))
        sums[n] += dot(scaled_dy, scaled_x, NT)
        dc_sum[n] += dot(scaled_dy, entering_low[n], NT)
        db_sum[n] += dot(scaled_x, leaving_low[n], NT)
    added = [a.T for a in added]
    edge = head_sums(jnp.concatenate(edges + [edges[0]] * (8 - blocks), axis=0), member)
    slopes = running(
        jnp.concatenate([a[:heads] for a in added], axis=0), lower.astype(BF16)
    )
    slope = jnp.concatenate(
        [slopes[n * heads : (n + 1) * heads] + edge[:, n : n + 1] for n in range(blocks)], axis=1
    )
    v = jnp.concatenate([a[heads : 2 * heads] for a in added], axis=1)
    raw = raw_ref[0] + column(bias_ref[...], piece, heads)
    step = softplus(raw)
    draw = (v / step - column(rate_ref[...], piece, heads) * slope) / (1.0 + jnp.exp(-raw))
    draw_ref[0] = draw
    values = (
        jnp.sum(draw, axis=1, keepdims=True),
        jnp.sum(head_sums(direct_ref[...], member), axis=1, keepdims=True),
        -jnp.sum(step * slope, axis=1, keepdims=True),
    )
    shape = (heads, par_ref.shape[1])
    spot = lax.broadcasted_iota(jnp.int32, shape, 1) == (
        lax.broadcasted_iota(jnp.int32, shape, 0) + piece * heads
    )
    for k, value in enumerate(values):
        par_ref[k : k + 1] += jnp.sum(jnp.where(spot, value * scale, 0.0), axis=0, keepdims=True)

    @pl.when(g == pl.num_programs(0) - 1)
    def _():
        for n in range(blocks):
            pair = jnp.where(lower, sums[n], 0.0).astype(BF16)
            dc = dot(pair, b_ref[rows[n], :], NN) + dc_sum[n]
            db = dot(pair, c_ref[rows[n], :], TN) + db_sum[n]
            if not first:
                dc = dc + dc_in[rows[n], :]
                db = db + db_in[rows[n], :]
            dc_ref[rows[n], :] = dc
            db_ref[rows[n], :] = db


def local_grads(part, scale, y, saved, dy, b, c, vectors, mine, other, before):
    xs, ys, direct, factor_columns, table = saved
    raw, bias, rate, _ = vectors
    length, channels = xs.shape
    pieces = 2 * PARTS
    heads = raw.shape[1] // pieces
    raw = raw.reshape(pieces, heads, length)
    width = channels // pieces
    states = b.shape[1]
    blocks = length // GROUP
    half = pieces // 2
    first = before is None
    whole = lambda g, y: (0, 0)
    place = lambda g, y: (0, g * half + part)
    columns = pl.BlockSpec((length, width), place)
    maps = pl.BlockSpec((length, states), whole)
    line = pl.BlockSpec(bias.shape, whole)
    lines = pl.BlockSpec((1, heads, length), lambda g, y: (g * half + part, 0, 0))
    held = pl.BlockSpec((2 * states, width), whole)
    params = pl.BlockSpec((8, 128), whole)
    anywhere = pl.BlockSpec(memory_space=pl.ANY)
    in_specs = [columns, columns, columns, pl.BlockSpec((8, width), place), maps, maps]
    in_specs += [
        pl.BlockSpec(factor_columns.shape, whole),
        pl.BlockSpec((table.shape[0], width), place),
    ]
    in_specs += [lines, line, line, held, held]
    args = [xs, ys, dy, direct, b, c, factor_columns, table, raw, bias, rate, mine, other]
    aliases = {}
    if not first:
        dx, dc, db, draw, par = before
        args += [dc, db, par, dx, draw]
        in_specs += [maps, maps, params, anywhere, anywhere]
        aliases = {17: 0, 18: 3}
    grid_spec = pltpu.PrefetchScalarGridSpec(
        num_scalar_prefetch=1,
        grid=(2,),
        in_specs=in_specs,
        out_specs=[columns, maps, maps, lines, params],
        scratch_shapes=[
            pltpu.VMEM((blocks, GROUP, GROUP), BF16),
            pltpu.VMEM((blocks, GROUP, GROUP), BF16),
            pltpu.VMEM((blocks, GROUP, GROUP), F32),
            pltpu.VMEM((blocks, GROUP, states), F32),
            pltpu.VMEM((blocks, GROUP, states), F32),
            pltpu.VMEM((states, length), BF16),
            pltpu.VMEM((states, length), BF16),
            pltpu.VMEM((3 * width, 128), BF16),
        ],
    )
    return pl.pallas_call(
        functools.partial(grads_kernel, first, scale, part, half),
        grid_spec=grid_spec,
        out_shape=[
            jax.ShapeDtypeStruct((length, channels), BF16),
            jax.ShapeDtypeStruct((length, states), F32),
            jax.ShapeDtypeStruct((length, states), F32),
            jax.ShapeDtypeStruct((pieces, heads, length), F32),
            jax.ShapeDtypeStruct((8, 128), F32),
        ],
        input_output_aliases=aliases,
        compiler_params=pltpu.CompilerParams(vmem_limit_bytes=40 * 1024 * 1024),
        cost_estimate=pl.CostEstimate(
            flops=24 * length * width * (GROUP + states),
            bytes_accessed=12 * length * width,
            transcendentals=0,
        ),
        name="local_grads",
    )(y, *args)


def summed_over(value, axis):
    size = lax.axis_size(axis)
    if size & (size - 1):
        return lax.psum(value, axis)
    bit = 1
    while bit < size:
        steps = (bit, 2 * bit, 3 * bit) if 4 * bit <= size else (bit,)
        got = [lax.ppermute(value, axis, [(i, i ^ s) for i in range(size)]) for s in steps]
        value = value + got[0]
        if len(got) == 3:
            value = value + (got[1] + got[2])
        bit *= 4 if len(got) == 3 else 2
    return value


def after(value, *earlier):
    return lax.optimization_barrier((value, *earlier))[0]


def entering(sent, kept, states, token):
    size = lax.axis_size("seq")
    pairs = size // 2
    index = lax.axis_index("seq")
    place, second = index // 2, index % 2 == 1
    swap = [(i, i ^ 1) for i in range(size)]

    def parts(a):
        return a[:states], a[states : 2 * states], a[2 * states : 2 * states + 1]

    message = sent if token is None else after(sent, token)
    arrived = lax.ppermute(message, "seq", swap)
    token = yield message, arrived
    (own_l, own_k, own_d), (got_l, got_k, got_d) = parts(kept), parts(after(arrived, token))
    l1, k1, d1 = [jnp.where(second, b, a) for a, b in ((own_l, got_l), (own_k, got_k), (own_d, got_d))]
    l2, k2, d2 = [jnp.where(second, a, b) for a, b in ((own_l, got_l), (own_k, got_k), (own_d, got_d))]
    whole_l = d2 * l1 + l2
    whole_k = k1 + d1 * k2
    whole_d = d1 * d2
    start = jnp.zeros_like(whole_l)
    end = jnp.zeros_like(whole_k)
    for hop in range(1, pairs):
        message = jnp.where(place == hop - 1, whole_d * start + whole_l, whole_d * end + whole_k)
        route = []
        for y in range(2):
            route.append((2 * (hop - 1) + y, 2 * hop + y))
            route.append((2 * (pairs - hop) + y, 2 * (pairs - hop - 1) + y))
        arrived = lax.ppermute(message, "seq", route)
        token = yield message, arrived
        arrived = after(arrived, token)
        start = jnp.where(place == hop, arrived, start)
        end = jnp.where(place == pairs - 1 - hop, arrived, end)
    for_first = jnp.concatenate([start, k2 + d2 * end], axis=0)
    for_second = jnp.concatenate([d1 * start + l1, end], axis=0)
    mine = jnp.where(second, for_second, for_first)
    message = jnp.where(second, for_first, for_second)
    other = lax.ppermute(message, "seq", swap)
    yield message, other
    yield mine, other


def shards(inputs, input_map, output_map, step_raw, step_bias, decay_rate, skip_gain, cotangent):
    length = inputs.shape[1]
    heads = step_raw.shape[1]
    states = input_map.shape[2]
    x, b, c, dy = inputs[0], input_map[0], output_map[0], cotangent[0]
    vectors = (
        step_raw,
        step_bias.reshape(1, heads),
        decay_rate.reshape(1, heads),
        skip_gain.reshape(1, heads),
    )
    size = lax.axis_size("seq")
    y = lax.axis_index("seq") % 2
    scale = 1.0 / math.sqrt(length * size * lax.axis_size("batch"))

    def local(half, part, count, before):
        at = jnp.reshape(half * PARTS + part, (1,)).astype(jnp.int32)
        out, saved = local_states(at, count, x, dy, b, c, vectors, before)
        return out, saved + list(before[3:] if before else [])

    sent, kept = [], []
    saved = None
    for part in range(PARTS):
        out, saved = local(1 - y, part, 1, saved)
        sent += out
    kept, saved = local(y, 0, PARTS, saved)

    transfers = size // 2 + 1
    order = [(0, 0), (1, 0)] + [
        pick for k in range(1, transfers) for pick in ((0, k), (1, k - 1)) if pick != (1, 0)
    ]
    order.append((1, transfers - 1))
    flows, token = {}, None
    for part, k in order:
        if k == 0:
            flows[part] = entering(sent[part], kept[part], states, token)
            message, arrived = next(flows[part])
            token = arrived if part == 0 else message
        else:
            token = flows[part].send(token)[0]
    here = jnp.reshape(y, (1,)).astype(jnp.int32)
    before = None
    for part in range(PARTS):
        mine, other = next(flows[part])
        other = after(other, token)
        before = local_grads(part, scale, here, saved, dy, b, c, vectors, mine, other, before)
    dx, dc, db, draw, params = before
    summed = summed_over(summed_over(params, "batch"), "seq")
    return (
        dx[None],
        db[None],
        dc[None],
        draw.reshape(heads, length)[None],
        summed[:2, :heads],
        summed[2, :heads],
    )


def solution(mesh):
    in_specs = (
        P("batch", "seq", None),
        P("batch", "seq", None),
        P("batch", "seq", None),
        P("batch", None, "seq"),
        P(),
        P(),
        P(),
        P("batch", "seq", None),
    )
    out_specs = (
        P("batch", "seq", None),
        P("batch", "seq", None),
        P("batch", "seq", None),
        P("batch", None, "seq"),
        P(),
        P(),
    )
    return jax.shard_map(shards, mesh=mesh, in_specs=in_specs, out_specs=out_specs, check_vma=False)
```

```python
import functools
import math

import jax
import jax.numpy as jnp
import numpy as np
from jax import lax
from jax.experimental import pallas as pl
from jax.experimental.pallas import tpu as pltpu
from jax.sharding import PartitionSpec as P

GROUP = 256
PARTS = 2
VMEM_LIMIT = 60 * 1024 * 1024
SMALL_LIMIT = 40 * 1024 * 1024
F32 = jnp.float32
BF16 = jnp.bfloat16


def dot(a, b, dims):
    return lax.dot_general(a, b, (dims, ((), ())), preferred_element_type=F32)


NN = ((1,), (0,))
NT = ((1,), (1,))
TN = ((0,), (0,))


def split2(a):
    hi = a.astype(BF16).astype(F32)
    return hi, a - hi


def head_matrix(heads, width):
    size = width // heads
    row = lax.broadcasted_iota(jnp.int32, (heads, width), 0)
    col = lax.broadcasted_iota(jnp.int32, (heads, width), 1)
    return ((col >= row * size) & (col < (row + 1) * size)).astype(F32)


def head_sums(values, member):
    hi, lo = split2(values)
    return dot(member, hi.astype(BF16), NT) + dot(member, lo.astype(BF16), NT)


def running(rows, upper):
    hi, rest = split2(rows)
    mid, lo = split2(rest)
    k = rows.shape[0]
    out = dot(jnp.concatenate([hi, mid, lo], axis=0).astype(BF16), upper, NN)
    return out[:k] + out[k : 2 * k] + out[2 * k :]


def triangle(width, lower):
    row = lax.broadcasted_iota(jnp.int32, (width, width), 0)
    col = lax.broadcasted_iota(jnp.int32, (width, width), 1)
    return (row >= col) if lower else (row <= col)


def softplus(v):
    return jnp.maximum(v, 0.0) + jnp.log1p(jnp.exp(-jnp.abs(v)))


def column(line, piece, heads):
    shape = (heads, line.shape[1])
    row = lax.broadcasted_iota(jnp.int32, shape, 0)
    col = lax.broadcasted_iota(jnp.int32, shape, 1)
    return jnp.sum(jnp.where(col == row + piece * heads, line, 0.0), axis=1, keepdims=True)


def block_sums(logs, blocks):
    heads = logs.shape[0]
    ones = triangle(GROUP, False).astype(BF16)
    stacked = jnp.concatenate([logs[:, n * GROUP : (n + 1) * GROUP] for n in range(blocks)], axis=0)
    cums = running(stacked, ones)
    return [cums[n * heads : (n + 1) * heads] for n in range(blocks)]


def factors(raw, bias, rate, skip, columns_ref, table_ref):
    heads, length = raw.shape
    width = table_ref.shape[1]
    blocks = length // GROUP
    step = softplus(raw + bias)
    cums = block_sums(-rate * step, blocks)
    totals = [cum[:, GROUP - 1 :] for cum in cums]
    before = [jnp.zeros((heads, 1), F32)]
    for total in totals:
        before.append(before[-1] + total)
    for n in range(blocks):
        rows = slice(n * GROUP, (n + 1) * GROUP)
        gain = split2(jnp.exp(totals[n] - cums[n]) * step[:, rows])
        lift = split2(jnp.exp(cums[n] - totals[n]))
        columns_ref[rows, :] = jnp.concatenate([*gain, *lift], axis=0).T.astype(BF16)
    whole = before[-1]
    lines = [jnp.exp(t) for t in totals]
    lines += [jnp.exp(whole - before[n + 1]) for n in range(blocks)]
    lines += [jnp.exp(before[n + 1]) for n in range(blocks)]
    lines += [jnp.exp(whole), skip]
    lines += [skip] * (-len(lines) % 8)
    hi, lo = split2(jnp.concatenate(lines, axis=1).T)
    member = head_matrix(heads, width).astype(BF16)
    table_ref[...] = dot(hi.astype(BF16), member, NN) + dot(lo.astype(BF16), member, NN)


def picker(piece, heads, all_heads, width, first):
    shape = (4 * all_heads, width)
    row = lax.broadcasted_iota(jnp.int32, shape, 0)
    col = lax.broadcasted_iota(jnp.int32, shape, 1)
    size = width // heads
    base = (0 if first else 2 * all_heads) + piece * heads
    hit = None
    for term in range(2):
        low = (row - (base + term * all_heads)) * size
        one = (col >= low) & (col < low + size)
        hit = one if hit is None else hit | one
    return hit.astype(BF16)


def local_kernel(first, last, count, *refs):
    at_ref, x_ref, dy_ref, b_ref, c_ref = refs[:5]
    if first:
        raw_ref, bias_ref, rate_ref, skip_ref = refs[5:9]
        outs = refs[9:-7]
        xs_ref, ys_ref, direct_ref, columns_ref, table_ref, bt, ct = refs[-7:]
    else:
        columns_ref, table_ref = refs[5:7]
        outs = refs[10 : 10 + count]
        xs_ref, ys_ref, direct_ref = refs[10 + count : 13 + count]
        if last:
            left, right, bt, ct = refs[13 + count :]
        else:
            bt, ct = refs[13 + count :]
    g = pl.program_id(0)
    length, width = x_ref.shape
    states = b_ref.shape[1]
    blocks = length // GROUP
    piece = at_ref[0] + g
    all_heads = columns_ref.shape[1] // 4
    heads = all_heads * width // table_ref.shape[1]

    @pl.when(g == 0)
    def _():
        bt[...] = b_ref[...].T
        ct[...] = c_ref[...].T
        if first:
            factors(
                raw_ref[0],
                column(bias_ref[...], 0, all_heads),
                column(rate_ref[...], 0, all_heads),
                column(skip_ref[...], 0, all_heads),
                columns_ref,
                table_ref,
            )
        if last:
            for n in range(blocks):
                rows = slice(n * GROUP, (n + 1) * GROUP)
                scores = dot(c_ref[rows, :], b_ref[rows, :], NT)
                left[n] = jnp.where(triangle(GROUP, True), scores, 0.0).astype(BF16)
                scores = dot(b_ref[rows, :], c_ref[rows, :], NT)
                right[n] = jnp.where(triangle(GROUP, False), scores, 0.0).astype(BF16)

    gain = picker(piece, heads, all_heads, width, True)
    lift = picker(piece, heads, all_heads, width, False)
    table = table_ref[:, pl.ds(pl.multiple_of(piece * width, width), width)]
    state = jnp.zeros((states, width), F32)
    grad = jnp.zeros((states, width), F32)
    direct = jnp.zeros((8, width), F32)
    for n in range(blocks):
        rows = slice(n * GROUP, (n + 1) * GROUP)
        x = x_ref[rows, :].astype(F32)
        dy = dy_ref[rows, :].astype(F32)
        direct = direct + jnp.sum((dy * x).reshape(GROUP // 8, 8, width), axis=0)
        scaled_x = (x * dot(columns_ref[rows, :], gain, NN)).astype(BF16)
        scaled_dy = (dy * dot(columns_ref[rows, :], lift, NN)).astype(BF16)
        xs_ref[rows, :] = scaled_x
        ys_ref[rows, :] = scaled_dy
        later = table[blocks + n : blocks + n + 1]
        earlier = table[2 * blocks + n : 2 * blocks + n + 1]
        state = state + later * dot(bt[:, rows], scaled_x, NN)
        grad = grad + earlier * dot(ct[:, rows], scaled_dy, NN)
    direct_ref[...] = direct
    decay = jnp.broadcast_to(table[3 * blocks : 3 * blocks + 1], (8, width))
    for k, out_ref in enumerate(outs):

        @pl.when(g == k)
        def _():
            out_ref[:states] = state
            out_ref[states : 2 * states] = grad
            out_ref[2 * states :] = decay


def local_states(at, count, last, x, dy, b, c, vectors, before):
    length, channels = x.shape
    states = b.shape[1]
    pieces = 2 * PARTS
    width = channels // pieces
    lines = 3 * (length // GROUP) + 2
    lines += -lines % 8
    first = before is None
    whole = lambda g, at: (0, 0)
    columns = pl.BlockSpec((length, width), lambda g, at: (0, at[0] + g))
    strip = pl.BlockSpec((8, width), lambda g, at: (0, at[0] + g))
    maps = pl.BlockSpec((length, states), whole)
    anywhere = pl.BlockSpec(memory_space=pl.ANY)
    in_specs = [columns, columns, maps, maps]
    out_specs = [pl.BlockSpec((2 * states + 8, width), whole)] * count + [columns, columns, strip]
    out_shape = [jax.ShapeDtypeStruct((2 * states + 8, width), F32)] * count + [
        jax.ShapeDtypeStruct((length, channels), BF16),
        jax.ShapeDtypeStruct((length, channels), BF16),
        jax.ShapeDtypeStruct((8, channels), F32),
    ]
    aliases = {}
    if first:
        raw, bias, rate, skip = vectors
        heads = raw.shape[1]
        args = [raw, bias, rate, skip]
        in_specs += [pl.BlockSpec(raw.shape, lambda g, at: (0, 0, 0))]
        in_specs += [pl.BlockSpec(bias.shape, whole)] * 3
        tables = [
            jax.ShapeDtypeStruct((length, 4 * heads), BF16),
            jax.ShapeDtypeStruct((lines, channels), F32),
        ]
        out_shape += tables
        out_specs += [pl.BlockSpec(t.shape, whole) for t in tables]
    else:
        xs, ys, direct, factor_columns, table = before
        args = [factor_columns, table, xs, ys, direct]
        in_specs += [pl.BlockSpec(factor_columns.shape, whole), pl.BlockSpec(table.shape, whole)]
        in_specs += [anywhere] * 3
        aliases = {7: count, 8: count + 1, 9: count + 2}
    scratch = [pltpu.VMEM((states, length), BF16)] * 2
    if last:
        blocks = length // GROUP
        extra = [jax.ShapeDtypeStruct((blocks, GROUP, GROUP), BF16)] * 2
        extra += [jax.ShapeDtypeStruct((states, length), BF16)] * 2
        out_shape += extra
        out_specs += [pl.BlockSpec(e.shape, lambda g, at, n=len(e.shape): (0,) * n) for e in extra]
        scratch = []
    grid_spec = pltpu.PrefetchScalarGridSpec(
        num_scalar_prefetch=1,
        grid=(count,),
        in_specs=in_specs,
        out_specs=out_specs,
        scratch_shapes=scratch,
    )
    out = pl.pallas_call(
        functools.partial(local_kernel, first, last, count),
        grid_spec=grid_spec,
        out_shape=out_shape,
        input_output_aliases=aliases,
        compiler_params=pltpu.CompilerParams(vmem_limit_bytes=VMEM_LIMIT),
        cost_estimate=pl.CostEstimate(
            flops=8 * count * length * width * states,
            bytes_accessed=8 * count * length * width,
            transcendentals=0,
        ),
        name="local_states",
    )(at, x, dy, b, c, *args)
    return out[:count], list(out[count:])


def adding(width, heads, places):
    out = np.zeros((len(places) * width, 128), np.float32)
    size = width // heads
    for k, place in enumerate(places):
        for channel in range(width):
            out[k * width + channel, place * heads + channel // size] = 1.0
    return jnp.asarray(out, BF16)


def lanes_of(values, piece, shape):
    row = lax.broadcasted_iota(jnp.int32, shape, 0)
    col = lax.broadcasted_iota(jnp.int32, shape, 1)
    return jnp.sum(jnp.where(col == row + piece * shape[0], values, 0.0), axis=0, keepdims=True)


def inner_kernel(first, scale, piece, *refs):
    xs_ref, ys_ref, dy_ref, direct_ref, b_ref, c_ref, bt, ct, left, right = refs[:10]
    adder, columns_ref, table_ref, raw_ref, bias_ref, rate_ref = refs[10:16]
    refs = refs[16:]
    if not first:
        dc_in, db_in, par_in = refs[:3]
        refs = refs[5:]
    dx_ref, dc_ref, db_ref, draw_ref, par_ref = refs
    heads = raw_ref.shape[1]
    length, width = xs_ref.shape
    states = b_ref.shape[1]
    blocks = length // GROUP
    all_heads = columns_ref.shape[1] // 4
    member = head_matrix(heads, width).astype(BF16)
    lower = triangle(GROUP, True)
    rows = [slice(n * GROUP, (n + 1) * GROUP) for n in range(blocks)]
    table = table_ref[...]
    skip = table[3 * blocks + 1 : 3 * blocks + 2]
    state = grad = None
    entering_low, ends = [], []
    for n in range(blocks):
        fresh = dot(bt[:, rows[n]], xs_ref[rows[n], :], NN)
        if state is not None:
            state = table[n : n + 1] * state
            entering_low.append(state.astype(BF16))
            state = state + fresh
        else:
            entering_low.append(None)
            state = fresh
        ends.append(state)
    leaving_low, edges = [None] * blocks, [jnp.zeros((1, width), F32)] * blocks
    for n in reversed(range(blocks)):
        if grad is not None:
            leaving_low[n] = grad.astype(BF16)
            edges[n] = jnp.sum(ends[n] * grad, axis=0, keepdims=True)
        if n:
            fresh = dot(ct[:, rows[n]], ys_ref[rows[n], :], NN)
            grad = table[n : n + 1] * (fresh if grad is None else grad + fresh)
    gain = picker(piece, heads, all_heads, width, True)
    added = []
    for n in range(blocks):
        scaled_x, scaled_dy = xs_ref[rows[n], :], ys_ref[rows[n], :]
        forward = dot(left[n], scaled_x, NN)
        if entering_low[n] is not None:
            forward = forward + dot(c_ref[rows[n], :], entering_low[n], NN)
        backward = dot(right[n], scaled_dy, NN)
        if leaving_low[n] is not None:
            backward = backward + dot(b_ref[rows[n], :], leaving_low[n], NN)
        weight = dot(columns_ref[rows[n], :], gain, NN)
        dx_ref[rows[n], :] = (weight * backward + skip * dy_ref[rows[n], :].astype(F32)).astype(
            dx_ref.dtype
        )
        v = scaled_x.astype(F32) * backward
        difference = scaled_dy.astype(F32) * forward - v
        hi = difference.astype(BF16)
        lo = (difference - hi.astype(F32)).astype(BF16)
        added.append(dot(jnp.concatenate([hi, lo, v.astype(BF16)], axis=1), adder[...], NN))
        pair = jnp.where(lower, dot(scaled_dy, scaled_x, NT), 0.0).astype(BF16)
        dc = dot(pair, b_ref[rows[n], :], NN)
        db = dot(pair, c_ref[rows[n], :], TN)
        if entering_low[n] is not None:
            dc = dc + dot(scaled_dy, entering_low[n], NT)
        if leaving_low[n] is not None:
            db = db + dot(scaled_x, leaving_low[n], NT)
        dc_ref[rows[n], :] = dc if first else dc + dc_in[rows[n], :]
        db_ref[rows[n], :] = db if first else db + db_in[rows[n], :]
    added = [a.T for a in added]
    edge = head_sums(jnp.concatenate(edges + [edges[0]] * (8 - blocks), axis=0), member)
    slopes = running(jnp.concatenate([a[:heads] for a in added], axis=0), lower.astype(BF16))
    slope = jnp.concatenate(
        [slopes[n * heads : (n + 1) * heads] + edge[:, n : n + 1] for n in range(blocks)], axis=1
    )
    v = jnp.concatenate([a[heads : 2 * heads] for a in added], axis=1)
    raw = raw_ref[0] + column(bias_ref[...], piece, heads)
    step = softplus(raw)
    draw = (v / step - column(rate_ref[...], piece, heads) * slope) / (1.0 + jnp.exp(-raw))
    draw_ref[0] = draw
    values = (
        jnp.sum(draw, axis=1, keepdims=True),
        jnp.sum(head_sums(direct_ref[...], member), axis=1, keepdims=True),
        -jnp.sum(step * slope, axis=1, keepdims=True),
    )
    par_ref[...] = jnp.zeros_like(par_ref) if first else par_in[...]
    for k, value in enumerate(values):
        par_ref[k : k + 1] += lanes_of(value * scale, piece, (heads, par_ref.shape[1]))


def inner_grads(piece, scale, saved, dy, b, c, vectors, before):
    xs, ys, direct, factor_columns, table, left, right, bt, ct = saved
    raw, bias, rate, _ = vectors
    length, channels = xs.shape
    pieces = 2 * PARTS
    heads = raw.shape[1] // pieces
    raw = raw.reshape(pieces, heads, length)
    width = channels // pieces
    states = b.shape[1]
    first = before is None
    adder = adding(width, heads, (0, 0, 1))
    place = lambda g: (0, piece)
    all_of = lambda a: pl.BlockSpec(a.shape, lambda g, n=len(a.shape): (0,) * n)
    columns = pl.BlockSpec((length, width), place)
    maps = pl.BlockSpec((length, states), lambda g: (0, 0))
    lines = pl.BlockSpec((1, heads, length), lambda g: (piece, 0, 0))
    params = pl.BlockSpec((8, 128), lambda g: (0, 0))
    anywhere = pl.BlockSpec(memory_space=pl.ANY)
    args = [xs, ys, dy, direct, b, c, bt, ct, left, right]
    args += [adder, factor_columns, table, raw, bias, rate]
    in_specs = [columns, columns, columns, pl.BlockSpec((8, width), place)]
    in_specs += [all_of(a) for a in (b, c, bt, ct, left, right, adder, factor_columns)]
    in_specs += [pl.BlockSpec((table.shape[0], width), place), lines, all_of(bias), all_of(rate)]
    aliases = {}
    if not first:
        dx, dc, db, draw, par = before
        args += [dc, db, par, dx, draw]
        in_specs += [maps, maps, params, anywhere, anywhere]
        aliases = {19: 0, 20: 3}
    return pl.pallas_call(
        functools.partial(inner_kernel, first, scale, piece),
        grid=(1,),
        in_specs=in_specs,
        out_specs=[columns, maps, maps, lines, params],
        out_shape=[
            jax.ShapeDtypeStruct((length, channels), BF16),
            jax.ShapeDtypeStruct((length, states), F32),
            jax.ShapeDtypeStruct((length, states), F32),
            jax.ShapeDtypeStruct((pieces, heads, length), F32),
            jax.ShapeDtypeStruct((8, 128), F32),
        ],
        input_output_aliases=aliases,
        compiler_params=pltpu.CompilerParams(vmem_limit_bytes=VMEM_LIMIT),
        cost_estimate=pl.CostEstimate(
            flops=24 * length * width * (GROUP + states),
            bytes_accessed=10 * length * width,
            transcendentals=0,
        ),
        name="inner_grads",
    )(*args)


def entering_kernel(scale, part, half, *refs):
    y_ref, xs_ref, ys_ref, b_ref, c_ref, adder, columns_ref, table_ref = refs[:8]
    raw_ref, bias_ref, rate_ref, mine_ref, other_ref, dx_in, draw_in, par_in = refs[8:16]
    dx_ref, draw_ref, par_ref = refs[16:]
    g = pl.program_id(0)
    heads = raw_ref.shape[1]
    length, width = xs_ref.shape
    states = b_ref.shape[1]
    blocks = length // GROUP
    piece = g * half + part
    all_heads = columns_ref.shape[1] // 4
    member = head_matrix(heads, width).astype(BF16)
    rows = [slice(n * GROUP, (n + 1) * GROUP) for n in range(blocks)]

    @pl.when(g == 0)
    def _():
        par_ref[...] = par_in[...]

    own = g == y_ref[0]
    state = jnp.where(own, mine_ref[:states], other_ref[:states])
    grad = jnp.where(own, mine_ref[states:], other_ref[states:])
    table = table_ref[...]
    gain = picker(piece, heads, all_heads, width, True)
    added = []
    for n in range(blocks):
        entered = (table[2 * blocks + n : 2 * blocks + n + 1] * state).astype(BF16)
        leaving = (table[blocks + n : blocks + n + 1] * grad).astype(BF16)
        forward = dot(c_ref[rows[n], :], entered, NN)
        backward = dot(b_ref[rows[n], :], leaving, NN)
        weight = dot(columns_ref[rows[n], :], gain, NN)
        dx_ref[rows[n], :] = (dx_in[rows[n], :].astype(F32) + weight * backward).astype(
            dx_ref.dtype
        )
        p = (xs_ref[rows[n], :].astype(F32) * backward).astype(BF16)
        q = (ys_ref[rows[n], :].astype(F32) * forward).astype(BF16)
        added.append(dot(jnp.concatenate([p, q], axis=1), adder[...], NN))
    added = [a.T for a in added]
    cross = jnp.sum(state * grad, axis=0, keepdims=True) * table[3 * blocks : 3 * blocks + 1]
    cross = head_sums(jnp.broadcast_to(cross, (8, width)), member)[:, :1]
    ps, qs = [a[:heads] for a in added], [a[heads : 2 * heads] for a in added]
    p_sums = running(jnp.concatenate(ps, axis=0), triangle(GROUP, False).astype(BF16))
    q_sums = running(jnp.concatenate(qs, axis=0), triangle(GROUP, True).astype(BF16))
    p_sums = [p_sums[n * heads : (n + 1) * heads] for n in range(blocks)]
    q_sums = [q_sums[n * heads : (n + 1) * heads] for n in range(blocks)]
    slopes = [None] * blocks
    before = cross
    for n in range(blocks):
        slopes[n] = p_sums[n] - ps[n] + before
        before = before + p_sums[n][:, GROUP - 1 :]
    later = jnp.zeros_like(cross)
    for n in reversed(range(blocks)):
        slopes[n] = slopes[n] + q_sums[n] + later
        later = later + q_sums[n][:, :1]
    slope = jnp.concatenate(slopes, axis=1)
    raw = raw_ref[0] + column(bias_ref[...], piece, heads)
    step = softplus(raw)
    more = jnp.concatenate(ps, axis=1) / step - column(rate_ref[...], piece, heads) * slope
    more = more / (1.0 + jnp.exp(-raw))
    draw_ref[0] = draw_in[0] + more
    shape = (heads, par_ref.shape[1])
    par_ref[:1] += lanes_of(jnp.sum(more, axis=1, keepdims=True) * scale, piece, shape)
    par_ref[2:3] -= lanes_of(jnp.sum(step * slope, axis=1, keepdims=True) * scale, piece, shape)


def entering_grads(part, scale, y, saved, b, c, vectors, mine, other, dx, draw, par):
    xs, ys, _, factor_columns, table = saved[:5]
    raw, bias, rate, _ = vectors
    length, channels = xs.shape
    pieces = 2 * PARTS
    heads = raw.shape[1] // pieces
    raw = raw.reshape(pieces, heads, length)
    width = channels // pieces
    half = pieces // 2
    adder = adding(width, heads, (0, 1))
    place = lambda g, y: (0, g * half + part)
    all_of = lambda a: pl.BlockSpec(a.shape, lambda g, y, n=len(a.shape): (0,) * n)
    columns = pl.BlockSpec((length, width), place)
    lines = pl.BlockSpec((1, heads, length), lambda g, y: (g * half + part, 0, 0))
    in_specs = [columns, columns] + [all_of(a) for a in (b, c, adder, factor_columns)]
    in_specs += [pl.BlockSpec((table.shape[0], width), place), lines]
    in_specs += [all_of(a) for a in (bias, rate, mine, other)] + [columns, lines, all_of(par)]
    return pl.pallas_call(
        functools.partial(entering_kernel, scale, part, half),
        grid_spec=pltpu.PrefetchScalarGridSpec(
            num_scalar_prefetch=1,
            grid=(2,),
            in_specs=in_specs,
            out_specs=[columns, lines, all_of(par)],
        ),
        out_shape=[jax.ShapeDtypeStruct(a.shape, a.dtype) for a in (dx, draw, par)],
        input_output_aliases={13: 0, 14: 1},
        compiler_params=pltpu.CompilerParams(vmem_limit_bytes=SMALL_LIMIT),
        cost_estimate=pl.CostEstimate(
            flops=24 * length * width * GROUP, bytes_accessed=16 * length * width, transcendentals=0
        ),
        name="entering_grads",
    )(y, xs, ys, b, c, adder, factor_columns, table, raw, bias, rate, mine, other, dx, draw, par)


def maps_kernel(*refs):
    y_ref, xs_ref, ys_ref, table_ref, dc_in, db_in = refs[:6]
    held, (dc_ref, db_ref) = refs[6:-2], refs[-2:]
    g = pl.program_id(0)
    length = xs_ref.shape[0]
    states = dc_in.shape[1]
    blocks = length // GROUP

    @pl.when(g == 0)
    def _():
        dc_ref[...] = dc_in[...]
        db_ref[...] = db_in[...]

    own = g // PARTS == y_ref[0]
    both = None
    for part in range(PARTS):
        mine, other = held[2 * part], held[2 * part + 1]
        one = jnp.where(own, mine[...], other[...])
        both = one if both is None else jnp.where(g % PARTS == part, one, both)
    state, grad = both[:states], both[states:]
    table = table_ref[...]
    for n in range(blocks):
        rows = slice(n * GROUP, (n + 1) * GROUP)
        entered = (table[2 * blocks + n : 2 * blocks + n + 1] * state).astype(BF16)
        leaving = (table[blocks + n : blocks + n + 1] * grad).astype(BF16)
        dc_ref[rows, :] += dot(ys_ref[rows, :], entered, NT)
        db_ref[rows, :] += dot(xs_ref[rows, :], leaving, NT)


def maps_grads(y, saved, dc, db, held):
    xs, ys, _, _, table = saved[:5]
    length, channels = xs.shape
    pieces = 2 * PARTS
    width = channels // pieces
    place = lambda g, y: (0, g)
    all_of = lambda a: pl.BlockSpec(a.shape, lambda g, y: (0, 0))
    columns = pl.BlockSpec((length, width), place)
    return pl.pallas_call(
        maps_kernel,
        grid_spec=pltpu.PrefetchScalarGridSpec(
            num_scalar_prefetch=1,
            grid=(pieces,),
            in_specs=[columns, columns, pl.BlockSpec((table.shape[0], width), place)]
            + [all_of(a) for a in (dc, db, *held)],
            out_specs=[all_of(dc), all_of(db)],
        ),
        out_shape=[jax.ShapeDtypeStruct(a.shape, a.dtype) for a in (dc, db)],
        compiler_params=pltpu.CompilerParams(vmem_limit_bytes=SMALL_LIMIT),
        cost_estimate=pl.CostEstimate(
            flops=16 * length * channels * dc.shape[1],
            bytes_accessed=4 * length * channels,
            transcendentals=0,
        ),
        name="maps_grads",
    )(y, xs, ys, table, dc, db, *held)


def summed_over(value, axis):
    size = lax.axis_size(axis)
    if size & (size - 1):
        return lax.psum(value, axis)
    bit = 1
    while bit < size:
        count = min(8, size // bit)
        got = [
            lax.ppermute(value, axis, [(i, i ^ (k * bit)) for i in range(size)])
            for k in range(1, count)
        ]
        terms = [value] + got
        while len(terms) > 1:
            terms = [terms[k] + terms[k + 1] for k in range(0, len(terms), 2)]
        value = terms[0]
        bit *= count
    return value


def after(value, *earlier):
    return lax.optimization_barrier((value, *earlier))[0]


def entering(sent, kept, states, token):
    size = lax.axis_size("seq")
    pairs = size // 2
    index = lax.axis_index("seq")
    place, second = index // 2, index % 2 == 1
    swap = [(i, i ^ 1) for i in range(size)]

    def parts(a):
        return a[:states], a[states : 2 * states], a[2 * states : 2 * states + 1]

    message = sent if token is None else after(sent, token)
    arrived = lax.ppermute(message, "seq", swap)
    token = yield message, arrived
    (own_l, own_k, own_d), (got_l, got_k, got_d) = parts(kept), parts(after(arrived, token))
    l1, k1, d1 = [jnp.where(second, b, a) for a, b in ((own_l, got_l), (own_k, got_k), (own_d, got_d))]
    l2, k2, d2 = [jnp.where(second, a, b) for a, b in ((own_l, got_l), (own_k, got_k), (own_d, got_d))]
    whole_l = d2 * l1 + l2
    whole_k = k1 + d1 * k2
    whole_d = d1 * d2
    start = jnp.zeros_like(whole_l)
    end = jnp.zeros_like(whole_k)
    for hop in range(1, pairs):
        message = jnp.where(place == hop - 1, whole_d * start + whole_l, whole_d * end + whole_k)
        route = []
        for y in range(2):
            route.append((2 * (hop - 1) + y, 2 * hop + y))
            route.append((2 * (pairs - hop) + y, 2 * (pairs - hop - 1) + y))
        arrived = lax.ppermute(message, "seq", route)
        token = yield message, arrived
        arrived = after(arrived, token)
        start = jnp.where(place == hop, arrived, start)
        end = jnp.where(place == pairs - 1 - hop, arrived, end)
    for_first = jnp.concatenate([start, k2 + d2 * end], axis=0)
    for_second = jnp.concatenate([d1 * start + l1, end], axis=0)
    mine = jnp.where(second, for_second, for_first)
    message = jnp.where(second, for_first, for_second)
    other = lax.ppermute(message, "seq", swap)
    yield message, other
    yield mine, other


def shards(inputs, input_map, output_map, step_raw, step_bias, decay_rate, skip_gain, cotangent):
    length = inputs.shape[1]
    heads = step_raw.shape[1]
    states = input_map.shape[2]
    x, b, c, dy = inputs[0], input_map[0], output_map[0], cotangent[0]
    vectors = (
        step_raw,
        step_bias.reshape(1, heads),
        decay_rate.reshape(1, heads),
        skip_gain.reshape(1, heads),
    )
    size = lax.axis_size("seq")
    y = lax.axis_index("seq") % 2
    scale = 1.0 / math.sqrt(length * size * lax.axis_size("batch"))

    def local(half, part, count, before):
        at = jnp.reshape(half * PARTS + part, (1,)).astype(jnp.int32)
        last = count == PARTS
        out, saved = local_states(at, count, last, x, dy, b, c, vectors, before)
        return out, saved[:3] + list(before[3:] if before else []) + saved[3:]

    sent, kept = [], []
    saved = None
    for part in range(PARTS):
        out, saved = local(1 - y, part, 1, saved)
        sent += out
    kept, saved = local(y, 0, PARTS, saved)

    transfers = size // 2 + 1
    order = [(0, 0), (1, 0)] + [
        pick for k in range(1, transfers) for pick in ((0, k), (1, k - 1)) if pick != (1, 0)
    ]
    order.append((1, transfers - 1))
    flows, token = {}, None
    inner, piece = None, 0

    def inner_piece(token):
        bias = vectors[1] if token is None else after(vectors[1], token)
        moved = (vectors[0], bias, *vectors[2:])
        return inner_grads(piece, scale, saved, dy, b, c, moved, inner)

    for part, k in order:
        if k == 0:
            flows[part] = entering(sent[part], kept[part], states, token)
            message, arrived = next(flows[part])
            token = arrived if part == 0 else message
        else:
            token = flows[part].send(token)[0]
        if (part, k) == (0, 1) or (part == 1 and 0 < k < transfers - 1):
            if piece < 2 * PARTS:
                inner = inner_piece(token)
                token = inner[-1]
                piece += 1
    while piece < 2 * PARTS:
        inner = inner_piece(token)
        token = inner[-1]
        piece += 1
    here = jnp.reshape(y, (1,)).astype(jnp.int32)
    dx, dc, db, draw, params = inner
    held = []
    for part in range(PARTS):
        mine, other = next(flows[part])
        other = after(other, token)
        held += [mine, other]
        dx, draw, params = entering_grads(
            part, scale, here, saved, b, c, vectors, mine, other, dx, draw, params
        )
    dc, db = maps_grads(after(here, params), saved, dc, db, held)
    summed = summed_over(summed_over(params, "batch"), "seq")
    return (
        dx[None],
        db[None],
        dc[None],
        draw.reshape(heads, length)[None],
        summed[:2, :heads],
        summed[2, :heads],
    )


def solution(mesh):
    in_specs = (
        P("batch", "seq", None),
        P("batch", "seq", None),
        P("batch", "seq", None),
        P("batch", None, "seq"),
        P(),
        P(),
        P(),
        P("batch", "seq", None),
    )
    out_specs = (
        P("batch", "seq", None),
        P("batch", "seq", None),
        P("batch", "seq", None),
        P("batch", None, "seq"),
        P(),
        P(),
    )
    return jax.shard_map(shards, mesh=mesh, in_specs=in_specs, out_specs=out_specs, check_vma=False)
```

```python
import functools
import math

import jax
import jax.numpy as jnp
from jax import lax
from jax.experimental import pallas as pl
from jax.experimental.pallas import tpu as pltpu
from jax.sharding import PartitionSpec as P

GROUP = 256
PARTS = 2
VMEM_LIMIT = 60 * 1024 * 1024
F32 = jnp.float32
BF16 = jnp.bfloat16


def dot(a, b, dims):
    return lax.dot_general(a, b, (dims, ((), ())), preferred_element_type=F32)


NN = ((1,), (0,))
NT = ((1,), (1,))
TN = ((0,), (0,))


def split2(a):
    hi = a.astype(BF16).astype(F32)
    return hi, a - hi


def head_matrix(heads, width):
    size = width // heads
    row = lax.broadcasted_iota(jnp.int32, (heads, width), 0)
    col = lax.broadcasted_iota(jnp.int32, (heads, width), 1)
    return ((col >= row * size) & (col < (row + 1) * size)).astype(F32)


def head_sums(values, member):
    hi, lo = split2(values)
    return dot(member, hi.astype(BF16), NT) + dot(member, lo.astype(BF16), NT)


def running(rows, upper):
    hi, rest = split2(rows)
    mid, lo = split2(rest)
    k = rows.shape[0]
    out = dot(jnp.concatenate([hi, mid, lo], axis=0).astype(BF16), upper, NN)
    return out[:k] + out[k : 2 * k] + out[2 * k :]


def triangle(width, lower):
    row = lax.broadcasted_iota(jnp.int32, (width, width), 0)
    col = lax.broadcasted_iota(jnp.int32, (width, width), 1)
    return (row >= col) if lower else (row <= col)


def softplus(v):
    return jnp.maximum(v, 0.0) + jnp.log1p(jnp.exp(-jnp.abs(v)))


def column(line, piece, heads):
    shape = (heads, line.shape[1])
    row = lax.broadcasted_iota(jnp.int32, shape, 0)
    col = lax.broadcasted_iota(jnp.int32, shape, 1)
    return jnp.sum(jnp.where(col == row + piece * heads, line, 0.0), axis=1, keepdims=True)


def block_sums(logs, blocks):
    heads = logs.shape[0]
    ones = triangle(GROUP, False).astype(BF16)
    stacked = jnp.concatenate([logs[:, n * GROUP : (n + 1) * GROUP] for n in range(blocks)], axis=0)
    cums = running(stacked, ones)
    return [cums[n * heads : (n + 1) * heads] for n in range(blocks)]


def factors(raw, bias, rate, skip, columns_ref, table_ref):
    heads, length = raw.shape
    width = table_ref.shape[1]
    blocks = length // GROUP
    step = softplus(raw + bias)
    cums = block_sums(-rate * step, blocks)
    totals = [cum[:, GROUP - 1 :] for cum in cums]
    before = [jnp.zeros((heads, 1), F32)]
    for total in totals:
        before.append(before[-1] + total)
    for n in range(blocks):
        rows = slice(n * GROUP, (n + 1) * GROUP)
        gain = split2(jnp.exp(totals[n] - cums[n]) * step[:, rows])
        lift = split2(jnp.exp(cums[n] - totals[n]))
        columns_ref[rows, :] = jnp.concatenate([*gain, *lift], axis=0).T.astype(BF16)
    whole = before[-1]
    lines = [jnp.exp(t) for t in totals]
    lines += [jnp.exp(whole - before[n + 1]) for n in range(blocks)]
    lines += [jnp.exp(before[n + 1]) for n in range(blocks)]
    lines += [jnp.exp(whole), skip]
    lines += [skip] * (-len(lines) % 8)
    hi, lo = split2(jnp.concatenate(lines, axis=1).T)
    member = head_matrix(heads, width).astype(BF16)
    table_ref[...] = dot(hi.astype(BF16), member, NN) + dot(lo.astype(BF16), member, NN)


def picker(piece, heads, all_heads, width, first):
    shape = (4 * all_heads, width)
    row = lax.broadcasted_iota(jnp.int32, shape, 0)
    col = lax.broadcasted_iota(jnp.int32, shape, 1)
    size = width // heads
    base = (0 if first else 2 * all_heads) + piece * heads
    hit = None
    for term in range(2):
        low = (row - (base + term * all_heads)) * size
        one = (col >= low) & (col < low + size)
        hit = one if hit is None else hit | one
    return hit.astype(BF16)


def local_kernel(first, *refs):
    at_ref, x_ref, dy_ref, b_ref, c_ref = refs[:5]
    if first:
        raw_ref, bias_ref, rate_ref, skip_ref = refs[5:9]
        outs = refs[9:-7]
        xs_ref, ys_ref, direct_ref, columns_ref, table_ref, bt, ct = refs[-7:]
    else:
        columns_ref, table_ref = refs[5:7]
        outs = refs[10:-5]
        xs_ref, ys_ref, direct_ref, bt, ct = refs[-5:]
    g = pl.program_id(0)
    length, width = x_ref.shape
    states = b_ref.shape[1]
    blocks = length // GROUP
    piece = at_ref[0] + g
    all_heads = columns_ref.shape[1] // 4
    heads = all_heads * width // table_ref.shape[1]

    @pl.when(g == 0)
    def _():
        bt[...] = b_ref[...].T
        ct[...] = c_ref[...].T
        if first:
            factors(
                raw_ref[0],
                column(bias_ref[...], 0, all_heads),
                column(rate_ref[...], 0, all_heads),
                column(skip_ref[...], 0, all_heads),
                columns_ref,
                table_ref,
            )

    gain = dot(columns_ref[...], picker(piece, heads, all_heads, width, True), NN)
    lift = dot(columns_ref[...], picker(piece, heads, all_heads, width, False), NN)
    table = table_ref[:, pl.ds(pl.multiple_of(piece * width, width), width)]
    state = jnp.zeros((states, width), F32)
    grad = jnp.zeros((states, width), F32)
    direct = jnp.zeros((8, width), F32)
    for n in range(blocks):
        rows = slice(n * GROUP, (n + 1) * GROUP)
        x = x_ref[rows, :].astype(F32)
        dy = dy_ref[rows, :].astype(F32)
        direct = direct + jnp.sum((dy * x).reshape(GROUP // 8, 8, width), axis=0)
        scaled_x = (x * gain[rows]).astype(BF16)
        scaled_dy = (dy * lift[rows]).astype(BF16)
        xs_ref[rows, :] = scaled_x
        ys_ref[rows, :] = scaled_dy
        later = table[blocks + n : blocks + n + 1]
        earlier = table[2 * blocks + n : 2 * blocks + n + 1]
        state = state + later * dot(bt[:, rows], scaled_x, NN)
        grad = grad + earlier * dot(ct[:, rows], scaled_dy, NN)
    direct_ref[...] = direct
    decay = jnp.broadcast_to(table[3 * blocks : 3 * blocks + 1], (8, width))
    for k, out_ref in enumerate(outs):

        @pl.when(g == k)
        def _():
            out_ref[:states] = state
            out_ref[states : 2 * states] = grad
            out_ref[2 * states :] = decay


def local_states(at, count, x, dy, b, c, vectors, before):
    length, channels = x.shape
    states = b.shape[1]
    pieces = 2 * PARTS
    width = channels // pieces
    lines = 3 * (length // GROUP) + 2
    lines += -lines % 8
    first = before is None
    whole = lambda g, at: (0, 0)
    columns = pl.BlockSpec((length, width), lambda g, at: (0, at[0] + g))
    strip = pl.BlockSpec((8, width), lambda g, at: (0, at[0] + g))
    maps = pl.BlockSpec((length, states), whole)
    anywhere = pl.BlockSpec(memory_space=pl.ANY)
    in_specs = [columns, columns, maps, maps]
    out_specs = [pl.BlockSpec((2 * states + 8, width), whole)] * count + [columns, columns, strip]
    out_shape = [jax.ShapeDtypeStruct((2 * states + 8, width), F32)] * count + [
        jax.ShapeDtypeStruct((length, channels), BF16),
        jax.ShapeDtypeStruct((length, channels), BF16),
        jax.ShapeDtypeStruct((8, channels), F32),
    ]
    aliases = {}
    if first:
        raw, bias, rate, skip = vectors
        heads = raw.shape[1]
        args = [raw, bias, rate, skip]
        in_specs += [pl.BlockSpec(raw.shape, lambda g, at: (0, 0, 0))]
        in_specs += [pl.BlockSpec(bias.shape, whole)] * 3
        tables = [
            jax.ShapeDtypeStruct((length, 4 * heads), BF16),
            jax.ShapeDtypeStruct((lines, channels), F32),
        ]
        out_shape += tables
        out_specs += [pl.BlockSpec(t.shape, whole) for t in tables]
    else:
        xs, ys, direct, factor_columns, table = before
        args = [factor_columns, table, xs, ys, direct]
        in_specs += [pl.BlockSpec(factor_columns.shape, whole), pl.BlockSpec(table.shape, whole)]
        in_specs += [anywhere] * 3
        aliases = {7: count, 8: count + 1, 9: count + 2}
    grid_spec = pltpu.PrefetchScalarGridSpec(
        num_scalar_prefetch=1,
        grid=(count,),
        in_specs=in_specs,
        out_specs=out_specs,
        scratch_shapes=[
            pltpu.VMEM((states, length), BF16),
            pltpu.VMEM((states, length), BF16),
        ],
    )
    out = pl.pallas_call(
        functools.partial(local_kernel, first),
        grid_spec=grid_spec,
        out_shape=out_shape,
        input_output_aliases=aliases,
        compiler_params=pltpu.CompilerParams(vmem_limit_bytes=VMEM_LIMIT),
        cost_estimate=pl.CostEstimate(
            flops=8 * count * length * width * states,
            bytes_accessed=8 * count * length * width,
            transcendentals=0,
        ),
        name="local_states",
    )(at, x, dy, b, c, *args)
    return out[:count], list(out[count:])


def grads_kernel(first, scale, part, half, *refs):
    y_ref, xs_ref, ys_ref, dy_ref, direct_ref, b_ref, c_ref, columns_ref, table_ref = refs[:9]
    raw_ref, bias_ref, rate_ref, mine_ref, other_ref = refs[9:14]
    refs = refs[14:]
    if not first:
        dc_in, db_in, par_in = refs[:3]
        refs = refs[5:]
    dx_ref, dc_ref, db_ref, draw_ref, par_ref = refs[:5]
    left, right, sums, dc_sum, db_sum, bt, ct, adder, terms = refs[5:]
    g = pl.program_id(0)
    heads = raw_ref.shape[1]
    length, width = xs_ref.shape
    states = b_ref.shape[1]
    blocks = length // GROUP
    piece = g * half + part
    all_heads = columns_ref.shape[1] // 4
    member = head_matrix(heads, width).astype(BF16)
    lower = triangle(GROUP, True)
    rows = [slice(n * GROUP, (n + 1) * GROUP) for n in range(blocks)]

    @pl.when(g == 0)
    def _():
        bt[...] = b_ref[...].T
        ct[...] = c_ref[...].T
        upper = triangle(GROUP, False)
        for n in range(blocks):
            b, c = b_ref[rows[n], :], c_ref[rows[n], :]
            left[n] = jnp.where(lower, dot(c, b, NT), 0.0).astype(BF16)
            right[n] = jnp.where(upper, dot(b, c, NT), 0.0).astype(BF16)
        sums[...] = jnp.zeros_like(sums)
        dc_sum[...] = jnp.zeros_like(dc_sum)
        db_sum[...] = jnp.zeros_like(db_sum)
        par_ref[...] = jnp.zeros_like(par_ref) if first else par_in[...]
        row = lax.broadcasted_iota(jnp.int32, (width, 128), 0)
        col = lax.broadcasted_iota(jnp.int32, (width, 128), 1)
        size = width // heads
        one = ((row >= col * size) & (row < (col + 1) * size)).astype(BF16)
        col = col - heads
        two = ((row >= col * size) & (row < (col + 1) * size)).astype(BF16)
        adder[:width] = one
        adder[width : 2 * width] = one
        adder[2 * width :] = two

    own = g == y_ref[0]
    state = jnp.where(own, mine_ref[:states], other_ref[:states])
    grad = jnp.where(own, mine_ref[states:], other_ref[states:])
    table = table_ref[...]
    skip = table[3 * blocks + 1 : 3 * blocks + 2]
    entering_low, ends = [], []
    for n in range(blocks):
        state = table[n : n + 1] * state
        entering_low.append(state.astype(BF16))
        state = state + dot(bt[:, rows[n]], xs_ref[rows[n], :], NN)
        ends.append(state)
    leaving_low, edges = [None] * blocks, [None] * blocks
    for n in reversed(range(blocks)):
        leaving_low[n] = grad.astype(BF16)
        edges[n] = jnp.sum(ends[n] * grad, axis=0, keepdims=True)
        grad = table[n : n + 1] * (grad + dot(ct[:, rows[n]], ys_ref[rows[n], :], NN))
    gain = dot(columns_ref[...], picker(piece, heads, all_heads, width, True), NN)
    for n in range(blocks):
        scaled_x, scaled_dy = xs_ref[rows[n], :], ys_ref[rows[n], :]
        forward = dot(left[n], scaled_x, NN) + dot(c_ref[rows[n], :], entering_low[n], NN)
        backward = dot(right[n], scaled_dy, NN) + dot(b_ref[rows[n], :], leaving_low[n], NN)
        weight = gain[rows[n]]
        dx_ref[rows[n], :] = (weight * backward + skip * dy_ref[rows[n], :].astype(F32)).astype(
            dx_ref.dtype
        )
        v = scaled_x.astype(F32) * backward
        difference = scaled_dy.astype(F32) * forward - v
        hi = difference.astype(BF16)
        lo = (difference - hi.astype(F32)).astype(BF16)
        terms[rows[n], :width] = hi
        terms[rows[n], width : 2 * width] = lo
        terms[rows[n], 2 * width :] = v.astype(BF16)
        sums[n] += dot(scaled_dy, scaled_x, NT)
        dc_sum[n] += dot(scaled_dy, entering_low[n], NT)
        db_sum[n] += dot(scaled_x, leaving_low[n], NT)
    added = dot(terms[...], adder[...], NN).T
    added = [added[:, rows[n]] for n in range(blocks)]
    edge = head_sums(jnp.concatenate(edges + [edges[0]] * (8 - blocks), axis=0), member)
    slopes = running(
        jnp.concatenate([a[:heads] for a in added], axis=0), lower.astype(BF16)
    )
    slope = jnp.concatenate(
        [slopes[n * heads : (n + 1) * heads] + edge[:, n : n + 1] for n in range(blocks)], axis=1
    )
    v = jnp.concatenate([a[heads : 2 * heads] for a in added], axis=1)
    raw = raw_ref[0] + column(bias_ref[...], piece, heads)
    step = softplus(raw)
    draw = (v / step - column(rate_ref[...], piece, heads) * slope) / (1.0 + jnp.exp(-raw))
    draw_ref[0] = draw
    values = (
        jnp.sum(draw, axis=1, keepdims=True),
        jnp.sum(head_sums(direct_ref[...], member), axis=1, keepdims=True),
        -jnp.sum(step * slope, axis=1, keepdims=True),
    )
    shape = (heads, par_ref.shape[1])
    spot = lax.broadcasted_iota(jnp.int32, shape, 1) == (
        lax.broadcasted_iota(jnp.int32, shape, 0) + piece * heads
    )
    for k, value in enumerate(values):
        par_ref[k : k + 1] += jnp.sum(jnp.where(spot, value * scale, 0.0), axis=0, keepdims=True)

    @pl.when(g == pl.num_programs(0) - 1)
    def _():
        for n in range(blocks):
            pair = jnp.where(lower, sums[n], 0.0).astype(BF16)
            dc = dot(pair, b_ref[rows[n], :], NN) + dc_sum[n]
            db = dot(pair, c_ref[rows[n], :], TN) + db_sum[n]
            if not first:
                dc = dc + dc_in[rows[n], :]
                db = db + db_in[rows[n], :]
            dc_ref[rows[n], :] = dc
            db_ref[rows[n], :] = db


def local_grads(part, scale, y, saved, dy, b, c, vectors, mine, other, before):
    xs, ys, direct, factor_columns, table = saved
    raw, bias, rate, _ = vectors
    length, channels = xs.shape
    pieces = 2 * PARTS
    heads = raw.shape[1] // pieces
    raw = raw.reshape(pieces, heads, length)
    width = channels // pieces
    states = b.shape[1]
    blocks = length // GROUP
    half = pieces // 2
    first = before is None
    whole = lambda g, y: (0, 0)
    place = lambda g, y: (0, g * half + part)
    columns = pl.BlockSpec((length, width), place)
    maps = pl.BlockSpec((length, states), whole)
    line = pl.BlockSpec(bias.shape, whole)
    lines = pl.BlockSpec((1, heads, length), lambda g, y: (g * half + part, 0, 0))
    held = pl.BlockSpec((2 * states, width), whole)
    params = pl.BlockSpec((8, 128), whole)
    anywhere = pl.BlockSpec(memory_space=pl.ANY)
    in_specs = [columns, columns, columns, pl.BlockSpec((8, width), place), maps, maps]
    in_specs += [
        pl.BlockSpec(factor_columns.shape, whole),
        pl.BlockSpec((table.shape[0], width), place),
    ]
    in_specs += [lines, line, line, held, held]
    args = [xs, ys, dy, direct, b, c, factor_columns, table, raw, bias, rate, mine, other]
    aliases = {}
    if not first:
        dx, dc, db, draw, par = before
        args += [dc, db, par, dx, draw]
        in_specs += [maps, maps, params, anywhere, anywhere]
        aliases = {17: 0, 18: 3}
    grid_spec = pltpu.PrefetchScalarGridSpec(
        num_scalar_prefetch=1,
        grid=(2,),
        in_specs=in_specs,
        out_specs=[columns, maps, maps, lines, params],
        scratch_shapes=[
            pltpu.VMEM((blocks, GROUP, GROUP), BF16),
            pltpu.VMEM((blocks, GROUP, GROUP), BF16),
            pltpu.VMEM((blocks, GROUP, GROUP), F32),
            pltpu.VMEM((blocks, GROUP, states), F32),
            pltpu.VMEM((blocks, GROUP, states), F32),
            pltpu.VMEM((states, length), BF16),
            pltpu.VMEM((states, length), BF16),
            pltpu.VMEM((3 * width, 128), BF16),
            pltpu.VMEM((length, 3 * width), BF16),
        ],
    )
    return pl.pallas_call(
        functools.partial(grads_kernel, first, scale, part, half),
        grid_spec=grid_spec,
        out_shape=[
            jax.ShapeDtypeStruct((length, channels), BF16),
            jax.ShapeDtypeStruct((length, states), F32),
            jax.ShapeDtypeStruct((length, states), F32),
            jax.ShapeDtypeStruct((pieces, heads, length), F32),
            jax.ShapeDtypeStruct((8, 128), F32),
        ],
        input_output_aliases=aliases,
        compiler_params=pltpu.CompilerParams(vmem_limit_bytes=40 * 1024 * 1024),
        cost_estimate=pl.CostEstimate(
            flops=24 * length * width * (GROUP + states),
            bytes_accessed=12 * length * width,
            transcendentals=0,
        ),
        name="local_grads",
    )(y, *args)


def summed_over(value, axis):
    size = lax.axis_size(axis)
    if size & (size - 1):
        return lax.psum(value, axis)
    bit = 1
    while bit < size:
        count = min(8, size // bit)
        got = [
            lax.ppermute(value, axis, [(i, i ^ (k * bit)) for i in range(size)])
            for k in range(1, count)
        ]
        terms = [value] + got
        while len(terms) > 1:
            terms = [terms[k] + terms[k + 1] for k in range(0, len(terms), 2)]
        value = terms[0]
        bit *= count
    return value


def after(value, *earlier):
    return lax.optimization_barrier((value, *earlier))[0]


def halves(place_ref, kept_ref, got_ref, states):
    second = place_ref[0] == 1

    def rows(low, high):
        own, got = kept_ref[low:high], got_ref[low:high]
        return jnp.where(second, got, own), jnp.where(second, own, got)

    l1, l2 = rows(0, states)
    k1, k2 = rows(states, 2 * states)
    d1, d2 = rows(2 * states, 2 * states + 1)
    return l1, l2, k1, k2, d1, d2


def send_kernel(states, forward_from, *refs):
    place_ref, kept_ref, got_ref = refs[:3]
    out_ref = refs[-1]
    l1, l2, k1, k2, d1, d2 = halves(place_ref, kept_ref, got_ref, states)
    up = place_ref[1] == forward_from[0]
    for place in forward_from[1:]:
        up = up | (place_ref[1] == place)
    value = jnp.where(up, d2 * l1 + l2, k1 + d1 * k2)
    if len(refs) == 5:
        value = value + (d1 * d2) * refs[3][:states]
    out_ref[:states] = value
    out_ref[states:] = jnp.broadcast_to(d1 * d2, (8, out_ref.shape[1]))


def leave_kernel(states, pairs, *refs):
    place_ref, kept_ref, got_ref = refs[:3]
    arrived = refs[3:-2]
    mine_ref, message_ref = refs[-2:]
    l1, l2, k1, k2, d1, d2 = halves(place_ref, kept_ref, got_ref, states)
    place = place_ref[1]
    zero = jnp.zeros(l1.shape, F32)
    if pairs == 4:
        near, middle, far = [r[:states] for r in arrived]
        outer = arrived[0][states : states + 1] * far + near
        starts = [zero, near, middle, outer]
        ends = [outer, middle, near, zero]
    else:
        hops = [r[:states] for r in arrived]
        starts = [zero] + hops
        ends = hops[::-1] + [zero]
    start, end = starts[0], ends[0]
    for k in range(1, pairs):
        start = jnp.where(place == k, starts[k], start)
        end = jnp.where(place == k, ends[k], end)
    first_end = k2 + d2 * end
    second_start = d1 * start + l1
    second = place_ref[0] == 1
    mine_ref[:states] = jnp.where(second, second_start, start)
    mine_ref[states:] = jnp.where(second, end, first_end)
    message_ref[:states] = jnp.where(second, start, second_start)
    message_ref[states:] = jnp.where(second, first_end, end)


def joined(kernel, rows, count, where, *arrays):
    width = arrays[0].shape[1]
    out = [jax.ShapeDtypeStruct((rows, width), F32)] * count
    return pl.pallas_call(
        kernel,
        in_specs=[pl.BlockSpec(memory_space=pltpu.SMEM)]
        + [pl.BlockSpec(memory_space=pltpu.VMEM)] * len(arrays),
        out_specs=[pl.BlockSpec(memory_space=pltpu.VMEM)] * count,
        out_shape=out,
        cost_estimate=pl.CostEstimate(
            flops=8 * rows * width, bytes_accessed=16 * rows * width, transcendentals=0
        ),
        name="join_states",
    )(where, *arrays)


def entering(sent, kept, states, token):
    size = lax.axis_size("seq")
    pairs = size // 2
    index = lax.axis_index("seq")
    where = jnp.stack([index % 2, index // 2]).astype(jnp.int32)
    swap = [(i, i ^ 1) for i in range(size)]
    both = lambda moves: [(2 * a + y, 2 * b + y) for a, b in moves for y in range(2)]
    if pairs == 4:
        steps = [((0, 2), ([(0, 1), (1, 0), (2, 3), (3, 2)],)), ((1,), ([(1, 2), (2, 1)], [(1, 3), (2, 0)]))]
    else:
        steps = [
            ((k - 1,), ([(k - 1, k), (pairs - k, pairs - k - 1)],)) for k in range(1, pairs)
        ]

    message = sent if token is None else after(sent, *token)
    got = lax.ppermute(message, "seq", swap)
    token = yield message, got
    arrived = []
    for senders, routes in steps:
        if arrived:
            last = arrived[-1] = after(arrived[-1], token)
            inputs = (kept, got, last)
        else:
            got = after(got, token)
            inputs = (kept, got)
        kernel = functools.partial(send_kernel, states, senders)
        (message,) = joined(kernel, states + 8, 1, where, *inputs)
        arrived += [lax.ppermute(message, "seq", both(route)) for route in routes]
        token = yield message, arrived[-1]
    arrived[-1] = after(arrived[-1], token)
    kernel = functools.partial(leave_kernel, states, pairs)
    mine, message = joined(kernel, 2 * states, 2, where, kept, got, *arrived)
    other = lax.ppermute(message, "seq", swap)
    yield message, other
    yield mine, other


def shards(inputs, input_map, output_map, step_raw, step_bias, decay_rate, skip_gain, cotangent):
    length = inputs.shape[1]
    heads = step_raw.shape[1]
    states = input_map.shape[2]
    x, b, c, dy = inputs[0], input_map[0], output_map[0], cotangent[0]
    vectors = (
        step_raw,
        step_bias.reshape(1, heads),
        decay_rate.reshape(1, heads),
        skip_gain.reshape(1, heads),
    )
    size = lax.axis_size("seq")
    y = lax.axis_index("seq") % 2
    scale = 1.0 / math.sqrt(length * size * lax.axis_size("batch"))

    def local(half, part, count, before):
        at = jnp.reshape(half * PARTS + part, (1,)).astype(jnp.int32)
        out, saved = local_states(at, count, x, dy, b, c, vectors, before)
        return out, saved + list(before[3:] if before else [])

    sent, kept = [], []
    saved = None
    for part in range(PARTS):
        out, saved = local(1 - y, part, 1, saved)
        sent += out
    kept, saved = local(y, 0, PARTS, saved)

    transfers = 4 if size == 8 else size // 2 + 1
    order = [(0, 0), (1, 0)] + [
        pick for k in range(1, transfers) for pick in ((0, k), (1, k - 1)) if pick != (1, 0)
    ]
    order.append((1, transfers - 1))
    flows, token = {}, None
    for part, k in order:
        if k == 0:
            flows[part] = entering(sent[part], kept[part], states, token)
            message, arrived = next(flows[part])
            token = (arrived, kept[-1]) if part == 0 else message
        else:
            token = flows[part].send(token)[0]
    here = jnp.reshape(y, (1,)).astype(jnp.int32)
    before = None
    for part in range(PARTS):
        mine, other = next(flows[part])
        other = after(other, token)
        before = local_grads(part, scale, here, saved, dy, b, c, vectors, mine, other, before)
    dx, dc, db, draw, params = before
    summed = summed_over(summed_over(params, "batch"), "seq")
    return (
        dx[None],
        db[None],
        dc[None],
        draw.reshape(heads, length)[None],
        summed[:2, :heads],
        summed[2, :heads],
    )


def solution(mesh):
    in_specs = (
        P("batch", "seq", None),
        P("batch", "seq", None),
        P("batch", "seq", None),
        P("batch", None, "seq"),
        P(),
        P(),
        P(),
        P("batch", "seq", None),
    )
    out_specs = (
        P("batch", "seq", None),
        P("batch", "seq", None),
        P("batch", "seq", None),
        P("batch", None, "seq"),
        P(),
        P(),
    )
    return jax.shard_map(shards, mesh=mesh, in_specs=in_specs, out_specs=out_specs, check_vma=False)
```

```python
import functools
import math

import jax
import jax.numpy as jnp
from jax import lax
from jax.experimental import pallas as pl
from jax.experimental.pallas import tpu as pltpu
from jax.sharding import PartitionSpec as P

GROUP = 256
PARTS = 2
VMEM_LIMIT = 60 * 1024 * 1024
F32 = jnp.float32
BF16 = jnp.bfloat16


def dot(a, b, dims):
    return lax.dot_general(a, b, (dims, ((), ())), preferred_element_type=F32)


NN = ((1,), (0,))
NT = ((1,), (1,))
TN = ((0,), (0,))


def split2(a):
    hi = a.astype(BF16).astype(F32)
    return hi, a - hi


def head_matrix(heads, width):
    size = width // heads
    row = lax.broadcasted_iota(jnp.int32, (heads, width), 0)
    col = lax.broadcasted_iota(jnp.int32, (heads, width), 1)
    return ((col >= row * size) & (col < (row + 1) * size)).astype(F32)


def head_sums(values, member):
    hi, lo = split2(values)
    return dot(member, hi.astype(BF16), NT) + dot(member, lo.astype(BF16), NT)


def running(rows, upper):
    hi, rest = split2(rows)
    mid, lo = split2(rest)
    k = rows.shape[0]
    out = dot(jnp.concatenate([hi, mid, lo], axis=0).astype(BF16), upper, NN)
    return out[:k] + out[k : 2 * k] + out[2 * k :]


def triangle(width, lower):
    row = lax.broadcasted_iota(jnp.int32, (width, width), 0)
    col = lax.broadcasted_iota(jnp.int32, (width, width), 1)
    return (row >= col) if lower else (row <= col)


def softplus(v):
    return jnp.maximum(v, 0.0) + jnp.log1p(jnp.exp(-jnp.abs(v)))


def column(line, piece, heads):
    shape = (heads, line.shape[1])
    row = lax.broadcasted_iota(jnp.int32, shape, 0)
    col = lax.broadcasted_iota(jnp.int32, shape, 1)
    return jnp.sum(jnp.where(col == row + piece * heads, line, 0.0), axis=1, keepdims=True)


def block_sums(logs, blocks):
    heads = logs.shape[0]
    ones = triangle(GROUP, False).astype(BF16)
    stacked = jnp.concatenate([logs[:, n * GROUP : (n + 1) * GROUP] for n in range(blocks)], axis=0)
    cums = running(stacked, ones)
    return [cums[n * heads : (n + 1) * heads] for n in range(blocks)]


def factors(raw, bias, rate, skip, columns_ref, table_ref):
    heads, length = raw.shape
    width = table_ref.shape[1]
    blocks = length // GROUP
    step = softplus(raw + bias)
    cums = block_sums(-rate * step, blocks)
    totals = [cum[:, GROUP - 1 :] for cum in cums]
    before = [jnp.zeros((heads, 1), F32)]
    for total in totals:
        before.append(before[-1] + total)
    for n in range(blocks):
        rows = slice(n * GROUP, (n + 1) * GROUP)
        gain = split2(jnp.exp(totals[n] - cums[n]) * step[:, rows])
        lift = split2(jnp.exp(cums[n] - totals[n]))
        columns_ref[rows, :] = jnp.concatenate([*gain, *lift], axis=0).T.astype(BF16)
    whole = before[-1]
    lines = [jnp.exp(t) for t in totals]
    lines += [jnp.exp(whole - before[n + 1]) for n in range(blocks)]
    lines += [jnp.exp(before[n + 1]) for n in range(blocks)]
    lines += [jnp.exp(whole), skip]
    lines += [skip] * (-len(lines) % 8)
    hi, lo = split2(jnp.concatenate(lines, axis=1).T)
    member = head_matrix(heads, width).astype(BF16)
    table_ref[...] = dot(hi.astype(BF16), member, NN) + dot(lo.astype(BF16), member, NN)


def picker(piece, heads, all_heads, width, first):
    shape = (4 * all_heads, width)
    row = lax.broadcasted_iota(jnp.int32, shape, 0)
    col = lax.broadcasted_iota(jnp.int32, shape, 1)
    size = width // heads
    base = (0 if first else 2 * all_heads) + piece * heads
    hit = None
    for term in range(2):
        low = (row - (base + term * all_heads)) * size
        one = (col >= low) & (col < low + size)
        hit = one if hit is None else hit | one
    return hit.astype(BF16)


def local_kernel(first, *refs):
    at_ref, x_ref, dy_ref, b_ref, c_ref = refs[:5]
    if first:
        raw_ref, bias_ref, rate_ref, skip_ref = refs[5:9]
        outs = refs[9:-7]
        xs_ref, ys_ref, direct_ref, columns_ref, table_ref, bt, ct = refs[-7:]
    else:
        columns_ref, table_ref = refs[5:7]
        outs = refs[10:-5]
        xs_ref, ys_ref, direct_ref, bt, ct = refs[-5:]
    g = pl.program_id(0)
    length, width = x_ref.shape
    states = b_ref.shape[1]
    blocks = length // GROUP
    piece = at_ref[0] + g
    all_heads = columns_ref.shape[1] // 4
    heads = all_heads * width // table_ref.shape[1]

    @pl.when(g == 0)
    def _():
        bt[...] = b_ref[...].T
        ct[...] = c_ref[...].T
        if first:
            factors(
                raw_ref[0],
                column(bias_ref[...], 0, all_heads),
                column(rate_ref[...], 0, all_heads),
                column(skip_ref[...], 0, all_heads),
                columns_ref,
                table_ref,
            )

    gain = dot(columns_ref[...], picker(piece, heads, all_heads, width, True), NN)
    lift = dot(columns_ref[...], picker(piece, heads, all_heads, width, False), NN)
    table = table_ref[:, pl.ds(pl.multiple_of(piece * width, width), width)]
    state = jnp.zeros((states, width), F32)
    grad = jnp.zeros((states, width), F32)
    direct = jnp.zeros((8, width), F32)
    for n in range(blocks):
        rows = slice(n * GROUP, (n + 1) * GROUP)
        x = x_ref[rows, :].astype(F32)
        dy = dy_ref[rows, :].astype(F32)
        direct = direct + jnp.sum((dy * x).reshape(GROUP // 8, 8, width), axis=0)
        scaled_x = (x * gain[rows]).astype(BF16)
        scaled_dy = (dy * lift[rows]).astype(BF16)
        xs_ref[rows, :] = scaled_x
        ys_ref[rows, :] = scaled_dy
        later = table[blocks + n : blocks + n + 1]
        earlier = table[2 * blocks + n : 2 * blocks + n + 1]
        state = state + later * dot(bt[:, rows], scaled_x, NN)
        grad = grad + earlier * dot(ct[:, rows], scaled_dy, NN)
    direct_ref[...] = direct
    decay = jnp.broadcast_to(table[3 * blocks : 3 * blocks + 1], (8, width))
    for k, out_ref in enumerate(outs):

        @pl.when(g == k)
        def _():
            out_ref[:states] = state
            out_ref[states : 2 * states] = grad
            out_ref[2 * states :] = decay


def local_states(at, count, x, dy, b, c, vectors, before):
    length, channels = x.shape
    states = b.shape[1]
    pieces = 2 * PARTS
    width = channels // pieces
    lines = 3 * (length // GROUP) + 2
    lines += -lines % 8
    first = before is None
    whole = lambda g, at: (0, 0)
    columns = pl.BlockSpec((length, width), lambda g, at: (0, at[0] + g))
    strip = pl.BlockSpec((8, width), lambda g, at: (0, at[0] + g))
    maps = pl.BlockSpec((length, states), whole)
    anywhere = pl.BlockSpec(memory_space=pl.ANY)
    in_specs = [columns, columns, maps, maps]
    out_specs = [pl.BlockSpec((2 * states + 8, width), whole)] * count + [columns, columns, strip]
    out_shape = [jax.ShapeDtypeStruct((2 * states + 8, width), F32)] * count + [
        jax.ShapeDtypeStruct((length, channels), BF16),
        jax.ShapeDtypeStruct((length, channels), BF16),
        jax.ShapeDtypeStruct((8, channels), F32),
    ]
    aliases = {}
    if first:
        raw, bias, rate, skip = vectors
        heads = raw.shape[1]
        args = [raw, bias, rate, skip]
        in_specs += [pl.BlockSpec(raw.shape, lambda g, at: (0, 0, 0))]
        in_specs += [pl.BlockSpec(bias.shape, whole)] * 3
        tables = [
            jax.ShapeDtypeStruct((length, 4 * heads), BF16),
            jax.ShapeDtypeStruct((lines, channels), F32),
        ]
        out_shape += tables
        out_specs += [pl.BlockSpec(t.shape, whole) for t in tables]
    else:
        xs, ys, direct, factor_columns, table = before
        args = [factor_columns, table, xs, ys, direct]
        in_specs += [pl.BlockSpec(factor_columns.shape, whole), pl.BlockSpec(table.shape, whole)]
        in_specs += [anywhere] * 3
        aliases = {7: count, 8: count + 1, 9: count + 2}
    grid_spec = pltpu.PrefetchScalarGridSpec(
        num_scalar_prefetch=1,
        grid=(count,),
        in_specs=in_specs,
        out_specs=out_specs,
        scratch_shapes=[
            pltpu.VMEM((states, length), BF16),
            pltpu.VMEM((states, length), BF16),
        ],
    )
    out = pl.pallas_call(
        functools.partial(local_kernel, first),
        grid_spec=grid_spec,
        out_shape=out_shape,
        input_output_aliases=aliases,
        compiler_params=pltpu.CompilerParams(vmem_limit_bytes=VMEM_LIMIT),
        cost_estimate=pl.CostEstimate(
            flops=8 * count * length * width * states,
            bytes_accessed=8 * count * length * width,
            transcendentals=0,
        ),
        name="local_states",
    )(at, x, dy, b, c, *args)
    return out[:count], list(out[count:])


def grads_kernel(first, scale, part, half, *refs):
    y_ref, xs_ref, ys_ref, dy_ref, direct_ref, b_ref, c_ref, columns_ref, table_ref = refs[:9]
    raw_ref, bias_ref, rate_ref, mine_ref, other_ref = refs[9:14]
    refs = refs[14:]
    if not first:
        dc_in, db_in, par_in = refs[:3]
        refs = refs[5:]
    dx_ref, dc_ref, db_ref, draw_ref, par_ref = refs[:5]
    left, right, sums, dc_sum, db_sum, bt, ct, adder, terms = refs[5:]
    g = pl.program_id(0)
    heads = raw_ref.shape[1]
    length, width = xs_ref.shape
    states = b_ref.shape[1]
    blocks = length // GROUP
    piece = g * half + part
    all_heads = columns_ref.shape[1] // 4
    member = head_matrix(heads, width).astype(BF16)
    lower = triangle(GROUP, True)
    rows = [slice(n * GROUP, (n + 1) * GROUP) for n in range(blocks)]

    @pl.when(g == 0)
    def _():
        bt[...] = b_ref[...].T
        ct[...] = c_ref[...].T
        upper = triangle(GROUP, False)
        for n in range(blocks):
            b, c = b_ref[rows[n], :], c_ref[rows[n], :]
            left[n] = jnp.where(lower, dot(c, b, NT), 0.0).astype(BF16)
            right[n] = jnp.where(upper, dot(b, c, NT), 0.0).astype(BF16)
        sums[...] = jnp.zeros_like(sums)
        dc_sum[...] = jnp.zeros_like(dc_sum)
        db_sum[...] = jnp.zeros_like(db_sum)
        par_ref[...] = jnp.zeros_like(par_ref) if first else par_in[...]
        row = lax.broadcasted_iota(jnp.int32, (width, 128), 0)
        col = lax.broadcasted_iota(jnp.int32, (width, 128), 1)
        size = width // heads
        one = ((row >= col * size) & (row < (col + 1) * size)).astype(BF16)
        col = col - heads
        two = ((row >= col * size) & (row < (col + 1) * size)).astype(BF16)
        adder[:width] = one
        adder[width : 2 * width] = one
        adder[2 * width :] = two

    own = g == y_ref[0]
    state = jnp.where(own, mine_ref[:states], other_ref[:states])
    grad = jnp.where(own, mine_ref[states:], other_ref[states:])
    table = table_ref[...]
    skip = table[3 * blocks + 1 : 3 * blocks + 2]
    entering_low, ends = [], []
    for n in range(blocks):
        state = table[n : n + 1] * state
        entering_low.append(state.astype(BF16))
        state = state + dot(bt[:, rows[n]], xs_ref[rows[n], :], NN)
        ends.append(state)
    leaving_low, edges = [None] * blocks, [None] * blocks
    for n in reversed(range(blocks)):
        leaving_low[n] = grad.astype(BF16)
        edges[n] = jnp.sum(ends[n] * grad, axis=0, keepdims=True)
        grad = table[n : n + 1] * (grad + dot(ct[:, rows[n]], ys_ref[rows[n], :], NN))
    gain = dot(columns_ref[...], picker(piece, heads, all_heads, width, True), NN)
    for n in range(blocks):
        scaled_x, scaled_dy = xs_ref[rows[n], :], ys_ref[rows[n], :]
        forward = dot(left[n], scaled_x, NN) + dot(c_ref[rows[n], :], entering_low[n], NN)
        backward = dot(right[n], scaled_dy, NN) + dot(b_ref[rows[n], :], leaving_low[n], NN)
        weight = gain[rows[n]]
        dx_ref[rows[n], :] = (weight * backward + skip * dy_ref[rows[n], :].astype(F32)).astype(
            dx_ref.dtype
        )
        v = scaled_x.astype(F32) * backward
        difference = scaled_dy.astype(F32) * forward - v
        hi = difference.astype(BF16)
        lo = (difference - hi.astype(F32)).astype(BF16)
        terms[rows[n], :width] = hi
        terms[rows[n], width : 2 * width] = lo
        terms[rows[n], 2 * width :] = v.astype(BF16)
        sums[n] += dot(scaled_dy, scaled_x, NT)
        dc_sum[n] += dot(scaled_dy, entering_low[n], NT)
        db_sum[n] += dot(scaled_x, leaving_low[n], NT)
    added = dot(terms[...], adder[...], NN).T
    added = [added[:, rows[n]] for n in range(blocks)]
    edge = head_sums(jnp.concatenate(edges + [edges[0]] * (8 - blocks), axis=0), member)
    slopes = running(
        jnp.concatenate([a[:heads] for a in added], axis=0), lower.astype(BF16)
    )
    slope = jnp.concatenate(
        [slopes[n * heads : (n + 1) * heads] + edge[:, n : n + 1] for n in range(blocks)], axis=1
    )
    v = jnp.concatenate([a[heads : 2 * heads] for a in added], axis=1)
    raw = raw_ref[0] + column(bias_ref[...], piece, heads)
    step = softplus(raw)
    draw = (v / step - column(rate_ref[...], piece, heads) * slope) / (1.0 + jnp.exp(-raw))
    draw_ref[0] = draw
    values = (
        jnp.sum(draw, axis=1, keepdims=True),
        jnp.sum(head_sums(direct_ref[...], member), axis=1, keepdims=True),
        -jnp.sum(step * slope, axis=1, keepdims=True),
    )
    shape = (heads, par_ref.shape[1])
    spot = lax.broadcasted_iota(jnp.int32, shape, 1) == (
        lax.broadcasted_iota(jnp.int32, shape, 0) + piece * heads
    )
    for k, value in enumerate(values):
        par_ref[k : k + 1] += jnp.sum(jnp.where(spot, value * scale, 0.0), axis=0, keepdims=True)

    @pl.when(g == pl.num_programs(0) - 1)
    def _():
        for n in range(blocks):
            pair = jnp.where(lower, sums[n], 0.0).astype(BF16)
            dc = dot(pair, b_ref[rows[n], :], NN) + dc_sum[n]
            db = dot(pair, c_ref[rows[n], :], TN) + db_sum[n]
            if not first:
                dc = dc + dc_in[rows[n], :]
                db = db + db_in[rows[n], :]
            dc_ref[rows[n], :] = dc
            db_ref[rows[n], :] = db


def local_grads(part, scale, y, saved, dy, b, c, vectors, mine, other, before):
    xs, ys, direct, factor_columns, table = saved
    raw, bias, rate, _ = vectors
    length, channels = xs.shape
    pieces = 2 * PARTS
    heads = raw.shape[1] // pieces
    raw = raw.reshape(pieces, heads, length)
    width = channels // pieces
    states = b.shape[1]
    blocks = length // GROUP
    half = pieces // 2
    first = before is None
    whole = lambda g, y: (0, 0)
    place = lambda g, y: (0, g * half + part)
    columns = pl.BlockSpec((length, width), place)
    maps = pl.BlockSpec((length, states), whole)
    line = pl.BlockSpec(bias.shape, whole)
    lines = pl.BlockSpec((1, heads, length), lambda g, y: (g * half + part, 0, 0))
    held = pl.BlockSpec((2 * states, width), whole)
    params = pl.BlockSpec((8, 128), whole)
    anywhere = pl.BlockSpec(memory_space=pl.ANY)
    in_specs = [columns, columns, columns, pl.BlockSpec((8, width), place), maps, maps]
    in_specs += [
        pl.BlockSpec(factor_columns.shape, whole),
        pl.BlockSpec((table.shape[0], width), place),
    ]
    in_specs += [lines, line, line, held, held]
    args = [xs, ys, dy, direct, b, c, factor_columns, table, raw, bias, rate, mine, other]
    aliases = {}
    if not first:
        dx, dc, db, draw, par = before
        args += [dc, db, par, dx, draw]
        in_specs += [maps, maps, params, anywhere, anywhere]
        aliases = {17: 0, 18: 3}
    grid_spec = pltpu.PrefetchScalarGridSpec(
        num_scalar_prefetch=1,
        grid=(2,),
        in_specs=in_specs,
        out_specs=[columns, maps, maps, lines, params],
        scratch_shapes=[
            pltpu.VMEM((blocks, GROUP, GROUP), BF16),
            pltpu.VMEM((blocks, GROUP, GROUP), BF16),
            pltpu.VMEM((blocks, GROUP, GROUP), F32),
            pltpu.VMEM((blocks, GROUP, states), F32),
            pltpu.VMEM((blocks, GROUP, states), F32),
            pltpu.VMEM((states, length), BF16),
            pltpu.VMEM((states, length), BF16),
            pltpu.VMEM((3 * width, 128), BF16),
            pltpu.VMEM((length, 3 * width), BF16),
        ],
    )
    return pl.pallas_call(
        functools.partial(grads_kernel, first, scale, part, half),
        grid_spec=grid_spec,
        out_shape=[
            jax.ShapeDtypeStruct((length, channels), BF16),
            jax.ShapeDtypeStruct((length, states), F32),
            jax.ShapeDtypeStruct((length, states), F32),
            jax.ShapeDtypeStruct((pieces, heads, length), F32),
            jax.ShapeDtypeStruct((8, 128), F32),
        ],
        input_output_aliases=aliases,
        compiler_params=pltpu.CompilerParams(vmem_limit_bytes=40 * 1024 * 1024),
        cost_estimate=pl.CostEstimate(
            flops=24 * length * width * (GROUP + states),
            bytes_accessed=12 * length * width,
            transcendentals=0,
        ),
        name="local_grads",
    )(y, *args)


def summed_over(value, axis):
    size = lax.axis_size(axis)
    if size & (size - 1):
        return lax.psum(value, axis)
    bit = 1
    while bit < size:
        steps = (bit, 2 * bit, 3 * bit) if 4 * bit <= size else (bit,)
        got = [lax.ppermute(value, axis, [(i, i ^ s) for i in range(size)]) for s in steps]
        value = value + got[0]
        if len(got) == 3:
            value = value + (got[1] + got[2])
        bit *= 4 if len(got) == 3 else 2
    return value


def after(value, *earlier):
    return lax.optimization_barrier((value, *earlier))[0]


def entering(sent, kept, states, token):
    size = lax.axis_size("seq")
    pairs = size // 2
    index = lax.axis_index("seq")
    place, second = index // 2, index % 2 == 1
    swap = [(i, i ^ 1) for i in range(size)]
    both = lambda moves: [(2 * a + y, 2 * b + y) for a, b in moves for y in range(2)]
    if pairs == 4:
        steps = [([(0, 1), (1, 0), (2, 3), (3, 2)],), ([(1, 2), (2, 1)], [(1, 3), (2, 0)])]
        up = [(place == 0) | (place == 2), place == 1]
    else:
        steps = [([(k - 1, k), (pairs - k, pairs - k - 1)],) for k in range(1, pairs)]
        up = [place == k - 1 for k in range(1, pairs)]

    def halves(got, copy):
        spans = ((0, states), (states, 2 * states), (2 * states + copy, 2 * states + copy + 1))
        for low, high in spans:
            own, other = kept[low:high], got[low:high]
            yield jnp.where(second, other, own), jnp.where(second, own, other)

    message = sent if token is None else after(sent, *token)
    got = lax.ppermute(message, "seq", swap)
    token = yield message, got
    arrived = []
    for k, routes in enumerate(steps):
        if arrived:
            arrived[-1] = after(arrived[-1], token)
        else:
            got = after(got, token)
        (l1, l2), (k1, k2), (d1, d2) = halves(got, min(k, 3))
        message = jnp.where(up[k], d2 * l1 + l2, k1 + d1 * k2)
        if arrived:
            message = message + d1 * d2 * arrived[-1][:states]
        if len(steps) == 2 and k == 0:
            message = jnp.concatenate([message, jnp.broadcast_to(d1 * d2, (8, message.shape[1]))])
        arrived += [lax.ppermute(message, "seq", both(route)) for route in routes]
        token = yield message, arrived[-1]
    arrived[-1] = after(arrived[-1], token)

    def leaving(copy):
        (l1, _), (_, k2), (d1, d2) = halves(got, copy)
        zero = jnp.zeros_like(l1)
        if pairs == 4:
            near, middle, far = [a[:states] for a in arrived]
            outer = arrived[0][states + copy : states + copy + 1] * far + near
            starts, ends = [zero, near, middle, outer], [outer, middle, near, zero]
        else:
            starts, ends = [zero] + arrived, arrived[::-1] + [zero]
        start, end = starts[0], ends[0]
        for k in range(1, pairs):
            start = jnp.where(place == k, starts[k], start)
            end = jnp.where(place == k, ends[k], end)
        return start, d1 * start + l1, k2 + d2 * end, end

    first_start, second_start, first_end, second_end = leaving(4)
    message = jnp.concatenate(
        [
            jnp.where(second, first_start, second_start),
            jnp.where(second, first_end, second_end),
        ]
    )
    other = lax.ppermute(message, "seq", swap)
    yield message, other
    first_start, second_start, first_end, second_end = leaving(5)
    mine = jnp.concatenate(
        [
            jnp.where(second, second_start, first_start),
            jnp.where(second, second_end, first_end),
        ]
    )
    yield mine, other


def shards(inputs, input_map, output_map, step_raw, step_bias, decay_rate, skip_gain, cotangent):
    length = inputs.shape[1]
    heads = step_raw.shape[1]
    states = input_map.shape[2]
    x, b, c, dy = inputs[0], input_map[0], output_map[0], cotangent[0]
    vectors = (
        step_raw,
        step_bias.reshape(1, heads),
        decay_rate.reshape(1, heads),
        skip_gain.reshape(1, heads),
    )
    size = lax.axis_size("seq")
    y = lax.axis_index("seq") % 2
    scale = 1.0 / math.sqrt(length * size * lax.axis_size("batch"))

    def local(half, part, count, before):
        at = jnp.reshape(half * PARTS + part, (1,)).astype(jnp.int32)
        out, saved = local_states(at, count, x, dy, b, c, vectors, before)
        return out, saved + list(before[3:] if before else [])

    sent, kept = [], []
    saved = None
    for part in range(PARTS):
        out, saved = local(1 - y, part, 1, saved)
        sent += out
    kept, saved = local(y, 0, PARTS, saved)

    transfers = 4 if size == 8 else size // 2 + 1
    order = [(0, 0), (1, 0)] + [
        pick for k in range(1, transfers) for pick in ((0, k), (1, k - 1)) if pick != (1, 0)
    ]
    order.append((1, transfers - 1))
    flows, token = {}, None
    for part, k in order:
        if k == 0:
            flows[part] = entering(sent[part], kept[part], states, token)
            message, arrived = next(flows[part])
            token = None if part == 0 else message
        else:
            token = flows[part].send(token)[0]
    here = jnp.reshape(y, (1,)).astype(jnp.int32)
    before = None
    for part in range(PARTS):
        mine, other = next(flows[part])
        other = after(other, token)
        before = local_grads(part, scale, here, saved, dy, b, c, vectors, mine, other, before)
    dx, dc, db, draw, params = before
    summed = summed_over(summed_over(params, "batch"), "seq")
    return (
        dx[None],
        db[None],
        dc[None],
        draw.reshape(heads, length)[None],
        summed[:2, :heads],
        summed[2, :heads],
    )


def solution(mesh):
    in_specs = (
        P("batch", "seq", None),
        P("batch", "seq", None),
        P("batch", "seq", None),
        P("batch", None, "seq"),
        P(),
        P(),
        P(),
        P("batch", "seq", None),
    )
    out_specs = (
        P("batch", "seq", None),
        P("batch", "seq", None),
        P("batch", "seq", None),
        P("batch", None, "seq"),
        P(),
        P(),
    )
    return jax.shard_map(shards, mesh=mesh, in_specs=in_specs, out_specs=out_specs, check_vma=False)
```

```python
import functools
import math

import jax
import jax.numpy as jnp
import numpy as np
from jax import lax
from jax.experimental import pallas as pl
from jax.experimental.pallas import tpu as pltpu
from jax.sharding import PartitionSpec as P

GROUP = 256
PARTS = 2
VMEM_LIMIT = 60 * 1024 * 1024
SMALL_LIMIT = 40 * 1024 * 1024
F32 = jnp.float32
BF16 = jnp.bfloat16


def dot(a, b, dims):
    return lax.dot_general(a, b, (dims, ((), ())), preferred_element_type=F32)


NN = ((1,), (0,))
NT = ((1,), (1,))
TN = ((0,), (0,))


def split2(a):
    hi = a.astype(BF16).astype(F32)
    return hi, a - hi


def head_matrix(heads, width):
    size = width // heads
    row = lax.broadcasted_iota(jnp.int32, (heads, width), 0)
    col = lax.broadcasted_iota(jnp.int32, (heads, width), 1)
    return ((col >= row * size) & (col < (row + 1) * size)).astype(F32)


def head_sums(values, member):
    hi, lo = split2(values)
    return dot(member, hi.astype(BF16), NT) + dot(member, lo.astype(BF16), NT)


def running(rows, upper):
    hi, rest = split2(rows)
    mid, lo = split2(rest)
    k = rows.shape[0]
    out = dot(jnp.concatenate([hi, mid, lo], axis=0).astype(BF16), upper, NN)
    return out[:k] + out[k : 2 * k] + out[2 * k :]


def triangle(width, lower):
    row = lax.broadcasted_iota(jnp.int32, (width, width), 0)
    col = lax.broadcasted_iota(jnp.int32, (width, width), 1)
    return (row >= col) if lower else (row <= col)


def softplus(v):
    return jnp.maximum(v, 0.0) + jnp.log1p(jnp.exp(-jnp.abs(v)))


def column(line, piece, heads):
    shape = (heads, line.shape[1])
    row = lax.broadcasted_iota(jnp.int32, shape, 0)
    col = lax.broadcasted_iota(jnp.int32, shape, 1)
    return jnp.sum(jnp.where(col == row + piece * heads, line, 0.0), axis=1, keepdims=True)


def block_sums(logs, blocks):
    heads = logs.shape[0]
    ones = triangle(GROUP, False).astype(BF16)
    stacked = jnp.concatenate([logs[:, n * GROUP : (n + 1) * GROUP] for n in range(blocks)], axis=0)
    cums = running(stacked, ones)
    return [cums[n * heads : (n + 1) * heads] for n in range(blocks)]


def factors(raw, bias, rate, skip, columns_ref, table_ref):
    heads, length = raw.shape
    width = table_ref.shape[1]
    blocks = length // GROUP
    step = softplus(raw + bias)
    cums = block_sums(-rate * step, blocks)
    totals = [cum[:, GROUP - 1 :] for cum in cums]
    before = [jnp.zeros((heads, 1), F32)]
    for total in totals:
        before.append(before[-1] + total)
    for n in range(blocks):
        rows = slice(n * GROUP, (n + 1) * GROUP)
        gain = split2(jnp.exp(totals[n] - cums[n]) * step[:, rows])
        lift = split2(jnp.exp(cums[n] - totals[n]))
        columns_ref[rows, :] = jnp.concatenate([*gain, *lift], axis=0).T.astype(BF16)
    whole = before[-1]
    lines = [jnp.exp(t) for t in totals]
    lines += [jnp.exp(whole - before[n + 1]) for n in range(blocks)]
    lines += [jnp.exp(before[n + 1]) for n in range(blocks)]
    lines += [jnp.exp(whole), skip]
    lines += [skip] * (-len(lines) % 8)
    hi, lo = split2(jnp.concatenate(lines, axis=1).T)
    member = head_matrix(heads, width).astype(BF16)
    table_ref[...] = dot(hi.astype(BF16), member, NN) + dot(lo.astype(BF16), member, NN)


def picker(piece, heads, all_heads, width, first):
    shape = (4 * all_heads, width)
    row = lax.broadcasted_iota(jnp.int32, shape, 0)
    col = lax.broadcasted_iota(jnp.int32, shape, 1)
    size = width // heads
    base = (0 if first else 2 * all_heads) + piece * heads
    hit = None
    for term in range(2):
        low = (row - (base + term * all_heads)) * size
        one = (col >= low) & (col < low + size)
        hit = one if hit is None else hit | one
    return hit.astype(BF16)


def local_kernel(first, last, count, *refs):
    at_ref, x_ref, dy_ref, b_ref, c_ref = refs[:5]
    if first:
        raw_ref, bias_ref, rate_ref, skip_ref = refs[5:9]
        outs = refs[9:-7]
        xs_ref, ys_ref, direct_ref, columns_ref, table_ref, bt, ct = refs[-7:]
    else:
        columns_ref, table_ref = refs[5:7]
        outs = refs[10 : 10 + count]
        xs_ref, ys_ref, direct_ref = refs[10 + count : 13 + count]
        if last:
            left, right, bt, ct = refs[13 + count :]
        else:
            bt, ct = refs[13 + count :]
    g = pl.program_id(0)
    length, width = x_ref.shape
    states = b_ref.shape[1]
    blocks = length // GROUP
    piece = at_ref[0] + g
    all_heads = columns_ref.shape[1] // 4
    heads = all_heads * width // table_ref.shape[1]

    @pl.when(g == 0)
    def _():
        bt[...] = b_ref[...].T
        ct[...] = c_ref[...].T
        if first:
            factors(
                raw_ref[0],
                column(bias_ref[...], 0, all_heads),
                column(rate_ref[...], 0, all_heads),
                column(skip_ref[...], 0, all_heads),
                columns_ref,
                table_ref,
            )
        if last:
            for n in range(blocks):
                rows = slice(n * GROUP, (n + 1) * GROUP)
                scores = dot(c_ref[rows, :], b_ref[rows, :], NT)
                left[n] = jnp.where(triangle(GROUP, True), scores, 0.0).astype(BF16)
                scores = dot(b_ref[rows, :], c_ref[rows, :], NT)
                right[n] = jnp.where(triangle(GROUP, False), scores, 0.0).astype(BF16)

    gain = dot(columns_ref[...], picker(piece, heads, all_heads, width, True), NN)
    lift = dot(columns_ref[...], picker(piece, heads, all_heads, width, False), NN)
    table = table_ref[:, pl.ds(pl.multiple_of(piece * width, width), width)]
    state = jnp.zeros((states, width), F32)
    grad = jnp.zeros((states, width), F32)
    direct = jnp.zeros((8, width), F32)
    for n in range(blocks):
        rows = slice(n * GROUP, (n + 1) * GROUP)
        x = x_ref[rows, :].astype(F32)
        dy = dy_ref[rows, :].astype(F32)
        direct = direct + jnp.sum((dy * x).reshape(GROUP // 8, 8, width), axis=0)
        scaled_x = (x * gain[rows]).astype(BF16)
        scaled_dy = (dy * lift[rows]).astype(BF16)
        xs_ref[rows, :] = scaled_x
        ys_ref[rows, :] = scaled_dy
        later = table[blocks + n : blocks + n + 1]
        earlier = table[2 * blocks + n : 2 * blocks + n + 1]
        state = state + later * dot(bt[:, rows], scaled_x, NN)
        grad = grad + earlier * dot(ct[:, rows], scaled_dy, NN)
    direct_ref[...] = direct
    decay = jnp.broadcast_to(table[3 * blocks : 3 * blocks + 1], (8, width))
    for k, out_ref in enumerate(outs):

        @pl.when(g == k)
        def _():
            out_ref[:states] = state
            out_ref[states : 2 * states] = grad
            out_ref[2 * states :] = decay


def local_states(at, count, last, x, dy, b, c, vectors, before):
    length, channels = x.shape
    states = b.shape[1]
    pieces = 2 * PARTS
    width = channels // pieces
    lines = 3 * (length // GROUP) + 2
    lines += -lines % 8
    first = before is None
    whole = lambda g, at: (0, 0)
    columns = pl.BlockSpec((length, width), lambda g, at: (0, at[0] + g))
    strip = pl.BlockSpec((8, width), lambda g, at: (0, at[0] + g))
    maps = pl.BlockSpec((length, states), whole)
    anywhere = pl.BlockSpec(memory_space=pl.ANY)
    in_specs = [columns, columns, maps, maps]
    out_specs = [pl.BlockSpec((2 * states + 8, width), whole)] * count + [columns, columns, strip]
    out_shape = [jax.ShapeDtypeStruct((2 * states + 8, width), F32)] * count + [
        jax.ShapeDtypeStruct((length, channels), BF16),
        jax.ShapeDtypeStruct((length, channels), BF16),
        jax.ShapeDtypeStruct((8, channels), F32),
    ]
    aliases = {}
    if first:
        raw, bias, rate, skip = vectors
        heads = raw.shape[1]
        args = [raw, bias, rate, skip]
        in_specs += [pl.BlockSpec(raw.shape, lambda g, at: (0, 0, 0))]
        in_specs += [pl.BlockSpec(bias.shape, whole)] * 3
        tables = [
            jax.ShapeDtypeStruct((length, 4 * heads), BF16),
            jax.ShapeDtypeStruct((lines, channels), F32),
        ]
        out_shape += tables
        out_specs += [pl.BlockSpec(t.shape, whole) for t in tables]
    else:
        xs, ys, direct, factor_columns, table = before
        args = [factor_columns, table, xs, ys, direct]
        in_specs += [pl.BlockSpec(factor_columns.shape, whole), pl.BlockSpec(table.shape, whole)]
        in_specs += [anywhere] * 3
        aliases = {7: count, 8: count + 1, 9: count + 2}
    scratch = [pltpu.VMEM((states, length), BF16)] * 2
    if last:
        blocks = length // GROUP
        extra = [jax.ShapeDtypeStruct((blocks, GROUP, GROUP), BF16)] * 2
        extra += [jax.ShapeDtypeStruct((states, length), BF16)] * 2
        out_shape += extra
        out_specs += [pl.BlockSpec(e.shape, lambda g, at, n=len(e.shape): (0,) * n) for e in extra]
        scratch = []
    grid_spec = pltpu.PrefetchScalarGridSpec(
        num_scalar_prefetch=1,
        grid=(count,),
        in_specs=in_specs,
        out_specs=out_specs,
        scratch_shapes=scratch,
    )
    out = pl.pallas_call(
        functools.partial(local_kernel, first, last, count),
        grid_spec=grid_spec,
        out_shape=out_shape,
        input_output_aliases=aliases,
        compiler_params=pltpu.CompilerParams(vmem_limit_bytes=VMEM_LIMIT),
        cost_estimate=pl.CostEstimate(
            flops=8 * count * length * width * states,
            bytes_accessed=8 * count * length * width,
            transcendentals=0,
        ),
        name="local_states",
    )(at, x, dy, b, c, *args)
    return out[:count], list(out[count:])


def grads_kernel(first, scale, part, half, *refs):
    y_ref, xs_ref, ys_ref, dy_ref, direct_ref, b_ref, c_ref, columns_ref, table_ref = refs[:9]
    raw_ref, bias_ref, rate_ref, mine_ref, other_ref, bt, ct, left, right, adder = refs[9:19]
    refs = refs[19:]
    if not first:
        dc_in, db_in, par_in = refs[:3]
        refs = refs[5:]
    dx_ref, dc_ref, db_ref, draw_ref, par_ref = refs[:5]
    sums, dc_sum, db_sum, terms = refs[5:]
    g = pl.program_id(0)
    heads = raw_ref.shape[1]
    length, width = xs_ref.shape
    states = b_ref.shape[1]
    blocks = length // GROUP
    piece = g * half + part
    all_heads = columns_ref.shape[1] // 4
    member = head_matrix(heads, width).astype(BF16)
    lower = triangle(GROUP, True)
    rows = [slice(n * GROUP, (n + 1) * GROUP) for n in range(blocks)]

    @pl.when(g == 0)
    def _():
        sums[...] = jnp.zeros_like(sums)
        dc_sum[...] = jnp.zeros_like(dc_sum)
        db_sum[...] = jnp.zeros_like(db_sum)
        par_ref[...] = jnp.zeros_like(par_ref) if first else par_in[...]

    own = g == y_ref[0]
    state = jnp.where(own, mine_ref[:states], other_ref[:states])
    grad = jnp.where(own, mine_ref[states:], other_ref[states:])
    table = table_ref[...]
    skip = table[3 * blocks + 1 : 3 * blocks + 2]
    entering_low, ends = [], []
    for n in range(blocks):
        state = table[n : n + 1] * state
        entering_low.append(state.astype(BF16))
        state = state + dot(bt[:, rows[n]], xs_ref[rows[n], :], NN)
        ends.append(state)
    leaving_low, edges = [None] * blocks, [None] * blocks
    for n in reversed(range(blocks)):
        leaving_low[n] = grad.astype(BF16)
        edges[n] = jnp.sum(ends[n] * grad, axis=0, keepdims=True)
        grad = table[n : n + 1] * (grad + dot(ct[:, rows[n]], ys_ref[rows[n], :], NN))
    gain = dot(columns_ref[...], picker(piece, heads, all_heads, width, True), NN)
    for n in range(blocks):
        scaled_x, scaled_dy = xs_ref[rows[n], :], ys_ref[rows[n], :]
        forward = dot(left[n], scaled_x, NN) + dot(c_ref[rows[n], :], entering_low[n], NN)
        backward = dot(right[n], scaled_dy, NN) + dot(b_ref[rows[n], :], leaving_low[n], NN)
        weight = gain[rows[n]]
        dx_ref[rows[n], :] = (weight * backward + skip * dy_ref[rows[n], :].astype(F32)).astype(
            dx_ref.dtype
        )
        v = scaled_x.astype(F32) * backward
        difference = scaled_dy.astype(F32) * forward - v
        hi = difference.astype(BF16)
        lo = (difference - hi.astype(F32)).astype(BF16)
        terms[rows[n], :width] = hi
        terms[rows[n], width : 2 * width] = lo
        terms[rows[n], 2 * width :] = v.astype(BF16)
        sums[n] += dot(scaled_dy, scaled_x, NT)
        dc_sum[n] += dot(scaled_dy, entering_low[n], NT)
        db_sum[n] += dot(scaled_x, leaving_low[n], NT)
    added = dot(terms[...], adder[...], NN).T
    added = [added[:, rows[n]] for n in range(blocks)]
    edge = head_sums(jnp.concatenate(edges + [edges[0]] * (8 - blocks), axis=0), member)
    slopes = running(
        jnp.concatenate([a[:heads] for a in added], axis=0), lower.astype(BF16)
    )
    slope = jnp.concatenate(
        [slopes[n * heads : (n + 1) * heads] + edge[:, n : n + 1] for n in range(blocks)], axis=1
    )
    v = jnp.concatenate([a[heads : 2 * heads] for a in added], axis=1)
    raw = raw_ref[0] + column(bias_ref[...], piece, heads)
    step = softplus(raw)
    draw = (v / step - column(rate_ref[...], piece, heads) * slope) / (1.0 + jnp.exp(-raw))
    draw_ref[0] = draw
    values = (
        jnp.sum(draw, axis=1, keepdims=True),
        jnp.sum(head_sums(direct_ref[...], member), axis=1, keepdims=True),
        -jnp.sum(step * slope, axis=1, keepdims=True),
    )
    for k, value in enumerate(values):
        par_ref[k : k + 1] += lanes_of(value * scale, piece, (heads, par_ref.shape[1]))

    @pl.when(g == pl.num_programs(0) - 1)
    def _():
        for n in range(blocks):
            pair = jnp.where(lower, sums[n], 0.0).astype(BF16)
            dc = dot(pair, b_ref[rows[n], :], NN) + dc_sum[n]
            db = dot(pair, c_ref[rows[n], :], TN) + db_sum[n]
            if not first:
                dc = dc + dc_in[rows[n], :]
                db = db + db_in[rows[n], :]
            dc_ref[rows[n], :] = dc
            db_ref[rows[n], :] = db


def local_grads(part, scale, y, saved, dy, b, c, vectors, mine, other, before):
    xs, ys, direct, factor_columns, table, left, right, bt, ct = saved
    raw, bias, rate, _ = vectors
    length, channels = xs.shape
    pieces = 2 * PARTS
    heads = raw.shape[1] // pieces
    raw = raw.reshape(pieces, heads, length)
    width = channels // pieces
    states = b.shape[1]
    blocks = length // GROUP
    half = pieces // 2
    first = before is None
    whole = lambda g, y: (0, 0)
    place = lambda g, y: (0, g * half + part)
    columns = pl.BlockSpec((length, width), place)
    maps = pl.BlockSpec((length, states), whole)
    line = pl.BlockSpec(bias.shape, whole)
    lines = pl.BlockSpec((1, heads, length), lambda g, y: (g * half + part, 0, 0))
    held = pl.BlockSpec((2 * states, width), whole)
    params = pl.BlockSpec((8, 128), whole)
    anywhere = pl.BlockSpec(memory_space=pl.ANY)
    in_specs = [columns, columns, columns, pl.BlockSpec((8, width), place), maps, maps]
    in_specs += [
        pl.BlockSpec(factor_columns.shape, whole),
        pl.BlockSpec((table.shape[0], width), place),
    ]
    in_specs += [lines, line, line, held, held]
    args = [xs, ys, dy, direct, b, c, factor_columns, table, raw, bias, rate, mine, other]
    fixed = [bt, ct, left, right, adding(width, heads, (0, 0, 1))]
    in_specs += [pl.BlockSpec(a.shape, lambda g, y, n=len(a.shape): (0,) * n) for a in fixed]
    args += fixed
    aliases = {}
    if not first:
        dx, dc, db, draw, par = before
        args += [dc, db, par, dx, draw]
        in_specs += [maps, maps, params, anywhere, anywhere]
        aliases = {22: 0, 23: 3}
    grid_spec = pltpu.PrefetchScalarGridSpec(
        num_scalar_prefetch=1,
        grid=(2,),
        in_specs=in_specs,
        out_specs=[columns, maps, maps, lines, params],
        scratch_shapes=[
            pltpu.VMEM((blocks, GROUP, GROUP), F32),
            pltpu.VMEM((blocks, GROUP, states), F32),
            pltpu.VMEM((blocks, GROUP, states), F32),
            pltpu.VMEM((length, 3 * width), BF16),
        ],
    )
    return pl.pallas_call(
        functools.partial(grads_kernel, first, scale, part, half),
        grid_spec=grid_spec,
        out_shape=[
            jax.ShapeDtypeStruct((length, channels), BF16),
            jax.ShapeDtypeStruct((length, states), F32),
            jax.ShapeDtypeStruct((length, states), F32),
            jax.ShapeDtypeStruct((pieces, heads, length), F32),
            jax.ShapeDtypeStruct((8, 128), F32),
        ],
        input_output_aliases=aliases,
        compiler_params=pltpu.CompilerParams(vmem_limit_bytes=SMALL_LIMIT),
        cost_estimate=pl.CostEstimate(
            flops=24 * length * width * (GROUP + states),
            bytes_accessed=12 * length * width,
            transcendentals=0,
        ),
        name="local_grads",
    )(y, *args)


def adding(width, heads, places):
    out = np.zeros((len(places) * width, 128), np.float32)
    size = width // heads
    for k, place in enumerate(places):
        for channel in range(width):
            out[k * width + channel, place * heads + channel // size] = 1.0
    return jnp.asarray(out, BF16)


def lanes_of(values, piece, shape):
    row = lax.broadcasted_iota(jnp.int32, shape, 0)
    col = lax.broadcasted_iota(jnp.int32, shape, 1)
    return jnp.sum(jnp.where(col == row + piece * shape[0], values, 0.0), axis=0, keepdims=True)


def inner_kernel(first, scale, piece, *refs):
    xs_ref, ys_ref, dy_ref, direct_ref, b_ref, c_ref, bt, ct, left, right = refs[:10]
    adder, columns_ref, table_ref, raw_ref, bias_ref, rate_ref = refs[10:16]
    refs = refs[16:]
    if not first:
        dc_in, db_in, par_in = refs[:3]
        refs = refs[5:]
    dx_ref, dc_ref, db_ref, draw_ref, par_ref, terms = refs
    heads = raw_ref.shape[1]
    length, width = xs_ref.shape
    states = b_ref.shape[1]
    blocks = length // GROUP
    all_heads = columns_ref.shape[1] // 4
    member = head_matrix(heads, width).astype(BF16)
    lower = triangle(GROUP, True)
    rows = [slice(n * GROUP, (n + 1) * GROUP) for n in range(blocks)]
    table = table_ref[...]
    skip = table[3 * blocks + 1 : 3 * blocks + 2]
    state = grad = None
    entering_low, ends = [], []
    for n in range(blocks):
        fresh = dot(bt[:, rows[n]], xs_ref[rows[n], :], NN)
        if state is not None:
            state = table[n : n + 1] * state
            entering_low.append(state.astype(BF16))
            state = state + fresh
        else:
            entering_low.append(None)
            state = fresh
        ends.append(state)
    leaving_low, edges = [None] * blocks, [jnp.zeros((1, width), F32)] * blocks
    for n in reversed(range(blocks)):
        if grad is not None:
            leaving_low[n] = grad.astype(BF16)
            edges[n] = jnp.sum(ends[n] * grad, axis=0, keepdims=True)
        if n:
            fresh = dot(ct[:, rows[n]], ys_ref[rows[n], :], NN)
            grad = table[n : n + 1] * (fresh if grad is None else grad + fresh)
    gain = dot(columns_ref[...], picker(piece, heads, all_heads, width, True), NN)
    for n in range(blocks):
        scaled_x, scaled_dy = xs_ref[rows[n], :], ys_ref[rows[n], :]
        forward = dot(left[n], scaled_x, NN)
        if entering_low[n] is not None:
            forward = forward + dot(c_ref[rows[n], :], entering_low[n], NN)
        backward = dot(right[n], scaled_dy, NN)
        if leaving_low[n] is not None:
            backward = backward + dot(b_ref[rows[n], :], leaving_low[n], NN)
        dx_ref[rows[n], :] = (gain[rows[n]] * backward + skip * dy_ref[rows[n], :].astype(F32)).astype(
            dx_ref.dtype
        )
        v = scaled_x.astype(F32) * backward
        difference = scaled_dy.astype(F32) * forward - v
        hi = difference.astype(BF16)
        lo = (difference - hi.astype(F32)).astype(BF16)
        terms[rows[n], :width] = hi
        terms[rows[n], width : 2 * width] = lo
        terms[rows[n], 2 * width :] = v.astype(BF16)
        pair = jnp.where(lower, dot(scaled_dy, scaled_x, NT), 0.0).astype(BF16)
        dc = dot(pair, b_ref[rows[n], :], NN)
        db = dot(pair, c_ref[rows[n], :], TN)
        if entering_low[n] is not None:
            dc = dc + dot(scaled_dy, entering_low[n], NT)
        if leaving_low[n] is not None:
            db = db + dot(scaled_x, leaving_low[n], NT)
        dc_ref[rows[n], :] = dc if first else dc + dc_in[rows[n], :]
        db_ref[rows[n], :] = db if first else db + db_in[rows[n], :]
    added = dot(terms[...], adder[...], NN).T
    added = [added[:, rows[n]] for n in range(blocks)]
    edge = head_sums(jnp.concatenate(edges + [edges[0]] * (8 - blocks), axis=0), member)
    slopes = running(jnp.concatenate([a[:heads] for a in added], axis=0), lower.astype(BF16))
    slope = jnp.concatenate(
        [slopes[n * heads : (n + 1) * heads] + edge[:, n : n + 1] for n in range(blocks)], axis=1
    )
    v = jnp.concatenate([a[heads : 2 * heads] for a in added], axis=1)
    raw = raw_ref[0] + column(bias_ref[...], piece, heads)
    step = softplus(raw)
    draw = (v / step - column(rate_ref[...], piece, heads) * slope) / (1.0 + jnp.exp(-raw))
    draw_ref[0] = draw
    values = (
        jnp.sum(draw, axis=1, keepdims=True),
        jnp.sum(head_sums(direct_ref[...], member), axis=1, keepdims=True),
        -jnp.sum(step * slope, axis=1, keepdims=True),
    )
    par_ref[...] = jnp.zeros_like(par_ref) if first else par_in[...]
    for k, value in enumerate(values):
        par_ref[k : k + 1] += lanes_of(value * scale, piece, (heads, par_ref.shape[1]))


def inner_grads(piece, scale, saved, dy, b, c, vectors, before):
    xs, ys, direct, factor_columns, table, left, right, bt, ct = saved
    raw, bias, rate, _ = vectors
    length, channels = xs.shape
    pieces = 2 * PARTS
    heads = raw.shape[1] // pieces
    raw = raw.reshape(pieces, heads, length)
    width = channels // pieces
    states = b.shape[1]
    first = before is None
    adder = adding(width, heads, (0, 0, 1))
    place = lambda g: (0, piece)
    all_of = lambda a: pl.BlockSpec(a.shape, lambda g, n=len(a.shape): (0,) * n)
    columns = pl.BlockSpec((length, width), place)
    maps = pl.BlockSpec((length, states), lambda g: (0, 0))
    lines = pl.BlockSpec((1, heads, length), lambda g: (piece, 0, 0))
    params = pl.BlockSpec((8, 128), lambda g: (0, 0))
    anywhere = pl.BlockSpec(memory_space=pl.ANY)
    args = [xs, ys, dy, direct, b, c, bt, ct, left, right]
    args += [adder, factor_columns, table, raw, bias, rate]
    in_specs = [columns, columns, columns, pl.BlockSpec((8, width), place)]
    in_specs += [all_of(a) for a in (b, c, bt, ct, left, right, adder, factor_columns)]
    in_specs += [pl.BlockSpec((table.shape[0], width), place), lines, all_of(bias), all_of(rate)]
    aliases = {}
    if not first:
        dx, dc, db, draw, par = before
        args += [dc, db, par, dx, draw]
        in_specs += [maps, maps, params, anywhere, anywhere]
        aliases = {19: 0, 20: 3}
    return pl.pallas_call(
        functools.partial(inner_kernel, first, scale, piece),
        grid=(1,),
        in_specs=in_specs,
        out_specs=[columns, maps, maps, lines, params],
        out_shape=[
            jax.ShapeDtypeStruct((length, channels), BF16),
            jax.ShapeDtypeStruct((length, states), F32),
            jax.ShapeDtypeStruct((length, states), F32),
            jax.ShapeDtypeStruct((pieces, heads, length), F32),
            jax.ShapeDtypeStruct((8, 128), F32),
        ],
        scratch_shapes=[pltpu.VMEM((length, 3 * width), BF16)],
        input_output_aliases=aliases,
        compiler_params=pltpu.CompilerParams(vmem_limit_bytes=VMEM_LIMIT if first else SMALL_LIMIT),
        cost_estimate=pl.CostEstimate(
            flops=24 * length * width * (GROUP + states),
            bytes_accessed=10 * length * width,
            transcendentals=0,
        ),
        name="inner_grads",
    )(*args)


def entering_kernel(scale, part, half, *refs):
    y_ref, xs_ref, ys_ref, b_ref, c_ref, adder, columns_ref, table_ref = refs[:8]
    raw_ref, bias_ref, rate_ref, mine_ref, other_ref, dx_in, draw_in, par_in = refs[8:16]
    dx_ref, draw_ref, par_ref, terms = refs[16:]
    g = pl.program_id(0)
    heads = raw_ref.shape[1]
    length, width = xs_ref.shape
    states = b_ref.shape[1]
    blocks = length // GROUP
    piece = g * half + part
    all_heads = columns_ref.shape[1] // 4
    member = head_matrix(heads, width).astype(BF16)
    rows = [slice(n * GROUP, (n + 1) * GROUP) for n in range(blocks)]

    @pl.when(g == 0)
    def _():
        par_ref[...] = par_in[...]

    own = g == y_ref[0]
    state = jnp.where(own, mine_ref[:states], other_ref[:states])
    grad = jnp.where(own, mine_ref[states:], other_ref[states:])
    table = table_ref[...]
    gain = dot(columns_ref[...], picker(piece, heads, all_heads, width, True), NN)
    for n in range(blocks):
        entered = (table[2 * blocks + n : 2 * blocks + n + 1] * state).astype(BF16)
        leaving = (table[blocks + n : blocks + n + 1] * grad).astype(BF16)
        forward = dot(c_ref[rows[n], :], entered, NN)
        backward = dot(b_ref[rows[n], :], leaving, NN)
        dx_ref[rows[n], :] = (dx_in[rows[n], :].astype(F32) + gain[rows[n]] * backward).astype(
            dx_ref.dtype
        )
        terms[rows[n], :width] = (xs_ref[rows[n], :].astype(F32) * backward).astype(BF16)
        terms[rows[n], width:] = (ys_ref[rows[n], :].astype(F32) * forward).astype(BF16)
    added = dot(terms[...], adder[...], NN).T
    added = [added[:, rows[n]] for n in range(blocks)]
    cross = jnp.sum(state * grad, axis=0, keepdims=True) * table[3 * blocks : 3 * blocks + 1]
    cross = head_sums(jnp.broadcast_to(cross, (8, width)), member)[:, :1]
    ps, qs = [a[:heads] for a in added], [a[heads : 2 * heads] for a in added]
    p_sums = running(jnp.concatenate(ps, axis=0), triangle(GROUP, False).astype(BF16))
    q_sums = running(jnp.concatenate(qs, axis=0), triangle(GROUP, True).astype(BF16))
    p_sums = [p_sums[n * heads : (n + 1) * heads] for n in range(blocks)]
    q_sums = [q_sums[n * heads : (n + 1) * heads] for n in range(blocks)]
    slopes = [None] * blocks
    before = cross
    for n in range(blocks):
        slopes[n] = p_sums[n] - ps[n] + before
        before = before + p_sums[n][:, GROUP - 1 :]
    later = jnp.zeros_like(cross)
    for n in reversed(range(blocks)):
        slopes[n] = slopes[n] + q_sums[n] + later
        later = later + q_sums[n][:, :1]
    slope = jnp.concatenate(slopes, axis=1)
    raw = raw_ref[0] + column(bias_ref[...], piece, heads)
    step = softplus(raw)
    more = jnp.concatenate(ps, axis=1) / step - column(rate_ref[...], piece, heads) * slope
    more = more / (1.0 + jnp.exp(-raw))
    draw_ref[0] = draw_in[0] + more
    shape = (heads, par_ref.shape[1])
    par_ref[:1] += lanes_of(jnp.sum(more, axis=1, keepdims=True) * scale, piece, shape)
    par_ref[2:3] -= lanes_of(jnp.sum(step * slope, axis=1, keepdims=True) * scale, piece, shape)


def entering_grads(part, scale, y, saved, b, c, vectors, mine, other, dx, draw, par):
    xs, ys, _, factor_columns, table = saved[:5]
    raw, bias, rate, _ = vectors
    length, channels = xs.shape
    pieces = 2 * PARTS
    heads = raw.shape[1] // pieces
    raw = raw.reshape(pieces, heads, length)
    width = channels // pieces
    half = pieces // 2
    adder = adding(width, heads, (0, 1))
    place = lambda g, y: (0, g * half + part)
    all_of = lambda a: pl.BlockSpec(a.shape, lambda g, y, n=len(a.shape): (0,) * n)
    columns = pl.BlockSpec((length, width), place)
    lines = pl.BlockSpec((1, heads, length), lambda g, y: (g * half + part, 0, 0))
    in_specs = [columns, columns] + [all_of(a) for a in (b, c, adder, factor_columns)]
    in_specs += [pl.BlockSpec((table.shape[0], width), place), lines]
    in_specs += [all_of(a) for a in (bias, rate, mine, other)] + [columns, lines, all_of(par)]
    return pl.pallas_call(
        functools.partial(entering_kernel, scale, part, half),
        grid_spec=pltpu.PrefetchScalarGridSpec(
            num_scalar_prefetch=1,
            grid=(2,),
            in_specs=in_specs,
            out_specs=[columns, lines, all_of(par)],
            scratch_shapes=[pltpu.VMEM((length, 2 * width), BF16)],
        ),
        out_shape=[jax.ShapeDtypeStruct(a.shape, a.dtype) for a in (dx, draw, par)],
        input_output_aliases={13: 0, 14: 1},
        compiler_params=pltpu.CompilerParams(vmem_limit_bytes=SMALL_LIMIT),
        cost_estimate=pl.CostEstimate(
            flops=24 * length * width * GROUP, bytes_accessed=16 * length * width, transcendentals=0
        ),
        name="entering_grads",
    )(y, xs, ys, b, c, adder, factor_columns, table, raw, bias, rate, mine, other, dx, draw, par)


def maps_kernel(y_ref, xs_ref, ys_ref, table_ref, dc_in, db_in, mine, other, dc_ref, db_ref):
    g = pl.program_id(0)
    length = xs_ref.shape[0]
    states = dc_in.shape[1]
    blocks = length // GROUP

    @pl.when(g == 0)
    def _():
        dc_ref[...] = dc_in[...]
        db_ref[...] = db_in[...]

    both = jnp.where(g == y_ref[0], mine[...], other[...])
    state, grad = both[:states], both[states:]
    table = table_ref[...]
    for n in range(blocks):
        rows = slice(n * GROUP, (n + 1) * GROUP)
        entered = (table[2 * blocks + n : 2 * blocks + n + 1] * state).astype(BF16)
        leaving = (table[blocks + n : blocks + n + 1] * grad).astype(BF16)
        dc_ref[rows, :] += dot(ys_ref[rows, :], entered, NT)
        db_ref[rows, :] += dot(xs_ref[rows, :], leaving, NT)


def maps_grads(part, y, saved, dc, db, mine, other):
    xs, ys, _, _, table = saved[:5]
    length, channels = xs.shape
    width = channels // (2 * PARTS)
    place = lambda g, y: (0, g * PARTS + part)
    all_of = lambda a: pl.BlockSpec(a.shape, lambda g, y: (0, 0))
    columns = pl.BlockSpec((length, width), place)
    return pl.pallas_call(
        maps_kernel,
        grid_spec=pltpu.PrefetchScalarGridSpec(
            num_scalar_prefetch=1,
            grid=(2,),
            in_specs=[columns, columns, pl.BlockSpec((table.shape[0], width), place)]
            + [all_of(a) for a in (dc, db, mine, other)],
            out_specs=[all_of(dc), all_of(db)],
        ),
        out_shape=[jax.ShapeDtypeStruct(a.shape, a.dtype) for a in (dc, db)],
        compiler_params=pltpu.CompilerParams(vmem_limit_bytes=SMALL_LIMIT),
        cost_estimate=pl.CostEstimate(
            flops=16 * length * width * dc.shape[1],
            bytes_accessed=8 * length * width,
            transcendentals=0,
        ),
        name="maps_grads",
    )(y, xs, ys, table, dc, db, mine, other)


def summed_over(value, axis):
    size = lax.axis_size(axis)
    if size & (size - 1):
        return lax.psum(value, axis)
    bit = 1
    while bit < size:
        steps = (bit, 2 * bit, 3 * bit) if 4 * bit <= size else (bit,)
        got = [lax.ppermute(value, axis, [(i, i ^ s) for i in range(size)]) for s in steps]
        value = value + got[0]
        if len(got) == 3:
            value = value + (got[1] + got[2])
        bit *= 4 if len(got) == 3 else 2
    return value


def after(value, *earlier):
    return lax.optimization_barrier((value, *earlier))[0]


def entering(sent, kept, states, token):
    size = lax.axis_size("seq")
    pairs = size // 2
    index = lax.axis_index("seq")
    place, second = index // 2, index % 2 == 1
    swap = [(i, i ^ 1) for i in range(size)]
    both = lambda moves: [(2 * a + y, 2 * b + y) for a, b in moves for y in range(2)]
    if pairs == 4:
        steps = [([(0, 1), (1, 0), (2, 3), (3, 2)],), ([(1, 2), (2, 1)], [(1, 3), (2, 0)])]
        up = [(place == 0) | (place == 2), place == 1]
    else:
        steps = [([(k - 1, k), (pairs - k, pairs - k - 1)],) for k in range(1, pairs)]
        up = [place == k - 1 for k in range(1, pairs)]

    def halves(got, copy):
        spans = ((0, states), (states, 2 * states), (2 * states + copy, 2 * states + copy + 1))
        for low, high in spans:
            own, other = kept[low:high], got[low:high]
            yield jnp.where(second, other, own), jnp.where(second, own, other)

    message = sent if token is None else after(sent, *token)
    got = lax.ppermute(message, "seq", swap)
    token = yield message, got
    arrived = []
    for k, routes in enumerate(steps):
        if arrived:
            arrived[-1] = after(arrived[-1], token)
        else:
            got = after(got, token)
        (l1, l2), (k1, k2), (d1, d2) = halves(got, min(k, 3))
        message = jnp.where(up[k], d2 * l1 + l2, k1 + d1 * k2)
        if arrived:
            message = message + d1 * d2 * arrived[-1][:states]
        if len(steps) == 2 and k == 0:
            message = jnp.concatenate([message, jnp.broadcast_to(d1 * d2, (8, message.shape[1]))])
        arrived += [lax.ppermute(message, "seq", both(route)) for route in routes]
        token = yield message, arrived[-1]
    arrived[-1] = after(arrived[-1], token)

    def leaving(copy):
        (l1, _), (_, k2), (d1, d2) = halves(got, copy)
        zero = jnp.zeros_like(l1)
        if pairs == 4:
            near, middle, far = [a[:states] for a in arrived]
            outer = arrived[0][states + copy : states + copy + 1] * far + near
            starts, ends = [zero, near, middle, outer], [outer, middle, near, zero]
        else:
            starts, ends = [zero] + arrived, arrived[::-1] + [zero]
        start, end = starts[0], ends[0]
        for k in range(1, pairs):
            start = jnp.where(place == k, starts[k], start)
            end = jnp.where(place == k, ends[k], end)
        return start, d1 * start + l1, k2 + d2 * end, end

    first_start, second_start, first_end, second_end = leaving(4)
    message = jnp.concatenate(
        [
            jnp.where(second, first_start, second_start),
            jnp.where(second, first_end, second_end),
        ]
    )
    other = lax.ppermute(message, "seq", swap)
    yield message, other
    first_start, second_start, first_end, second_end = leaving(5)
    mine = jnp.concatenate(
        [
            jnp.where(second, second_start, first_start),
            jnp.where(second, second_end, first_end),
        ]
    )
    yield mine, other


def shards(inputs, input_map, output_map, step_raw, step_bias, decay_rate, skip_gain, cotangent):
    length = inputs.shape[1]
    heads = step_raw.shape[1]
    states = input_map.shape[2]
    x, b, c, dy = inputs[0], input_map[0], output_map[0], cotangent[0]
    vectors = (
        step_raw,
        step_bias.reshape(1, heads),
        decay_rate.reshape(1, heads),
        skip_gain.reshape(1, heads),
    )
    size = lax.axis_size("seq")
    y = lax.axis_index("seq") % 2
    scale = 1.0 / math.sqrt(length * size * lax.axis_size("batch"))

    def local(half, part, count, before):
        at = jnp.reshape(half * PARTS + part, (1,)).astype(jnp.int32)
        last = count == PARTS
        out, saved = local_states(at, count, last, x, dy, b, c, vectors, before)
        return out, saved[:3] + list(before[3:] if before else []) + saved[3:]

    sent, kept = [], []
    saved = None
    for part in range(PARTS):
        out, saved = local(1 - y, part, 1, saved)
        sent += out
    kept, saved = local(y, 0, PARTS, saved)

    transfers = 4 if size == 8 else size // 2 + 1
    order = [(0, 0), (1, 0)] + [
        pick for k in range(1, transfers) for pick in ((0, k), (1, k - 1)) if pick != (1, 0)
    ]
    order.append((1, transfers - 1))
    flows, token = {}, None
    inner, piece = None, 0
    last = PARTS - 1
    windows = [(0, 2), (1, 2)] if transfers == 4 else []

    def inner_piece(token):
        bias = vectors[1] if token is None else after(vectors[1], token)
        moved = (vectors[0], bias, *vectors[2:])
        return inner_grads(piece * PARTS + last, scale, saved, dy, b, c, moved, inner)

    for part, k in order:
        if k == 0:
            flows[part] = entering(sent[part], kept[part], states, token)
            message, arrived = next(flows[part])
            token = None if part == 0 else message
        else:
            token = flows[part].send(token)[0]
        if (part, k) in windows:
            inner = inner_piece(token)
            token = inner[-1]
            piece += 1
    while piece < 2:
        inner = inner_piece(token)
        token = inner[-1]
        piece += 1
    here = jnp.reshape(y, (1,)).astype(jnp.int32)
    for part in range(PARTS):
        mine, other = next(flows[part])
        other = after(other, token)
        if part < last:
            inner = local_grads(part, scale, here, saved, dy, b, c, vectors, mine, other, inner)
    dx, dc, db, draw, params = inner
    dx, draw, params = entering_grads(
        last, scale, here, saved, b, c, vectors, mine, other, dx, draw, params
    )
    dc, db = maps_grads(last, after(here, params), saved, dc, db, mine, other)
    summed = summed_over(summed_over(params, "batch"), "seq")
    return (
        dx[None],
        db[None],
        dc[None],
        draw.reshape(heads, length)[None],
        summed[:2, :heads],
        summed[2, :heads],
    )


def solution(mesh):
    in_specs = (
        P("batch", "seq", None),
        P("batch", "seq", None),
        P("batch", "seq", None),
        P("batch", None, "seq"),
        P(),
        P(),
        P(),
        P("batch", "seq", None),
    )
    out_specs = (
        P("batch", "seq", None),
        P("batch", "seq", None),
        P("batch", "seq", None),
        P("batch", None, "seq"),
        P(),
        P(),
    )
    return jax.shard_map(shards, mesh=mesh, in_specs=in_specs, out_specs=out_specs, check_vma=False)
```

```python
import functools
import math

import jax
import jax.numpy as jnp
import numpy as np
from jax import lax
from jax.experimental import pallas as pl
from jax.experimental.pallas import tpu as pltpu
from jax.sharding import PartitionSpec as P

GROUP = 256
PARTS = 2
VMEM_LIMIT = 60 * 1024 * 1024
SMALL_LIMIT = 40 * 1024 * 1024
F32 = jnp.float32
BF16 = jnp.bfloat16


def dot(a, b, dims):
    return lax.dot_general(a, b, (dims, ((), ())), preferred_element_type=F32)


NN = ((1,), (0,))
NT = ((1,), (1,))
TN = ((0,), (0,))


def split2(a):
    hi = a.astype(BF16).astype(F32)
    return hi, a - hi


def head_matrix(heads, width):
    size = width // heads
    row = lax.broadcasted_iota(jnp.int32, (heads, width), 0)
    col = lax.broadcasted_iota(jnp.int32, (heads, width), 1)
    return ((col >= row * size) & (col < (row + 1) * size)).astype(F32)


def head_sums(values, member):
    hi, lo = split2(values)
    return dot(member, hi.astype(BF16), NT) + dot(member, lo.astype(BF16), NT)


def running(rows, upper):
    hi, rest = split2(rows)
    mid, lo = split2(rest)
    k = rows.shape[0]
    out = dot(jnp.concatenate([hi, mid, lo], axis=0).astype(BF16), upper, NN)
    return out[:k] + out[k : 2 * k] + out[2 * k :]


def triangle(width, lower):
    row = lax.broadcasted_iota(jnp.int32, (width, width), 0)
    col = lax.broadcasted_iota(jnp.int32, (width, width), 1)
    return (row >= col) if lower else (row <= col)


def softplus(v):
    return jnp.maximum(v, 0.0) + jnp.log1p(jnp.exp(-jnp.abs(v)))


def column(line, piece, heads):
    shape = (heads, line.shape[1])
    row = lax.broadcasted_iota(jnp.int32, shape, 0)
    col = lax.broadcasted_iota(jnp.int32, shape, 1)
    return jnp.sum(jnp.where(col == row + piece * heads, line, 0.0), axis=1, keepdims=True)


def block_sums(logs, blocks):
    heads = logs.shape[0]
    ones = triangle(GROUP, False).astype(BF16)
    stacked = jnp.concatenate([logs[:, n * GROUP : (n + 1) * GROUP] for n in range(blocks)], axis=0)
    cums = running(stacked, ones)
    return [cums[n * heads : (n + 1) * heads] for n in range(blocks)]


def factors(raw, bias, rate, skip, columns_ref, table_ref):
    heads, length = raw.shape
    width = table_ref.shape[1]
    blocks = length // GROUP
    step = softplus(raw + bias)
    cums = block_sums(-rate * step, blocks)
    totals = [cum[:, GROUP - 1 :] for cum in cums]
    before = [jnp.zeros((heads, 1), F32)]
    for total in totals:
        before.append(before[-1] + total)
    for n in range(blocks):
        rows = slice(n * GROUP, (n + 1) * GROUP)
        gain = split2(jnp.exp(totals[n] - cums[n]) * step[:, rows])
        lift = split2(jnp.exp(cums[n] - totals[n]))
        columns_ref[rows, :] = jnp.concatenate([*gain, *lift], axis=0).T.astype(BF16)
    whole = before[-1]
    lines = [jnp.exp(t) for t in totals]
    lines += [jnp.exp(whole - before[n + 1]) for n in range(blocks)]
    lines += [jnp.exp(before[n + 1]) for n in range(blocks)]
    lines += [jnp.exp(whole), skip]
    lines += [skip] * (-len(lines) % 8)
    hi, lo = split2(jnp.concatenate(lines, axis=1).T)
    member = head_matrix(heads, width).astype(BF16)
    table_ref[...] = dot(hi.astype(BF16), member, NN) + dot(lo.astype(BF16), member, NN)


def picker(piece, heads, all_heads, width, first):
    shape = (4 * all_heads, width)
    row = lax.broadcasted_iota(jnp.int32, shape, 0)
    col = lax.broadcasted_iota(jnp.int32, shape, 1)
    size = width // heads
    base = (0 if first else 2 * all_heads) + piece * heads
    hit = None
    for term in range(2):
        low = (row - (base + term * all_heads)) * size
        one = (col >= low) & (col < low + size)
        hit = one if hit is None else hit | one
    return hit.astype(BF16)


def local_kernel(first, last, count, *refs):
    at_ref, x_ref, dy_ref, b_ref, c_ref = refs[:5]
    if first:
        raw_ref, bias_ref, rate_ref, skip_ref = refs[5:9]
        outs = refs[9:-7]
        xs_ref, ys_ref, direct_ref, columns_ref, table_ref, bt, ct = refs[-7:]
    else:
        columns_ref, table_ref = refs[5:7]
        outs = refs[10 : 10 + count]
        xs_ref, ys_ref, direct_ref = refs[10 + count : 13 + count]
        if last:
            left, right, bt, ct = refs[13 + count :]
        else:
            bt, ct = refs[13 + count :]
    g = pl.program_id(0)
    length, width = x_ref.shape
    states = b_ref.shape[1]
    blocks = length // GROUP
    piece = at_ref[0] + g
    all_heads = columns_ref.shape[1] // 4
    heads = all_heads * width // table_ref.shape[1]

    @pl.when(g == 0)
    def _():
        bt[...] = b_ref[...].T
        ct[...] = c_ref[...].T
        if first:
            factors(
                raw_ref[0],
                column(bias_ref[...], 0, all_heads),
                column(rate_ref[...], 0, all_heads),
                column(skip_ref[...], 0, all_heads),
                columns_ref,
                table_ref,
            )
        if last:
            for n in range(blocks):
                rows = slice(n * GROUP, (n + 1) * GROUP)
                scores = dot(c_ref[rows, :], b_ref[rows, :], NT)
                left[n] = jnp.where(triangle(GROUP, True), scores, 0.0).astype(BF16)
                scores = dot(b_ref[rows, :], c_ref[rows, :], NT)
                right[n] = jnp.where(triangle(GROUP, False), scores, 0.0).astype(BF16)

    gain = dot(columns_ref[...], picker(piece, heads, all_heads, width, True), NN)
    lift = dot(columns_ref[...], picker(piece, heads, all_heads, width, False), NN)
    table = table_ref[:, pl.ds(pl.multiple_of(piece * width, width), width)]
    state = jnp.zeros((states, width), F32)
    grad = jnp.zeros((states, width), F32)
    direct = jnp.zeros((8, width), F32)
    for n in range(blocks):
        rows = slice(n * GROUP, (n + 1) * GROUP)
        x = x_ref[rows, :].astype(F32)
        dy = dy_ref[rows, :].astype(F32)
        direct = direct + jnp.sum((dy * x).reshape(GROUP // 8, 8, width), axis=0)
        scaled_x = (x * gain[rows]).astype(BF16)
        scaled_dy = (dy * lift[rows]).astype(BF16)
        xs_ref[rows, :] = scaled_x
        ys_ref[rows, :] = scaled_dy
        later = table[blocks + n : blocks + n + 1]
        earlier = table[2 * blocks + n : 2 * blocks + n + 1]
        state = state + later * dot(bt[:, rows], scaled_x, NN)
        grad = grad + earlier * dot(ct[:, rows], scaled_dy, NN)
    direct_ref[...] = direct
    decay = jnp.broadcast_to(table[3 * blocks : 3 * blocks + 1], (8, width))
    for k, out_ref in enumerate(outs):

        @pl.when(g == k)
        def _():
            out_ref[:states] = state
            out_ref[states : 2 * states] = grad
            out_ref[2 * states :] = decay


def local_states(at, count, last, x, dy, b, c, vectors, before):
    length, channels = x.shape
    states = b.shape[1]
    pieces = 2 * PARTS
    width = channels // pieces
    lines = 3 * (length // GROUP) + 2
    lines += -lines % 8
    first = before is None
    whole = lambda g, at: (0, 0)
    columns = pl.BlockSpec((length, width), lambda g, at: (0, at[0] + g))
    strip = pl.BlockSpec((8, width), lambda g, at: (0, at[0] + g))
    maps = pl.BlockSpec((length, states), whole)
    anywhere = pl.BlockSpec(memory_space=pl.ANY)
    in_specs = [columns, columns, maps, maps]
    out_specs = [pl.BlockSpec((2 * states + 8, width), whole)] * count + [columns, columns, strip]
    out_shape = [jax.ShapeDtypeStruct((2 * states + 8, width), F32)] * count + [
        jax.ShapeDtypeStruct((length, channels), BF16),
        jax.ShapeDtypeStruct((length, channels), BF16),
        jax.ShapeDtypeStruct((8, channels), F32),
    ]
    aliases = {}
    if first:
        raw, bias, rate, skip = vectors
        heads = raw.shape[1]
        args = [raw, bias, rate, skip]
        in_specs += [pl.BlockSpec(raw.shape, lambda g, at: (0, 0, 0))]
        in_specs += [pl.BlockSpec(bias.shape, whole)] * 3
        tables = [
            jax.ShapeDtypeStruct((length, 4 * heads), BF16),
            jax.ShapeDtypeStruct((lines, channels), F32),
        ]
        out_shape += tables
        out_specs += [pl.BlockSpec(t.shape, whole) for t in tables]
    else:
        xs, ys, direct, factor_columns, table = before
        args = [factor_columns, table, xs, ys, direct]
        in_specs += [pl.BlockSpec(factor_columns.shape, whole), pl.BlockSpec(table.shape, whole)]
        in_specs += [anywhere] * 3
        aliases = {7: count, 8: count + 1, 9: count + 2}
    scratch = [pltpu.VMEM((states, length), BF16)] * 2
    if last:
        blocks = length // GROUP
        extra = [jax.ShapeDtypeStruct((blocks, GROUP, GROUP), BF16)] * 2
        extra += [jax.ShapeDtypeStruct((states, length), BF16)] * 2
        out_shape += extra
        out_specs += [pl.BlockSpec(e.shape, lambda g, at, n=len(e.shape): (0,) * n) for e in extra]
        scratch = []
    grid_spec = pltpu.PrefetchScalarGridSpec(
        num_scalar_prefetch=1,
        grid=(count,),
        in_specs=in_specs,
        out_specs=out_specs,
        scratch_shapes=scratch,
    )
    out = pl.pallas_call(
        functools.partial(local_kernel, first, last, count),
        grid_spec=grid_spec,
        out_shape=out_shape,
        input_output_aliases=aliases,
        compiler_params=pltpu.CompilerParams(vmem_limit_bytes=VMEM_LIMIT),
        cost_estimate=pl.CostEstimate(
            flops=8 * count * length * width * states,
            bytes_accessed=8 * count * length * width,
            transcendentals=0,
        ),
        name="local_states",
    )(at, x, dy, b, c, *args)
    return out[:count], list(out[count:])


def grads_kernel(first, scale, part, half, begin, *refs):
    y_ref, xs_ref, ys_ref, dy_ref, direct_ref, b_ref, c_ref, columns_ref, table_ref = refs[:9]
    raw_ref, bias_ref, rate_ref, bt, ct, left, right, adder = refs[9:17]
    held = refs[17:21]
    refs = refs[21:]
    if not first:
        dc_in, db_in, par_in = refs[:3]
        refs = refs[5:]
    dx_ref, dc_ref, db_ref, draw_ref, par_ref = refs[:5]
    sums, dc_sum, db_sum, terms = refs[5:9]
    if not first:
        dc_old, db_old, sems = refs[9:]
        old = [(dc_in, dc_old, sems.at[0]), (db_in, db_old, sems.at[1])]
    g = pl.program_id(0)
    heads = raw_ref.shape[1]
    length, width = xs_ref.shape
    states = b_ref.shape[1]
    blocks = length // GROUP
    piece = (begin + g) * half + part
    all_heads = columns_ref.shape[1] // 4
    member = head_matrix(heads, width).astype(BF16)
    lower = triangle(GROUP, True)
    rows = [slice(n * GROUP, (n + 1) * GROUP) for n in range(blocks)]

    @pl.when(g == 0)
    def _():
        if not first:
            for source, target, sem in old:
                pltpu.make_async_copy(source, target, sem).start()
        sums[...] = jnp.zeros_like(sums)
        dc_sum[...] = jnp.zeros_like(dc_sum)
        db_sum[...] = jnp.zeros_like(db_sum)
        par_ref[...] = jnp.zeros_like(par_ref) if first else par_in[...]

    own = begin + g == y_ref[0]
    early = jnp.where(own, held[0][...], held[2][...])
    late = jnp.where(own, held[1][...], held[3][...])
    state_early = y_ref[1] == 1
    state = jnp.where(state_early, early, late)
    grad = jnp.where(state_early, late, early)
    table = table_ref[...]
    skip = table[3 * blocks + 1 : 3 * blocks + 2]
    entering_low, ends = [], []
    for n in range(blocks):
        state = table[n : n + 1] * state
        entering_low.append(state.astype(BF16))
        state = state + dot(bt[:, rows[n]], xs_ref[rows[n], :], NN)
        ends.append(state)
    leaving_low, edges = [None] * blocks, [None] * blocks
    for n in reversed(range(blocks)):
        leaving_low[n] = grad.astype(BF16)
        edges[n] = jnp.sum(ends[n] * grad, axis=0, keepdims=True)
        grad = table[n : n + 1] * (grad + dot(ct[:, rows[n]], ys_ref[rows[n], :], NN))
    gain = dot(columns_ref[...], picker(piece, heads, all_heads, width, True), NN)
    for n in range(blocks):
        scaled_x, scaled_dy = xs_ref[rows[n], :], ys_ref[rows[n], :]
        forward = dot(left[n], scaled_x, NN) + dot(c_ref[rows[n], :], entering_low[n], NN)
        backward = dot(right[n], scaled_dy, NN) + dot(b_ref[rows[n], :], leaving_low[n], NN)
        weight = gain[rows[n]]
        dx_ref[rows[n], :] = (weight * backward + skip * dy_ref[rows[n], :].astype(F32)).astype(
            dx_ref.dtype
        )
        v = scaled_x.astype(F32) * backward
        difference = scaled_dy.astype(F32) * forward - v
        hi = difference.astype(BF16)
        lo = (difference - hi.astype(F32)).astype(BF16)
        terms[rows[n], :width] = hi
        terms[rows[n], width : 2 * width] = lo
        terms[rows[n], 2 * width :] = v.astype(BF16)
        sums[n] += dot(scaled_dy, scaled_x, NT)
        dc_sum[n] += dot(scaled_dy, entering_low[n], NT)
        db_sum[n] += dot(scaled_x, leaving_low[n], NT)
    added = dot(terms[...], adder[...], NN).T
    added = [added[:, rows[n]] for n in range(blocks)]
    edge = head_sums(jnp.concatenate(edges + [edges[0]] * (8 - blocks), axis=0), member)
    slopes = running(
        jnp.concatenate([a[:heads] for a in added], axis=0), lower.astype(BF16)
    )
    slope = jnp.concatenate(
        [slopes[n * heads : (n + 1) * heads] + edge[:, n : n + 1] for n in range(blocks)], axis=1
    )
    v = jnp.concatenate([a[heads : 2 * heads] for a in added], axis=1)
    raw = raw_ref[0] + column(bias_ref[...], piece, heads)
    step = softplus(raw)
    draw = (v / step - column(rate_ref[...], piece, heads) * slope) / (1.0 + jnp.exp(-raw))
    draw_ref[0] = draw
    values = (
        jnp.sum(draw, axis=1, keepdims=True),
        jnp.sum(head_sums(direct_ref[...], member), axis=1, keepdims=True),
        -jnp.sum(step * slope, axis=1, keepdims=True),
    )
    for k, value in enumerate(values):
        par_ref[k : k + 1] += lanes_of(value * scale, piece, (heads, par_ref.shape[1]))

    @pl.when(g == pl.num_programs(0) - 1)
    def _():
        if not first:
            for source, target, sem in old:
                pltpu.make_async_copy(source, target, sem).wait()
        for n in range(blocks):
            pair = jnp.where(lower, sums[n], 0.0).astype(BF16)
            dc = dot(pair, b_ref[rows[n], :], NN) + dc_sum[n]
            db = dot(pair, c_ref[rows[n], :], TN) + db_sum[n]
            if not first:
                dc = dc + dc_old[rows[n], :]
                db = db + db_old[rows[n], :]
            dc_ref[rows[n], :] = dc
            db_ref[rows[n], :] = db


def local_grads(part, begin, count, scale, y, saved, dy, b, c, vectors, held, before):
    xs, ys, direct, factor_columns, table, left, right, bt, ct = saved
    raw, bias, rate, _ = vectors
    length, channels = xs.shape
    pieces = 2 * PARTS
    heads = raw.shape[1] // pieces
    raw = raw.reshape(pieces, heads, length)
    width = channels // pieces
    states = b.shape[1]
    blocks = length // GROUP
    half = pieces // 2
    first = before is None
    whole = lambda g, y: (0, 0)
    place = lambda g, y: (0, (begin + g) * half + part)
    columns = pl.BlockSpec((length, width), place)
    maps = pl.BlockSpec((length, states), whole)
    line = pl.BlockSpec(bias.shape, whole)
    lines = pl.BlockSpec((1, heads, length), lambda g, y: ((begin + g) * half + part, 0, 0))
    params = pl.BlockSpec((8, 128), whole)
    anywhere = pl.BlockSpec(memory_space=pl.ANY)
    in_specs = [columns, columns, columns, pl.BlockSpec((8, width), place), maps, maps]
    in_specs += [
        pl.BlockSpec(factor_columns.shape, whole),
        pl.BlockSpec((table.shape[0], width), place),
    ]
    in_specs += [lines, line, line]
    args = [xs, ys, dy, direct, b, c, factor_columns, table, raw, bias, rate]
    fixed = [bt, ct, left, right, adding(width, heads, (0, 0, 1)), *held]
    in_specs += [pl.BlockSpec(a.shape, lambda g, y, n=len(a.shape): (0,) * n) for a in fixed]
    args += fixed
    aliases = {}
    if not first:
        dx, dc, db, draw, par = before
        args += [dc, db, par, dx, draw]
        in_specs += [anywhere, anywhere, params, anywhere, anywhere]
        aliases = {24: 0, 25: 3}
    grid_spec = pltpu.PrefetchScalarGridSpec(
        num_scalar_prefetch=1,
        grid=(count,),
        in_specs=in_specs,
        out_specs=[columns, maps, maps, lines, params],
        scratch_shapes=[
            pltpu.VMEM((blocks, GROUP, GROUP), F32),
            pltpu.VMEM((blocks, GROUP, states), F32),
            pltpu.VMEM((blocks, GROUP, states), F32),
            pltpu.VMEM((length, 3 * width), BF16),
        ]
        + [
            pltpu.VMEM((length, states), F32),
            pltpu.VMEM((length, states), F32),
            pltpu.SemaphoreType.DMA((2,)),
        ]
        * (not first),
    )
    return pl.pallas_call(
        functools.partial(grads_kernel, first, scale, part, half, begin),
        grid_spec=grid_spec,
        out_shape=[
            jax.ShapeDtypeStruct((length, channels), BF16),
            jax.ShapeDtypeStruct((length, states), F32),
            jax.ShapeDtypeStruct((length, states), F32),
            jax.ShapeDtypeStruct((pieces, heads, length), F32),
            jax.ShapeDtypeStruct((8, 128), F32),
        ],
        input_output_aliases=aliases,
        compiler_params=pltpu.CompilerParams(vmem_limit_bytes=SMALL_LIMIT),
        cost_estimate=pl.CostEstimate(
            flops=12 * count * length * width * (GROUP + states),
            bytes_accessed=6 * count * length * width,
            transcendentals=0,
        ),
        name="local_grads",
    )(y, *args)


def adding(width, heads, places):
    out = np.zeros((len(places) * width, 128), np.float32)
    size = width // heads
    for k, place in enumerate(places):
        for channel in range(width):
            out[k * width + channel, place * heads + channel // size] = 1.0
    return jnp.asarray(out, BF16)


def lanes_of(values, piece, shape):
    row = lax.broadcasted_iota(jnp.int32, shape, 0)
    col = lax.broadcasted_iota(jnp.int32, shape, 1)
    return jnp.sum(jnp.where(col == row + piece * shape[0], values, 0.0), axis=0, keepdims=True)


def summed_over(value, axis):
    size = lax.axis_size(axis)
    if size & (size - 1):
        return lax.psum(value, axis)
    bit = 1
    while bit < size:
        steps = (bit, 2 * bit, 3 * bit) if 4 * bit <= size else (bit,)
        got = [lax.ppermute(value, axis, [(i, i ^ s) for i in range(size)]) for s in steps]
        value = value + got[0]
        if len(got) == 3:
            value = value + (got[1] + got[2])
        bit *= 4 if len(got) == 3 else 2
    return value


def after(value, *earlier):
    return lax.optimization_barrier((value, *earlier))[0]


def entering(sent, kept, states, token):
    size = lax.axis_size("seq")
    pairs = size // 2
    index = lax.axis_index("seq")
    place, second = index // 2, index % 2 == 1
    swap = [(i, i ^ 1) for i in range(size)]
    both = lambda moves: [(2 * a + y, 2 * b + y) for a, b in moves for y in range(2)]

    def halves(got, copy):
        spans = ((0, states), (states, 2 * states), (2 * states + copy, 2 * states + copy + 1))
        for low, high in spans:
            own, other = kept[low:high], got[low:high]
            yield jnp.where(second, other, own), jnp.where(second, own, other)

    def message_of(up, got, arrived, copy):
        (l1, l2), (k1, k2), (d1, d2) = halves(got, copy)
        message = jnp.where(up, d2 * l1 + l2, k1 + d1 * k2)
        return message if arrived is None else message + d1 * d2 * arrived[:states]

    def shares(is_state, value, got, copy):
        (l1, _), (_, k2), (d1, d2) = halves(got, copy)
        for_first = jnp.where(is_state, value, k2 + d2 * value)
        for_second = jnp.where(is_state, d1 * value + l1, value)
        return jnp.where(second, for_second, for_first), jnp.where(second, for_first, for_second)

    message = sent if token is None else after(sent, *token)
    got = lax.ppermute(message, "seq", swap)
    token = yield message, got
    got = after(got, token)
    lower = place < pairs // 2
    if pairs == 4:
        message = message_of((place == 0) | (place == 2), got, None, 0)
        (_, _), (_, _), (d1, d2) = halves(got, 0)
        message = jnp.concatenate([message, jnp.broadcast_to(d1 * d2, (8, message.shape[1]))])
        near = lax.ppermute(message, "seq", both([(0, 1), (1, 0), (2, 3), (3, 2)]))
        token = yield message, near
        near = after(near, token)
        message = message_of(place == 1, got, near, 1)
        middle = lax.ppermute(message, "seq", both([(1, 2), (2, 1)]))
        far = lax.ppermute(message, "seq", both([(1, 3), (2, 0)]))
        inside = (place == 1) | (place == 2)
        known = jnp.where(inside, near[:states], 0.0)
        mine_early, early = shares(lower, known, got, 2)
        other_early = lax.ppermute(early, "seq", swap)
        token = yield early, far
        far = after(far, token)
        outer = near[states : states + 1] * far + near[:states]
        mine_late, late = shares(~lower, jnp.where(inside, middle, outer), got, 3)
        other_late = lax.ppermute(late, "seq", swap)
        yield late, other_late
    else:
        arrived = []
        for k in range(1, pairs):
            message = message_of(place == k - 1, got, arrived[-1] if arrived else None, min(k, 4))
            routes = both([(k - 1, k), (pairs - k, pairs - k - 1)])
            arrived.append(lax.ppermute(message, "seq", routes))
            token = yield message, arrived[-1]
            arrived[-1] = after(arrived[-1], token)
        start = end = jnp.zeros_like(arrived[0])
        for k in range(1, pairs):
            start = jnp.where(place == k, arrived[k - 1], start)
            end = jnp.where(place == pairs - 1 - k, arrived[k - 1], end)
        mine_early, early = shares(lower, jnp.where(lower, start, end), got, 5)
        mine_late, late = shares(~lower, jnp.where(lower, end, start), got, 6)
        other_early = lax.ppermute(early, "seq", swap)
        other_late = lax.ppermute(late, "seq", swap)
        yield late, other_late
    yield mine_early, mine_late, other_early, other_late


def shards(inputs, input_map, output_map, step_raw, step_bias, decay_rate, skip_gain, cotangent):
    length = inputs.shape[1]
    heads = step_raw.shape[1]
    states = input_map.shape[2]
    x, b, c, dy = inputs[0], input_map[0], output_map[0], cotangent[0]
    vectors = (
        step_raw,
        step_bias.reshape(1, heads),
        decay_rate.reshape(1, heads),
        skip_gain.reshape(1, heads),
    )
    size = lax.axis_size("seq")
    y = lax.axis_index("seq") % 2
    scale = 1.0 / math.sqrt(length * size * lax.axis_size("batch"))

    def local(half, part, count, before):
        at = jnp.reshape(half * PARTS + part, (1,)).astype(jnp.int32)
        last = count == PARTS
        out, saved = local_states(at, count, last, x, dy, b, c, vectors, before)
        return out, saved[:3] + list(before[3:] if before else []) + saved[3:]

    sent, kept = [], []
    saved = None
    for part in range(PARTS):
        out, saved = local(1 - y, part, 1, saved)
        sent += out
    kept, saved = local(y, 0, PARTS, saved)

    transfers = 4 if size == 8 else size // 2 + 1
    order = [(0, 0), (1, 0)] + [
        pick for k in range(1, transfers) for pick in ((0, k), (1, k - 1)) if pick != (1, 0)
    ]
    order.append((1, transfers - 1))
    flows, token = {}, None
    lower = lax.axis_index("seq") < size // 2
    here = jnp.stack([y, lower.astype(y.dtype)]).astype(jnp.int32)
    found = None

    def grads(part, begin, count, token, held):
        *most, final = held
        held = (*most, after(final, token))
        return local_grads(
            part, begin, count, scale, here, saved, dy, b, c, vectors, held, found
        )

    for part, k in order:
        if (part, k) == (1, transfers - 1):
            held = next(flows[0])
            found = grads(0, 0, 1, token, held)
            token = found[-1]
        if k == 0:
            flows[part] = entering(sent[part], kept[part], states, token)
            message, arrived = next(flows[part])
            token = None if part == 0 else message
        else:
            token = flows[part].send(token)[0]
    found = grads(0, 1, 1, token, held)
    found = grads(1, 0, 2, found[-1], next(flows[1]))
    dx, dc, db, draw, params = found
    summed = summed_over(summed_over(params, "batch"), "seq")
    return (
        dx[None],
        db[None],
        dc[None],
        draw.reshape(heads, length)[None],
        summed[:2, :heads],
        summed[2, :heads],
    )


def solution(mesh):
    in_specs = (
        P("batch", "seq", None),
        P("batch", "seq", None),
        P("batch", "seq", None),
        P("batch", None, "seq"),
        P(),
        P(),
        P(),
        P("batch", "seq", None),
    )
    out_specs = (
        P("batch", "seq", None),
        P("batch", "seq", None),
        P("batch", "seq", None),
        P("batch", None, "seq"),
        P(),
        P(),
    )
    return jax.shard_map(shards, mesh=mesh, in_specs=in_specs, out_specs=out_specs, check_vma=False)
```

```python
import functools
import math

import jax
import jax.numpy as jnp
import numpy as np
from jax import lax
from jax.experimental import pallas as pl
from jax.experimental.pallas import tpu as pltpu
from jax.sharding import PartitionSpec as P

GROUP = 256
PARTS = 2
VMEM_LIMIT = 60 * 1024 * 1024
SMALL_LIMIT = 40 * 1024 * 1024
F32 = jnp.float32
BF16 = jnp.bfloat16


def dot(a, b, dims):
    return lax.dot_general(a, b, (dims, ((), ())), preferred_element_type=F32)


NN = ((1,), (0,))
NT = ((1,), (1,))
TN = ((0,), (0,))


def split2(a):
    hi = a.astype(BF16).astype(F32)
    return hi, a - hi


def head_matrix(heads, width):
    size = width // heads
    row = lax.broadcasted_iota(jnp.int32, (heads, width), 0)
    col = lax.broadcasted_iota(jnp.int32, (heads, width), 1)
    return ((col >= row * size) & (col < (row + 1) * size)).astype(F32)


def head_sums(values, member):
    hi, lo = split2(values)
    return dot(member, hi.astype(BF16), NT) + dot(member, lo.astype(BF16), NT)


def running(rows, upper):
    hi, rest = split2(rows)
    mid, lo = split2(rest)
    k = rows.shape[0]
    out = dot(jnp.concatenate([hi, mid, lo], axis=0).astype(BF16), upper, NN)
    return out[:k] + out[k : 2 * k] + out[2 * k :]


def triangle(width, lower):
    row = lax.broadcasted_iota(jnp.int32, (width, width), 0)
    col = lax.broadcasted_iota(jnp.int32, (width, width), 1)
    return (row >= col) if lower else (row <= col)


def softplus(v):
    return jnp.maximum(v, 0.0) + jnp.log1p(jnp.exp(-jnp.abs(v)))


def column(line, piece, heads):
    shape = (heads, line.shape[1])
    row = lax.broadcasted_iota(jnp.int32, shape, 0)
    col = lax.broadcasted_iota(jnp.int32, shape, 1)
    return jnp.sum(jnp.where(col == row + piece * heads, line, 0.0), axis=1, keepdims=True)


def block_sums(logs, blocks):
    heads = logs.shape[0]
    ones = triangle(GROUP, False).astype(BF16)
    stacked = jnp.concatenate([logs[:, n * GROUP : (n + 1) * GROUP] for n in range(blocks)], axis=0)
    cums = running(stacked, ones)
    return [cums[n * heads : (n + 1) * heads] for n in range(blocks)]


def factors(raw, bias, rate, skip, columns_ref, table_ref):
    heads, length = raw.shape
    width = table_ref.shape[1]
    blocks = length // GROUP
    step = softplus(raw + bias)
    cums = block_sums(-rate * step, blocks)
    totals = [cum[:, GROUP - 1 :] for cum in cums]
    before = [jnp.zeros((heads, 1), F32)]
    for total in totals:
        before.append(before[-1] + total)
    for n in range(blocks):
        rows = slice(n * GROUP, (n + 1) * GROUP)
        gain = split2(jnp.exp(totals[n] - cums[n]) * step[:, rows])
        lift = split2(jnp.exp(cums[n] - totals[n]))
        columns_ref[rows, :] = jnp.concatenate([*gain, *lift], axis=0).T.astype(BF16)
    whole = before[-1]
    lines = [jnp.exp(t) for t in totals]
    lines += [jnp.exp(whole - before[n + 1]) for n in range(blocks)]
    lines += [jnp.exp(before[n + 1]) for n in range(blocks)]
    lines += [jnp.exp(whole), skip]
    lines += [skip] * (-len(lines) % 8)
    hi, lo = split2(jnp.concatenate(lines, axis=1).T)
    member = head_matrix(heads, width).astype(BF16)
    table_ref[...] = dot(hi.astype(BF16), member, NN) + dot(lo.astype(BF16), member, NN)


def picker(piece, heads, all_heads, width, first):
    shape = (4 * all_heads, width)
    row = lax.broadcasted_iota(jnp.int32, shape, 0)
    col = lax.broadcasted_iota(jnp.int32, shape, 1)
    size = width // heads
    base = (0 if first else 2 * all_heads) + piece * heads
    hit = None
    for term in range(2):
        low = (row - (base + term * all_heads)) * size
        one = (col >= low) & (col < low + size)
        hit = one if hit is None else hit | one
    return hit.astype(BF16)


def local_kernel(first, last, count, *refs):
    at_ref, x_ref, dy_ref, b_ref, c_ref = refs[:5]
    if first:
        raw_ref, bias_ref, rate_ref, skip_ref = refs[5:9]
        outs = refs[9 : 9 + count]
        xs_ref, ys_ref, direct_ref, columns_ref, table_ref, bt, ct = refs[9 + count : 16 + count]
    else:
        columns_ref, table_ref = refs[5:7]
        outs = refs[10 : 10 + count]
        xs_ref, ys_ref, direct_ref = refs[10 + count : 13 + count]
        if last:
            left, right, bt, ct = refs[13 + count :]
        else:
            bt, ct = refs[13 + count : 15 + count]
    if not last:
        near_x, near_dy, near_xs, near_ys, sems = refs[-5:]
    g = pl.program_id(0)
    states = b_ref.shape[1]
    length, width = columns_ref.shape[0], outs[0].shape[1]
    blocks = length // GROUP
    piece = at_ref[0] + g
    writes = []
    if not last:
        place = pl.ds(pl.multiple_of(piece * width, width), width)
        reads = [
            pltpu.make_async_copy(x_ref.at[:, place], near_x, sems.at[0]),
            pltpu.make_async_copy(dy_ref.at[:, place], near_dy, sems.at[1]),
        ]
        for n in range(blocks):
            rows = slice(n * GROUP, (n + 1) * GROUP)
            for k, (near, far) in enumerate(((near_xs, xs_ref), (near_ys, ys_ref))):
                target = far.at[rows, place]
                writes.append(
                    pltpu.make_async_copy(near.at[rows, :], target, sems.at[2 + 2 * n + k])
                )
        for copy in reads:
            copy.start()
        x_ref, dy_ref, xs_ref, ys_ref = near_x, near_dy, near_xs, near_ys
    all_heads = columns_ref.shape[1] // 4
    heads = all_heads * width // table_ref.shape[1]

    @pl.when(g == 0)
    def _():
        bt[...] = b_ref[...].T
        ct[...] = c_ref[...].T
        if first:
            factors(
                raw_ref[0],
                column(bias_ref[...], 0, all_heads),
                column(rate_ref[...], 0, all_heads),
                column(skip_ref[...], 0, all_heads),
                columns_ref,
                table_ref,
            )
        if last:
            for n in range(blocks):
                rows = slice(n * GROUP, (n + 1) * GROUP)
                scores = dot(c_ref[rows, :], b_ref[rows, :], NT)
                left[n] = jnp.where(triangle(GROUP, True), scores, 0.0).astype(BF16)
                scores = dot(b_ref[rows, :], c_ref[rows, :], NT)
                right[n] = jnp.where(triangle(GROUP, False), scores, 0.0).astype(BF16)

    gain = dot(columns_ref[...], picker(piece, heads, all_heads, width, True), NN)
    lift = dot(columns_ref[...], picker(piece, heads, all_heads, width, False), NN)
    if not last:
        for copy in reads:
            copy.wait()
    table = table_ref[:, pl.ds(pl.multiple_of(piece * width, width), width)]
    state = jnp.zeros((states, width), F32)
    grad = jnp.zeros((states, width), F32)
    direct = jnp.zeros((8, width), F32)
    for n in range(blocks):
        rows = slice(n * GROUP, (n + 1) * GROUP)
        x = x_ref[rows, :].astype(F32)
        dy = dy_ref[rows, :].astype(F32)
        direct = direct + jnp.sum((dy * x).reshape(GROUP // 8, 8, width), axis=0)
        scaled_x = (x * gain[rows]).astype(BF16)
        scaled_dy = (dy * lift[rows]).astype(BF16)
        xs_ref[rows, :] = scaled_x
        ys_ref[rows, :] = scaled_dy
        for copy in writes[2 * n : 2 * n + 2]:
            copy.start()
        later = table[blocks + n : blocks + n + 1]
        earlier = table[2 * blocks + n : 2 * blocks + n + 1]
        state = state + later * dot(bt[:, rows], scaled_x, NN)
        grad = grad + earlier * dot(ct[:, rows], scaled_dy, NN)
    direct_ref[...] = direct
    decay = jnp.broadcast_to(table[3 * blocks : 3 * blocks + 1], (8, width))
    for k, out_ref in enumerate(outs):

        @pl.when(g == k)
        def _():
            out_ref[:states] = state
            out_ref[states : 2 * states] = grad
            out_ref[2 * states :] = decay

    for copy in writes:
        copy.wait()


def local_states(at, count, last, x, dy, b, c, vectors, before):
    length, channels = x.shape
    states = b.shape[1]
    pieces = 2 * PARTS
    width = channels // pieces
    lines = 3 * (length // GROUP) + 2
    lines += -lines % 8
    first = before is None
    whole = lambda g, at: (0, 0)
    columns = pl.BlockSpec((length, width), lambda g, at: (0, at[0] + g))
    strip = pl.BlockSpec((8, width), lambda g, at: (0, at[0] + g))
    maps = pl.BlockSpec((length, states), whole)
    anywhere = pl.BlockSpec(memory_space=pl.ANY)
    wide = columns if last else anywhere
    in_specs = [wide, wide, maps, maps]
    out_specs = [pl.BlockSpec((2 * states + 8, width), whole)] * count + [wide, wide, strip]
    out_shape = [jax.ShapeDtypeStruct((2 * states + 8, width), F32)] * count + [
        jax.ShapeDtypeStruct((length, channels), BF16),
        jax.ShapeDtypeStruct((length, channels), BF16),
        jax.ShapeDtypeStruct((8, channels), F32),
    ]
    aliases = {}
    if first:
        raw, bias, rate, skip = vectors
        heads = raw.shape[1]
        args = [raw, bias, rate, skip]
        in_specs += [pl.BlockSpec(raw.shape, lambda g, at: (0, 0, 0))]
        in_specs += [pl.BlockSpec(bias.shape, whole)] * 3
        tables = [
            jax.ShapeDtypeStruct((length, 4 * heads), BF16),
            jax.ShapeDtypeStruct((lines, channels), F32),
        ]
        out_shape += tables
        out_specs += [pl.BlockSpec(t.shape, whole) for t in tables]
    else:
        xs, ys, direct, factor_columns, table = before
        args = [factor_columns, table, xs, ys, direct]
        in_specs += [pl.BlockSpec(factor_columns.shape, whole), pl.BlockSpec(table.shape, whole)]
        in_specs += [anywhere] * 3
        aliases = {7: count, 8: count + 1, 9: count + 2}
    scratch = [pltpu.VMEM((states, length), BF16)] * 2
    scratch += [pltpu.VMEM((length, width), BF16)] * 4
    scratch += [pltpu.SemaphoreType.DMA((2 + 2 * (length // GROUP),))]
    if last:
        blocks = length // GROUP
        extra = [jax.ShapeDtypeStruct((blocks, GROUP, GROUP), BF16)] * 2
        extra += [jax.ShapeDtypeStruct((states, length), BF16)] * 2
        out_shape += extra
        out_specs += [pl.BlockSpec(e.shape, lambda g, at, n=len(e.shape): (0,) * n) for e in extra]
        scratch = []
    grid_spec = pltpu.PrefetchScalarGridSpec(
        num_scalar_prefetch=1,
        grid=(count,),
        in_specs=in_specs,
        out_specs=out_specs,
        scratch_shapes=scratch,
    )
    out = pl.pallas_call(
        functools.partial(local_kernel, first, last, count),
        grid_spec=grid_spec,
        out_shape=out_shape,
        input_output_aliases=aliases,
        compiler_params=pltpu.CompilerParams(vmem_limit_bytes=VMEM_LIMIT),
        cost_estimate=pl.CostEstimate(
            flops=8 * count * length * width * states,
            bytes_accessed=8 * count * length * width,
            transcendentals=0,
        ),
        name="local_states",
    )(at, x, dy, b, c, *args)
    return out[:count], list(out[count:])


def grads_kernel(first, scale, part, half, begin, *refs):
    y_ref, xs_ref, ys_ref, dy_far, direct_ref, b_ref, c_ref, columns_far, table_ref = refs[:9]
    raw_ref, bias_ref, rate_ref, bt, ct, left_far, right_far, adder_far = refs[9:17]
    held = refs[17:21]
    refs = refs[21:]
    if not first:
        dc_in, db_in, par_in = refs[:3]
        refs = refs[5:]
    dx_ref, dc_ref, db_ref, draw_ref, par_ref = refs[:5]
    sums, dc_sum, db_sum, terms, dy_ref, columns_ref, left, right, adder, sems = refs[5:15]
    if not first:
        dc_old, db_old = refs[15:]
        old = [(dc_in, dc_old, sems.at[0]), (db_in, db_old, sems.at[1])]
    fixed = [
        (left_far, left, sems.at[2]),
        (right_far, right, sems.at[3]),
        (adder_far, adder, sems.at[4]),
        (columns_far, columns_ref, sems.at[5]),
    ]
    g = pl.program_id(0)
    heads = raw_ref.shape[1]
    length, width = xs_ref.shape
    states = b_ref.shape[1]
    blocks = length // GROUP
    piece = (begin + g) * half + part
    all_heads = columns_ref.shape[1] // 4
    member = head_matrix(heads, width).astype(BF16)
    lower = triangle(GROUP, True)
    rows = [slice(n * GROUP, (n + 1) * GROUP) for n in range(blocks)]

    own_columns = pl.ds(pl.multiple_of(piece * width, width), width)
    dy_copy = pltpu.make_async_copy(dy_far.at[:, own_columns], dy_ref, sems.at[6])
    dy_copy.start()

    @pl.when(g == 0)
    def _():
        for source, target, sem in fixed:
            pltpu.make_async_copy(source, target, sem).start()
        if not first:
            for source, target, sem in old:
                pltpu.make_async_copy(source, target, sem).start()
        sums[...] = jnp.zeros_like(sums)
        dc_sum[...] = jnp.zeros_like(dc_sum)
        db_sum[...] = jnp.zeros_like(db_sum)
        par_ref[...] = jnp.zeros_like(par_ref) if first else par_in[...]

    own = begin + g == y_ref[0]
    early = jnp.where(own, held[0][...], held[2][...])
    late = jnp.where(own, held[1][...], held[3][...])
    state_early = y_ref[1] == 1
    state = jnp.where(state_early, early, late)
    grad = jnp.where(state_early, late, early)
    table = table_ref[...]
    skip = table[3 * blocks + 1 : 3 * blocks + 2]
    entering_low, ends = [], []
    for n in range(blocks):
        state = table[n : n + 1] * state
        entering_low.append(state.astype(BF16))
        state = state + dot(bt[:, rows[n]], xs_ref[rows[n], :], NN)
        ends.append(state)
    leaving_low, edges = [None] * blocks, [None] * blocks
    for n in reversed(range(blocks)):
        leaving_low[n] = grad.astype(BF16)
        edges[n] = jnp.sum(ends[n] * grad, axis=0, keepdims=True)
        grad = table[n : n + 1] * (grad + dot(ct[:, rows[n]], ys_ref[rows[n], :], NN))

    @pl.when(g == 0)
    def _():
        for source, target, sem in fixed:
            pltpu.make_async_copy(source, target, sem).wait()

    dy_copy.wait()
    gain = dot(columns_ref[...], picker(piece, heads, all_heads, width, True), NN)
    for n in range(blocks):
        scaled_x, scaled_dy = xs_ref[rows[n], :], ys_ref[rows[n], :]
        forward = dot(left[n], scaled_x, NN) + dot(c_ref[rows[n], :], entering_low[n], NN)
        backward = dot(right[n], scaled_dy, NN) + dot(b_ref[rows[n], :], leaving_low[n], NN)
        weight = gain[rows[n]]
        dx_ref[rows[n], :] = (weight * backward + skip * dy_ref[rows[n], :].astype(F32)).astype(
            dx_ref.dtype
        )
        v = scaled_x.astype(F32) * backward
        difference = scaled_dy.astype(F32) * forward - v
        hi = difference.astype(BF16)
        lo = (difference - hi.astype(F32)).astype(BF16)
        terms[rows[n], :width] = hi
        terms[rows[n], width : 2 * width] = lo
        terms[rows[n], 2 * width :] = v.astype(BF16)
        sums[n] += dot(scaled_dy, scaled_x, NT)
        dc_sum[n] += dot(scaled_dy, entering_low[n], NT)
        db_sum[n] += dot(scaled_x, leaving_low[n], NT)
    added = dot(terms[...], adder[...], NN).T
    added = [added[:, rows[n]] for n in range(blocks)]
    edge = head_sums(jnp.concatenate(edges + [edges[0]] * (8 - blocks), axis=0), member)
    slopes = running(
        jnp.concatenate([a[:heads] for a in added], axis=0), lower.astype(BF16)
    )
    slope = jnp.concatenate(
        [slopes[n * heads : (n + 1) * heads] + edge[:, n : n + 1] for n in range(blocks)], axis=1
    )
    v = jnp.concatenate([a[heads : 2 * heads] for a in added], axis=1)
    raw = raw_ref[0] + column(bias_ref[...], piece, heads)
    step = softplus(raw)
    draw = (v / step - column(rate_ref[...], piece, heads) * slope) / (1.0 + jnp.exp(-raw))
    draw_ref[0] = draw
    values = (
        jnp.sum(draw, axis=1, keepdims=True),
        jnp.sum(head_sums(direct_ref[...], member), axis=1, keepdims=True),
        -jnp.sum(step * slope, axis=1, keepdims=True),
    )
    for k, value in enumerate(values):
        par_ref[k : k + 1] += lanes_of(value * scale, piece, (heads, par_ref.shape[1]))

    @pl.when(g == pl.num_programs(0) - 1)
    def _():
        if not first:
            for source, target, sem in old:
                pltpu.make_async_copy(source, target, sem).wait()
        for n in range(blocks):
            pair = jnp.where(lower, sums[n], 0.0).astype(BF16)
            dc = dot(pair, b_ref[rows[n], :], NN) + dc_sum[n]
            db = dot(pair, c_ref[rows[n], :], TN) + db_sum[n]
            if not first:
                dc = dc + dc_old[rows[n], :]
                db = db + db_old[rows[n], :]
            dc_ref[rows[n], :] = dc
            db_ref[rows[n], :] = db


def local_grads(part, begin, count, scale, y, saved, dy, b, c, vectors, held, before):
    xs, ys, direct, factor_columns, table, left, right, bt, ct = saved
    raw, bias, rate, _ = vectors
    length, channels = xs.shape
    pieces = 2 * PARTS
    heads = raw.shape[1] // pieces
    raw = raw.reshape(pieces, heads, length)
    width = channels // pieces
    states = b.shape[1]
    blocks = length // GROUP
    half = pieces // 2
    first = before is None
    whole = lambda g, y: (0, 0)
    place = lambda g, y: (0, (begin + g) * half + part)
    columns = pl.BlockSpec((length, width), place)
    maps = pl.BlockSpec((length, states), whole)
    line = pl.BlockSpec(bias.shape, whole)
    lines = pl.BlockSpec((1, heads, length), lambda g, y: ((begin + g) * half + part, 0, 0))
    params = pl.BlockSpec((8, 128), whole)
    anywhere = pl.BlockSpec(memory_space=pl.ANY)
    in_specs = [columns, columns, anywhere, pl.BlockSpec((8, width), place), maps, maps]
    in_specs += [
        anywhere,
        pl.BlockSpec((table.shape[0], width), place),
    ]
    in_specs += [lines, line, line]
    args = [xs, ys, dy, direct, b, c, factor_columns, table, raw, bias, rate]
    args += [bt, ct, left, right, adding(width, heads, (0, 0, 1)), *held]
    in_specs += [pl.BlockSpec(bt.shape, whole)] * 2 + [anywhere] * 3
    in_specs += [pl.BlockSpec(h.shape, whole) for h in held]
    aliases = {}
    if not first:
        dx, dc, db, draw, par = before
        args += [dc, db, par, dx, draw]
        in_specs += [anywhere, anywhere, params, anywhere, anywhere]
        aliases = {24: 0, 25: 3}
    grid_spec = pltpu.PrefetchScalarGridSpec(
        num_scalar_prefetch=1,
        grid=(count,),
        in_specs=in_specs,
        out_specs=[columns, maps, maps, lines, params],
        scratch_shapes=[
            pltpu.VMEM((blocks, GROUP, GROUP), F32),
            pltpu.VMEM((blocks, GROUP, states), F32),
            pltpu.VMEM((blocks, GROUP, states), F32),
            pltpu.VMEM((length, 3 * width), BF16),
            pltpu.VMEM((length, width), BF16),
            pltpu.VMEM(factor_columns.shape, BF16),
            pltpu.VMEM(left.shape, BF16),
            pltpu.VMEM(right.shape, BF16),
            pltpu.VMEM((3 * width, 128), BF16),
            pltpu.SemaphoreType.DMA((7,)),
        ]
        + [
            pltpu.VMEM((length, states), F32),
            pltpu.VMEM((length, states), F32),
        ]
        * (not first),
    )
    return pl.pallas_call(
        functools.partial(grads_kernel, first, scale, part, half, begin),
        grid_spec=grid_spec,
        out_shape=[
            jax.ShapeDtypeStruct((length, channels), BF16),
            jax.ShapeDtypeStruct((length, states), F32),
            jax.ShapeDtypeStruct((length, states), F32),
            jax.ShapeDtypeStruct((pieces, heads, length), F32),
            jax.ShapeDtypeStruct((8, 128), F32),
        ],
        input_output_aliases=aliases,
        compiler_params=pltpu.CompilerParams(vmem_limit_bytes=SMALL_LIMIT),
        cost_estimate=pl.CostEstimate(
            flops=12 * count * length * width * (GROUP + states),
            bytes_accessed=6 * count * length * width,
            transcendentals=0,
        ),
        name="local_grads",
    )(y, *args)


def adding(width, heads, places):
    out = np.zeros((len(places) * width, 128), np.float32)
    size = width // heads
    for k, place in enumerate(places):
        for channel in range(width):
            out[k * width + channel, place * heads + channel // size] = 1.0
    return jnp.asarray(out, BF16)


def lanes_of(values, piece, shape):
    row = lax.broadcasted_iota(jnp.int32, shape, 0)
    col = lax.broadcasted_iota(jnp.int32, shape, 1)
    return jnp.sum(jnp.where(col == row + piece * shape[0], values, 0.0), axis=0, keepdims=True)


def summed_over(value, axis):
    size = lax.axis_size(axis)
    if size & (size - 1):
        return lax.psum(value, axis)
    bit = 1
    while bit < size:
        steps = (bit, 2 * bit, 3 * bit) if 4 * bit <= size else (bit,)
        got = [lax.ppermute(value, axis, [(i, i ^ s) for i in range(size)]) for s in steps]
        value = value + got[0]
        if len(got) == 3:
            value = value + (got[1] + got[2])
        bit *= 4 if len(got) == 3 else 2
    return value


def after(value, *earlier):
    return lax.optimization_barrier((value, *earlier))[0]


def entering(sent, kept, states, token):
    size = lax.axis_size("seq")
    pairs = size // 2
    index = lax.axis_index("seq")
    place, second = index // 2, index % 2 == 1
    swap = [(i, i ^ 1) for i in range(size)]
    both = lambda moves: [(2 * a + y, 2 * b + y) for a, b in moves for y in range(2)]

    def halves(got):
        spans = ((0, states), (states, 2 * states), (2 * states, 2 * states + 1))
        for low, high in spans:
            own, other = kept[low:high], got[low:high]
            yield jnp.where(second, other, own), jnp.where(second, own, other)

    def message_of(up, got, arrived):
        (l1, l2), (k1, k2), (d1, d2) = halves(got)
        message = jnp.where(up, d2 * l1 + l2, k1 + d1 * k2)
        return message if arrived is None else message + d1 * d2 * arrived[:states]

    def shares(is_state, value, got):
        (l1, _), (_, k2), (d1, d2) = halves(got)
        for_first = jnp.where(is_state, value, k2 + d2 * value)
        for_second = jnp.where(is_state, d1 * value + l1, value)
        return jnp.where(second, for_second, for_first), jnp.where(second, for_first, for_second)

    message = sent if token is None else after(sent, *token)
    got = lax.ppermute(message, "seq", swap)
    token = yield message, got
    got = after(got, token)
    lower = place < pairs // 2
    if pairs == 4:
        message = message_of((place == 0) | (place == 2), got, None)
        (_, _), (_, _), (d1, d2) = halves(got)
        message = jnp.concatenate([message, jnp.broadcast_to(d1 * d2, (8, message.shape[1]))])
        near = lax.ppermute(message, "seq", both([(0, 1), (1, 0), (2, 3), (3, 2)]))
        token = yield message, near
        near = after(near, token)
        message = message_of(place == 1, got, near)
        middle = lax.ppermute(message, "seq", both([(1, 2), (2, 1)]))
        far = lax.ppermute(message, "seq", both([(1, 3), (2, 0)]))
        inside = (place == 1) | (place == 2)
        known = jnp.where(inside, near[:states], 0.0)
        mine_early, early = shares(lower, known, got)
        other_early = lax.ppermute(early, "seq", swap)
        token = yield early, far
        far = after(far, token)
        outer = near[states : states + 1] * far + near[:states]
        mine_late, late = shares(~lower, jnp.where(inside, middle, outer), got)
        other_late = lax.ppermute(late, "seq", swap)
        yield late, other_late
    else:
        arrived = []
        for k in range(1, pairs):
            message = message_of(place == k - 1, got, arrived[-1] if arrived else None)
            routes = both([(k - 1, k), (pairs - k, pairs - k - 1)])
            arrived.append(lax.ppermute(message, "seq", routes))
            token = yield message, arrived[-1]
            arrived[-1] = after(arrived[-1], token)
        start = end = jnp.zeros_like(arrived[0])
        for k in range(1, pairs):
            start = jnp.where(place == k, arrived[k - 1], start)
            end = jnp.where(place == pairs - 1 - k, arrived[k - 1], end)
        mine_early, early = shares(lower, jnp.where(lower, start, end), got)
        mine_late, late = shares(~lower, jnp.where(lower, end, start), got)
        other_early = lax.ppermute(early, "seq", swap)
        other_late = lax.ppermute(late, "seq", swap)
        yield late, other_late
    yield mine_early, mine_late, other_early, other_late


def shards(inputs, input_map, output_map, step_raw, step_bias, decay_rate, skip_gain, cotangent):
    length = inputs.shape[1]
    heads = step_raw.shape[1]
    states = input_map.shape[2]
    x, b, c, dy = inputs[0], input_map[0], output_map[0], cotangent[0]
    vectors = (
        step_raw,
        step_bias.reshape(1, heads),
        decay_rate.reshape(1, heads),
        skip_gain.reshape(1, heads),
    )
    size = lax.axis_size("seq")
    y = lax.axis_index("seq") % 2
    scale = 1.0 / math.sqrt(length * size * lax.axis_size("batch"))

    def local(half, part, count, before):
        at = jnp.reshape(half * PARTS + part, (1,)).astype(jnp.int32)
        last = count == PARTS
        out, saved = local_states(at, count, last, x, dy, b, c, vectors, before)
        return out, saved[:3] + list(before[3:] if before else []) + saved[3:]

    sent, kept = [], []
    saved = None
    for part in range(PARTS):
        out, saved = local(1 - y, part, 1, saved)
        sent += out
    kept, saved = local(y, 0, PARTS, saved)

    transfers = 4 if size == 8 else size // 2 + 1
    order = [(0, 0), (1, 0)] + [
        pick for k in range(1, transfers) for pick in ((0, k), (1, k - 1)) if pick != (1, 0)
    ]
    order.append((1, transfers - 1))
    flows, token = {}, None
    lower = lax.axis_index("seq") < size // 2
    here = jnp.stack([y, lower.astype(y.dtype)]).astype(jnp.int32)
    found = None

    def grads(part, begin, count, token, held):
        *most, final = held
        held = (*most, after(final, token))
        return local_grads(
            part, begin, count, scale, here, saved, dy, b, c, vectors, held, found
        )

    for part, k in order:
        if (part, k) == (1, transfers - 1):
            held = next(flows[0])
            found = grads(0, 0, 1, token, held)
            token = found[-1]
        if k == 0:
            flows[part] = entering(sent[part], kept[part], states, token)
            message, arrived = next(flows[part])
            token = None if part == 0 else message
        else:
            token = flows[part].send(token)[0]
    found = grads(0, 1, 1, token, held)
    found = grads(1, 0, 2, found[-1], next(flows[1]))
    dx, dc, db, draw, params = found
    summed = summed_over(summed_over(params, "batch"), "seq")
    return (
        dx[None],
        db[None],
        dc[None],
        draw.reshape(heads, length)[None],
        summed[:2, :heads],
        summed[2, :heads],
    )


def solution(mesh):
    in_specs = (
        P("batch", "seq", None),
        P("batch", "seq", None),
        P("batch", "seq", None),
        P("batch", None, "seq"),
        P(),
        P(),
        P(),
        P("batch", "seq", None),
    )
    out_specs = (
        P("batch", "seq", None),
        P("batch", "seq", None),
        P("batch", "seq", None),
        P("batch", None, "seq"),
        P(),
        P(),
    )
    return jax.shard_map(shards, mesh=mesh, in_specs=in_specs, out_specs=out_specs, check_vma=False)
```

```python
import functools
import math

import jax
import jax.numpy as jnp
import numpy as np
from jax import lax
from jax.experimental import pallas as pl
from jax.experimental.pallas import tpu as pltpu
from jax.sharding import PartitionSpec as P

GROUP = 256
PARTS = 2
VMEM_LIMIT = 60 * 1024 * 1024
SMALL_LIMIT = 40 * 1024 * 1024
F32 = jnp.float32
BF16 = jnp.bfloat16


def dot(a, b, dims):
    return lax.dot_general(a, b, (dims, ((), ())), preferred_element_type=F32)


NN = ((1,), (0,))
NT = ((1,), (1,))
TN = ((0,), (0,))


def split2(a):
    hi = a.astype(BF16).astype(F32)
    return hi, a - hi


def head_matrix(heads, width):
    size = width // heads
    row = lax.broadcasted_iota(jnp.int32, (heads, width), 0)
    col = lax.broadcasted_iota(jnp.int32, (heads, width), 1)
    return ((col >= row * size) & (col < (row + 1) * size)).astype(F32)


def head_sums(values, member):
    hi, lo = split2(values)
    return dot(member, hi.astype(BF16), NT) + dot(member, lo.astype(BF16), NT)


def running(rows, upper):
    hi, rest = split2(rows)
    mid, lo = split2(rest)
    k = rows.shape[0]
    out = dot(jnp.concatenate([hi, mid, lo], axis=0).astype(BF16), upper, NN)
    return out[:k] + out[k : 2 * k] + out[2 * k :]


def triangle(width, lower):
    row = lax.broadcasted_iota(jnp.int32, (width, width), 0)
    col = lax.broadcasted_iota(jnp.int32, (width, width), 1)
    return (row >= col) if lower else (row <= col)


def softplus(v):
    return jnp.maximum(v, 0.0) + jnp.log1p(jnp.exp(-jnp.abs(v)))


def column(line, piece, heads):
    shape = (heads, line.shape[1])
    row = lax.broadcasted_iota(jnp.int32, shape, 0)
    col = lax.broadcasted_iota(jnp.int32, shape, 1)
    return jnp.sum(jnp.where(col == row + piece * heads, line, 0.0), axis=1, keepdims=True)


def block_sums(logs, blocks):
    heads = logs.shape[0]
    ones = triangle(GROUP, False).astype(BF16)
    stacked = jnp.concatenate([logs[:, n * GROUP : (n + 1) * GROUP] for n in range(blocks)], axis=0)
    cums = running(stacked, ones)
    return [cums[n * heads : (n + 1) * heads] for n in range(blocks)]


def factors(raw, bias, rate, skip, columns_ref, table_ref):
    heads, length = raw.shape
    width = table_ref.shape[1]
    blocks = length // GROUP
    step = softplus(raw + bias)
    cums = block_sums(-rate * step, blocks)
    totals = [cum[:, GROUP - 1 :] for cum in cums]
    before = [jnp.zeros((heads, 1), F32)]
    for total in totals:
        before.append(before[-1] + total)
    for n in range(blocks):
        rows = slice(n * GROUP, (n + 1) * GROUP)
        gain = split2(jnp.exp(totals[n] - cums[n]) * step[:, rows])
        lift = split2(jnp.exp(cums[n] - totals[n]))
        columns_ref[rows, :] = jnp.concatenate([*gain, *lift], axis=0).T.astype(BF16)
    whole = before[-1]
    lines = [jnp.exp(t) for t in totals]
    lines += [jnp.exp(whole - before[n + 1]) for n in range(blocks)]
    lines += [jnp.exp(before[n + 1]) for n in range(blocks)]
    lines += [jnp.exp(whole), skip]
    lines += [skip] * (-len(lines) % 8)
    hi, lo = split2(jnp.concatenate(lines, axis=1).T)
    member = head_matrix(heads, width).astype(BF16)
    table_ref[...] = dot(hi.astype(BF16), member, NN) + dot(lo.astype(BF16), member, NN)


def picker(piece, heads, all_heads, width, first):
    shape = (4 * all_heads, width)
    row = lax.broadcasted_iota(jnp.int32, shape, 0)
    col = lax.broadcasted_iota(jnp.int32, shape, 1)
    size = width // heads
    base = (0 if first else 2 * all_heads) + piece * heads
    hit = None
    for term in range(2):
        low = (row - (base + term * all_heads)) * size
        one = (col >= low) & (col < low + size)
        hit = one if hit is None else hit | one
    return hit.astype(BF16)


def local_kernel(first, last, count, *refs):
    at_ref, x_ref, dy_ref, b_ref, c_ref = refs[:5]
    if first:
        raw_ref, bias_ref, rate_ref, skip_ref = refs[5:9]
        outs = refs[9:-7]
        xs_ref, ys_ref, direct_ref, columns_ref, table_ref, bt, ct = refs[-7:]
    else:
        columns_ref, table_ref = refs[5:7]
        outs = refs[10 : 10 + count]
        xs_ref, ys_ref, direct_ref = refs[10 + count : 13 + count]
        if last:
            left, right, bt, ct = refs[13 + count :]
        else:
            bt, ct = refs[13 + count :]
    g = pl.program_id(0)
    length, width = x_ref.shape
    states = b_ref.shape[1]
    blocks = length // GROUP
    piece = at_ref[0] + g
    all_heads = columns_ref.shape[1] // 4
    heads = all_heads * width // table_ref.shape[1]

    @pl.when(g == 0)
    def _():
        bt[...] = b_ref[...].T
        ct[...] = c_ref[...].T
        if first:
            factors(
                raw_ref[0],
                column(bias_ref[...], 0, all_heads),
                column(rate_ref[...], 0, all_heads),
                column(skip_ref[...], 0, all_heads),
                columns_ref,
                table_ref,
            )
        if last:
            for n in range(blocks):
                rows = slice(n * GROUP, (n + 1) * GROUP)
                scores = dot(c_ref[rows, :], b_ref[rows, :], NT)
                left[n] = jnp.where(triangle(GROUP, True), scores, 0.0).astype(BF16)
                scores = dot(b_ref[rows, :], c_ref[rows, :], NT)
                right[n] = jnp.where(triangle(GROUP, False), scores, 0.0).astype(BF16)

    gain = dot(columns_ref[...], picker(piece, heads, all_heads, width, True), NN)
    lift = dot(columns_ref[...], picker(piece, heads, all_heads, width, False), NN)
    table = table_ref[:, pl.ds(pl.multiple_of(piece * width, width), width)]
    state = jnp.zeros((states, width), F32)
    grad = jnp.zeros((states, width), F32)
    direct = jnp.zeros((8, width), F32)
    for n in range(blocks):
        rows = slice(n * GROUP, (n + 1) * GROUP)
        x = x_ref[rows, :].astype(F32)
        dy = dy_ref[rows, :].astype(F32)
        direct = direct + jnp.sum((dy * x).reshape(GROUP // 8, 8, width), axis=0)
        scaled_x = (x * gain[rows]).astype(BF16)
        scaled_dy = (dy * lift[rows]).astype(BF16)
        xs_ref[rows, :] = scaled_x
        ys_ref[rows, :] = scaled_dy
        later = table[blocks + n : blocks + n + 1]
        earlier = table[2 * blocks + n : 2 * blocks + n + 1]
        state = state + later * dot(bt[:, rows], scaled_x, NN)
        grad = grad + earlier * dot(ct[:, rows], scaled_dy, NN)
    direct_ref[...] = direct
    decay = jnp.broadcast_to(table[3 * blocks : 3 * blocks + 1], (8, width))
    for k, out_ref in enumerate(outs):

        @pl.when(g == k)
        def _():
            out_ref[:states] = state
            out_ref[states : 2 * states] = grad
            out_ref[2 * states :] = decay


def local_states(at, count, last, x, dy, b, c, vectors, before):
    length, channels = x.shape
    states = b.shape[1]
    pieces = 2 * PARTS
    width = channels // pieces
    lines = 3 * (length // GROUP) + 2
    lines += -lines % 8
    first = before is None
    whole = lambda g, at: (0, 0)
    columns = pl.BlockSpec((length, width), lambda g, at: (0, at[0] + g))
    strip = pl.BlockSpec((8, width), lambda g, at: (0, at[0] + g))
    maps = pl.BlockSpec((length, states), whole)
    anywhere = pl.BlockSpec(memory_space=pl.ANY)
    in_specs = [columns, columns, maps, maps]
    out_specs = [pl.BlockSpec((2 * states + 8, width), whole)] * count + [columns, columns, strip]
    out_shape = [jax.ShapeDtypeStruct((2 * states + 8, width), F32)] * count + [
        jax.ShapeDtypeStruct((length, channels), BF16),
        jax.ShapeDtypeStruct((length, channels), BF16),
        jax.ShapeDtypeStruct((8, channels), F32),
    ]
    aliases = {}
    if first:
        raw, bias, rate, skip = vectors
        heads = raw.shape[1]
        args = [raw, bias, rate, skip]
        in_specs += [pl.BlockSpec(raw.shape, lambda g, at: (0, 0, 0))]
        in_specs += [pl.BlockSpec(bias.shape, whole)] * 3
        tables = [
            jax.ShapeDtypeStruct((length, 4 * heads), BF16),
            jax.ShapeDtypeStruct((lines, channels), F32),
        ]
        out_shape += tables
        out_specs += [pl.BlockSpec(t.shape, whole) for t in tables]
    else:
        xs, ys, direct, factor_columns, table = before
        args = [factor_columns, table, xs, ys, direct]
        in_specs += [pl.BlockSpec(factor_columns.shape, whole), pl.BlockSpec(table.shape, whole)]
        in_specs += [anywhere] * 3
        aliases = {7: count, 8: count + 1, 9: count + 2}
    scratch = [pltpu.VMEM((states, length), BF16)] * 2
    if last:
        blocks = length // GROUP
        extra = [jax.ShapeDtypeStruct((blocks, GROUP, GROUP), BF16)] * 2
        extra += [jax.ShapeDtypeStruct((states, length), BF16)] * 2
        out_shape += extra
        out_specs += [pl.BlockSpec(e.shape, lambda g, at, n=len(e.shape): (0,) * n) for e in extra]
        scratch = []
    grid_spec = pltpu.PrefetchScalarGridSpec(
        num_scalar_prefetch=1,
        grid=(count,),
        in_specs=in_specs,
        out_specs=out_specs,
        scratch_shapes=scratch,
    )
    out = pl.pallas_call(
        functools.partial(local_kernel, first, last, count),
        grid_spec=grid_spec,
        out_shape=out_shape,
        input_output_aliases=aliases,
        compiler_params=pltpu.CompilerParams(vmem_limit_bytes=VMEM_LIMIT),
        cost_estimate=pl.CostEstimate(
            flops=8 * count * length * width * states,
            bytes_accessed=8 * count * length * width,
            transcendentals=0,
        ),
        name="local_states",
    )(at, x, dy, b, c, *args)
    return out[:count], list(out[count:])


def grads_kernel(first, scale, part, half, begin, *refs):
    y_ref, xs_ref, ys_ref, dy_ref, direct_ref, b_ref, c_ref, columns_ref, table_ref = refs[:9]
    raw_ref, bias_ref, rate_ref, bt, ct, left, right, adder = refs[9:17]
    held = refs[17:21]
    refs = refs[21:]
    if not first:
        dc_in, db_in, par_in = refs[:3]
        refs = refs[5:]
    dx_ref, dc_ref, db_ref, draw_ref, par_ref = refs[:5]
    sums, dc_sum, db_sum, terms = refs[5:9]
    if not first:
        dc_old, db_old, sems = refs[9:]
        old = [(dc_in, dc_old, sems.at[0]), (db_in, db_old, sems.at[1])]
    g = pl.program_id(0)
    heads = raw_ref.shape[1]
    length, width = xs_ref.shape
    states = b_ref.shape[1]
    blocks = length // GROUP
    piece = (begin + g) * half + part
    all_heads = columns_ref.shape[1] // 4
    member = head_matrix(heads, width).astype(BF16)
    lower = triangle(GROUP, True)
    rows = [slice(n * GROUP, (n + 1) * GROUP) for n in range(blocks)]

    @pl.when(g == 0)
    def _():
        if not first:
            for source, target, sem in old:
                pltpu.make_async_copy(source, target, sem).start()
        sums[...] = jnp.zeros_like(sums)
        dc_sum[...] = jnp.zeros_like(dc_sum)
        db_sum[...] = jnp.zeros_like(db_sum)
        par_ref[...] = jnp.zeros_like(par_ref) if first else par_in[...]

    own = begin + g == y_ref[0]
    early = jnp.where(own, held[0][...], held[2][...])
    late = jnp.where(own, held[1][...], held[3][...])
    state_early = y_ref[1] == 1
    state = jnp.where(state_early, early, late)
    grad = jnp.where(state_early, late, early)
    table = table_ref[...]
    skip = table[3 * blocks + 1 : 3 * blocks + 2]
    entering_low, ends = [], []
    for n in range(blocks):
        state = table[n : n + 1] * state
        entering_low.append(state.astype(BF16))
        state = state + dot(bt[:, rows[n]], xs_ref[rows[n], :], NN)
        ends.append(state)
    leaving_low, edges = [None] * blocks, [None] * blocks
    for n in reversed(range(blocks)):
        leaving_low[n] = grad.astype(BF16)
        edges[n] = jnp.sum(ends[n] * grad, axis=0, keepdims=True)
        grad = table[n : n + 1] * (grad + dot(ct[:, rows[n]], ys_ref[rows[n], :], NN))
    gain = dot(columns_ref[...], picker(piece, heads, all_heads, width, True), NN)
    for n in range(blocks):
        scaled_x, scaled_dy = xs_ref[rows[n], :], ys_ref[rows[n], :]
        forward = dot(left[n], scaled_x, NN) + dot(c_ref[rows[n], :], entering_low[n], NN)
        backward = dot(right[n], scaled_dy, NN) + dot(b_ref[rows[n], :], leaving_low[n], NN)
        weight = gain[rows[n]]
        dx_ref[rows[n], :] = (weight * backward + skip * dy_ref[rows[n], :].astype(F32)).astype(
            dx_ref.dtype
        )
        v = scaled_x.astype(F32) * backward
        difference = scaled_dy.astype(F32) * forward - v
        hi = difference.astype(BF16)
        lo = (difference - hi.astype(F32)).astype(BF16)
        terms[rows[n], :width] = hi
        terms[rows[n], width : 2 * width] = lo
        terms[rows[n], 2 * width :] = v.astype(BF16)
        sums[n] += dot(scaled_dy, scaled_x, NT)
        dc_sum[n] += dot(scaled_dy, entering_low[n], NT)
        db_sum[n] += dot(scaled_x, leaving_low[n], NT)
    added = dot(terms[...], adder[...], NN).T
    added = [added[:, rows[n]] for n in range(blocks)]
    edge = head_sums(jnp.concatenate(edges + [edges[0]] * (8 - blocks), axis=0), member)
    slopes = running(
        jnp.concatenate([a[:heads] for a in added], axis=0), lower.astype(BF16)
    )
    slope = jnp.concatenate(
        [slopes[n * heads : (n + 1) * heads] + edge[:, n : n + 1] for n in range(blocks)], axis=1
    )
    v = jnp.concatenate([a[heads : 2 * heads] for a in added], axis=1)
    raw = raw_ref[0] + column(bias_ref[...], piece, heads)
    step = softplus(raw)
    draw = (v / step - column(rate_ref[...], piece, heads) * slope) / (1.0 + jnp.exp(-raw))
    draw_ref[0] = draw
    values = (
        jnp.sum(draw, axis=1, keepdims=True),
        jnp.sum(head_sums(direct_ref[...], member), axis=1, keepdims=True),
        -jnp.sum(step * slope, axis=1, keepdims=True),
    )
    for k, value in enumerate(values):
        par_ref[k : k + 1] += lanes_of(value * scale, piece, (heads, par_ref.shape[1]))

    @pl.when(g == pl.num_programs(0) - 1)
    def _():
        if not first:
            for source, target, sem in old:
                pltpu.make_async_copy(source, target, sem).wait()
        for n in range(blocks):
            pair = jnp.where(lower, sums[n], 0.0).astype(BF16)
            dc = dot(pair, b_ref[rows[n], :], NN) + dc_sum[n]
            db = dot(pair, c_ref[rows[n], :], TN) + db_sum[n]
            if not first:
                dc = dc + dc_old[rows[n], :]
                db = db + db_old[rows[n], :]
            dc_ref[rows[n], :] = dc
            db_ref[rows[n], :] = db


def local_grads(part, begin, count, scale, y, saved, dy, b, c, vectors, held, before):
    xs, ys, direct, factor_columns, table, left, right, bt, ct = saved
    raw, bias, rate, _ = vectors
    length, channels = xs.shape
    pieces = 2 * PARTS
    heads = raw.shape[1] // pieces
    raw = raw.reshape(pieces, heads, length)
    width = channels // pieces
    states = b.shape[1]
    blocks = length // GROUP
    half = pieces // 2
    first = before is None
    whole = lambda g, y: (0, 0)
    place = lambda g, y: (0, (begin + g) * half + part)
    columns = pl.BlockSpec((length, width), place)
    maps = pl.BlockSpec((length, states), whole)
    line = pl.BlockSpec(bias.shape, whole)
    lines = pl.BlockSpec((1, heads, length), lambda g, y: ((begin + g) * half + part, 0, 0))
    params = pl.BlockSpec((8, 128), whole)
    anywhere = pl.BlockSpec(memory_space=pl.ANY)
    in_specs = [columns, columns, columns, pl.BlockSpec((8, width), place), maps, maps]
    in_specs += [
        pl.BlockSpec(factor_columns.shape, whole),
        pl.BlockSpec((table.shape[0], width), place),
    ]
    in_specs += [lines, line, line]
    args = [xs, ys, dy, direct, b, c, factor_columns, table, raw, bias, rate]
    fixed = [bt, ct, left, right, adding(width, heads, (0, 0, 1)), *held]
    in_specs += [pl.BlockSpec(a.shape, lambda g, y, n=len(a.shape): (0,) * n) for a in fixed]
    args += fixed
    aliases = {}
    if not first:
        dx, dc, db, draw, par = before
        args += [dc, db, par, dx, draw]
        in_specs += [anywhere, anywhere, params, anywhere, anywhere]
        aliases = {24: 0, 25: 3}
    grid_spec = pltpu.PrefetchScalarGridSpec(
        num_scalar_prefetch=1,
        grid=(count,),
        in_specs=in_specs,
        out_specs=[columns, maps, maps, lines, params],
        scratch_shapes=[
            pltpu.VMEM((blocks, GROUP, GROUP), F32),
            pltpu.VMEM((blocks, GROUP, states), F32),
            pltpu.VMEM((blocks, GROUP, states), F32),
            pltpu.VMEM((length, 3 * width), BF16),
        ]
        + [
            pltpu.VMEM((length, states), F32),
            pltpu.VMEM((length, states), F32),
            pltpu.SemaphoreType.DMA((2,)),
        ]
        * (not first),
    )
    return pl.pallas_call(
        functools.partial(grads_kernel, first, scale, part, half, begin),
        grid_spec=grid_spec,
        out_shape=[
            jax.ShapeDtypeStruct((length, channels), BF16),
            jax.ShapeDtypeStruct((length, states), F32),
            jax.ShapeDtypeStruct((length, states), F32),
            jax.ShapeDtypeStruct((pieces, heads, length), F32),
            jax.ShapeDtypeStruct((8, 128), F32),
        ],
        input_output_aliases=aliases,
        compiler_params=pltpu.CompilerParams(vmem_limit_bytes=SMALL_LIMIT),
        cost_estimate=pl.CostEstimate(
            flops=12 * count * length * width * (GROUP + states),
            bytes_accessed=6 * count * length * width,
            transcendentals=0,
        ),
        name="local_grads",
    )(y, *args)


def adding(width, heads, places):
    out = np.zeros((len(places) * width, 128), np.float32)
    size = width // heads
    for k, place in enumerate(places):
        for channel in range(width):
            out[k * width + channel, place * heads + channel // size] = 1.0
    return jnp.asarray(out, BF16)


def lanes_of(values, piece, shape):
    row = lax.broadcasted_iota(jnp.int32, shape, 0)
    col = lax.broadcasted_iota(jnp.int32, shape, 1)
    return jnp.sum(jnp.where(col == row + piece * shape[0], values, 0.0), axis=0, keepdims=True)


def summed_over(value, axis):
    size = lax.axis_size(axis)
    if size & (size - 1):
        return lax.psum(value, axis)
    bit = 1
    while bit < size:
        steps = (bit, 2 * bit, 3 * bit) if 4 * bit <= size else (bit,)
        got = [lax.ppermute(value, axis, [(i, i ^ s) for i in range(size)]) for s in steps]
        value = value + got[0]
        if len(got) == 3:
            value = value + (got[1] + got[2])
        bit *= 4 if len(got) == 3 else 2
    return value


def after(value, *earlier):
    return lax.optimization_barrier((value, *earlier))[0]


def entering(sent, kept, states, token):
    size = lax.axis_size("seq")
    pairs = size // 2
    index = lax.axis_index("seq")
    place, second = index // 2, index % 2 == 1
    swap = [(i, i ^ 1) for i in range(size)]
    both = lambda moves: [(2 * a + y, 2 * b + y) for a, b in moves for y in range(2)]

    def halves(got, copy):
        spans = ((0, states), (states, 2 * states), (2 * states + copy, 2 * states + copy + 1))
        for low, high in spans:
            own, other = kept[low:high], got[low:high]
            yield jnp.where(second, other, own), jnp.where(second, own, other)

    def message_of(up, got, arrived, copy):
        (l1, l2), (k1, k2), (d1, d2) = halves(got, copy)
        message = jnp.where(up, d2 * l1 + l2, k1 + d1 * k2)
        return message if arrived is None else message + d1 * d2 * arrived[:states]

    def shares(is_state, value, got, copy):
        (l1, _), (_, k2), (d1, d2) = halves(got, copy)
        for_first = jnp.where(is_state, value, k2 + d2 * value)
        for_second = jnp.where(is_state, d1 * value + l1, value)
        return jnp.where(second, for_second, for_first), jnp.where(second, for_first, for_second)

    message = sent if token is None else after(sent, *token)
    got = lax.ppermute(message, "seq", swap)
    token = yield message, got
    got = after(got, token)
    lower = place < pairs // 2
    start = end = None
    for k in range(1, pairs):
        last = start if k == 1 else arrived
        message = message_of(place == k - 1, got, last, 0)
        routes = both([(k - 1, k), (pairs - k, pairs - k - 1)])
        arriving = lax.ppermute(message, "seq", routes)
        if k == pairs // 2:
            known = jnp.where(lower, start, end)
            mine_early, early = shares(lower, known, got, 0)
            other_early = lax.ppermute(early, "seq", swap)
        token = yield message, arriving
        if k == pairs - 1:
            arrived, other_early, _ = lax.optimization_barrier((arriving, other_early, token))
        else:
            arrived = after(arriving, token)
        zero = jnp.zeros_like(arrived)
        start = jnp.where(place == k, arrived, zero if start is None else start)
        end = jnp.where(place == pairs - 1 - k, arrived, zero if end is None else end)
    mine_late, late = shares(~lower, jnp.where(lower, end, start), got, 0)
    other_late = lax.ppermute(late, "seq", swap)
    yield late, other_late
    yield mine_early, mine_late, other_early, other_late


def shards(inputs, input_map, output_map, step_raw, step_bias, decay_rate, skip_gain, cotangent):
    length = inputs.shape[1]
    heads = step_raw.shape[1]
    states = input_map.shape[2]
    x, b, c, dy = inputs[0], input_map[0], output_map[0], cotangent[0]
    vectors = (
        step_raw,
        step_bias.reshape(1, heads),
        decay_rate.reshape(1, heads),
        skip_gain.reshape(1, heads),
    )
    size = lax.axis_size("seq")
    y = lax.axis_index("seq") % 2
    scale = 1.0 / math.sqrt(length * size * lax.axis_size("batch"))

    def local(half, part, count, before):
        at = jnp.reshape(half * PARTS + part, (1,)).astype(jnp.int32)
        last = count == PARTS
        out, saved = local_states(at, count, last, x, dy, b, c, vectors, before)
        return out, saved[:3] + list(before[3:] if before else []) + saved[3:]

    sent, kept = [], []
    saved = None
    for part in range(PARTS):
        out, saved = local(1 - y, part, 1, saved)
        sent += out
    kept, saved = local(y, 0, PARTS, saved)

    transfers = size // 2 + 1
    order = [(0, 0), (1, 0)] + [
        pick for k in range(1, transfers) for pick in ((0, k), (1, k - 1)) if pick != (1, 0)
    ]
    order.append((1, transfers - 1))
    flows, token = {}, None
    lower = lax.axis_index("seq") < size // 2
    here = jnp.stack([y, lower.astype(y.dtype)]).astype(jnp.int32)
    found = None

    def grads(part, begin, count, token, held):
        *most, final = held
        held = (*most, after(final, token))
        return local_grads(
            part, begin, count, scale, here, saved, dy, b, c, vectors, held, found
        )

    for part, k in order:
        if (part, k) == (1, transfers - 1):
            held = next(flows[0])
            found = grads(0, 0, 1, token, held)
            token = found[-1]
        if k == 0:
            flows[part] = entering(sent[part], kept[part], states, token)
            message, arrived = next(flows[part])
            token = None if part == 0 else message
        else:
            token = flows[part].send(token)[0]
    found = grads(0, 1, 1, token, held)
    found = grads(1, 0, 2, found[-1], next(flows[1]))
    dx, dc, db, draw, params = found
    summed = summed_over(summed_over(params, "batch"), "seq")
    return (
        dx[None],
        db[None],
        dc[None],
        draw.reshape(heads, length)[None],
        summed[:2, :heads],
        summed[2, :heads],
    )


def solution(mesh):
    in_specs = (
        P("batch", "seq", None),
        P("batch", "seq", None),
        P("batch", "seq", None),
        P("batch", None, "seq"),
        P(),
        P(),
        P(),
        P("batch", "seq", None),
    )
    out_specs = (
        P("batch", "seq", None),
        P("batch", "seq", None),
        P("batch", "seq", None),
        P("batch", None, "seq"),
        P(),
        P(),
    )
    return jax.shard_map(shards, mesh=mesh, in_specs=in_specs, out_specs=out_specs, check_vma=False)
```

```python
import functools
import math

import jax
import jax.numpy as jnp
import numpy as np
from jax import lax
from jax.experimental import pallas as pl
from jax.experimental.pallas import tpu as pltpu
from jax.sharding import PartitionSpec as P

GROUP = 256
PARTS = 2
VMEM_LIMIT = 60 * 1024 * 1024
SMALL_LIMIT = 40 * 1024 * 1024
F32 = jnp.float32
BF16 = jnp.bfloat16


def dot(a, b, dims):
    return lax.dot_general(a, b, (dims, ((), ())), preferred_element_type=F32)


NN = ((1,), (0,))
NT = ((1,), (1,))
TN = ((0,), (0,))


def split2(a):
    hi = a.astype(BF16).astype(F32)
    return hi, a - hi


def head_matrix(heads, width):
    size = width // heads
    row = lax.broadcasted_iota(jnp.int32, (heads, width), 0)
    col = lax.broadcasted_iota(jnp.int32, (heads, width), 1)
    return ((col >= row * size) & (col < (row + 1) * size)).astype(F32)


def head_sums(values, member):
    hi, lo = split2(values)
    return dot(member, hi.astype(BF16), NT) + dot(member, lo.astype(BF16), NT)


def running(rows, upper):
    hi, rest = split2(rows)
    mid, lo = split2(rest)
    k = rows.shape[0]
    out = dot(jnp.concatenate([hi, mid, lo], axis=0).astype(BF16), upper, NN)
    return out[:k] + out[k : 2 * k] + out[2 * k :]


def triangle(width, lower):
    row = lax.broadcasted_iota(jnp.int32, (width, width), 0)
    col = lax.broadcasted_iota(jnp.int32, (width, width), 1)
    return (row >= col) if lower else (row <= col)


def softplus(v):
    return jnp.maximum(v, 0.0) + jnp.log1p(jnp.exp(-jnp.abs(v)))


def column(line, piece, heads):
    shape = (heads, line.shape[1])
    row = lax.broadcasted_iota(jnp.int32, shape, 0)
    col = lax.broadcasted_iota(jnp.int32, shape, 1)
    return jnp.sum(jnp.where(col == row + piece * heads, line, 0.0), axis=1, keepdims=True)


def block_sums(logs, blocks):
    heads = logs.shape[0]
    ones = triangle(GROUP, False).astype(BF16)
    stacked = jnp.concatenate([logs[:, n * GROUP : (n + 1) * GROUP] for n in range(blocks)], axis=0)
    cums = running(stacked, ones)
    return [cums[n * heads : (n + 1) * heads] for n in range(blocks)]


def factors(raw, bias, rate, skip, columns_ref, table_ref):
    heads, length = raw.shape
    width = table_ref.shape[1]
    blocks = length // GROUP
    step = softplus(raw + bias)
    cums = block_sums(-rate * step, blocks)
    totals = [cum[:, GROUP - 1 :] for cum in cums]
    before = [jnp.zeros((heads, 1), F32)]
    for total in totals:
        before.append(before[-1] + total)
    for n in range(blocks):
        rows = slice(n * GROUP, (n + 1) * GROUP)
        gain = split2(jnp.exp(totals[n] - cums[n]) * step[:, rows])
        lift = split2(jnp.exp(cums[n] - totals[n]))
        columns_ref[rows, :] = jnp.concatenate([*gain, *lift], axis=0).T.astype(BF16)
    whole = before[-1]
    lines = [jnp.exp(t) for t in totals]
    lines += [jnp.exp(whole - before[n + 1]) for n in range(blocks)]
    lines += [jnp.exp(before[n + 1]) for n in range(blocks)]
    lines += [jnp.exp(whole), skip]
    lines += [skip] * (-len(lines) % 8)
    hi, lo = split2(jnp.concatenate(lines, axis=1).T)
    member = head_matrix(heads, width).astype(BF16)
    table_ref[...] = dot(hi.astype(BF16), member, NN) + dot(lo.astype(BF16), member, NN)


def picker(piece, heads, all_heads, width, first):
    shape = (4 * all_heads, width)
    row = lax.broadcasted_iota(jnp.int32, shape, 0)
    col = lax.broadcasted_iota(jnp.int32, shape, 1)
    size = width // heads
    base = (0 if first else 2 * all_heads) + piece * heads
    hit = None
    for term in range(2):
        low = (row - (base + term * all_heads)) * size
        one = (col >= low) & (col < low + size)
        hit = one if hit is None else hit | one
    return hit.astype(BF16)


def local_kernel(first, last, count, *refs):
    at_ref, x_ref, dy_ref, b_ref, c_ref = refs[:5]
    if first:
        raw_ref, bias_ref, rate_ref, skip_ref = refs[5:9]
        outs = refs[9:-7]
        xs_ref, ys_ref, direct_ref, columns_ref, table_ref, bt, ct = refs[-7:]
    else:
        columns_ref, table_ref = refs[5:7]
        outs = refs[10 : 10 + count]
        xs_ref, ys_ref, direct_ref = refs[10 + count : 13 + count]
        if last:
            left, right, bt, ct = refs[13 + count :]
        else:
            bt, ct = refs[13 + count :]
    g = pl.program_id(0)
    length, width = x_ref.shape
    states = b_ref.shape[1]
    blocks = length // GROUP
    piece = at_ref[0] + g
    all_heads = columns_ref.shape[1] // 4
    heads = all_heads * width // table_ref.shape[1]

    @pl.when(g == 0)
    def _():
        bt[...] = b_ref[...].T
        ct[...] = c_ref[...].T
        if first:
            factors(
                raw_ref[0],
                column(bias_ref[...], 0, all_heads),
                column(rate_ref[...], 0, all_heads),
                column(skip_ref[...], 0, all_heads),
                columns_ref,
                table_ref,
            )
        if last:
            for n in range(blocks):
                rows = slice(n * GROUP, (n + 1) * GROUP)
                scores = dot(c_ref[rows, :], b_ref[rows, :], NT)
                left[n] = jnp.where(triangle(GROUP, True), scores, 0.0).astype(BF16)
                scores = dot(b_ref[rows, :], c_ref[rows, :], NT)
                right[n] = jnp.where(triangle(GROUP, False), scores, 0.0).astype(BF16)

    gain = dot(columns_ref[...], picker(piece, heads, all_heads, width, True), NN)
    lift = dot(columns_ref[...], picker(piece, heads, all_heads, width, False), NN)
    table = table_ref[:, pl.ds(pl.multiple_of(piece * width, width), width)]
    state = jnp.zeros((states, width), F32)
    grad = jnp.zeros((states, width), F32)
    direct = jnp.zeros((8, width), F32)
    for n in range(blocks):
        rows = slice(n * GROUP, (n + 1) * GROUP)
        x = x_ref[rows, :].astype(F32)
        dy = dy_ref[rows, :].astype(F32)
        direct = direct + jnp.sum((dy * x).reshape(GROUP // 8, 8, width), axis=0)
        scaled_x = (x * gain[rows]).astype(BF16)
        scaled_dy = (dy * lift[rows]).astype(BF16)
        xs_ref[rows, :] = scaled_x
        ys_ref[rows, :] = scaled_dy
        later = table[blocks + n : blocks + n + 1]
        earlier = table[2 * blocks + n : 2 * blocks + n + 1]
        state = state + later * dot(bt[:, rows], scaled_x, NN)
        grad = grad + earlier * dot(ct[:, rows], scaled_dy, NN)
    direct_ref[...] = direct
    decay = jnp.broadcast_to(table[3 * blocks : 3 * blocks + 1], (8, width))
    for k, out_ref in enumerate(outs):

        @pl.when(g == k)
        def _():
            out_ref[:states] = state
            out_ref[states : 2 * states] = grad
            out_ref[2 * states :] = decay


def local_states(at, count, last, x, dy, b, c, vectors, before):
    length, channels = x.shape
    states = b.shape[1]
    pieces = 2 * PARTS
    width = channels // pieces
    lines = 3 * (length // GROUP) + 2
    lines += -lines % 8
    first = before is None
    whole = lambda g, at: (0, 0)
    columns = pl.BlockSpec((length, width), lambda g, at: (0, at[0] + g))
    strip = pl.BlockSpec((8, width), lambda g, at: (0, at[0] + g))
    maps = pl.BlockSpec((length, states), whole)
    anywhere = pl.BlockSpec(memory_space=pl.ANY)
    in_specs = [columns, columns, maps, maps]
    out_specs = [pl.BlockSpec((2 * states + 8, width), whole)] * count + [columns, columns, strip]
    out_shape = [jax.ShapeDtypeStruct((2 * states + 8, width), F32)] * count + [
        jax.ShapeDtypeStruct((length, channels), BF16),
        jax.ShapeDtypeStruct((length, channels), BF16),
        jax.ShapeDtypeStruct((8, channels), F32),
    ]
    aliases = {}
    if first:
        raw, bias, rate, skip = vectors
        heads = raw.shape[1]
        args = [raw, bias, rate, skip]
        in_specs += [pl.BlockSpec(raw.shape, lambda g, at: (0, 0, 0))]
        in_specs += [pl.BlockSpec(bias.shape, whole)] * 3
        tables = [
            jax.ShapeDtypeStruct((length, 4 * heads), BF16),
            jax.ShapeDtypeStruct((lines, channels), F32),
        ]
        out_shape += tables
        out_specs += [pl.BlockSpec(t.shape, whole) for t in tables]
    else:
        xs, ys, direct, factor_columns, table = before
        args = [factor_columns, table, xs, ys, direct]
        in_specs += [pl.BlockSpec(factor_columns.shape, whole), pl.BlockSpec(table.shape, whole)]
        in_specs += [anywhere] * 3
        aliases = {7: count, 8: count + 1, 9: count + 2}
    scratch = [pltpu.VMEM((states, length), BF16)] * 2
    if last:
        blocks = length // GROUP
        extra = [jax.ShapeDtypeStruct((blocks, GROUP, GROUP), BF16)] * 2
        extra += [jax.ShapeDtypeStruct((states, length), BF16)] * 2
        out_shape += extra
        out_specs += [pl.BlockSpec(e.shape, lambda g, at, n=len(e.shape): (0,) * n) for e in extra]
        scratch = []
    grid_spec = pltpu.PrefetchScalarGridSpec(
        num_scalar_prefetch=1,
        grid=(count,),
        in_specs=in_specs,
        out_specs=out_specs,
        scratch_shapes=scratch,
    )
    out = pl.pallas_call(
        functools.partial(local_kernel, first, last, count),
        grid_spec=grid_spec,
        out_shape=out_shape,
        input_output_aliases=aliases,
        compiler_params=pltpu.CompilerParams(vmem_limit_bytes=VMEM_LIMIT),
        cost_estimate=pl.CostEstimate(
            flops=8 * count * length * width * states,
            bytes_accessed=8 * count * length * width,
            transcendentals=0,
        ),
        name="local_states",
    )(at, x, dy, b, c, *args)
    return out[:count], list(out[count:])


def pairs_kernel(xs_ref, ys_ref, b_ref, c_ref, dc_ref, db_ref):
    pair = jnp.where(triangle(GROUP, True), dot(ys_ref[...], xs_ref[...], NT), 0.0).astype(BF16)
    dc_ref[...] = dot(pair, b_ref[...], NN)
    db_ref[...] = dot(pair, c_ref[...], TN)


def pairs_grads(saved, b, c):
    xs, ys = saved[:2]
    length, channels = xs.shape
    states = b.shape[1]
    columns = pl.BlockSpec((GROUP, channels), lambda n: (n, 0))
    maps = pl.BlockSpec((GROUP, states), lambda n: (n, 0))
    return pl.pallas_call(
        pairs_kernel,
        grid=(length // GROUP,),
        in_specs=[columns, columns, maps, maps],
        out_specs=[maps, maps],
        out_shape=[jax.ShapeDtypeStruct((length, states), F32)] * 2,
        compiler_params=pltpu.CompilerParams(vmem_limit_bytes=VMEM_LIMIT),
        cost_estimate=pl.CostEstimate(
            flops=2 * length * GROUP * channels,
            bytes_accessed=4 * length * channels,
            transcendentals=0,
        ),
        name="pairs_grads",
    )(xs, ys, b, c)


def grads_kernel(first, scale, part, half, begin, *refs):
    y_ref, xs_ref, ys_ref, dy_ref, direct_ref, b_ref, c_ref, columns_ref, table_ref = refs[:9]
    raw_ref, bias_ref, rate_ref, bt, ct, left, right, adder = refs[9:17]
    held = refs[17:21]
    refs = refs[21:]
    dc_in, db_in = refs[:2]
    refs = refs[2:]
    if not first:
        par_in = refs[0]
        refs = refs[3:]
    dx_ref, dc_ref, db_ref, draw_ref, par_ref = refs[:5]
    dc_sum, db_sum, terms, dc_old, db_old, sems = refs[5:]
    old = [(dc_in, dc_old, sems.at[0]), (db_in, db_old, sems.at[1])]
    g = pl.program_id(0)
    heads = raw_ref.shape[1]
    length, width = xs_ref.shape
    states = b_ref.shape[1]
    blocks = length // GROUP
    piece = (begin + g) * half + part
    all_heads = columns_ref.shape[1] // 4
    member = head_matrix(heads, width).astype(BF16)
    lower = triangle(GROUP, True)
    rows = [slice(n * GROUP, (n + 1) * GROUP) for n in range(blocks)]

    @pl.when(g == 0)
    def _():
        for source, target, sem in old:
            pltpu.make_async_copy(source, target, sem).start()
        dc_sum[...] = jnp.zeros_like(dc_sum)
        db_sum[...] = jnp.zeros_like(db_sum)
        par_ref[...] = jnp.zeros_like(par_ref) if first else par_in[...]

    own = begin + g == y_ref[0]
    early = jnp.where(own, held[0][...], held[2][...])
    late = jnp.where(own, held[1][...], held[3][...])
    state_early = y_ref[1] == 1
    state = jnp.where(state_early, early, late)
    grad = jnp.where(state_early, late, early)
    table = table_ref[...]
    skip = table[3 * blocks + 1 : 3 * blocks + 2]
    entering_low, ends = [], []
    for n in range(blocks):
        state = table[n : n + 1] * state
        entering_low.append(state.astype(BF16))
        state = state + dot(bt[:, rows[n]], xs_ref[rows[n], :], NN)
        ends.append(state)
    leaving_low, edges = [None] * blocks, [None] * blocks
    for n in reversed(range(blocks)):
        leaving_low[n] = grad.astype(BF16)
        edges[n] = jnp.sum(ends[n] * grad, axis=0, keepdims=True)
        grad = table[n : n + 1] * (grad + dot(ct[:, rows[n]], ys_ref[rows[n], :], NN))
    gain = dot(columns_ref[...], picker(piece, heads, all_heads, width, True), NN)
    for n in range(blocks):
        scaled_x, scaled_dy = xs_ref[rows[n], :], ys_ref[rows[n], :]
        forward = dot(left[n], scaled_x, NN) + dot(c_ref[rows[n], :], entering_low[n], NN)
        backward = dot(right[n], scaled_dy, NN) + dot(b_ref[rows[n], :], leaving_low[n], NN)
        weight = gain[rows[n]]
        dx_ref[rows[n], :] = (weight * backward + skip * dy_ref[rows[n], :].astype(F32)).astype(
            dx_ref.dtype
        )
        v = scaled_x.astype(F32) * backward
        difference = scaled_dy.astype(F32) * forward - v
        hi = difference.astype(BF16)
        lo = (difference - hi.astype(F32)).astype(BF16)
        terms[rows[n], :width] = hi
        terms[rows[n], width : 2 * width] = lo
        terms[rows[n], 2 * width :] = v.astype(BF16)
        dc_sum[n] += dot(scaled_dy, entering_low[n], NT)
        db_sum[n] += dot(scaled_x, leaving_low[n], NT)
    added = dot(terms[...], adder[...], NN).T
    added = [added[:, rows[n]] for n in range(blocks)]
    edge = head_sums(jnp.concatenate(edges + [edges[0]] * (8 - blocks), axis=0), member)
    slopes = running(
        jnp.concatenate([a[:heads] for a in added], axis=0), lower.astype(BF16)
    )
    slope = jnp.concatenate(
        [slopes[n * heads : (n + 1) * heads] + edge[:, n : n + 1] for n in range(blocks)], axis=1
    )
    v = jnp.concatenate([a[heads : 2 * heads] for a in added], axis=1)
    raw = raw_ref[0] + column(bias_ref[...], piece, heads)
    step = softplus(raw)
    draw = (v / step - column(rate_ref[...], piece, heads) * slope) / (1.0 + jnp.exp(-raw))
    draw_ref[0] = draw
    values = (
        jnp.sum(draw, axis=1, keepdims=True),
        jnp.sum(head_sums(direct_ref[...], member), axis=1, keepdims=True),
        -jnp.sum(step * slope, axis=1, keepdims=True),
    )
    for k, value in enumerate(values):
        par_ref[k : k + 1] += lanes_of(value * scale, piece, (heads, par_ref.shape[1]))

    @pl.when(g == pl.num_programs(0) - 1)
    def _():
        for source, target, sem in old:
            pltpu.make_async_copy(source, target, sem).wait()
        for n in range(blocks):
            dc_ref[rows[n], :] = dc_old[rows[n], :] + dc_sum[n]
            db_ref[rows[n], :] = db_old[rows[n], :] + db_sum[n]


def local_grads(part, begin, count, scale, y, saved, dy, b, c, vectors, held, before):
    xs, ys, direct, factor_columns, table, left, right, bt, ct = saved
    raw, bias, rate, _ = vectors
    length, channels = xs.shape
    pieces = 2 * PARTS
    heads = raw.shape[1] // pieces
    raw = raw.reshape(pieces, heads, length)
    width = channels // pieces
    states = b.shape[1]
    blocks = length // GROUP
    half = pieces // 2
    first = before[0] is None
    whole = lambda g, y: (0, 0)
    place = lambda g, y: (0, (begin + g) * half + part)
    columns = pl.BlockSpec((length, width), place)
    maps = pl.BlockSpec((length, states), whole)
    line = pl.BlockSpec(bias.shape, whole)
    lines = pl.BlockSpec((1, heads, length), lambda g, y: ((begin + g) * half + part, 0, 0))
    params = pl.BlockSpec((8, 128), whole)
    anywhere = pl.BlockSpec(memory_space=pl.ANY)
    in_specs = [columns, columns, columns, pl.BlockSpec((8, width), place), maps, maps]
    in_specs += [
        pl.BlockSpec(factor_columns.shape, whole),
        pl.BlockSpec((table.shape[0], width), place),
    ]
    in_specs += [lines, line, line]
    args = [xs, ys, dy, direct, b, c, factor_columns, table, raw, bias, rate]
    fixed = [bt, ct, left, right, adding(width, heads, (0, 0, 1)), *held]
    in_specs += [pl.BlockSpec(a.shape, lambda g, y, n=len(a.shape): (0,) * n) for a in fixed]
    args += fixed
    aliases = {}
    dx, dc, db, draw, par = before
    args += [dc, db]
    in_specs += [anywhere, anywhere]
    if not first:
        args += [par, dx, draw]
        in_specs += [params, anywhere, anywhere]
        aliases = {24: 0, 25: 3}
    grid_spec = pltpu.PrefetchScalarGridSpec(
        num_scalar_prefetch=1,
        grid=(count,),
        in_specs=in_specs,
        out_specs=[columns, maps, maps, lines, params],
        scratch_shapes=[
            pltpu.VMEM((blocks, GROUP, states), F32),
            pltpu.VMEM((blocks, GROUP, states), F32),
            pltpu.VMEM((length, 3 * width), BF16),
            pltpu.VMEM((length, states), F32),
            pltpu.VMEM((length, states), F32),
            pltpu.SemaphoreType.DMA((2,)),
        ],
    )
    return pl.pallas_call(
        functools.partial(grads_kernel, first, scale, part, half, begin),
        grid_spec=grid_spec,
        out_shape=[
            jax.ShapeDtypeStruct((length, channels), BF16),
            jax.ShapeDtypeStruct((length, states), F32),
            jax.ShapeDtypeStruct((length, states), F32),
            jax.ShapeDtypeStruct((pieces, heads, length), F32),
            jax.ShapeDtypeStruct((8, 128), F32),
        ],
        input_output_aliases=aliases,
        compiler_params=pltpu.CompilerParams(vmem_limit_bytes=SMALL_LIMIT),
        cost_estimate=pl.CostEstimate(
            flops=12 * count * length * width * (GROUP + states),
            bytes_accessed=6 * count * length * width,
            transcendentals=0,
        ),
        name="local_grads",
    )(y, *args)


def adding(width, heads, places):
    out = np.zeros((len(places) * width, 128), np.float32)
    size = width // heads
    for k, place in enumerate(places):
        for channel in range(width):
            out[k * width + channel, place * heads + channel // size] = 1.0
    return jnp.asarray(out, BF16)


def lanes_of(values, piece, shape):
    row = lax.broadcasted_iota(jnp.int32, shape, 0)
    col = lax.broadcasted_iota(jnp.int32, shape, 1)
    return jnp.sum(jnp.where(col == row + piece * shape[0], values, 0.0), axis=0, keepdims=True)


def summed_over(value, axis):
    size = lax.axis_size(axis)
    if size & (size - 1):
        return lax.psum(value, axis)
    bit = 1
    while bit < size:
        steps = (bit, 2 * bit, 3 * bit) if 4 * bit <= size else (bit,)
        got = [lax.ppermute(value, axis, [(i, i ^ s) for i in range(size)]) for s in steps]
        value = value + got[0]
        if len(got) == 3:
            value = value + (got[1] + got[2])
        bit *= 4 if len(got) == 3 else 2
    return value


def after(value, *earlier):
    return lax.optimization_barrier((value, *earlier))[0]


def entering(sent, kept, states, token):
    size = lax.axis_size("seq")
    pairs = size // 2
    index = lax.axis_index("seq")
    place, second = index // 2, index % 2 == 1
    swap = [(i, i ^ 1) for i in range(size)]
    both = lambda moves: [(2 * a + y, 2 * b + y) for a, b in moves for y in range(2)]

    def halves(got, copy):
        spans = ((0, states), (states, 2 * states), (2 * states + copy, 2 * states + copy + 1))
        for low, high in spans:
            own, other = kept[low:high], got[low:high]
            yield jnp.where(second, other, own), jnp.where(second, own, other)

    def message_of(up, got, arrived, copy):
        (l1, l2), (k1, k2), (d1, d2) = halves(got, copy)
        message = jnp.where(up, d2 * l1 + l2, k1 + d1 * k2)
        return message if arrived is None else message + d1 * d2 * arrived[:states]

    def shares(is_state, value, got, copy):
        (l1, _), (_, k2), (d1, d2) = halves(got, copy)
        for_first = jnp.where(is_state, value, k2 + d2 * value)
        for_second = jnp.where(is_state, d1 * value + l1, value)
        return jnp.where(second, for_second, for_first), jnp.where(second, for_first, for_second)

    message = sent if token is None else after(sent, *token)
    got = lax.ppermute(message, "seq", swap)
    token = yield message, got
    got = after(got, token)
    lower = place < pairs // 2
    if pairs == 4:
        message = message_of((place == 0) | (place == 2), got, None, 0)
        (_, _), (_, _), (d1, d2) = halves(got, 0)
        message = jnp.concatenate([message, jnp.broadcast_to(d1 * d2, (8, message.shape[1]))])
        near = lax.ppermute(message, "seq", both([(0, 1), (1, 0), (2, 3), (3, 2)]))
        token = yield message, near
        near = after(near, token)
        message = message_of(place == 1, got, near, 1)
        middle = lax.ppermute(message, "seq", both([(1, 2), (2, 1)]))
        far = lax.ppermute(message, "seq", both([(1, 3), (2, 0)]))
        inside = (place == 1) | (place == 2)
        known = jnp.where(inside, near[:states], 0.0)
        mine_early, early = shares(lower, known, got, 2)
        other_early = lax.ppermute(early, "seq", swap)
        token = yield early, far
        far = after(far, token)
        outer = near[states : states + 1] * far + near[:states]
        mine_late, late = shares(~lower, jnp.where(inside, middle, outer), got, 3)
        other_late = lax.ppermute(late, "seq", swap)
        yield late, other_late
    else:
        arrived = []
        for k in range(1, pairs):
            message = message_of(place == k - 1, got, arrived[-1] if arrived else None, min(k, 4))
            routes = both([(k - 1, k), (pairs - k, pairs - k - 1)])
            arrived.append(lax.ppermute(message, "seq", routes))
            token = yield message, arrived[-1]
            arrived[-1] = after(arrived[-1], token)
        start = end = jnp.zeros_like(arrived[0])
        for k in range(1, pairs):
            start = jnp.where(place == k, arrived[k - 1], start)
            end = jnp.where(place == pairs - 1 - k, arrived[k - 1], end)
        mine_early, early = shares(lower, jnp.where(lower, start, end), got, 5)
        mine_late, late = shares(~lower, jnp.where(lower, end, start), got, 6)
        other_early = lax.ppermute(early, "seq", swap)
        other_late = lax.ppermute(late, "seq", swap)
        yield late, other_late
    yield mine_early, mine_late, other_early, other_late


def shards(inputs, input_map, output_map, step_raw, step_bias, decay_rate, skip_gain, cotangent):
    length = inputs.shape[1]
    heads = step_raw.shape[1]
    states = input_map.shape[2]
    x, b, c, dy = inputs[0], input_map[0], output_map[0], cotangent[0]
    vectors = (
        step_raw,
        step_bias.reshape(1, heads),
        decay_rate.reshape(1, heads),
        skip_gain.reshape(1, heads),
    )
    size = lax.axis_size("seq")
    y = lax.axis_index("seq") % 2
    scale = 1.0 / math.sqrt(length * size * lax.axis_size("batch"))

    def local(half, part, count, before):
        at = jnp.reshape(half * PARTS + part, (1,)).astype(jnp.int32)
        last = count == PARTS
        out, saved = local_states(at, count, last, x, dy, b, c, vectors, before)
        return out, saved[:3] + list(before[3:] if before else []) + saved[3:]

    sent, kept = [], []
    saved = None
    for part in range(PARTS):
        out, saved = local(1 - y, part, 1, saved)
        sent += out
    kept, saved = local(y, 0, PARTS, saved)

    transfers = 4 if size == 8 else size // 2 + 1
    order = [(0, 0), (1, 0)] + [
        pick for k in range(1, transfers) for pick in ((0, k), (1, k - 1)) if pick != (1, 0)
    ]
    order.append((1, transfers - 1))
    flows, token = {}, None
    lower = lax.axis_index("seq") < size // 2
    here = jnp.stack([y, lower.astype(y.dtype)]).astype(jnp.int32)
    found = None

    def grads(part, begin, count, token, held):
        *most, final = held
        held = (*most, after(final, token))
        return local_grads(
            part, begin, count, scale, here, saved, dy, b, c, vectors, held, found
        )

    for part, k in order:
        if (part, k) == (1, transfers - 1):
            held = next(flows[0])
            found = grads(0, 0, 1, token, held)
            token = found[-1]
        if k == 0:
            flows[part] = entering(sent[part], kept[part], states, token)
            message, arrived = next(flows[part])
            token = None if part == 0 else message
        else:
            token = flows[part].send(token)[0]
        if (part, k) == (0, 1):
            dc, db = pairs_grads(saved, after(b, token), c)
            token = dc
            found = (None, dc, db, None, None)
    found = grads(0, 1, 1, token, held)
    found = grads(1, 0, 2, found[-1], next(flows[1]))
    dx, dc, db, draw, params = found
    summed = summed_over(summed_over(params, "batch"), "seq")
    return (
        dx[None],
        db[None],
        dc[None],
        draw.reshape(heads, length)[None],
        summed[:2, :heads],
        summed[2, :heads],
    )


def solution(mesh):
    in_specs = (
        P("batch", "seq", None),
        P("batch", "seq", None),
        P("batch", "seq", None),
        P("batch", None, "seq"),
        P(),
        P(),
        P(),
        P("batch", "seq", None),
    )
    out_specs = (
        P("batch", "seq", None),
        P("batch", "seq", None),
        P("batch", "seq", None),
        P("batch", None, "seq"),
        P(),
        P(),
    )
    return jax.shard_map(shards, mesh=mesh, in_specs=in_specs, out_specs=out_specs, check_vma=False)
```

```python
import functools
import math

import jax
import jax.numpy as jnp
import numpy as np
from jax import lax
from jax.experimental import pallas as pl
from jax.experimental.pallas import tpu as pltpu
from jax.sharding import PartitionSpec as P

GROUP = 256
PARTS = 2
VMEM_LIMIT = 60 * 1024 * 1024
SMALL_LIMIT = 40 * 1024 * 1024
F32 = jnp.float32
BF16 = jnp.bfloat16


def dot(a, b, dims):
    return lax.dot_general(a, b, (dims, ((), ())), preferred_element_type=F32)


NN = ((1,), (0,))
NT = ((1,), (1,))
TN = ((0,), (0,))


def split2(a):
    hi = a.astype(BF16).astype(F32)
    return hi, a - hi


def head_matrix(heads, width):
    size = width // heads
    row = lax.broadcasted_iota(jnp.int32, (heads, width), 0)
    col = lax.broadcasted_iota(jnp.int32, (heads, width), 1)
    return ((col >= row * size) & (col < (row + 1) * size)).astype(F32)


def head_sums(values, member):
    hi, lo = split2(values)
    return dot(member, hi.astype(BF16), NT) + dot(member, lo.astype(BF16), NT)


def running(rows, upper):
    hi, rest = split2(rows)
    mid, lo = split2(rest)
    k = rows.shape[0]
    out = dot(jnp.concatenate([hi, mid, lo], axis=0).astype(BF16), upper, NN)
    return out[:k] + out[k : 2 * k] + out[2 * k :]


def triangle(width, lower):
    row = lax.broadcasted_iota(jnp.int32, (width, width), 0)
    col = lax.broadcasted_iota(jnp.int32, (width, width), 1)
    return (row >= col) if lower else (row <= col)


def softplus(v):
    return jnp.maximum(v, 0.0) + jnp.log1p(jnp.exp(-jnp.abs(v)))


def column(line, piece, heads):
    shape = (heads, line.shape[1])
    row = lax.broadcasted_iota(jnp.int32, shape, 0)
    col = lax.broadcasted_iota(jnp.int32, shape, 1)
    return jnp.sum(jnp.where(col == row + piece * heads, line, 0.0), axis=1, keepdims=True)


def block_sums(logs, blocks):
    heads = logs.shape[0]
    ones = triangle(GROUP, False).astype(BF16)
    stacked = jnp.concatenate([logs[:, n * GROUP : (n + 1) * GROUP] for n in range(blocks)], axis=0)
    cums = running(stacked, ones)
    return [cums[n * heads : (n + 1) * heads] for n in range(blocks)]


def factors(raw, bias, rate, skip, columns_ref, table_ref):
    heads, length = raw.shape
    width = table_ref.shape[1]
    blocks = length // GROUP
    step = softplus(raw + bias)
    cums = block_sums(-rate * step, blocks)
    totals = [cum[:, GROUP - 1 :] for cum in cums]
    before = [jnp.zeros((heads, 1), F32)]
    for total in totals:
        before.append(before[-1] + total)
    for n in range(blocks):
        rows = slice(n * GROUP, (n + 1) * GROUP)
        gain = split2(jnp.exp(totals[n] - cums[n]) * step[:, rows])
        lift = split2(jnp.exp(cums[n] - totals[n]))
        columns_ref[rows, :] = jnp.concatenate([*gain, *lift], axis=0).T.astype(BF16)
    whole = before[-1]
    lines = [jnp.exp(t) for t in totals]
    lines += [jnp.exp(whole - before[n + 1]) for n in range(blocks)]
    lines += [jnp.exp(before[n + 1]) for n in range(blocks)]
    lines += [jnp.exp(whole), skip]
    lines += [skip] * (-len(lines) % 8)
    hi, lo = split2(jnp.concatenate(lines, axis=1).T)
    member = head_matrix(heads, width).astype(BF16)
    table_ref[...] = dot(hi.astype(BF16), member, NN) + dot(lo.astype(BF16), member, NN)


def picker(piece, heads, all_heads, width, first):
    shape = (4 * all_heads, width)
    row = lax.broadcasted_iota(jnp.int32, shape, 0)
    col = lax.broadcasted_iota(jnp.int32, shape, 1)
    size = width // heads
    base = (0 if first else 2 * all_heads) + piece * heads
    hit = None
    for term in range(2):
        low = (row - (base + term * all_heads)) * size
        one = (col >= low) & (col < low + size)
        hit = one if hit is None else hit | one
    return hit.astype(BF16)


def local_kernel(first, last, count, *refs):
    at_ref, x_ref, dy_ref, b_ref, c_ref = refs[:5]
    if first:
        raw_ref, bias_ref, rate_ref, skip_ref = refs[5:9]
        outs = refs[9:-7]
        xs_ref, ys_ref, direct_ref, columns_ref, table_ref, bt, ct = refs[-7:]
    else:
        columns_ref, table_ref = refs[5:7]
        outs = refs[10 : 10 + count]
        xs_ref, ys_ref, direct_ref = refs[10 + count : 13 + count]
        if last:
            left, right, bt, ct = refs[13 + count :]
        else:
            bt, ct = refs[13 + count :]
    g = pl.program_id(0)
    length, width = x_ref.shape
    states = b_ref.shape[1]
    blocks = length // GROUP
    piece = at_ref[0] + g
    all_heads = columns_ref.shape[1] // 4
    heads = all_heads * width // table_ref.shape[1]

    @pl.when(g == 0)
    def _():
        bt[...] = b_ref[...].T
        ct[...] = c_ref[...].T
        if first:
            factors(
                raw_ref[0],
                column(bias_ref[...], 0, all_heads),
                column(rate_ref[...], 0, all_heads),
                column(skip_ref[...], 0, all_heads),
                columns_ref,
                table_ref,
            )
        if last:
            for n in range(blocks):
                rows = slice(n * GROUP, (n + 1) * GROUP)
                scores = dot(c_ref[rows, :], b_ref[rows, :], NT)
                left[n] = jnp.where(triangle(GROUP, True), scores, 0.0).astype(BF16)
                scores = dot(b_ref[rows, :], c_ref[rows, :], NT)
                right[n] = jnp.where(triangle(GROUP, False), scores, 0.0).astype(BF16)

    gain = dot(columns_ref[...], picker(piece, heads, all_heads, width, True), NN)
    lift = dot(columns_ref[...], picker(piece, heads, all_heads, width, False), NN)
    table = table_ref[:, pl.ds(pl.multiple_of(piece * width, width), width)]
    state = jnp.zeros((states, width), F32)
    grad = jnp.zeros((states, width), F32)
    direct = jnp.zeros((8, width), F32)
    for n in range(blocks):
        rows = slice(n * GROUP, (n + 1) * GROUP)
        x = x_ref[rows, :].astype(F32)
        dy = dy_ref[rows, :].astype(F32)
        direct = direct + jnp.sum((dy * x).reshape(GROUP // 8, 8, width), axis=0)
        scaled_x = (x * gain[rows]).astype(BF16)
        scaled_dy = (dy * lift[rows]).astype(BF16)
        xs_ref[rows, :] = scaled_x
        ys_ref[rows, :] = scaled_dy
        later = table[blocks + n : blocks + n + 1]
        earlier = table[2 * blocks + n : 2 * blocks + n + 1]
        state = state + later * dot(bt[:, rows], scaled_x, NN)
        grad = grad + earlier * dot(ct[:, rows], scaled_dy, NN)
    direct_ref[...] = direct
    decay = jnp.broadcast_to(table[3 * blocks : 3 * blocks + 1], (8, width))
    for k, out_ref in enumerate(outs):

        @pl.when(g == k)
        def _():
            out_ref[:states] = state
            out_ref[states : 2 * states] = grad
            out_ref[2 * states :] = decay


def local_states(at, count, last, x, dy, b, c, vectors, before):
    length, channels = x.shape
    states = b.shape[1]
    pieces = 2 * PARTS
    width = channels // pieces
    lines = 3 * (length // GROUP) + 2
    lines += -lines % 8
    first = before is None
    whole = lambda g, at: (0, 0)
    columns = pl.BlockSpec((length, width), lambda g, at: (0, at[0] + g))
    strip = pl.BlockSpec((8, width), lambda g, at: (0, at[0] + g))
    maps = pl.BlockSpec((length, states), whole)
    anywhere = pl.BlockSpec(memory_space=pl.ANY)
    in_specs = [columns, columns, maps, maps]
    out_specs = [pl.BlockSpec((2 * states + 8, width), whole)] * count + [columns, columns, strip]
    out_shape = [jax.ShapeDtypeStruct((2 * states + 8, width), F32)] * count + [
        jax.ShapeDtypeStruct((length, channels), BF16),
        jax.ShapeDtypeStruct((length, channels), BF16),
        jax.ShapeDtypeStruct((8, channels), F32),
    ]
    aliases = {}
    if first:
        raw, bias, rate, skip = vectors
        heads = raw.shape[1]
        args = [raw, bias, rate, skip]
        in_specs += [pl.BlockSpec(raw.shape, lambda g, at: (0, 0, 0))]
        in_specs += [pl.BlockSpec(bias.shape, whole)] * 3
        tables = [
            jax.ShapeDtypeStruct((length, 4 * heads), BF16),
            jax.ShapeDtypeStruct((lines, channels), F32),
        ]
        out_shape += tables
        out_specs += [pl.BlockSpec(t.shape, whole) for t in tables]
    else:
        xs, ys, direct, factor_columns, table = before
        args = [factor_columns, table, xs, ys, direct]
        in_specs += [pl.BlockSpec(factor_columns.shape, whole), pl.BlockSpec(table.shape, whole)]
        in_specs += [anywhere] * 3
        aliases = {7: count, 8: count + 1, 9: count + 2}
    scratch = [pltpu.VMEM((states, length), BF16)] * 2
    if last:
        blocks = length // GROUP
        extra = [jax.ShapeDtypeStruct((blocks, GROUP, GROUP), BF16)] * 2
        extra += [jax.ShapeDtypeStruct((states, length), BF16)] * 2
        out_shape += extra
        out_specs += [pl.BlockSpec(e.shape, lambda g, at, n=len(e.shape): (0,) * n) for e in extra]
        scratch = []
    grid_spec = pltpu.PrefetchScalarGridSpec(
        num_scalar_prefetch=1,
        grid=(count,),
        in_specs=in_specs,
        out_specs=out_specs,
        scratch_shapes=scratch,
    )
    out = pl.pallas_call(
        functools.partial(local_kernel, first, last, count),
        grid_spec=grid_spec,
        out_shape=out_shape,
        input_output_aliases=aliases,
        compiler_params=pltpu.CompilerParams(vmem_limit_bytes=VMEM_LIMIT),
        cost_estimate=pl.CostEstimate(
            flops=8 * count * length * width * states,
            bytes_accessed=8 * count * length * width,
            transcendentals=0,
        ),
        name="local_states",
    )(at, x, dy, b, c, *args)
    return out[:count], list(out[count:])


def pairs_kernel(xs_ref, ys_ref, b_ref, c_ref, dc_ref, db_ref):
    pair = jnp.where(triangle(GROUP, True), dot(ys_ref[...], xs_ref[...], NT), 0.0).astype(BF16)
    dc_ref[...] = dot(pair, b_ref[...], NN)
    db_ref[...] = dot(pair, c_ref[...], TN)


def pairs_grads(saved, b, c):
    xs, ys = saved[:2]
    length, channels = xs.shape
    states = b.shape[1]
    columns = pl.BlockSpec((GROUP, channels), lambda n: (n, 0))
    maps = pl.BlockSpec((GROUP, states), lambda n: (n, 0))
    return pl.pallas_call(
        pairs_kernel,
        grid=(length // GROUP,),
        in_specs=[columns, columns, maps, maps],
        out_specs=[maps, maps],
        out_shape=[jax.ShapeDtypeStruct((length, states), F32)] * 2,
        compiler_params=pltpu.CompilerParams(vmem_limit_bytes=VMEM_LIMIT),
        cost_estimate=pl.CostEstimate(
            flops=2 * length * GROUP * channels,
            bytes_accessed=4 * length * channels,
            transcendentals=0,
        ),
        name="pairs_grads",
    )(xs, ys, b, c)


def grads_kernel(first, part, half, begin, heads, *refs):
    y_ref, xs_ref, ys_ref, dy_ref, b_ref, c_ref, columns_ref, table_ref = refs[:8]
    bt, ct, left, right, adder = refs[8:13]
    held = refs[13:17]
    dc_in, db_in = refs[17:19]
    refs = refs[19:] if first else refs[21:]
    dx_ref, dc_ref, db_ref, sums_ref = refs[:4]
    dc_sum, db_sum, terms, dc_old, db_old, sems = refs[4:]
    old = [(dc_in, dc_old, sems.at[0]), (db_in, db_old, sems.at[1])]
    g = pl.program_id(0)
    length, width = xs_ref.shape
    states = b_ref.shape[1]
    blocks = length // GROUP
    piece = (begin + g) * half + part
    all_heads = columns_ref.shape[1] // 4
    member = head_matrix(heads, width).astype(BF16)
    lower = triangle(GROUP, True)
    rows = [slice(n * GROUP, (n + 1) * GROUP) for n in range(blocks)]

    @pl.when(g == 0)
    def _():
        for source, target, sem in old:
            pltpu.make_async_copy(source, target, sem).start()
        dc_sum[...] = jnp.zeros_like(dc_sum)
        db_sum[...] = jnp.zeros_like(db_sum)

    own = begin + g == y_ref[0]
    early = jnp.where(own, held[0][...], held[2][...])
    late = jnp.where(own, held[1][...], held[3][...])
    state_early = y_ref[1] == 1
    state = jnp.where(state_early, early, late)
    grad = jnp.where(state_early, late, early)
    table = table_ref[...]
    skip = table[3 * blocks + 1 : 3 * blocks + 2]
    entering_low, ends = [], []
    for n in range(blocks):
        state = table[n : n + 1] * state
        entering_low.append(state.astype(BF16))
        state = state + dot(bt[:, rows[n]], xs_ref[rows[n], :], NN)
        ends.append(state)
    leaving_low, edges = [None] * blocks, [None] * blocks
    for n in reversed(range(blocks)):
        leaving_low[n] = grad.astype(BF16)
        edges[n] = jnp.sum(ends[n] * grad, axis=0, keepdims=True)
        grad = table[n : n + 1] * (grad + dot(ct[:, rows[n]], ys_ref[rows[n], :], NN))
    gain = dot(columns_ref[...], picker(piece, heads, all_heads, width, True), NN)
    for n in range(blocks):
        scaled_x, scaled_dy = xs_ref[rows[n], :], ys_ref[rows[n], :]
        forward = dot(left[n], scaled_x, NN) + dot(c_ref[rows[n], :], entering_low[n], NN)
        backward = dot(right[n], scaled_dy, NN) + dot(b_ref[rows[n], :], leaving_low[n], NN)
        weight = gain[rows[n]]
        dx_ref[rows[n], :] = (weight * backward + skip * dy_ref[rows[n], :].astype(F32)).astype(
            dx_ref.dtype
        )
        v = scaled_x.astype(F32) * backward
        difference = scaled_dy.astype(F32) * forward - v
        hi = difference.astype(BF16)
        lo = (difference - hi.astype(F32)).astype(BF16)
        terms[rows[n], :width] = hi
        terms[rows[n], width : 2 * width] = lo
        terms[rows[n], 2 * width :] = v.astype(BF16)
        dc_sum[n] += dot(scaled_dy, entering_low[n], NT)
        db_sum[n] += dot(scaled_x, leaving_low[n], NT)
    added = dot(terms[...], adder[...], NN).T
    sums_ref[0, : 2 * heads] = added[: 2 * heads]
    edge = head_sums(jnp.concatenate(edges + [edges[0]] * (8 - blocks), axis=0), member)
    sums_ref[0, 2 * heads :, :8] = edge

    @pl.when(g == pl.num_programs(0) - 1)
    def _():
        for source, target, sem in old:
            pltpu.make_async_copy(source, target, sem).wait()
        for n in range(blocks):
            dc_ref[rows[n], :] = dc_old[rows[n], :] + dc_sum[n]
            db_ref[rows[n], :] = db_old[rows[n], :] + db_sum[n]


def local_grads(part, begin, count, heads, y, saved, dy, b, c, held, before):
    xs, ys, direct, factor_columns, table, left, right, bt, ct = saved
    length, channels = xs.shape
    pieces = 2 * PARTS
    width = channels // pieces
    states = b.shape[1]
    blocks = length // GROUP
    half = pieces // 2
    first = before[0] is None
    whole = lambda g, y: (0, 0)
    place = lambda g, y: (0, (begin + g) * half + part)
    columns = pl.BlockSpec((length, width), place)
    maps = pl.BlockSpec((length, states), whole)
    lines = pl.BlockSpec((1, 3 * heads, length), lambda g, y: ((begin + g) * half + part, 0, 0))
    anywhere = pl.BlockSpec(memory_space=pl.ANY)
    in_specs = [columns, columns, columns, maps, maps]
    in_specs += [
        pl.BlockSpec(factor_columns.shape, whole),
        pl.BlockSpec((table.shape[0], width), place),
    ]
    args = [xs, ys, dy, b, c, factor_columns, table]
    fixed = [bt, ct, left, right, adding(width, heads, (0, 0, 1)), *held]
    in_specs += [pl.BlockSpec(a.shape, lambda g, y, n=len(a.shape): (0,) * n) for a in fixed]
    args += fixed
    aliases = {}
    dx, dc, db, sums = before
    args += [dc, db]
    in_specs += [anywhere, anywhere]
    if not first:
        args += [dx, sums]
        in_specs += [anywhere, anywhere]
        aliases = {19: 0, 20: 3}
    grid_spec = pltpu.PrefetchScalarGridSpec(
        num_scalar_prefetch=1,
        grid=(count,),
        in_specs=in_specs,
        out_specs=[columns, maps, maps, lines],
        scratch_shapes=[
            pltpu.VMEM((blocks, GROUP, states), F32),
            pltpu.VMEM((blocks, GROUP, states), F32),
            pltpu.VMEM((length, 3 * width), BF16),
            pltpu.VMEM((length, states), F32),
            pltpu.VMEM((length, states), F32),
            pltpu.SemaphoreType.DMA((2,)),
        ],
    )
    return pl.pallas_call(
        functools.partial(grads_kernel, first, part, half, begin, heads),
        grid_spec=grid_spec,
        out_shape=[
            jax.ShapeDtypeStruct((length, channels), BF16),
            jax.ShapeDtypeStruct((length, states), F32),
            jax.ShapeDtypeStruct((length, states), F32),
            jax.ShapeDtypeStruct((pieces, 3 * heads, length), F32),
        ],
        input_output_aliases=aliases,
        compiler_params=pltpu.CompilerParams(vmem_limit_bytes=SMALL_LIMIT),
        cost_estimate=pl.CostEstimate(
            flops=12 * count * length * width * (GROUP + states),
            bytes_accessed=6 * count * length * width,
            transcendentals=0,
        ),
        name="local_grads",
    )(y, *args)


def steps_kernel(scale, sums_ref, raw_ref, bias_ref, rate_ref, direct_ref, draw_ref, par_ref):
    pieces, heads, length = draw_ref.shape
    all_heads = pieces * heads
    blocks = length // GROUP
    rows = [slice(n * GROUP, (n + 1) * GROUP) for n in range(blocks)]
    stacked = [sums_ref[p, :heads, rows[n]] for p in range(pieces) for n in range(blocks)]
    slopes = running(jnp.concatenate(stacked, axis=0), triangle(GROUP, True).astype(BF16))
    lines = []
    for p in range(pieces):
        edge = sums_ref[p, 2 * heads :, :8]
        at = [(p * blocks + n) * heads for n in range(blocks)]
        parts = [slopes[at[n] : at[n] + heads] + edge[:, n : n + 1] for n in range(blocks)]
        lines.append(jnp.concatenate(parts, axis=1))
    slope = jnp.concatenate(lines, axis=0)
    v = jnp.concatenate([sums_ref[p, heads : 2 * heads] for p in range(pieces)], axis=0)
    raw = raw_ref[0] + column(bias_ref[...], 0, all_heads)
    step = softplus(raw)
    draw = (v / step - column(rate_ref[...], 0, all_heads) * slope) / (1.0 + jnp.exp(-raw))
    for p in range(pieces):
        draw_ref[p] = draw[p * heads : (p + 1) * heads]
    member = head_matrix(all_heads, direct_ref.shape[1]).astype(BF16)
    values = (
        jnp.sum(draw, axis=1, keepdims=True),
        jnp.sum(head_sums(direct_ref[...], member), axis=1, keepdims=True),
        -jnp.sum(step * slope, axis=1, keepdims=True),
    )
    par_ref[...] = jnp.zeros_like(par_ref)
    for k, value in enumerate(values):
        par_ref[k : k + 1] = lanes_of(value * scale, 0, (all_heads, par_ref.shape[1]))


def steps_grads(scale, sums, vectors, direct):
    raw, bias, rate, _ = vectors
    pieces, rows, length = sums.shape
    return pl.pallas_call(
        functools.partial(steps_kernel, scale),
        out_shape=[
            jax.ShapeDtypeStruct((pieces, rows // 3, length), F32),
            jax.ShapeDtypeStruct((8, 128), F32),
        ],
        compiler_params=pltpu.CompilerParams(vmem_limit_bytes=SMALL_LIMIT),
        cost_estimate=pl.CostEstimate(
            flops=1000 * length * pieces, bytes_accessed=8 * sums.size, transcendentals=0
        ),
        name="steps_grads",
    )(sums, raw, bias, rate, direct)


def adding(width, heads, places):
    out = np.zeros((len(places) * width, 128), np.float32)
    size = width // heads
    for k, place in enumerate(places):
        for channel in range(width):
            out[k * width + channel, place * heads + channel // size] = 1.0
    return jnp.asarray(out, BF16)


def lanes_of(values, piece, shape):
    row = lax.broadcasted_iota(jnp.int32, shape, 0)
    col = lax.broadcasted_iota(jnp.int32, shape, 1)
    return jnp.sum(jnp.where(col == row + piece * shape[0], values, 0.0), axis=0, keepdims=True)


def summed_over(value, axis):
    size = lax.axis_size(axis)
    if size & (size - 1):
        return lax.psum(value, axis)
    bit = 1
    while bit < size:
        steps = (bit, 2 * bit, 3 * bit) if 4 * bit <= size else (bit,)
        got = [lax.ppermute(value, axis, [(i, i ^ s) for i in range(size)]) for s in steps]
        value = value + got[0]
        if len(got) == 3:
            value = value + (got[1] + got[2])
        bit *= 4 if len(got) == 3 else 2
    return value


def after(value, *earlier):
    return lax.optimization_barrier((value, *earlier))[0]


def entering(sent, kept, states, token):
    size = lax.axis_size("seq")
    pairs = size // 2
    index = lax.axis_index("seq")
    place, second = index // 2, index % 2 == 1
    swap = [(i, i ^ 1) for i in range(size)]
    both = lambda moves: [(2 * a + y, 2 * b + y) for a, b in moves for y in range(2)]

    def halves(got, copy):
        spans = ((0, states), (states, 2 * states), (2 * states + copy, 2 * states + copy + 1))
        for low, high in spans:
            own, other = kept[low:high], got[low:high]
            yield jnp.where(second, other, own), jnp.where(second, own, other)

    def message_of(up, got, arrived, copy):
        (l1, l2), (k1, k2), (d1, d2) = halves(got, copy)
        message = jnp.where(up, d2 * l1 + l2, k1 + d1 * k2)
        return message if arrived is None else message + d1 * d2 * arrived[:states]

    def shares(is_state, value, got, copy):
        (l1, _), (_, k2), (d1, d2) = halves(got, copy)
        for_first = jnp.where(is_state, value, k2 + d2 * value)
        for_second = jnp.where(is_state, d1 * value + l1, value)
        return jnp.where(second, for_second, for_first), jnp.where(second, for_first, for_second)

    message = sent if token is None else after(sent, *token)
    got = lax.ppermute(message, "seq", swap)
    token = yield message, got
    got = after(got, token)
    lower = place < pairs // 2
    if pairs == 4:
        message = message_of((place == 0) | (place == 2), got, None, 0)
        (_, _), (_, _), (d1, d2) = halves(got, 0)
        message = jnp.concatenate([message, jnp.broadcast_to(d1 * d2, (8, message.shape[1]))])
        near = lax.ppermute(message, "seq", both([(0, 1), (1, 0), (2, 3), (3, 2)]))
        token = yield message, near
        near = after(near, token)
        message = message_of(place == 1, got, near, 1)
        middle = lax.ppermute(message, "seq", both([(1, 2), (2, 1)]))
        far = lax.ppermute(message, "seq", both([(1, 3), (2, 0)]))
        inside = (place == 1) | (place == 2)
        known = jnp.where(inside, near[:states], 0.0)
        mine_early, early = shares(lower, known, got, 2)
        other_early = lax.ppermute(early, "seq", swap)
        token = yield early, far
        far = after(far, token)
        outer = near[states : states + 1] * far + near[:states]
        mine_late, late = shares(~lower, jnp.where(inside, middle, outer), got, 3)
        other_late = lax.ppermute(late, "seq", swap)
        yield late, other_late
    else:
        arrived = []
        for k in range(1, pairs):
            message = message_of(place == k - 1, got, arrived[-1] if arrived else None, min(k, 4))
            routes = both([(k - 1, k), (pairs - k, pairs - k - 1)])
            arrived.append(lax.ppermute(message, "seq", routes))
            token = yield message, arrived[-1]
            arrived[-1] = after(arrived[-1], token)
        start = end = jnp.zeros_like(arrived[0])
        for k in range(1, pairs):
            start = jnp.where(place == k, arrived[k - 1], start)
            end = jnp.where(place == pairs - 1 - k, arrived[k - 1], end)
        mine_early, early = shares(lower, jnp.where(lower, start, end), got, 5)
        mine_late, late = shares(~lower, jnp.where(lower, end, start), got, 6)
        other_early = lax.ppermute(early, "seq", swap)
        other_late = lax.ppermute(late, "seq", swap)
        yield late, other_late
    yield mine_early, mine_late, other_early, other_late


def shards(inputs, input_map, output_map, step_raw, step_bias, decay_rate, skip_gain, cotangent):
    length = inputs.shape[1]
    heads = step_raw.shape[1]
    states = input_map.shape[2]
    x, b, c, dy = inputs[0], input_map[0], output_map[0], cotangent[0]
    vectors = (
        step_raw,
        step_bias.reshape(1, heads),
        decay_rate.reshape(1, heads),
        skip_gain.reshape(1, heads),
    )
    size = lax.axis_size("seq")
    y = lax.axis_index("seq") % 2
    scale = 1.0 / math.sqrt(length * size * lax.axis_size("batch"))

    def local(half, part, count, before):
        at = jnp.reshape(half * PARTS + part, (1,)).astype(jnp.int32)
        last = count == PARTS
        out, saved = local_states(at, count, last, x, dy, b, c, vectors, before)
        return out, saved[:3] + list(before[3:] if before else []) + saved[3:]

    sent, kept = [], []
    saved = None
    for part in range(PARTS):
        out, saved = local(1 - y, part, 1, saved)
        sent += out
    kept, saved = local(y, 0, PARTS, saved)

    transfers = 4 if size == 8 else size // 2 + 1
    order = [(0, 0), (1, 0)] + [
        pick for k in range(1, transfers) for pick in ((0, k), (1, k - 1)) if pick != (1, 0)
    ]
    order.append((1, transfers - 1))
    flows, token = {}, None
    lower = lax.axis_index("seq") < size // 2
    here = jnp.stack([y, lower.astype(y.dtype)]).astype(jnp.int32)
    found = None

    def grads(part, begin, count, token, held):
        *most, final = held
        held = (*most, after(final, token))
        return local_grads(
            part, begin, count, heads // (2 * PARTS), here, saved, dy, b, c, held, found
        )

    for part, k in order:
        if (part, k) == (1, transfers - 1):
            held = next(flows[0])
            found = grads(0, 0, 1, token, held)
            token = found[-1]
        if k == 0:
            flows[part] = entering(sent[part], kept[part], states, token)
            message, arrived = next(flows[part])
            token = None if part == 0 else message
        else:
            token = flows[part].send(token)[0]
        if (part, k) == (0, 1):
            dc, db = pairs_grads(saved, after(b, token), c)
            token = dc
            found = (None, dc, db, None)
    found = grads(0, 1, 1, token, held)
    found = grads(1, 0, 2, found[-1], next(flows[1]))
    dx, dc, db, sums = found
    draw, params = steps_grads(scale, sums, vectors, saved[2])
    summed = summed_over(summed_over(params, "batch"), "seq")
    return (
        dx[None],
        db[None],
        dc[None],
        draw.reshape(heads, length)[None],
        summed[:2, :heads],
        summed[2, :heads],
    )


def solution(mesh):
    in_specs = (
        P("batch", "seq", None),
        P("batch", "seq", None),
        P("batch", "seq", None),
        P("batch", None, "seq"),
        P(),
        P(),
        P(),
        P("batch", "seq", None),
    )
    out_specs = (
        P("batch", "seq", None),
        P("batch", "seq", None),
        P("batch", "seq", None),
        P("batch", None, "seq"),
        P(),
        P(),
    )
    return jax.shard_map(shards, mesh=mesh, in_specs=in_specs, out_specs=out_specs, check_vma=False)
```

```python
import functools
import math

import jax
import jax.numpy as jnp
import numpy as np
from jax import lax
from jax.experimental import pallas as pl
from jax.experimental.pallas import tpu as pltpu
from jax.sharding import PartitionSpec as P

GROUP = 256
PARTS = 2
VMEM_LIMIT = 60 * 1024 * 1024
SMALL_LIMIT = 40 * 1024 * 1024
F32 = jnp.float32
BF16 = jnp.bfloat16


def dot(a, b, dims):
    return lax.dot_general(a, b, (dims, ((), ())), preferred_element_type=F32)


NN = ((1,), (0,))
NT = ((1,), (1,))
TN = ((0,), (0,))


def split2(a):
    hi = a.astype(BF16).astype(F32)
    return hi, a - hi


def head_matrix(heads, width):
    size = width // heads
    row = lax.broadcasted_iota(jnp.int32, (heads, width), 0)
    col = lax.broadcasted_iota(jnp.int32, (heads, width), 1)
    return ((col >= row * size) & (col < (row + 1) * size)).astype(F32)


def head_sums(values, member):
    hi, lo = split2(values)
    return dot(member, hi.astype(BF16), NT) + dot(member, lo.astype(BF16), NT)


def running(rows, upper):
    hi, rest = split2(rows)
    mid, lo = split2(rest)
    k = rows.shape[0]
    out = dot(jnp.concatenate([hi, mid, lo], axis=0).astype(BF16), upper, NN)
    return out[:k] + out[k : 2 * k] + out[2 * k :]


def triangle(width, lower):
    row = lax.broadcasted_iota(jnp.int32, (width, width), 0)
    col = lax.broadcasted_iota(jnp.int32, (width, width), 1)
    return (row >= col) if lower else (row <= col)


def softplus(v):
    return jnp.maximum(v, 0.0) + jnp.log1p(jnp.exp(-jnp.abs(v)))


def column(line, piece, heads):
    shape = (heads, line.shape[1])
    row = lax.broadcasted_iota(jnp.int32, shape, 0)
    col = lax.broadcasted_iota(jnp.int32, shape, 1)
    return jnp.sum(jnp.where(col == row + piece * heads, line, 0.0), axis=1, keepdims=True)


def block_sums(logs, blocks):
    heads = logs.shape[0]
    ones = triangle(GROUP, False).astype(BF16)
    stacked = jnp.concatenate([logs[:, n * GROUP : (n + 1) * GROUP] for n in range(blocks)], axis=0)
    cums = running(stacked, ones)
    return [cums[n * heads : (n + 1) * heads] for n in range(blocks)]


def factors(raw, bias, rate, skip, columns_ref, table_ref):
    heads, length = raw.shape
    width = table_ref.shape[1]
    blocks = length // GROUP
    step = softplus(raw + bias)
    cums = block_sums(-rate * step, blocks)
    totals = [cum[:, GROUP - 1 :] for cum in cums]
    before = [jnp.zeros((heads, 1), F32)]
    for total in totals:
        before.append(before[-1] + total)
    for n in range(blocks):
        rows = slice(n * GROUP, (n + 1) * GROUP)
        gain = split2(jnp.exp(totals[n] - cums[n]) * step[:, rows])
        lift = split2(jnp.exp(cums[n] - totals[n]))
        columns_ref[rows, :] = jnp.concatenate([*gain, *lift], axis=0).T.astype(BF16)
    whole = before[-1]
    lines = [jnp.exp(t) for t in totals]
    lines += [jnp.exp(whole - before[n + 1]) for n in range(blocks)]
    lines += [jnp.exp(before[n + 1]) for n in range(blocks)]
    lines += [jnp.exp(whole), skip]
    lines += [skip] * (-len(lines) % 8)
    hi, lo = split2(jnp.concatenate(lines, axis=1).T)
    member = head_matrix(heads, width).astype(BF16)
    table_ref[...] = dot(hi.astype(BF16), member, NN) + dot(lo.astype(BF16), member, NN)


def picker(piece, heads, all_heads, width, first):
    shape = (4 * all_heads, width)
    row = lax.broadcasted_iota(jnp.int32, shape, 0)
    col = lax.broadcasted_iota(jnp.int32, shape, 1)
    size = width // heads
    base = (0 if first else 2 * all_heads) + piece * heads
    hit = None
    for term in range(2):
        low = (row - (base + term * all_heads)) * size
        one = (col >= low) & (col < low + size)
        hit = one if hit is None else hit | one
    return hit.astype(BF16)


def local_kernel(first, last, count, *refs):
    at_ref, x_ref, dy_ref, b_ref, c_ref = refs[:5]
    if first:
        raw_ref, bias_ref, rate_ref, skip_ref = refs[5:9]
        outs = refs[9:-7]
        xs_ref, ys_ref, direct_ref, columns_ref, table_ref, bt, ct = refs[-7:]
    else:
        columns_ref, table_ref = refs[5:7]
        outs = refs[10 : 10 + count]
        xs_ref, ys_ref, direct_ref = refs[10 + count : 13 + count]
        if last:
            left, right, bt, ct = refs[13 + count :]
        else:
            bt, ct = refs[13 + count :]
    g = pl.program_id(0)
    length, width = x_ref.shape
    states = b_ref.shape[1]
    blocks = length // GROUP
    piece = at_ref[0] + g
    all_heads = columns_ref.shape[1] // 4
    heads = all_heads * width // table_ref.shape[1]

    @pl.when(g == 0)
    def _():
        bt[...] = b_ref[...].T
        ct[...] = c_ref[...].T
        if first:
            factors(
                raw_ref[0],
                column(bias_ref[...], 0, all_heads),
                column(rate_ref[...], 0, all_heads),
                column(skip_ref[...], 0, all_heads),
                columns_ref,
                table_ref,
            )
        if last:
            for n in range(blocks):
                rows = slice(n * GROUP, (n + 1) * GROUP)
                scores = dot(c_ref[rows, :], b_ref[rows, :], NT)
                left[n] = jnp.where(triangle(GROUP, True), scores, 0.0).astype(BF16)
                scores = dot(b_ref[rows, :], c_ref[rows, :], NT)
                right[n] = jnp.where(triangle(GROUP, False), scores, 0.0).astype(BF16)

    gain = dot(columns_ref[...], picker(piece, heads, all_heads, width, True), NN)
    lift = dot(columns_ref[...], picker(piece, heads, all_heads, width, False), NN)
    table = table_ref[:, pl.ds(pl.multiple_of(piece * width, width), width)]
    state = jnp.zeros((states, width), F32)
    grad = jnp.zeros((states, width), F32)
    direct = jnp.zeros((8, width), F32)
    for n in range(blocks):
        rows = slice(n * GROUP, (n + 1) * GROUP)
        x = x_ref[rows, :].astype(F32)
        dy = dy_ref[rows, :].astype(F32)
        direct = direct + jnp.sum((dy * x).reshape(GROUP // 8, 8, width), axis=0)
        scaled_x = (x * gain[rows]).astype(BF16)
        scaled_dy = (dy * lift[rows]).astype(BF16)
        xs_ref[rows, :] = scaled_x
        ys_ref[rows, :] = scaled_dy
        later = table[blocks + n : blocks + n + 1]
        earlier = table[2 * blocks + n : 2 * blocks + n + 1]
        state = state + later * dot(bt[:, rows], scaled_x, NN)
        grad = grad + earlier * dot(ct[:, rows], scaled_dy, NN)
    direct_ref[...] = direct
    decay = jnp.broadcast_to(table[3 * blocks : 3 * blocks + 1], (8, width))
    for k, out_ref in enumerate(outs):

        @pl.when(g == k)
        def _():
            out_ref[:states] = state
            out_ref[states : 2 * states] = grad
            out_ref[2 * states :] = decay


def local_states(at, count, last, x, dy, b, c, vectors, before):
    length, channels = x.shape
    states = b.shape[1]
    pieces = 2 * PARTS
    width = channels // pieces
    lines = 3 * (length // GROUP) + 2
    lines += -lines % 8
    first = before is None
    whole = lambda g, at: (0, 0)
    columns = pl.BlockSpec((length, width), lambda g, at: (0, at[0] + g))
    strip = pl.BlockSpec((8, width), lambda g, at: (0, at[0] + g))
    maps = pl.BlockSpec((length, states), whole)
    anywhere = pl.BlockSpec(memory_space=pl.ANY)
    in_specs = [columns, columns, maps, maps]
    out_specs = [pl.BlockSpec((2 * states + 8, width), whole)] * count + [columns, columns, strip]
    out_shape = [jax.ShapeDtypeStruct((2 * states + 8, width), F32)] * count + [
        jax.ShapeDtypeStruct((length, channels), BF16),
        jax.ShapeDtypeStruct((length, channels), BF16),
        jax.ShapeDtypeStruct((8, channels), F32),
    ]
    aliases = {}
    if first:
        raw, bias, rate, skip = vectors
        heads = raw.shape[1]
        args = [raw, bias, rate, skip]
        in_specs += [pl.BlockSpec(raw.shape, lambda g, at: (0, 0, 0))]
        in_specs += [pl.BlockSpec(bias.shape, whole)] * 3
        tables = [
            jax.ShapeDtypeStruct((length, 4 * heads), BF16),
            jax.ShapeDtypeStruct((lines, channels), F32),
        ]
        out_shape += tables
        out_specs += [pl.BlockSpec(t.shape, whole) for t in tables]
    else:
        xs, ys, direct, factor_columns, table = before
        args = [factor_columns, table, xs, ys, direct]
        in_specs += [pl.BlockSpec(factor_columns.shape, whole), pl.BlockSpec(table.shape, whole)]
        in_specs += [anywhere] * 3
        aliases = {7: count, 8: count + 1, 9: count + 2}
    scratch = [pltpu.VMEM((states, length), BF16)] * 2
    if last:
        blocks = length // GROUP
        extra = [jax.ShapeDtypeStruct((blocks, GROUP, GROUP), BF16)] * 2
        extra += [jax.ShapeDtypeStruct((states, length), BF16)] * 2
        out_shape += extra
        out_specs += [pl.BlockSpec(e.shape, lambda g, at, n=len(e.shape): (0,) * n) for e in extra]
        scratch = []
    grid_spec = pltpu.PrefetchScalarGridSpec(
        num_scalar_prefetch=1,
        grid=(count,),
        in_specs=in_specs,
        out_specs=out_specs,
        scratch_shapes=scratch,
    )
    out = pl.pallas_call(
        functools.partial(local_kernel, first, last, count),
        grid_spec=grid_spec,
        out_shape=out_shape,
        input_output_aliases=aliases,
        compiler_params=pltpu.CompilerParams(vmem_limit_bytes=VMEM_LIMIT),
        cost_estimate=pl.CostEstimate(
            flops=8 * count * length * width * states,
            bytes_accessed=8 * count * length * width,
            transcendentals=0,
        ),
        name="local_states",
    )(at, x, dy, b, c, *args)
    return out[:count], list(out[count:])


def pairs_kernel(xs_ref, ys_ref, b_ref, c_ref, dc_ref, db_ref):
    pair = jnp.where(triangle(GROUP, True), dot(ys_ref[...], xs_ref[...], NT), 0.0).astype(BF16)
    dc_ref[...] = dot(pair, b_ref[...], NN)
    db_ref[...] = dot(pair, c_ref[...], TN)


def pairs_grads(saved, b, c):
    xs, ys = saved[:2]
    length, channels = xs.shape
    states = b.shape[1]
    columns = pl.BlockSpec((GROUP, channels), lambda n: (n, 0))
    maps = pl.BlockSpec((GROUP, states), lambda n: (n, 0))
    return pl.pallas_call(
        pairs_kernel,
        grid=(length // GROUP,),
        in_specs=[columns, columns, maps, maps],
        out_specs=[maps, maps],
        out_shape=[jax.ShapeDtypeStruct((length, states), F32)] * 2,
        compiler_params=pltpu.CompilerParams(vmem_limit_bytes=VMEM_LIMIT),
        cost_estimate=pl.CostEstimate(
            flops=2 * length * GROUP * channels,
            bytes_accessed=4 * length * channels,
            transcendentals=0,
        ),
        name="pairs_grads",
    )(xs, ys, b, c)


def grads_kernel(first, scale, part, half, begin, *refs):
    y_ref, xs_ref, ys_ref, dy_ref, direct_ref, b_ref, c_ref, columns_ref, table_ref = refs[:9]
    raw_ref, bias_ref, rate_ref, bt, ct, left, right, adder = refs[9:17]
    held = refs[17:21]
    refs = refs[21:]
    dc_in, db_in = refs[:2]
    refs = refs[2:]
    if not first:
        par_in = refs[0]
        refs = refs[3:]
    dx_ref, dc_ref, db_ref, draw_ref, par_ref = refs[:5]
    dc_sum, db_sum, terms, dc_old, db_old, sems = refs[5:]
    old = [(dc_in, dc_old, sems.at[0]), (db_in, db_old, sems.at[1])]
    g = pl.program_id(0)
    heads = raw_ref.shape[1]
    length, width = xs_ref.shape
    states = b_ref.shape[1]
    blocks = length // GROUP
    piece = (begin + g) * half + part
    all_heads = columns_ref.shape[1] // 4
    member = head_matrix(heads, width).astype(BF16)
    lower = triangle(GROUP, True)
    rows = [slice(n * GROUP, (n + 1) * GROUP) for n in range(blocks)]

    @pl.when(g == 0)
    def _():
        for source, target, sem in old:
            pltpu.make_async_copy(source, target, sem).start()
        dc_sum[...] = jnp.zeros_like(dc_sum)
        db_sum[...] = jnp.zeros_like(db_sum)
        par_ref[...] = jnp.zeros_like(par_ref) if first else par_in[...]

    own = begin + g == y_ref[0]
    early = jnp.where(own, held[0][...], held[2][...])
    late = jnp.where(own, held[1][...], held[3][...])
    state_early = y_ref[1] == 1
    state = jnp.where(state_early, early, late)
    grad = jnp.where(state_early, late, early)
    table = table_ref[...]
    skip = table[3 * blocks + 1 : 3 * blocks + 2]
    entering_low, ends = [], []
    for n in range(blocks):
        state = table[n : n + 1] * state
        entering_low.append(state.astype(BF16))
        state = state + dot(bt[:, rows[n]], xs_ref[rows[n], :], NN)
        ends.append(state)
    leaving_low, edges = [None] * blocks, [None] * blocks
    for n in reversed(range(blocks)):
        leaving_low[n] = grad.astype(BF16)
        edges[n] = jnp.sum(ends[n] * grad, axis=0, keepdims=True)
        grad = table[n : n + 1] * (grad + dot(ct[:, rows[n]], ys_ref[rows[n], :], NN))
    gain = dot(columns_ref[...], picker(piece, heads, all_heads, width, True), NN)
    for n in range(blocks):
        scaled_x, scaled_dy = xs_ref[rows[n], :], ys_ref[rows[n], :]
        forward = dot(left[n], scaled_x, NN) + dot(c_ref[rows[n], :], entering_low[n], NN)
        backward = dot(right[n], scaled_dy, NN) + dot(b_ref[rows[n], :], leaving_low[n], NN)
        weight = gain[rows[n]]
        dx_ref[rows[n], :] = (weight * backward + skip * dy_ref[rows[n], :].astype(F32)).astype(
            dx_ref.dtype
        )
        v = scaled_x.astype(F32) * backward
        difference = scaled_dy.astype(F32) * forward - v
        hi = difference.astype(BF16)
        lo = (difference - hi.astype(F32)).astype(BF16)
        terms[rows[n], :width] = hi
        terms[rows[n], width : 2 * width] = lo
        terms[rows[n], 2 * width :] = v.astype(BF16)
        dc_sum[n] += dot(scaled_dy, entering_low[n], NT)
        db_sum[n] += dot(scaled_x, leaving_low[n], NT)
    added = dot(terms[...], adder[...], NN).T
    added = [added[:, rows[n]] for n in range(blocks)]
    edge = head_sums(jnp.concatenate(edges + [edges[0]] * (8 - blocks), axis=0), member)
    slopes = running(
        jnp.concatenate([a[:heads] for a in added], axis=0), lower.astype(BF16)
    )
    slope = jnp.concatenate(
        [slopes[n * heads : (n + 1) * heads] + edge[:, n : n + 1] for n in range(blocks)], axis=1
    )
    v = jnp.concatenate([a[heads : 2 * heads] for a in added], axis=1)
    raw = raw_ref[0] + column(bias_ref[...], piece, heads)
    step = softplus(raw)
    draw = (v / step - column(rate_ref[...], piece, heads) * slope) / (1.0 + jnp.exp(-raw))
    draw_ref[0] = draw
    values = (
        jnp.sum(draw, axis=1, keepdims=True),
        jnp.sum(head_sums(direct_ref[...], member), axis=1, keepdims=True),
        -jnp.sum(step * slope, axis=1, keepdims=True),
    )
    for k, value in enumerate(values):
        par_ref[k : k + 1] += lanes_of(value * scale, piece, (heads, par_ref.shape[1]))

    @pl.when(g == pl.num_programs(0) - 1)
    def _():
        for source, target, sem in old:
            pltpu.make_async_copy(source, target, sem).wait()
        for n in range(blocks):
            dc_ref[rows[n], :] = dc_old[rows[n], :] + dc_sum[n]
            db_ref[rows[n], :] = db_old[rows[n], :] + db_sum[n]


def local_grads(part, begin, count, scale, y, saved, dy, b, c, vectors, held, before):
    xs, ys, direct, factor_columns, table, left, right, bt, ct = saved
    raw, bias, rate, _ = vectors
    length, channels = xs.shape
    pieces = 2 * PARTS
    heads = raw.shape[1] // pieces
    raw = raw.reshape(pieces, heads, length)
    width = channels // pieces
    states = b.shape[1]
    blocks = length // GROUP
    half = pieces // 2
    first = before[0] is None
    whole = lambda g, y: (0, 0)
    place = lambda g, y: (0, (begin + g) * half + part)
    columns = pl.BlockSpec((length, width), place)
    maps = pl.BlockSpec((length, states), whole)
    line = pl.BlockSpec(bias.shape, whole)
    lines = pl.BlockSpec((1, heads, length), lambda g, y: ((begin + g) * half + part, 0, 0))
    params = pl.BlockSpec((8, 128), whole)
    anywhere = pl.BlockSpec(memory_space=pl.ANY)
    in_specs = [columns, columns, columns, pl.BlockSpec((8, width), place), maps, maps]
    in_specs += [
        pl.BlockSpec(factor_columns.shape, whole),
        pl.BlockSpec((table.shape[0], width), place),
    ]
    in_specs += [lines, line, line]
    args = [xs, ys, dy, direct, b, c, factor_columns, table, raw, bias, rate]
    fixed = [bt, ct, left, right, adding(width, heads, (0, 0, 1)), *held]
    in_specs += [pl.BlockSpec(a.shape, lambda g, y, n=len(a.shape): (0,) * n) for a in fixed]
    args += fixed
    aliases = {}
    dx, dc, db, draw, par = before
    args += [dc, db]
    in_specs += [anywhere, anywhere]
    if not first:
        args += [par, dx, draw]
        in_specs += [params, anywhere, anywhere]
        aliases = {24: 0, 25: 3}
    grid_spec = pltpu.PrefetchScalarGridSpec(
        num_scalar_prefetch=1,
        grid=(count,),
        in_specs=in_specs,
        out_specs=[columns, maps, maps, lines, params],
        scratch_shapes=[
            pltpu.VMEM((blocks, GROUP, states), F32),
            pltpu.VMEM((blocks, GROUP, states), F32),
            pltpu.VMEM((length, 3 * width), BF16),
            pltpu.VMEM((length, states), F32),
            pltpu.VMEM((length, states), F32),
            pltpu.SemaphoreType.DMA((2,)),
        ],
    )
    return pl.pallas_call(
        functools.partial(grads_kernel, first, scale, part, half, begin),
        grid_spec=grid_spec,
        out_shape=[
            jax.ShapeDtypeStruct((length, channels), BF16),
            jax.ShapeDtypeStruct((length, states), F32),
            jax.ShapeDtypeStruct((length, states), F32),
            jax.ShapeDtypeStruct((pieces, heads, length), F32),
            jax.ShapeDtypeStruct((8, 128), F32),
        ],
        input_output_aliases=aliases,
        compiler_params=pltpu.CompilerParams(vmem_limit_bytes=SMALL_LIMIT),
        cost_estimate=pl.CostEstimate(
            flops=12 * count * length * width * (GROUP + states),
            bytes_accessed=6 * count * length * width,
            transcendentals=0,
        ),
        name="local_grads",
    )(y, *args)


def adding(width, heads, places):
    out = np.zeros((len(places) * width, 128), np.float32)
    size = width // heads
    for k, place in enumerate(places):
        for channel in range(width):
            out[k * width + channel, place * heads + channel // size] = 1.0
    return jnp.asarray(out, BF16)


def lanes_of(values, piece, shape):
    row = lax.broadcasted_iota(jnp.int32, shape, 0)
    col = lax.broadcasted_iota(jnp.int32, shape, 1)
    return jnp.sum(jnp.where(col == row + piece * shape[0], values, 0.0), axis=0, keepdims=True)


def summed_over(value, axis):
    size = lax.axis_size(axis)
    if size & (size - 1):
        return lax.psum(value, axis)
    bit = 1
    while bit < size:
        steps = (bit, 2 * bit, 3 * bit) if 4 * bit <= size else (bit,)
        got = [lax.ppermute(value, axis, [(i, i ^ s) for i in range(size)]) for s in steps]
        value = value + got[0]
        if len(got) == 3:
            value = value + (got[1] + got[2])
        bit *= 4 if len(got) == 3 else 2
    return value


def after(value, *earlier):
    return lax.optimization_barrier((value, *earlier))[0]


def entering(sent, kept, states, token):
    size = lax.axis_size("seq")
    pairs = size // 2
    index = lax.axis_index("seq")
    place, second = index // 2, index % 2 == 1
    swap = [(i, i ^ 1) for i in range(size)]
    both = lambda moves: [(2 * a + y, 2 * b + y) for a, b in moves for y in range(2)]

    def halves(got, copy):
        spans = ((0, states), (states, 2 * states), (2 * states + copy, 2 * states + copy + 1))
        for low, high in spans:
            own, other = kept[low:high], got[low:high]
            yield jnp.where(second, other, own), jnp.where(second, own, other)

    def message_of(up, got, arrived, copy):
        (l1, l2), (k1, k2), (d1, d2) = halves(got, copy)
        message = jnp.where(up, d2 * l1 + l2, k1 + d1 * k2)
        return message if arrived is None else message + d1 * d2 * arrived[:states]

    def shares(is_state, value, got, copy):
        (l1, _), (_, k2), (d1, d2) = halves(got, copy)
        for_first = jnp.where(is_state, value, k2 + d2 * value)
        for_second = jnp.where(is_state, d1 * value + l1, value)
        return jnp.where(second, for_second, for_first), jnp.where(second, for_first, for_second)

    message = sent if token is None else after(sent, *token)
    got = lax.ppermute(message, "seq", swap)
    token = yield message, got
    got = after(got, token)
    lower = place < pairs // 2
    if pairs == 4:
        message = message_of((place == 0) | (place == 2), got, None, 0)
        (_, _), (_, _), (d1, d2) = halves(got, 0)
        message = jnp.concatenate([message, jnp.broadcast_to(d1 * d2, (8, message.shape[1]))])
        near = lax.ppermute(message, "seq", both([(0, 1), (1, 0), (2, 3), (3, 2)]))
        token = yield message, near
        near = after(near, token)
        message = message_of(place == 1, got, near, 1)
        middle = lax.ppermute(message, "seq", both([(1, 2), (2, 1)]))
        far = lax.ppermute(message, "seq", both([(1, 3), (2, 0)]))
        inside = (place == 1) | (place == 2)
        known = jnp.where(inside, near[:states], 0.0)
        mine_early, early = shares(lower, known, got, 2)
        other_early = lax.ppermute(early, "seq", swap)
        token = yield early, far
        far = after(far, token)
        outer = near[states : states + 1] * far + near[:states]
        mine_late, late = shares(~lower, jnp.where(inside, middle, outer), got, 3)
        other_late = lax.ppermute(late, "seq", swap)
        yield late, other_late
    else:
        arrived = []
        for k in range(1, pairs):
            message = message_of(place == k - 1, got, arrived[-1] if arrived else None, min(k, 4))
            routes = both([(k - 1, k), (pairs - k, pairs - k - 1)])
            arrived.append(lax.ppermute(message, "seq", routes))
            token = yield message, arrived[-1]
            arrived[-1] = after(arrived[-1], token)
        start = end = jnp.zeros_like(arrived[0])
        for k in range(1, pairs):
            start = jnp.where(place == k, arrived[k - 1], start)
            end = jnp.where(place == pairs - 1 - k, arrived[k - 1], end)
        mine_early, early = shares(lower, jnp.where(lower, start, end), got, 5)
        mine_late, late = shares(~lower, jnp.where(lower, end, start), got, 6)
        other_early = lax.ppermute(early, "seq", swap)
        other_late = lax.ppermute(late, "seq", swap)
        yield late, other_late
    yield mine_early, mine_late, other_early, other_late


def shards(inputs, input_map, output_map, step_raw, step_bias, decay_rate, skip_gain, cotangent):
    length = inputs.shape[1]
    heads = step_raw.shape[1]
    states = input_map.shape[2]
    x, b, c, dy = inputs[0], input_map[0], output_map[0], cotangent[0]
    vectors = (
        step_raw,
        step_bias.reshape(1, heads),
        decay_rate.reshape(1, heads),
        skip_gain.reshape(1, heads),
    )
    size = lax.axis_size("seq")
    y = lax.axis_index("seq") % 2
    scale = 1.0 / math.sqrt(length * size * lax.axis_size("batch"))

    def local(half, part, count, before):
        at = jnp.reshape(half * PARTS + part, (1,)).astype(jnp.int32)
        last = count == PARTS
        out, saved = local_states(at, count, last, x, dy, b, c, vectors, before)
        return out, saved[:3] + list(before[3:] if before else []) + saved[3:]

    sent, kept = [], []
    saved = None
    for part in range(PARTS):
        out, saved = local(1 - y, part, 1, saved)
        sent += out
    kept, saved = local(y, 0, PARTS, saved)

    transfers = 4 if size == 8 else size // 2 + 1
    order = [(0, 0), (1, 0)] + [
        pick for k in range(1, transfers) for pick in ((0, k), (1, k - 1)) if pick != (1, 0)
    ]
    order.append((1, transfers - 1))
    flows, token = {}, None
    lower = lax.axis_index("seq") < size // 2
    here = jnp.stack([y, lower.astype(y.dtype)]).astype(jnp.int32)
    found = None

    def grads(part, begin, count, token, held):
        *most, final = held
        held = (*most, after(final, token))
        return local_grads(
            part, begin, count, scale, here, saved, dy, b, c, vectors, held, found
        )

    for part, k in order:
        if (part, k) == (1, transfers - 1):
            held = next(flows[0])
            found = grads(0, 0, 1, token, held)
            token = found[-1]
        if k == 0:
            flows[part] = entering(sent[part], kept[part], states, token)
            message, arrived = next(flows[part])
            token = None if part == 0 else message
            second_got = arrived
        else:
            token = flows[part].send(token)[0]
        if (part, k) == (0, 1):
            dc, db = pairs_grads(saved, after(b, token), c)
            token = (dc, second_got)
            found = (None, dc, db, None, None)
    found = grads(0, 1, 1, token, held)
    found = grads(1, 0, 2, found[-1], next(flows[1]))
    dx, dc, db, draw, params = found
    summed = summed_over(summed_over(params, "batch"), "seq")
    return (
        dx[None],
        db[None],
        dc[None],
        draw.reshape(heads, length)[None],
        summed[:2, :heads],
        summed[2, :heads],
    )


def solution(mesh):
    in_specs = (
        P("batch", "seq", None),
        P("batch", "seq", None),
        P("batch", "seq", None),
        P("batch", None, "seq"),
        P(),
        P(),
        P(),
        P("batch", "seq", None),
    )
    out_specs = (
        P("batch", "seq", None),
        P("batch", "seq", None),
        P("batch", "seq", None),
        P("batch", None, "seq"),
        P(),
        P(),
    )
    return jax.shard_map(shards, mesh=mesh, in_specs=in_specs, out_specs=out_specs, check_vma=False)
```

```python
import functools
import math

import jax
import jax.numpy as jnp
import numpy as np
from jax import lax
from jax.experimental import pallas as pl
from jax.experimental.pallas import tpu as pltpu
from jax.sharding import PartitionSpec as P

GROUP = 256
PARTS = 2
VMEM_LIMIT = 60 * 1024 * 1024
SMALL_LIMIT = 40 * 1024 * 1024
F32 = jnp.float32
BF16 = jnp.bfloat16


def dot(a, b, dims):
    return lax.dot_general(a, b, (dims, ((), ())), preferred_element_type=F32)


NN = ((1,), (0,))
NT = ((1,), (1,))
TN = ((0,), (0,))


def split2(a):
    hi = a.astype(BF16).astype(F32)
    return hi, a - hi


def head_matrix(heads, width):
    size = width // heads
    row = lax.broadcasted_iota(jnp.int32, (heads, width), 0)
    col = lax.broadcasted_iota(jnp.int32, (heads, width), 1)
    return ((col >= row * size) & (col < (row + 1) * size)).astype(F32)


def head_sums(values, member):
    hi, lo = split2(values)
    return dot(member, hi.astype(BF16), NT) + dot(member, lo.astype(BF16), NT)


def running(rows, upper):
    hi, rest = split2(rows)
    mid, lo = split2(rest)
    k = rows.shape[0]
    out = dot(jnp.concatenate([hi, mid, lo], axis=0).astype(BF16), upper, NN)
    return out[:k] + out[k : 2 * k] + out[2 * k :]


def triangle(width, lower):
    row = lax.broadcasted_iota(jnp.int32, (width, width), 0)
    col = lax.broadcasted_iota(jnp.int32, (width, width), 1)
    return (row >= col) if lower else (row <= col)


def softplus(v):
    return jnp.maximum(v, 0.0) + jnp.log1p(jnp.exp(-jnp.abs(v)))


def column(line, piece, heads):
    shape = (heads, line.shape[1])
    row = lax.broadcasted_iota(jnp.int32, shape, 0)
    col = lax.broadcasted_iota(jnp.int32, shape, 1)
    return jnp.sum(jnp.where(col == row + piece * heads, line, 0.0), axis=1, keepdims=True)


def block_sums(logs, blocks):
    heads = logs.shape[0]
    ones = triangle(GROUP, False).astype(BF16)
    stacked = jnp.concatenate([logs[:, n * GROUP : (n + 1) * GROUP] for n in range(blocks)], axis=0)
    cums = running(stacked, ones)
    return [cums[n * heads : (n + 1) * heads] for n in range(blocks)]


def factors(raw, bias, rate, skip, columns_ref, table_ref):
    heads, length = raw.shape
    width = table_ref.shape[1]
    blocks = length // GROUP
    step = softplus(raw + bias)
    cums = block_sums(-rate * step, blocks)
    totals = [cum[:, GROUP - 1 :] for cum in cums]
    before = [jnp.zeros((heads, 1), F32)]
    for total in totals:
        before.append(before[-1] + total)
    for n in range(blocks):
        rows = slice(n * GROUP, (n + 1) * GROUP)
        gain = split2(jnp.exp(totals[n] - cums[n]) * step[:, rows])
        lift = split2(jnp.exp(cums[n] - totals[n]))
        columns_ref[rows, :] = jnp.concatenate([*gain, *lift], axis=0).T.astype(BF16)
    whole = before[-1]
    lines = [jnp.exp(t) for t in totals]
    lines += [jnp.exp(whole - before[n + 1]) for n in range(blocks)]
    lines += [jnp.exp(before[n + 1]) for n in range(blocks)]
    lines += [jnp.exp(whole), skip]
    lines += [skip] * (-len(lines) % 8)
    hi, lo = split2(jnp.concatenate(lines, axis=1).T)
    member = head_matrix(heads, width).astype(BF16)
    table_ref[...] = dot(hi.astype(BF16), member, NN) + dot(lo.astype(BF16), member, NN)


def picker(piece, heads, all_heads, width, first):
    shape = (4 * all_heads, width)
    row = lax.broadcasted_iota(jnp.int32, shape, 0)
    col = lax.broadcasted_iota(jnp.int32, shape, 1)
    size = width // heads
    base = (0 if first else 2 * all_heads) + piece * heads
    hit = None
    for term in range(2):
        low = (row - (base + term * all_heads)) * size
        one = (col >= low) & (col < low + size)
        hit = one if hit is None else hit | one
    return hit.astype(BF16)


def local_kernel(first, last, count, *refs):
    at_ref, x_ref, dy_ref, b_ref, c_ref = refs[:5]
    if first:
        raw_ref, bias_ref, rate_ref, skip_ref = refs[5:9]
        outs = refs[9:-8]
        xs_ref, ys_ref, direct_ref, fresh_ref, columns_ref, table_ref, bt, ct = refs[-8:]
    else:
        columns_ref, table_ref = refs[5:7]
        outs = refs[11 : 11 + count]
        xs_ref, ys_ref, direct_ref, fresh_ref = refs[11 + count : 15 + count]
        if last:
            left, right, bt, ct = refs[15 + count :]
        else:
            bt, ct = refs[15 + count :]
    g = pl.program_id(0)
    length, width = x_ref.shape
    states = b_ref.shape[1]
    blocks = length // GROUP
    piece = at_ref[0] + g
    all_heads = columns_ref.shape[1] // 4
    heads = all_heads * width // table_ref.shape[1]

    @pl.when(g == 0)
    def _():
        bt[...] = b_ref[...].T
        ct[...] = c_ref[...].T
        if first:
            factors(
                raw_ref[0],
                column(bias_ref[...], 0, all_heads),
                column(rate_ref[...], 0, all_heads),
                column(skip_ref[...], 0, all_heads),
                columns_ref,
                table_ref,
            )
        if last:
            for n in range(blocks):
                rows = slice(n * GROUP, (n + 1) * GROUP)
                scores = dot(c_ref[rows, :], b_ref[rows, :], NT)
                left[n] = jnp.where(triangle(GROUP, True), scores, 0.0).astype(BF16)
                scores = dot(b_ref[rows, :], c_ref[rows, :], NT)
                right[n] = jnp.where(triangle(GROUP, False), scores, 0.0).astype(BF16)

    gain = dot(columns_ref[...], picker(piece, heads, all_heads, width, True), NN)
    lift = dot(columns_ref[...], picker(piece, heads, all_heads, width, False), NN)
    table = table_ref[:, pl.ds(pl.multiple_of(piece * width, width), width)]
    state = jnp.zeros((states, width), F32)
    grad = jnp.zeros((states, width), F32)
    direct = jnp.zeros((8, width), F32)
    for n in range(blocks):
        rows = slice(n * GROUP, (n + 1) * GROUP)
        x = x_ref[rows, :].astype(F32)
        dy = dy_ref[rows, :].astype(F32)
        direct = direct + jnp.sum((dy * x).reshape(GROUP // 8, 8, width), axis=0)
        scaled_x = (x * gain[rows]).astype(BF16)
        scaled_dy = (dy * lift[rows]).astype(BF16)
        xs_ref[rows, :] = scaled_x
        ys_ref[rows, :] = scaled_dy
        later = table[blocks + n : blocks + n + 1]
        earlier = table[2 * blocks + n : 2 * blocks + n + 1]
        fresh_x = dot(bt[:, rows], scaled_x, NN)
        fresh_dy = dot(ct[:, rows], scaled_dy, NN)
        fresh_ref[n] = fresh_x.astype(BF16)
        fresh_ref[blocks + n] = fresh_dy.astype(BF16)
        state = state + later * fresh_x
        grad = grad + earlier * fresh_dy
    direct_ref[...] = direct
    decay = jnp.broadcast_to(table[3 * blocks : 3 * blocks + 1], (8, width))
    for k, out_ref in enumerate(outs):

        @pl.when(g == k)
        def _():
            out_ref[:states] = state
            out_ref[states : 2 * states] = grad
            out_ref[2 * states :] = decay


def local_states(at, count, last, x, dy, b, c, vectors, before):
    length, channels = x.shape
    states = b.shape[1]
    pieces = 2 * PARTS
    width = channels // pieces
    lines = 3 * (length // GROUP) + 2
    lines += -lines % 8
    first = before is None
    whole = lambda g, at: (0, 0)
    columns = pl.BlockSpec((length, width), lambda g, at: (0, at[0] + g))
    strip = pl.BlockSpec((8, width), lambda g, at: (0, at[0] + g))
    steps = 2 * (length // GROUP)
    made = pl.BlockSpec((steps, states, width), lambda g, at: (0, 0, at[0] + g))
    maps = pl.BlockSpec((length, states), whole)
    anywhere = pl.BlockSpec(memory_space=pl.ANY)
    in_specs = [columns, columns, maps, maps]
    out_specs = [pl.BlockSpec((2 * states + 8, width), whole)] * count + [columns, columns, strip, made]
    out_shape = [jax.ShapeDtypeStruct((2 * states + 8, width), F32)] * count + [
        jax.ShapeDtypeStruct((length, channels), BF16),
        jax.ShapeDtypeStruct((length, channels), BF16),
        jax.ShapeDtypeStruct((8, channels), F32),
        jax.ShapeDtypeStruct((steps, states, channels), BF16),
    ]
    aliases = {}
    if first:
        raw, bias, rate, skip = vectors
        heads = raw.shape[1]
        args = [raw, bias, rate, skip]
        in_specs += [pl.BlockSpec(raw.shape, lambda g, at: (0, 0, 0))]
        in_specs += [pl.BlockSpec(bias.shape, whole)] * 3
        tables = [
            jax.ShapeDtypeStruct((length, 4 * heads), BF16),
            jax.ShapeDtypeStruct((lines, channels), F32),
        ]
        out_shape += tables
        out_specs += [pl.BlockSpec(t.shape, whole) for t in tables]
    else:
        xs, ys, direct, fresh, factor_columns, table = before
        args = [factor_columns, table, xs, ys, direct, fresh]
        in_specs += [pl.BlockSpec(factor_columns.shape, whole), pl.BlockSpec(table.shape, whole)]
        in_specs += [anywhere] * 4
        aliases = {7: count, 8: count + 1, 9: count + 2, 10: count + 3}
    scratch = [pltpu.VMEM((states, length), BF16)] * 2
    if last:
        blocks = length // GROUP
        extra = [jax.ShapeDtypeStruct((blocks, GROUP, GROUP), BF16)] * 2
        extra += [jax.ShapeDtypeStruct((states, length), BF16)] * 2
        out_shape += extra
        out_specs += [pl.BlockSpec(e.shape, lambda g, at, n=len(e.shape): (0,) * n) for e in extra]
        scratch = []
    grid_spec = pltpu.PrefetchScalarGridSpec(
        num_scalar_prefetch=1,
        grid=(count,),
        in_specs=in_specs,
        out_specs=out_specs,
        scratch_shapes=scratch,
    )
    out = pl.pallas_call(
        functools.partial(local_kernel, first, last, count),
        grid_spec=grid_spec,
        out_shape=out_shape,
        input_output_aliases=aliases,
        compiler_params=pltpu.CompilerParams(vmem_limit_bytes=VMEM_LIMIT),
        cost_estimate=pl.CostEstimate(
            flops=8 * count * length * width * states,
            bytes_accessed=8 * count * length * width,
            transcendentals=0,
        ),
        name="local_states",
    )(at, x, dy, b, c, *args)
    return out[:count], list(out[count:])


def pairs_kernel(xs_ref, ys_ref, b_ref, c_ref, dc_ref, db_ref):
    pair = jnp.where(triangle(GROUP, True), dot(ys_ref[...], xs_ref[...], NT), 0.0).astype(BF16)
    dc_ref[...] = dot(pair, b_ref[...], NN)
    db_ref[...] = dot(pair, c_ref[...], TN)


def pairs_grads(saved, b, c):
    xs, ys = saved[:2]
    length, channels = xs.shape
    states = b.shape[1]
    columns = pl.BlockSpec((GROUP, channels), lambda n: (n, 0))
    maps = pl.BlockSpec((GROUP, states), lambda n: (n, 0))
    return pl.pallas_call(
        pairs_kernel,
        grid=(length // GROUP,),
        in_specs=[columns, columns, maps, maps],
        out_specs=[maps, maps],
        out_shape=[jax.ShapeDtypeStruct((length, states), F32)] * 2,
        compiler_params=pltpu.CompilerParams(vmem_limit_bytes=VMEM_LIMIT),
        cost_estimate=pl.CostEstimate(
            flops=2 * length * GROUP * channels,
            bytes_accessed=4 * length * channels,
            transcendentals=0,
        ),
        name="pairs_grads",
    )(xs, ys, b, c)


def grads_kernel(first, scale, part, half, begin, *refs):
    y_ref, xs_ref, ys_ref, dy_ref, direct_ref, b_ref, c_ref, columns_ref, table_ref = refs[:9]
    raw_ref, bias_ref, rate_ref, fresh_ref, left, right, adder = refs[9:16]
    held = refs[16:20]
    refs = refs[20:]
    dc_in, db_in = refs[:2]
    refs = refs[2:]
    if not first:
        par_in = refs[0]
        refs = refs[3:]
    dx_ref, dc_ref, db_ref, draw_ref, par_ref = refs[:5]
    dc_sum, db_sum, terms, dc_old, db_old, sems = refs[5:]
    old = [(dc_in, dc_old, sems.at[0]), (db_in, db_old, sems.at[1])]
    g = pl.program_id(0)
    heads = raw_ref.shape[1]
    length, width = xs_ref.shape
    states = b_ref.shape[1]
    blocks = length // GROUP
    piece = (begin + g) * half + part
    all_heads = columns_ref.shape[1] // 4
    member = head_matrix(heads, width).astype(BF16)
    lower = triangle(GROUP, True)
    rows = [slice(n * GROUP, (n + 1) * GROUP) for n in range(blocks)]

    @pl.when(g == 0)
    def _():
        for source, target, sem in old:
            pltpu.make_async_copy(source, target, sem).start()
        dc_sum[...] = jnp.zeros_like(dc_sum)
        db_sum[...] = jnp.zeros_like(db_sum)
        par_ref[...] = jnp.zeros_like(par_ref) if first else par_in[...]

    own = begin + g == y_ref[0]
    early = jnp.where(own, held[0][...], held[2][...])
    late = jnp.where(own, held[1][...], held[3][...])
    state_early = y_ref[1] == 1
    state = jnp.where(state_early, early, late)
    grad = jnp.where(state_early, late, early)
    table = table_ref[...]
    skip = table[3 * blocks + 1 : 3 * blocks + 2]
    entering_low, ends = [], []
    for n in range(blocks):
        state = table[n : n + 1] * state
        entering_low.append(state.astype(BF16))
        state = state + fresh_ref[n].astype(F32)
        ends.append(state)
    leaving_low, edges = [None] * blocks, [None] * blocks
    for n in reversed(range(blocks)):
        leaving_low[n] = grad.astype(BF16)
        edges[n] = jnp.sum(ends[n] * grad, axis=0, keepdims=True)
        grad = table[n : n + 1] * (grad + fresh_ref[blocks + n].astype(F32))
    gain = dot(columns_ref[...], picker(piece, heads, all_heads, width, True), NN)
    for n in range(blocks):
        scaled_x, scaled_dy = xs_ref[rows[n], :], ys_ref[rows[n], :]
        forward = dot(left[n], scaled_x, NN) + dot(c_ref[rows[n], :], entering_low[n], NN)
        backward = dot(right[n], scaled_dy, NN) + dot(b_ref[rows[n], :], leaving_low[n], NN)
        weight = gain[rows[n]]
        dx_ref[rows[n], :] = (weight * backward + skip * dy_ref[rows[n], :].astype(F32)).astype(
            dx_ref.dtype
        )
        v = scaled_x.astype(F32) * backward
        difference = scaled_dy.astype(F32) * forward - v
        hi = difference.astype(BF16)
        lo = (difference - hi.astype(F32)).astype(BF16)
        terms[rows[n], :width] = hi
        terms[rows[n], width : 2 * width] = lo
        terms[rows[n], 2 * width :] = v.astype(BF16)
        dc_sum[n] += dot(scaled_dy, entering_low[n], NT)
        db_sum[n] += dot(scaled_x, leaving_low[n], NT)
    added = dot(terms[...], adder[...], NN).T
    added = [added[:, rows[n]] for n in range(blocks)]
    edge = head_sums(jnp.concatenate(edges + [edges[0]] * (8 - blocks), axis=0), member)
    slopes = running(
        jnp.concatenate([a[:heads] for a in added], axis=0), lower.astype(BF16)
    )
    slope = jnp.concatenate(
        [slopes[n * heads : (n + 1) * heads] + edge[:, n : n + 1] for n in range(blocks)], axis=1
    )
    v = jnp.concatenate([a[heads : 2 * heads] for a in added], axis=1)
    raw = raw_ref[0] + column(bias_ref[...], piece, heads)
    step = softplus(raw)
    draw = (v / step - column(rate_ref[...], piece, heads) * slope) / (1.0 + jnp.exp(-raw))
    draw_ref[0] = draw
    values = (
        jnp.sum(draw, axis=1, keepdims=True),
        jnp.sum(head_sums(direct_ref[...], member), axis=1, keepdims=True),
        -jnp.sum(step * slope, axis=1, keepdims=True),
    )
    for k, value in enumerate(values):
        par_ref[k : k + 1] += lanes_of(value * scale, piece, (heads, par_ref.shape[1]))

    @pl.when(g == pl.num_programs(0) - 1)
    def _():
        for source, target, sem in old:
            pltpu.make_async_copy(source, target, sem).wait()
        for n in range(blocks):
            dc_ref[rows[n], :] = dc_old[rows[n], :] + dc_sum[n]
            db_ref[rows[n], :] = db_old[rows[n], :] + db_sum[n]


def local_grads(part, begin, count, scale, y, saved, dy, b, c, vectors, held, before):
    xs, ys, direct, fresh, factor_columns, table, left, right, _, _ = saved
    raw, bias, rate, _ = vectors
    length, channels = xs.shape
    pieces = 2 * PARTS
    heads = raw.shape[1] // pieces
    raw = raw.reshape(pieces, heads, length)
    width = channels // pieces
    states = b.shape[1]
    blocks = length // GROUP
    half = pieces // 2
    first = before[0] is None
    whole = lambda g, y: (0, 0)
    place = lambda g, y: (0, (begin + g) * half + part)
    columns = pl.BlockSpec((length, width), place)
    maps = pl.BlockSpec((length, states), whole)
    line = pl.BlockSpec(bias.shape, whole)
    lines = pl.BlockSpec((1, heads, length), lambda g, y: ((begin + g) * half + part, 0, 0))
    params = pl.BlockSpec((8, 128), whole)
    anywhere = pl.BlockSpec(memory_space=pl.ANY)
    in_specs = [columns, columns, columns, pl.BlockSpec((8, width), place), maps, maps]
    in_specs += [
        pl.BlockSpec(factor_columns.shape, whole),
        pl.BlockSpec((table.shape[0], width), place),
    ]
    in_specs += [lines, line, line]
    args = [xs, ys, dy, direct, b, c, factor_columns, table, raw, bias, rate]
    fixed = [left, right, adding(width, heads, (0, 0, 1)), *held]
    made = pl.BlockSpec((2 * blocks, states, width), lambda g, y: (0, *place(g, y)))
    in_specs += [made]
    in_specs += [pl.BlockSpec(a.shape, lambda g, y, n=len(a.shape): (0,) * n) for a in fixed]
    args += [fresh]
    args += fixed
    aliases = {}
    dx, dc, db, draw, par = before
    args += [dc, db]
    in_specs += [anywhere, anywhere]
    if not first:
        args += [par, dx, draw]
        in_specs += [params, anywhere, anywhere]
        aliases = {23: 0, 24: 3}
    grid_spec = pltpu.PrefetchScalarGridSpec(
        num_scalar_prefetch=1,
        grid=(count,),
        in_specs=in_specs,
        out_specs=[columns, maps, maps, lines, params],
        scratch_shapes=[
            pltpu.VMEM((blocks, GROUP, states), F32),
            pltpu.VMEM((blocks, GROUP, states), F32),
            pltpu.VMEM((length, 3 * width), BF16),
            pltpu.VMEM((length, states), F32),
            pltpu.VMEM((length, states), F32),
            pltpu.SemaphoreType.DMA((2,)),
        ],
    )
    return pl.pallas_call(
        functools.partial(grads_kernel, first, scale, part, half, begin),
        grid_spec=grid_spec,
        out_shape=[
            jax.ShapeDtypeStruct((length, channels), BF16),
            jax.ShapeDtypeStruct((length, states), F32),
            jax.ShapeDtypeStruct((length, states), F32),
            jax.ShapeDtypeStruct((pieces, heads, length), F32),
            jax.ShapeDtypeStruct((8, 128), F32),
        ],
        input_output_aliases=aliases,
        compiler_params=pltpu.CompilerParams(vmem_limit_bytes=SMALL_LIMIT),
        cost_estimate=pl.CostEstimate(
            flops=12 * count * length * width * (GROUP + states),
            bytes_accessed=6 * count * length * width,
            transcendentals=0,
        ),
        name="local_grads",
    )(y, *args)


def adding(width, heads, places):
    out = np.zeros((len(places) * width, 128), np.float32)
    size = width // heads
    for k, place in enumerate(places):
        for channel in range(width):
            out[k * width + channel, place * heads + channel // size] = 1.0
    return jnp.asarray(out, BF16)


def lanes_of(values, piece, shape):
    row = lax.broadcasted_iota(jnp.int32, shape, 0)
    col = lax.broadcasted_iota(jnp.int32, shape, 1)
    return jnp.sum(jnp.where(col == row + piece * shape[0], values, 0.0), axis=0, keepdims=True)


def summed_over(value, axis):
    size = lax.axis_size(axis)
    if size & (size - 1):
        return lax.psum(value, axis)
    bit = 1
    while bit < size:
        steps = (bit, 2 * bit, 3 * bit) if 4 * bit <= size else (bit,)
        got = [lax.ppermute(value, axis, [(i, i ^ s) for i in range(size)]) for s in steps]
        value = value + got[0]
        if len(got) == 3:
            value = value + (got[1] + got[2])
        bit *= 4 if len(got) == 3 else 2
    return value


def after(value, *earlier):
    return lax.optimization_barrier((value, *earlier))[0]


def entering(sent, kept, states, token):
    size = lax.axis_size("seq")
    pairs = size // 2
    index = lax.axis_index("seq")
    place, second = index // 2, index % 2 == 1
    swap = [(i, i ^ 1) for i in range(size)]
    both = lambda moves: [(2 * a + y, 2 * b + y) for a, b in moves for y in range(2)]

    def halves(got, copy):
        spans = ((0, states), (states, 2 * states), (2 * states + copy, 2 * states + copy + 1))
        for low, high in spans:
            own, other = kept[low:high], got[low:high]
            yield jnp.where(second, other, own), jnp.where(second, own, other)

    def message_of(up, got, arrived, copy):
        (l1, l2), (k1, k2), (d1, d2) = halves(got, copy)
        message = jnp.where(up, d2 * l1 + l2, k1 + d1 * k2)
        return message if arrived is None else message + d1 * d2 * arrived[:states]

    def shares(is_state, value, got, copy):
        (l1, _), (_, k2), (d1, d2) = halves(got, copy)
        for_first = jnp.where(is_state, value, k2 + d2 * value)
        for_second = jnp.where(is_state, d1 * value + l1, value)
        return jnp.where(second, for_second, for_first), jnp.where(second, for_first, for_second)

    message = sent if token is None else after(sent, *token)
    got = lax.ppermute(message, "seq", swap)
    token = yield message, got
    got = after(got, token)
    lower = place < pairs // 2
    if pairs == 4:
        message = message_of((place == 0) | (place == 2), got, None, 0)
        (_, _), (_, _), (d1, d2) = halves(got, 0)
        message = jnp.concatenate([message, jnp.broadcast_to(d1 * d2, (8, message.shape[1]))])
        near = lax.ppermute(message, "seq", both([(0, 1), (1, 0), (2, 3), (3, 2)]))
        token = yield message, near
        near = after(near, token)
        message = message_of(place == 1, got, near, 1)
        middle = lax.ppermute(message, "seq", both([(1, 2), (2, 1)]))
        far = lax.ppermute(message, "seq", both([(1, 3), (2, 0)]))
        inside = (place == 1) | (place == 2)
        known = jnp.where(inside, near[:states], 0.0)
        mine_early, early = shares(lower, known, got, 2)
        other_early = lax.ppermute(early, "seq", swap)
        token = yield early, far
        far = after(far, token)
        outer = near[states : states + 1] * far + near[:states]
        mine_late, late = shares(~lower, jnp.where(inside, middle, outer), got, 3)
        other_late = lax.ppermute(late, "seq", swap)
        yield late, other_late
    else:
        arrived = []
        for k in range(1, pairs):
            message = message_of(place == k - 1, got, arrived[-1] if arrived else None, min(k, 4))
            routes = both([(k - 1, k), (pairs - k, pairs - k - 1)])
            arrived.append(lax.ppermute(message, "seq", routes))
            token = yield message, arrived[-1]
            arrived[-1] = after(arrived[-1], token)
        start = end = jnp.zeros_like(arrived[0])
        for k in range(1, pairs):
            start = jnp.where(place == k, arrived[k - 1], start)
            end = jnp.where(place == pairs - 1 - k, arrived[k - 1], end)
        mine_early, early = shares(lower, jnp.where(lower, start, end), got, 5)
        mine_late, late = shares(~lower, jnp.where(lower, end, start), got, 6)
        other_early = lax.ppermute(early, "seq", swap)
        other_late = lax.ppermute(late, "seq", swap)
        yield late, other_late
    yield mine_early, mine_late, other_early, other_late


def shards(inputs, input_map, output_map, step_raw, step_bias, decay_rate, skip_gain, cotangent):
    length = inputs.shape[1]
    heads = step_raw.shape[1]
    states = input_map.shape[2]
    x, b, c, dy = inputs[0], input_map[0], output_map[0], cotangent[0]
    vectors = (
        step_raw,
        step_bias.reshape(1, heads),
        decay_rate.reshape(1, heads),
        skip_gain.reshape(1, heads),
    )
    size = lax.axis_size("seq")
    y = lax.axis_index("seq") % 2
    scale = 1.0 / math.sqrt(length * size * lax.axis_size("batch"))

    def local(half, part, count, before):
        at = jnp.reshape(half * PARTS + part, (1,)).astype(jnp.int32)
        last = count == PARTS
        out, saved = local_states(at, count, last, x, dy, b, c, vectors, before)
        return out, saved[:4] + list(before[4:] if before else []) + saved[4:]

    sent, kept = [], []
    saved = None
    for part in range(PARTS):
        out, saved = local(1 - y, part, 1, saved)
        sent += out
    kept, saved = local(y, 0, PARTS, saved)

    transfers = 4 if size == 8 else size // 2 + 1
    order = [(0, 0), (1, 0)] + [
        pick for k in range(1, transfers) for pick in ((0, k), (1, k - 1)) if pick != (1, 0)
    ]
    order.append((1, transfers - 1))
    flows, token = {}, None
    lower = lax.axis_index("seq") < size // 2
    here = jnp.stack([y, lower.astype(y.dtype)]).astype(jnp.int32)
    found = None

    def grads(part, begin, count, token, held):
        *most, final = held
        held = (*most, after(final, token))
        return local_grads(
            part, begin, count, scale, here, saved, dy, b, c, vectors, held, found
        )

    for part, k in order:
        if (part, k) == (1, transfers - 1):
            held = next(flows[0])
            found = grads(0, 0, 1, token, held)
            token = found[-1]
        if k == 0:
            flows[part] = entering(sent[part], kept[part], states, token)
            message, arrived = next(flows[part])
            token = None if part == 0 else message
        else:
            token = flows[part].send(token)[0]
        if (part, k) == (0, 1):
            dc, db = pairs_grads(saved, after(b, token), c)
            token = dc
            found = (None, dc, db, None, None)
    found = grads(0, 1, 1, token, held)
    found = grads(1, 0, 2, found[-1], next(flows[1]))
    dx, dc, db, draw, params = found
    summed = summed_over(summed_over(params, "batch"), "seq")
    return (
        dx[None],
        db[None],
        dc[None],
        draw.reshape(heads, length)[None],
        summed[:2, :heads],
        summed[2, :heads],
    )


def solution(mesh):
    in_specs = (
        P("batch", "seq", None),
        P("batch", "seq", None),
        P("batch", "seq", None),
        P("batch", None, "seq"),
        P(),
        P(),
        P(),
        P("batch", "seq", None),
    )
    out_specs = (
        P("batch", "seq", None),
        P("batch", "seq", None),
        P("batch", "seq", None),
        P("batch", None, "seq"),
        P(),
        P(),
    )
    return jax.shard_map(shards, mesh=mesh, in_specs=in_specs, out_specs=out_specs, check_vma=False)
```

```python
import functools
import math

import jax
import jax.numpy as jnp
import numpy as np
from jax import lax
from jax.experimental import pallas as pl
from jax.experimental.pallas import tpu as pltpu
from jax.sharding import PartitionSpec as P

GROUP = 256
PARTS = 2
VMEM_LIMIT = 60 * 1024 * 1024
SMALL_LIMIT = 40 * 1024 * 1024
F32 = jnp.float32
BF16 = jnp.bfloat16


def dot(a, b, dims):
    return lax.dot_general(a, b, (dims, ((), ())), preferred_element_type=F32)


NN = ((1,), (0,))
NT = ((1,), (1,))
TN = ((0,), (0,))


def split2(a):
    hi = a.astype(BF16).astype(F32)
    return hi, a - hi


def head_matrix(heads, width):
    size = width // heads
    row = lax.broadcasted_iota(jnp.int32, (heads, width), 0)
    col = lax.broadcasted_iota(jnp.int32, (heads, width), 1)
    return ((col >= row * size) & (col < (row + 1) * size)).astype(F32)


def head_sums(values, member):
    hi, lo = split2(values)
    return dot(member, hi.astype(BF16), NT) + dot(member, lo.astype(BF16), NT)


def running(rows, upper):
    hi, rest = split2(rows)
    mid, lo = split2(rest)
    k = rows.shape[0]
    out = dot(jnp.concatenate([hi, mid, lo], axis=0).astype(BF16), upper, NN)
    return out[:k] + out[k : 2 * k] + out[2 * k :]


def triangle(width, lower):
    row = lax.broadcasted_iota(jnp.int32, (width, width), 0)
    col = lax.broadcasted_iota(jnp.int32, (width, width), 1)
    return (row >= col) if lower else (row <= col)


def softplus(v):
    return jnp.maximum(v, 0.0) + jnp.log1p(jnp.exp(-jnp.abs(v)))


def column(line, piece, heads):
    shape = (heads, line.shape[1])
    row = lax.broadcasted_iota(jnp.int32, shape, 0)
    col = lax.broadcasted_iota(jnp.int32, shape, 1)
    return jnp.sum(jnp.where(col == row + piece * heads, line, 0.0), axis=1, keepdims=True)


def block_sums(logs, blocks):
    heads = logs.shape[0]
    ones = triangle(GROUP, False).astype(BF16)
    stacked = jnp.concatenate([logs[:, n * GROUP : (n + 1) * GROUP] for n in range(blocks)], axis=0)
    cums = running(stacked, ones)
    return [cums[n * heads : (n + 1) * heads] for n in range(blocks)]


def factors(raw, bias, rate, skip, columns_ref, table_ref):
    heads, length = raw.shape
    width = table_ref.shape[1]
    blocks = length // GROUP
    step = softplus(raw + bias)
    cums = block_sums(-rate * step, blocks)
    totals = [cum[:, GROUP - 1 :] for cum in cums]
    before = [jnp.zeros((heads, 1), F32)]
    for total in totals:
        before.append(before[-1] + total)
    for n in range(blocks):
        rows = slice(n * GROUP, (n + 1) * GROUP)
        gain = split2(jnp.exp(totals[n] - cums[n]) * step[:, rows])
        lift = split2(jnp.exp(cums[n] - totals[n]))
        columns_ref[rows, :] = jnp.concatenate([*gain, *lift], axis=0).T.astype(BF16)
    whole = before[-1]
    lines = [jnp.exp(t) for t in totals]
    lines += [jnp.exp(whole - before[n + 1]) for n in range(blocks)]
    lines += [jnp.exp(before[n + 1]) for n in range(blocks)]
    lines += [jnp.exp(whole), skip]
    lines += [skip] * (-len(lines) % 8)
    hi, lo = split2(jnp.concatenate(lines, axis=1).T)
    member = head_matrix(heads, width).astype(BF16)
    table_ref[...] = dot(hi.astype(BF16), member, NN) + dot(lo.astype(BF16), member, NN)


def picker(piece, heads, all_heads, width, first):
    shape = (4 * all_heads, width)
    row = lax.broadcasted_iota(jnp.int32, shape, 0)
    col = lax.broadcasted_iota(jnp.int32, shape, 1)
    size = width // heads
    base = (0 if first else 2 * all_heads) + piece * heads
    hit = None
    for term in range(2):
        low = (row - (base + term * all_heads)) * size
        one = (col >= low) & (col < low + size)
        hit = one if hit is None else hit | one
    return hit.astype(BF16)


def local_kernel(first, last, count, *refs):
    at_ref, x_ref, dy_ref, b_ref, c_ref = refs[:5]
    if first:
        raw_ref, bias_ref, rate_ref, skip_ref = refs[5:9]
        outs = refs[9:-7]
        xs_ref, ys_ref, direct_ref, columns_ref, table_ref, bt, ct = refs[-7:]
    else:
        columns_ref, table_ref = refs[5:7]
        outs = refs[10 : 10 + count]
        xs_ref, ys_ref, direct_ref = refs[10 + count : 13 + count]
        if last:
            left, right, bt, ct = refs[13 + count :]
        else:
            bt, ct = refs[13 + count :]
    g = pl.program_id(0)
    length, width = x_ref.shape
    states = b_ref.shape[1]
    blocks = length // GROUP
    piece = at_ref[0] + g
    all_heads = columns_ref.shape[1] // 4
    heads = all_heads * width // table_ref.shape[1]

    @pl.when(g == 0)
    def _():
        bt[...] = b_ref[...].T
        ct[...] = c_ref[...].T
        if first:
            factors(
                raw_ref[0],
                column(bias_ref[...], 0, all_heads),
                column(rate_ref[...], 0, all_heads),
                column(skip_ref[...], 0, all_heads),
                columns_ref,
                table_ref,
            )
        if last:
            for n in range(blocks):
                rows = slice(n * GROUP, (n + 1) * GROUP)
                scores = dot(c_ref[rows, :], b_ref[rows, :], NT)
                left[n] = jnp.where(triangle(GROUP, True), scores, 0.0).astype(BF16)
                scores = dot(b_ref[rows, :], c_ref[rows, :], NT)
                right[n] = jnp.where(triangle(GROUP, False), scores, 0.0).astype(BF16)

    gain = dot(columns_ref[...], picker(piece, heads, all_heads, width, True), NN)
    lift = dot(columns_ref[...], picker(piece, heads, all_heads, width, False), NN)
    table = table_ref[:, pl.ds(pl.multiple_of(piece * width, width), width)]
    state = jnp.zeros((states, width), F32)
    grad = jnp.zeros((states, width), F32)
    direct = jnp.zeros((8, width), F32)
    for n in range(blocks):
        rows = slice(n * GROUP, (n + 1) * GROUP)
        x = x_ref[rows, :].astype(F32)
        dy = dy_ref[rows, :].astype(F32)
        direct = direct + jnp.sum((dy * x).reshape(GROUP // 8, 8, width), axis=0)
        scaled_x = (x * gain[rows]).astype(BF16)
        scaled_dy = (dy * lift[rows]).astype(BF16)
        xs_ref[rows, :] = scaled_x
        ys_ref[rows, :] = scaled_dy
        later = table[blocks + n : blocks + n + 1]
        earlier = table[2 * blocks + n : 2 * blocks + n + 1]
        state = state + later * dot(bt[:, rows], scaled_x, NN)
        grad = grad + earlier * dot(ct[:, rows], scaled_dy, NN)
    direct_ref[...] = direct
    decay = jnp.broadcast_to(table[3 * blocks : 3 * blocks + 1], (8, width))
    for k, out_ref in enumerate(outs):

        @pl.when(g == k)
        def _():
            out_ref[:states] = state
            out_ref[states : 2 * states] = grad
            out_ref[2 * states :] = decay


def local_states(at, count, last, x, dy, b, c, vectors, before):
    length, channels = x.shape
    states = b.shape[1]
    pieces = 2 * PARTS
    width = channels // pieces
    lines = 3 * (length // GROUP) + 2
    lines += -lines % 8
    first = before is None
    whole = lambda g, at: (0, 0)
    columns = pl.BlockSpec((length, width), lambda g, at: (0, at[0] + g))
    strip = pl.BlockSpec((8, width), lambda g, at: (0, at[0] + g))
    maps = pl.BlockSpec((length, states), whole)
    anywhere = pl.BlockSpec(memory_space=pl.ANY)
    in_specs = [columns, columns, maps, maps]
    out_specs = [pl.BlockSpec((2 * states + 8, width), whole)] * count + [columns, columns, strip]
    out_shape = [jax.ShapeDtypeStruct((2 * states + 8, width), F32)] * count + [
        jax.ShapeDtypeStruct((length, channels), BF16),
        jax.ShapeDtypeStruct((length, channels), BF16),
        jax.ShapeDtypeStruct((8, channels), F32),
    ]
    aliases = {}
    if first:
        raw, bias, rate, skip = vectors
        heads = raw.shape[1]
        args = [raw, bias, rate, skip]
        in_specs += [pl.BlockSpec(raw.shape, lambda g, at: (0, 0, 0))]
        in_specs += [pl.BlockSpec(bias.shape, whole)] * 3
        tables = [
            jax.ShapeDtypeStruct((length, 4 * heads), BF16),
            jax.ShapeDtypeStruct((lines, channels), F32),
        ]
        out_shape += tables
        out_specs += [pl.BlockSpec(t.shape, whole) for t in tables]
    else:
        xs, ys, direct, factor_columns, table = before
        args = [factor_columns, table, xs, ys, direct]
        in_specs += [pl.BlockSpec(factor_columns.shape, whole), pl.BlockSpec(table.shape, whole)]
        in_specs += [anywhere] * 3
        aliases = {7: count, 8: count + 1, 9: count + 2}
    scratch = [pltpu.VMEM((states, length), BF16)] * 2
    if last:
        blocks = length // GROUP
        extra = [jax.ShapeDtypeStruct((blocks, GROUP, GROUP), BF16)] * 2
        extra += [jax.ShapeDtypeStruct((states, length), BF16)] * 2
        out_shape += extra
        out_specs += [pl.BlockSpec(e.shape, lambda g, at, n=len(e.shape): (0,) * n) for e in extra]
        scratch = []
    grid_spec = pltpu.PrefetchScalarGridSpec(
        num_scalar_prefetch=1,
        grid=(count,),
        in_specs=in_specs,
        out_specs=out_specs,
        scratch_shapes=scratch,
    )
    out = pl.pallas_call(
        functools.partial(local_kernel, first, last, count),
        grid_spec=grid_spec,
        out_shape=out_shape,
        input_output_aliases=aliases,
        compiler_params=pltpu.CompilerParams(vmem_limit_bytes=VMEM_LIMIT),
        cost_estimate=pl.CostEstimate(
            flops=8 * count * length * width * states,
            bytes_accessed=8 * count * length * width,
            transcendentals=0,
        ),
        name="local_states",
    )(at, x, dy, b, c, *args)
    return out[:count], list(out[count:])


def pairs_kernel(xs_ref, ys_ref, b_ref, c_ref, dc_ref, db_ref):
    pair = jnp.where(triangle(GROUP, True), dot(ys_ref[...], xs_ref[...], NT), 0.0).astype(BF16)
    dc_ref[...] = dot(pair, b_ref[...], NN)
    db_ref[...] = dot(pair, c_ref[...], TN)


def pairs_grads(saved, b, c):
    xs, ys = saved[:2]
    length, channels = xs.shape
    states = b.shape[1]
    columns = pl.BlockSpec((GROUP, channels), lambda n: (n, 0))
    maps = pl.BlockSpec((GROUP, states), lambda n: (n, 0))
    return pl.pallas_call(
        pairs_kernel,
        grid=(length // GROUP,),
        in_specs=[columns, columns, maps, maps],
        out_specs=[maps, maps],
        out_shape=[jax.ShapeDtypeStruct((length, states), F32)] * 2,
        compiler_params=pltpu.CompilerParams(vmem_limit_bytes=VMEM_LIMIT),
        cost_estimate=pl.CostEstimate(
            flops=2 * length * GROUP * channels,
            bytes_accessed=4 * length * channels,
            transcendentals=0,
        ),
        name="pairs_grads",
    )(xs, ys, b, c)


def grads_kernel(first, scale, part, half, begin, *refs):
    y_ref, xs_ref, ys_ref, dy_ref, direct_ref, b_ref, c_ref, columns_ref, table_ref = refs[:9]
    raw_ref, bias_ref, rate_ref, bt, ct, left, right, adder = refs[9:17]
    held = refs[17:21]
    refs = refs[21:]
    dc_in, db_in = refs[:2]
    refs = refs[2:]
    if not first:
        par_in = refs[0]
        refs = refs[3:]
    dx_ref, dc_ref, db_ref, draw_ref, par_ref = refs[:5]
    dc_sum, db_sum, terms, dc_old, db_old, sems = refs[5:]
    old = [(dc_in, dc_old, sems.at[0]), (db_in, db_old, sems.at[1])]
    g = pl.program_id(0)
    heads = raw_ref.shape[1]
    length, width = xs_ref.shape
    states = b_ref.shape[1]
    blocks = length // GROUP
    piece = (begin + g) * half + part
    all_heads = columns_ref.shape[1] // 4
    member = head_matrix(heads, width).astype(BF16)
    lower = triangle(GROUP, True)
    rows = [slice(n * GROUP, (n + 1) * GROUP) for n in range(blocks)]

    @pl.when(g == 0)
    def _():
        for source, target, sem in old:
            pltpu.make_async_copy(source, target, sem).start()
        dc_sum[...] = jnp.zeros_like(dc_sum)
        db_sum[...] = jnp.zeros_like(db_sum)
        par_ref[...] = jnp.zeros_like(par_ref) if first else par_in[...]

    own = begin + g == y_ref[0]
    early = jnp.where(own, held[0][...], held[2][...])
    late = jnp.where(own, held[1][...], held[3][...])
    state_early = y_ref[1] == 1
    state = jnp.where(state_early, early, late)
    grad = jnp.where(state_early, late, early)
    table = table_ref[...]
    skip = table[3 * blocks + 1 : 3 * blocks + 2]
    entering_low, ends = [], []
    for n in range(blocks):
        state = table[n : n + 1] * state
        entering_low.append(state.astype(BF16))
        state = state + dot(bt[:, rows[n]], xs_ref[rows[n], :], NN)
        ends.append(state)
    leaving_low, edges = [None] * blocks, [None] * blocks
    for n in reversed(range(blocks)):
        leaving_low[n] = grad.astype(BF16)
        edges[n] = jnp.sum(ends[n] * grad, axis=0, keepdims=True)
        grad = table[n : n + 1] * (grad + dot(ct[:, rows[n]], ys_ref[rows[n], :], NN))
    gain = dot(columns_ref[...], picker(piece, heads, all_heads, width, True), NN)
    for n in range(blocks):
        scaled_x, scaled_dy = xs_ref[rows[n], :], ys_ref[rows[n], :]
        forward = dot(left[n], scaled_x, NN) + dot(c_ref[rows[n], :], entering_low[n], NN)
        backward = dot(right[n], scaled_dy, NN) + dot(b_ref[rows[n], :], leaving_low[n], NN)
        weight = gain[rows[n]]
        dx_ref[rows[n], :] = (weight * backward + skip * dy_ref[rows[n], :].astype(F32)).astype(
            dx_ref.dtype
        )
        v = scaled_x.astype(F32) * backward
        difference = scaled_dy.astype(F32) * forward - v
        hi = difference.astype(BF16)
        lo = (difference - hi.astype(F32)).astype(BF16)
        terms[rows[n], :width] = hi
        terms[rows[n], width : 2 * width] = lo
        terms[rows[n], 2 * width :] = v.astype(BF16)
        dc_sum[n] += dot(scaled_dy, entering_low[n], NT)
        db_sum[n] += dot(scaled_x, leaving_low[n], NT)
    added = dot(terms[...], adder[...], NN).T
    added = [added[:, rows[n]] for n in range(blocks)]
    edge = head_sums(jnp.concatenate(edges + [edges[0]] * (8 - blocks), axis=0), member)
    slopes = running(
        jnp.concatenate([a[:heads] for a in added], axis=0), lower.astype(BF16)
    )
    slope = jnp.concatenate(
        [slopes[n * heads : (n + 1) * heads] + edge[:, n : n + 1] for n in range(blocks)], axis=1
    )
    v = jnp.concatenate([a[heads : 2 * heads] for a in added], axis=1)
    raw = raw_ref[0] + column(bias_ref[...], piece, heads)
    step = softplus(raw)
    draw = (v / step - column(rate_ref[...], piece, heads) * slope) / (1.0 + jnp.exp(-raw))
    draw_ref[0] = draw
    values = (
        jnp.sum(draw, axis=1, keepdims=True),
        jnp.sum(head_sums(direct_ref[...], member), axis=1, keepdims=True),
        -jnp.sum(step * slope, axis=1, keepdims=True),
    )
    for k, value in enumerate(values):
        par_ref[k : k + 1] += lanes_of(value * scale, piece, (heads, par_ref.shape[1]))

    @pl.when(g == pl.num_programs(0) - 1)
    def _():
        for source, target, sem in old:
            pltpu.make_async_copy(source, target, sem).wait()
        for n in range(blocks):
            dc_ref[rows[n], :] = dc_old[rows[n], :] + dc_sum[n]
            db_ref[rows[n], :] = db_old[rows[n], :] + db_sum[n]


def local_grads(part, begin, count, scale, y, saved, dy, b, c, vectors, held, before):
    xs, ys, direct, factor_columns, table, left, right, bt, ct = saved
    raw, bias, rate, _ = vectors
    length, channels = xs.shape
    pieces = 2 * PARTS
    heads = raw.shape[1] // pieces
    raw = raw.reshape(pieces, heads, length)
    width = channels // pieces
    states = b.shape[1]
    blocks = length // GROUP
    half = pieces // 2
    first = before[0] is None
    whole = lambda g, y: (0, 0)
    place = lambda g, y: (0, (begin + g) * half + part)
    columns = pl.BlockSpec((length, width), place)
    maps = pl.BlockSpec((length, states), whole)
    line = pl.BlockSpec(bias.shape, whole)
    lines = pl.BlockSpec((1, heads, length), lambda g, y: ((begin + g) * half + part, 0, 0))
    params = pl.BlockSpec((8, 128), whole)
    anywhere = pl.BlockSpec(memory_space=pl.ANY)
    in_specs = [columns, columns, columns, pl.BlockSpec((8, width), place), maps, maps]
    in_specs += [
        pl.BlockSpec(factor_columns.shape, whole),
        pl.BlockSpec((table.shape[0], width), place),
    ]
    in_specs += [lines, line, line]
    args = [xs, ys, dy, direct, b, c, factor_columns, table, raw, bias, rate]
    fixed = [bt, ct, left, right, adding(width, heads, (0, 0, 1)), *held]
    in_specs += [pl.BlockSpec(a.shape, lambda g, y, n=len(a.shape): (0,) * n) for a in fixed]
    args += fixed
    aliases = {}
    dx, dc, db, draw, par = before
    args += [dc, db]
    in_specs += [anywhere, anywhere]
    if not first:
        args += [par, dx, draw]
        in_specs += [params, anywhere, anywhere]
        aliases = {24: 0, 25: 3}
    grid_spec = pltpu.PrefetchScalarGridSpec(
        num_scalar_prefetch=1,
        grid=(count,),
        in_specs=in_specs,
        out_specs=[columns, maps, maps, lines, params],
        scratch_shapes=[
            pltpu.VMEM((blocks, GROUP, states), F32),
            pltpu.VMEM((blocks, GROUP, states), F32),
            pltpu.VMEM((length, 3 * width), BF16),
            pltpu.VMEM((length, states), F32),
            pltpu.VMEM((length, states), F32),
            pltpu.SemaphoreType.DMA((2,)),
        ],
    )
    return pl.pallas_call(
        functools.partial(grads_kernel, first, scale, part, half, begin),
        grid_spec=grid_spec,
        out_shape=[
            jax.ShapeDtypeStruct((length, channels), BF16),
            jax.ShapeDtypeStruct((length, states), F32),
            jax.ShapeDtypeStruct((length, states), F32),
            jax.ShapeDtypeStruct((pieces, heads, length), F32),
            jax.ShapeDtypeStruct((8, 128), F32),
        ],
        input_output_aliases=aliases,
        compiler_params=pltpu.CompilerParams(vmem_limit_bytes=SMALL_LIMIT),
        cost_estimate=pl.CostEstimate(
            flops=12 * count * length * width * (GROUP + states),
            bytes_accessed=6 * count * length * width,
            transcendentals=0,
        ),
        name="local_grads",
    )(y, *args)


def adding(width, heads, places):
    out = np.zeros((len(places) * width, 128), np.float32)
    size = width // heads
    for k, place in enumerate(places):
        for channel in range(width):
            out[k * width + channel, place * heads + channel // size] = 1.0
    return jnp.asarray(out, BF16)


def lanes_of(values, piece, shape):
    row = lax.broadcasted_iota(jnp.int32, shape, 0)
    col = lax.broadcasted_iota(jnp.int32, shape, 1)
    return jnp.sum(jnp.where(col == row + piece * shape[0], values, 0.0), axis=0, keepdims=True)


def summed_over(value, axis):
    size = lax.axis_size(axis)
    if size & (size - 1):
        return lax.psum(value, axis)
    bit = 1
    while bit < size:
        steps = (bit, 2 * bit, 3 * bit) if 4 * bit <= size else (bit,)
        got = [lax.ppermute(value, axis, [(i, i ^ s) for i in range(size)]) for s in steps]
        value = value + got[0]
        if len(got) == 3:
            value = value + (got[1] + got[2])
        bit *= 4 if len(got) == 3 else 2
    return value


def after(value, *earlier):
    return lax.optimization_barrier((value, *earlier))[0]


def entering(sent, kept, states, token):
    size = lax.axis_size("seq")
    pairs = size // 2
    index = lax.axis_index("seq")
    place, second = index // 2, index % 2 == 1
    swap = [(i, i ^ 1) for i in range(size)]
    both = lambda moves: [(2 * a + y, 2 * b + y) for a, b in moves for y in range(2)]

    def halves(got, copy):
        spans = ((0, states), (states, 2 * states), (2 * states + copy, 2 * states + copy + 1))
        for low, high in spans:
            own, other = kept[low:high], got[low:high]
            yield jnp.where(second, other, own), jnp.where(second, own, other)

    def message_of(up, got, arrived, copy):
        (l1, l2), (k1, k2), (d1, d2) = halves(got, copy)
        message = jnp.where(up, d2 * l1 + l2, k1 + d1 * k2)
        return message if arrived is None else message + d1 * d2 * arrived[:states]

    def shares(is_state, value, got, copy):
        (l1, _), (_, k2), (d1, d2) = halves(got, copy)
        for_first = jnp.where(is_state, value, k2 + d2 * value)
        for_second = jnp.where(is_state, d1 * value + l1, value)
        return jnp.where(second, for_second, for_first), jnp.where(second, for_first, for_second)

    message = sent if token is None else after(sent, *token)
    got = lax.ppermute(message, "seq", swap)
    token = yield message, got
    got = after(got, token)
    lower = place < pairs // 2
    if pairs == 4:
        message = message_of((place == 0) | (place == 2), got, None, 0)
        (_, _), (_, _), (d1, d2) = halves(got, 0)
        message = jnp.concatenate([message, jnp.broadcast_to(d1 * d2, (8, message.shape[1]))])
        near = lax.ppermute(message, "seq", both([(0, 1), (1, 0), (2, 3), (3, 2)]))
        token = yield message, near
        near = after(near, token)
        message = message_of(place == 1, got, near, 1)
        middle = lax.ppermute(message, "seq", both([(1, 2), (2, 1)]))
        far = lax.ppermute(message, "seq", both([(1, 3), (2, 0)]))
        inside = (place == 1) | (place == 2)
        known = jnp.where(inside, near[:states], 0.0)
        mine_early, early = shares(lower, known, got, 2)
        other_early = lax.ppermute(early, "seq", [m for m in swap if m not in ((1, 0), (size - 2, size - 1))])
        token = yield early, far
        far = after(far, token)
        outer = near[states : states + 1] * far + near[:states]
        mine_late, late = shares(~lower, jnp.where(inside, middle, outer), got, 3)
        other_late = lax.ppermute(late, "seq", swap)
        yield late, other_late
    else:
        arrived = []
        for k in range(1, pairs):
            message = message_of(place == k - 1, got, arrived[-1] if arrived else None, min(k, 4))
            routes = both([(k - 1, k), (pairs - k, pairs - k - 1)])
            arrived.append(lax.ppermute(message, "seq", routes))
            token = yield message, arrived[-1]
            arrived[-1] = after(arrived[-1], token)
        start = end = jnp.zeros_like(arrived[0])
        for k in range(1, pairs):
            start = jnp.where(place == k, arrived[k - 1], start)
            end = jnp.where(place == pairs - 1 - k, arrived[k - 1], end)
        mine_early, early = shares(lower, jnp.where(lower, start, end), got, 5)
        mine_late, late = shares(~lower, jnp.where(lower, end, start), got, 6)
        other_early = lax.ppermute(early, "seq", swap)
        other_late = lax.ppermute(late, "seq", swap)
        yield late, other_late
    yield mine_early, mine_late, other_early, other_late


def shards(inputs, input_map, output_map, step_raw, step_bias, decay_rate, skip_gain, cotangent):
    length = inputs.shape[1]
    heads = step_raw.shape[1]
    states = input_map.shape[2]
    x, b, c, dy = inputs[0], input_map[0], output_map[0], cotangent[0]
    vectors = (
        step_raw,
        step_bias.reshape(1, heads),
        decay_rate.reshape(1, heads),
        skip_gain.reshape(1, heads),
    )
    size = lax.axis_size("seq")
    y = lax.axis_index("seq") % 2
    scale = 1.0 / math.sqrt(length * size * lax.axis_size("batch"))

    def local(half, part, count, before):
        at = jnp.reshape(half * PARTS + part, (1,)).astype(jnp.int32)
        last = count == PARTS
        out, saved = local_states(at, count, last, x, dy, b, c, vectors, before)
        return out, saved[:3] + list(before[3:] if before else []) + saved[3:]

    sent, kept = [], []
    saved = None
    for part in range(PARTS):
        out, saved = local(1 - y, part, 1, saved)
        sent += out
    kept, saved = local(y, 0, PARTS, saved)

    transfers = 4 if size == 8 else size // 2 + 1
    order = [(0, 0), (1, 0)] + [
        pick for k in range(1, transfers) for pick in ((0, k), (1, k - 1)) if pick != (1, 0)
    ]
    order.append((1, transfers - 1))
    flows, token = {}, None
    lower = lax.axis_index("seq") < size // 2
    here = jnp.stack([y, lower.astype(y.dtype)]).astype(jnp.int32)
    found = None

    def grads(part, begin, count, token, held):
        *most, final = held
        held = (*most, after(final, token))
        return local_grads(
            part, begin, count, scale, here, saved, dy, b, c, vectors, held, found
        )

    for part, k in order:
        if (part, k) == (1, transfers - 1):
            held = next(flows[0])
            found = grads(0, 0, 1, token, held)
            token = found[-1]
        if k == 0:
            flows[part] = entering(sent[part], kept[part], states, token)
            message, arrived = next(flows[part])
            token = None if part == 0 else message
        else:
            token = flows[part].send(token)[0]
        if (part, k) == (0, 1):
            dc, db = pairs_grads(saved, after(b, token), c)
            token = dc
            found = (None, dc, db, None, None)
    found = grads(0, 1, 1, token, held)
    found = grads(1, 0, 2, found[-1], next(flows[1]))
    dx, dc, db, draw, params = found
    summed = summed_over(summed_over(params, "batch"), "seq")
    return (
        dx[None],
        db[None],
        dc[None],
        draw.reshape(heads, length)[None],
        summed[:2, :heads],
        summed[2, :heads],
    )


def solution(mesh):
    in_specs = (
        P("batch", "seq", None),
        P("batch", "seq", None),
        P("batch", "seq", None),
        P("batch", None, "seq"),
        P(),
        P(),
        P(),
        P("batch", "seq", None),
    )
    out_specs = (
        P("batch", "seq", None),
        P("batch", "seq", None),
        P("batch", "seq", None),
        P("batch", None, "seq"),
        P(),
        P(),
    )
    return jax.shard_map(shards, mesh=mesh, in_specs=in_specs, out_specs=out_specs, check_vma=False)
```
